32 devices in a mesh: ca: 4 (over y, core), fe: 8 (over z, x).
Axes of the slice: x: 2, y: 2, z: 4, core: 2. Of those that a mesh axis runs over, the one named last changes fastest.
Arguments:
- grain_ids: int32 [216, 65536], P(None, ('ca', 'fe')), may hold values from 0 to 4095
- euler_angles: float32 [3, 4096], replicated, may hold values from -3.140625 to 3.140625
- brick_active: int32 [65536], P(('ca', 'fe')), may hold values 0 or 1
- brick_owner: int32 [65536, 1], P(('ca', 'fe')), may hold values from 0 to 31, as said below
- brick_element: int32 [65536], P(('ca', 'fe')), may hold values from 0 to 224, as said below
- displacement: float32 [3, 32, 256], P(None, ('ca', 'fe')), may hold values from -0.3 to 0.3
- stress_old: float32 [6, 8, 7200], P(None, None, ('ca', 'fe')), may hold values from -3 to 3
- resistance: float32 [12, 8, 7200], P(None, None, ('ca', 'fe')), may hold values from 0.2 to 0.8
- quad_weights: int32 [8, 7200], P(None, ('ca', 'fe')), may hold values from 32768 to 98304
Outputs:
- stress_new: float32 [6, 8, 7200], P(None, None, ('ca', 'fe'))
- forces: float32 [3, 32, 256], P(None, ('ca', 'fe'))
The draws below stay inside these ranges and needn't reach their ends.
Inputs may be any that keep to these rules, and one draw needn't show every extreme that they name: `brick_owner`: the bricks of one device name each owner at least 2048 / 64 times and at most 160 times; one owner is named exactly 160 times by the bricks of every device. `brick_element`: every element of every owner is named by at least one brick.
All inputs are finite; a program needn't handle non-finite values. No bound on the sum of `brick_active` on one device may be relied on, other than what follows from the above.
Results may differ from the reference program's by a relative error of at most 0.0002.
Values sent between devices are 32-bit elements; how exact they have to be, the bound alone decides.
No kernel may reach another device: no remote copies, remote signals or barrier semaphores. Data moves between devices by JAX's collectives and lax.ppermute only.
A program may use at most 448 MiB of HBM per device.

```python
import math
import jax
import jax.numpy as jnp
from jax import lax

CELLS = 216
QP = 8
SLIPS = 12
GX = 15
GZL = 1
BR = 2048
GRAINS = 4096
LAYER_NODES = 256
ELEM_DEV = 225
BRICKS = 65536
ELEMS = 7200
NODE_LAYERS = 32
N_CA = 4
N_FE = 8


def brick_plan(key):
    devices = BRICKS // BR
    half_count = BR // 2
    hot_count = devices // 8
    hot_most = 4 * half_count // devices
    key_hot = jax.random.fold_in(key, 101)
    key_rank = jax.random.fold_in(key, 102)
    key_order = jax.random.fold_in(key, 103)
    key_cover = jax.random.fold_in(key, 104)
    key_tail = jax.random.fold_in(key, 105)
    key_extra = jax.random.fold_in(key, 106)
    common_hot = jax.random.randint(key_hot, (), 0, devices, dtype=jnp.int32)
    ranked = jax.vmap(lambda sub_key: jax.random.permutation(sub_key, devices - 1))(jax.random.split(key_rank, devices)).astype(jnp.int32)
    others = (common_hot + 1 + ranked) % devices
    owner_list = jnp.concatenate([jnp.zeros((devices, 1), jnp.int32) + common_hot, others], axis=1)
    sender = jnp.arange(devices, dtype=jnp.int32)[:, None]
    local_index = jnp.arange(half_count, dtype=jnp.int32)[None, :]
    cover_owner = (sender + local_index) % devices
    skew_index = jnp.arange(half_count, dtype=jnp.int32)
    hot_part = skew_index // hot_most
    cold_part = hot_count + (skew_index - hot_count * hot_most) % (devices - hot_count)
    list_index = jnp.where(skew_index < hot_count * hot_most, hot_part, cold_part).astype(jnp.int32)
    skew_owner = jnp.take(owner_list, list_index, axis=1)
    cover_perm = jax.vmap(lambda sub_key: jax.random.permutation(sub_key, ELEM_DEV))(jax.random.split(key_cover, devices)).astype(jnp.int32)
    cover_tail = jax.random.randint(key_tail, (devices, half_count - ELEM_DEV), 0, ELEM_DEV, dtype=jnp.int32)
    cover_table = jnp.concatenate([cover_perm, cover_tail], axis=1)
    cover_element = jnp.take_along_axis(cover_table.T, cover_owner.T, axis=1).T
    skew_element = jax.random.randint(key_extra, (devices, half_count), 0, ELEM_DEV, dtype=jnp.int32)
    owner_all = jnp.concatenate([cover_owner, skew_owner], axis=1).astype(jnp.int32)
    element_all = jnp.concatenate([cover_element, skew_element], axis=1).astype(jnp.int32)
    local_order = jax.vmap(lambda sub_key: jax.random.permutation(sub_key, BR))(jax.random.split(key_order, devices)).astype(jnp.int32)
    owner_all = jnp.take_along_axis(owner_all, local_order, axis=1).reshape(BRICKS)
    element_all = jnp.take_along_axis(element_all, local_order, axis=1).reshape(BRICKS)
    return (owner_all, element_all)


def draw_brick_owner(key, part):
    owner_all, element_all = brick_plan(key)
    return owner_all.reshape(BRICKS, 1).astype(jnp.int32)


def draw_brick_element(key, part):
    owner_all, element_all = brick_plan(key)
    return element_all.astype(jnp.int32)


def draw_grain_ids(key, part):
    owner_all, element_all = brick_plan(key)
    devices = BRICKS // BR
    per_octant = CELLS // 8
    key_dominant = jax.random.fold_in(key, 111)
    key_second = jax.random.fold_in(key, 112)
    key_third = jax.random.fold_in(key, 113)
    key_speckle = jax.random.fold_in(key, 114)
    key_code = jax.random.fold_in(key, 115)
    key_reach_two = jax.random.fold_in(key, 116)
    key_reach_three = jax.random.fold_in(key, 117)
    dominant = jax.random.randint(key_dominant, (devices * ELEM_DEV,), 0, GRAINS, dtype=jnp.int32)
    first_grain = jnp.take(dominant, owner_all * ELEM_DEV + element_all)
    second_grain = jax.random.randint(key_second, (BRICKS,), 0, GRAINS, dtype=jnp.int32)
    third_grain = jax.random.randint(key_third, (BRICKS,), 0, GRAINS, dtype=jnp.int32)
    speckle_grain = jax.random.randint(key_speckle, (CELLS, BRICKS), 0, GRAINS, dtype=jnp.int32)
    mixed_code = jax.random.randint(key_code, (CELLS, BRICKS), 0, 16 * per_octant, dtype=jnp.int32)
    cell_code = mixed_code % per_octant
    second_reach = jnp.repeat(jax.random.randint(key_reach_two, (8, BRICKS), 0, per_octant // 4 + 1, dtype=jnp.int32), per_octant, axis=0)
    third_reach = jnp.repeat(jax.random.randint(key_reach_three, (8, BRICKS), 0, per_octant // 8 + 1, dtype=jnp.int32), per_octant, axis=0)
    grains = jnp.where(cell_code < second_reach, second_grain[None], jnp.where(cell_code >= per_octant - third_reach, third_grain[None], first_grain[None]))
    return jnp.where(mixed_code < per_octant, speckle_grain, grains).astype(jnp.int32)


def with_ends(drawn, own_key, least, top_value):
    spot = [jax.random.randint(jax.random.fold_in(own_key, axis), (), 0, length) for axis, length in enumerate(drawn.shape)]
    main_axis = drawn.shape.index(max(drawn.shape))
    neighbour = spot[:main_axis] + [(spot[main_axis] + 1) % drawn.shape[main_axis]] + spot[main_axis + 1:]
    return drawn.at[tuple(spot)].set(least).at[tuple(neighbour)].set(top_value)


def level_of(key, shape, cuts, low, largest):
    factor_of, own = 1.0, jax.random.fold_in(key, 6)
    for dim, parts in cuts:
        heights = jnp.exp(jax.random.uniform(jax.random.fold_in(own, dim), (parts,), jnp.float32, low / len(cuts), largest / len(cuts)))
        factor_of = factor_of * jnp.repeat(heights, shape[dim] // parts).reshape([-1 if axis == dim else 1 for axis in range(len(shape))])
    return factor_of


def centred(stream_key, extent, deviation, reach, shards=(), kind=jnp.bfloat16):
    level = level_of(stream_key, extent, shards, -0.22, 0.18) if shards else 1.0
    values = jax.random.normal(stream_key, extent, jnp.float32) * deviation * level
    return jnp.minimum(jnp.maximum(values, -reach), reach).astype(kind)


def setup_inputs(seed: int = 0) -> dict:
    streams_of = jax.random.split(jax.random.key(seed), 10)
    return {
        "grain_ids": draw_grain_ids(jax.random.fold_in(streams_of[9], 71), 0),
        "euler_angles": jnp.clip(jax.random.uniform(streams_of[1], (3, GRAINS), jnp.float32, -3.140625, 3.140625), -3.140625, 3.140625),
        "brick_active": with_ends((jax.random.randint(streams_of[2], (BRICKS,), 0, 8) < 7).astype(jnp.int32), jax.random.fold_in(streams_of[2], 1), 0, 1),
        "brick_owner": draw_brick_owner(jax.random.fold_in(streams_of[9], 71), 0),
        "brick_element": draw_brick_element(jax.random.fold_in(streams_of[9], 71), 0),
        "displacement": centred(streams_of[5], (3, NODE_LAYERS, LAYER_NODES), 0.05, 0.3, ((1, 32),), jnp.float32),
        "stress_old": centred(streams_of[6], (6, QP, ELEMS), 0.5, 3.0, ((2, 32),), jnp.float32),
        "resistance": jnp.clip(jnp.exp(math.log(0.8) - 1.3862944 * jax.random.uniform(streams_of[7], (SLIPS, QP, ELEMS), jnp.float32) ** level_of(streams_of[7], (SLIPS, QP, ELEMS), ((2, 32),), -0.2, 0.2)), 0.2, 0.8),
        "quad_weights": with_ends(jax.random.randint(streams_of[8], (QP, ELEMS), 32768, 98305), jax.random.fold_in(streams_of[8], 1), 32768, 98304).astype(jnp.int32),
    }


SLIP_PLANES = [[value / math.sqrt(3.0) for value in row] for row in [[1, 1, 1]] * 3 + [[-1, 1, 1]] * 3 + [[1, -1, 1]] * 3 + [[1, 1, -1]] * 3]
SLIP_DIRECTIONS = [[value / math.sqrt(2.0) for value in row] for row in [[0, 1, -1], [1, 0, -1], [1, -1, 0], [0, 1, -1], [1, 0, 1], [1, 1, 0], [0, 1, 1], [1, 0, -1], [1, 1, 0], [0, 1, 1], [1, 0, 1], [1, -1, 0]]]
LAMBDA_ELASTIC = 1.5
SHEAR_MODULUS = 1.0
RATE_STEP = 0.1
FIXED_POINT = 65536.0

def shape_gradients():
    grad_table = [[[0.0, 0.0, 0.0] for corner in range(8)] for quadrature in range(8)]
    point_offset = 1.0 / math.sqrt(3.0)
    for quadrature in range(8):
        natural = [(2 * (quadrature >> shift_bits & 1) - 1) * point_offset for shift_bits in (2, 1, 0)]
        for corner in range(8):
            sign_list = [2 * (corner >> shift_bits & 1) - 1 for shift_bits in (2, 1, 0)]
            factors = [1.0 + sign_list[axis_id] * natural[axis_id] for axis_id in range(3)]
            for direction in range(3):
                others = 1.0
                for axis_id in range(3):
                    if axis_id != direction:
                        others = others * factors[axis_id]
                grad_table[quadrature][corner][direction] = 2.0 * sign_list[direction] * others / 8.0
    return grad_table

def rotation_table(euler_angles):
    cos_one, sin_one = (jnp.cos(euler_angles[0]), jnp.sin(euler_angles[0]))
    cos_mid, sin_mid = (jnp.cos(euler_angles[1]), jnp.sin(euler_angles[1]))
    cos_two, sin_two = (jnp.cos(euler_angles[2]), jnp.sin(euler_angles[2]))
    entries_list = [cos_one * cos_two - sin_one * sin_two * cos_mid, -cos_one * sin_two - sin_one * cos_two * cos_mid, sin_one * sin_mid, sin_one * cos_two + cos_one * sin_two * cos_mid, -sin_one * sin_two + cos_one * cos_two * cos_mid, -cos_one * sin_mid, sin_two * sin_mid, cos_two * sin_mid, cos_mid]
    return jnp.stack(entries_list).astype(jnp.float32)

def octant_sums(rotation, grain_ids):
    per_octant = grain_ids.shape[0] // 8
    pieces = []
    for octant in range(8):
        picked = jnp.take(rotation, grain_ids[octant * per_octant:(octant + 1) * per_octant], axis=1)
        pieces.append(lax.optimization_barrier(jnp.sum(picked, axis=1)))
    return jnp.concatenate(pieces, axis=0)

def corner_values(padded, layers):
    corners = []
    for corner in range(8):
        step_x, step_y, step_z = (corner >> 2 & 1, corner >> 1 & 1, corner & 1)
        block_values = padded[:, :, step_z:step_z + layers, step_y:step_y + GX, step_x:step_x + GX]
        corners.append(block_values.reshape(3, -1))
    return jnp.stack(corners, axis=1)

def element_update(padded, layers, orient, stress_old, resistance, quad_weights):
    grad_table = jnp.asarray(shape_gradients(), dtype=jnp.float32)
    corners = corner_values(padded, layers)
    gradients = jnp.einsum('cne,qnd->cdqe', corners, grad_table, precision=lax.Precision.HIGHEST)
    strain = [gradients[0, 0], gradients[1, 1], gradients[2, 2], 0.5 * (gradients[1, 2] + gradients[2, 1]), 0.5 * (gradients[0, 2] + gradients[2, 0]), 0.5 * (gradients[0, 1] + gradients[1, 0])]
    volume = strain[0] + strain[1] + strain[2]
    trial_stress = []
    for component in range(6):
        change = 2.0 * SHEAR_MODULUS * strain[component]
        if component < 3:
            change = change + LAMBDA_ELASTIC * volume
        trial_stress.append(stress_old[component] + change)
    frames = orient.reshape(8, 3, 3, -1)
    correction = [jnp.zeros_like(trial_stress[0]) for component in range(6)]
    for system in range(12):
        rotated_dir = [frames[:, row_index, 0] * float(SLIP_DIRECTIONS[system][0]) + frames[:, row_index, 1] * float(SLIP_DIRECTIONS[system][1]) + frames[:, row_index, 2] * float(SLIP_DIRECTIONS[system][2]) for row_index in range(3)]
        rotated_normal = [frames[:, row_index, 0] * float(SLIP_PLANES[system][0]) + frames[:, row_index, 1] * float(SLIP_PLANES[system][1]) + frames[:, row_index, 2] * float(SLIP_PLANES[system][2]) for row_index in range(3)]
        schmid = [rotated_dir[0] * rotated_normal[0], rotated_dir[1] * rotated_normal[1], rotated_dir[2] * rotated_normal[2], 0.5 * (rotated_dir[1] * rotated_normal[2] + rotated_dir[2] * rotated_normal[1]), 0.5 * (rotated_dir[0] * rotated_normal[2] + rotated_dir[2] * rotated_normal[0]), 0.5 * (rotated_dir[0] * rotated_normal[1] + rotated_dir[1] * rotated_normal[0])]
        resolved = trial_stress[0] * schmid[0] + trial_stress[1] * schmid[1] + trial_stress[2] * schmid[2] + 2.0 * (trial_stress[3] * schmid[3] + trial_stress[4] * schmid[4] + trial_stress[5] * schmid[5])
        slip_ratio = resolved / resistance[system]
        slip_step = RATE_STEP * slip_ratio * jnp.abs(slip_ratio)
        correction = [correction[component] + slip_step * schmid[component] for component in range(6)]
    updated = [trial_stress[component] - 2.0 * SHEAR_MODULUS * correction[component] for component in range(6)]
    stress_new = jnp.stack(updated)
    tensor = jnp.stack([jnp.stack([updated[0], updated[5], updated[4]]), jnp.stack([updated[5], updated[1], updated[3]]), jnp.stack([updated[4], updated[3], updated[2]])])
    point_scale = quad_weights.astype(jnp.float32) * (1.0 / (FIXED_POINT * 8.0))
    element_forces = jnp.einsum('cdqe,qnd->cne', tensor * point_scale, grad_table, precision=lax.Precision.HIGHEST)
    component_count = padded.shape[1]
    nodal = jnp.zeros((3, component_count, layers + 1, GX + 1, GX + 1), jnp.float32)
    for corner in range(8):
        step_x, step_y, step_z = (corner >> 2 & 1, corner >> 1 & 1, corner & 1)
        nodal = nodal.at[:, :, step_z:step_z + layers, step_y:step_y + GX, step_x:step_x + GX].add(element_forces[:, corner].reshape(3, component_count, layers, GX, GX))
    return (stress_new, nodal)

def reference(grain_ids, euler_angles, brick_active, brick_owner, brick_element, displacement, stress_old, resistance, quad_weights):
    rotation = rotation_table(euler_angles)
    active = brick_active.astype(jnp.float32)
    block_count = BRICKS // BR
    blocks = jnp.transpose(grain_ids.reshape(CELLS, block_count, BR), (1, 0, 2))
    brick_sums = lax.map(lambda id_block: octant_sums(rotation, id_block), blocks)
    octant_total = jnp.transpose(brick_sums, (1, 0, 2)).reshape(72, BRICKS) * active[None]
    target = (brick_owner[:, 0] * ELEM_DEV + brick_element).astype(jnp.int32)
    gathered = jnp.zeros((72, ELEMS), jnp.float32).at[:, target].add(octant_total)
    counts = jnp.zeros((ELEMS,), jnp.float32).at[target].add(active)
    orient = gathered / (8.0 * jnp.maximum(counts, 1.0))
    layers = N_FE * GZL
    node_field = displacement.reshape(3, N_CA, layers, GX + 1, GX + 1)
    padded = jnp.pad(node_field, ((0, 0), (0, 0), (0, 1), (0, 0), (0, 0)))
    stress_new, nodal = element_update(padded, layers, orient, stress_old, resistance, quad_weights)
    forces = nodal[:, :, :layers].reshape(3, NODE_LAYERS, LAYER_NODES)
    return (stress_new, forces)
```

```python
import functools
import math

import jax
import jax.numpy as jnp
from jax import lax
from jax.experimental import pallas as pl
from jax.experimental.pallas import tpu as pltpu
from jax.sharding import PartitionSpec as P

GX = 15
LANES = 128
COLUMNS = 256
ROWS = 80
QUANTUM = 32767.0

SLIP_PLANES = [
    [value / math.sqrt(3.0) for value in row]
    for row in [[1, 1, 1]] * 3 + [[-1, 1, 1]] * 3 + [[1, -1, 1]] * 3 + [[1, 1, -1]] * 3
]
SLIP_DIRECTIONS = [
    [value / math.sqrt(2.0) for value in row]
    for row in [
        [0, 1, -1],
        [1, 0, -1],
        [1, -1, 0],
        [0, 1, -1],
        [1, 0, 1],
        [1, 1, 0],
        [0, 1, 1],
        [1, 0, -1],
        [1, 1, 0],
        [0, 1, 1],
        [1, 0, 1],
        [1, -1, 0],
    ]
]
LAMBDA_ELASTIC = 1.5
SHEAR_MODULUS = 1.0
RATE_STEP = 0.1
FIXED_POINT = 65536.0


def passed_along(block, axis, distance):
    devices = range(lax.axis_size(axis))
    route = [(i - distance, i) for i in devices if i - distance in devices]
    return lax.ppermute(block, axis, route)


def shape_gradients():
    grad_table = [[[0.0, 0.0, 0.0] for corner in range(8)] for quadrature in range(8)]
    point_offset = 1.0 / math.sqrt(3.0)
    for quadrature in range(8):
        natural = [
            (2 * (quadrature >> shift_bits & 1) - 1) * point_offset for shift_bits in (2, 1, 0)
        ]
        for corner in range(8):
            sign_list = [2 * (corner >> shift_bits & 1) - 1 for shift_bits in (2, 1, 0)]
            factors = [1.0 + sign_list[axis_id] * natural[axis_id] for axis_id in range(3)]
            for direction in range(3):
                others = 1.0
                for axis_id in range(3):
                    if axis_id != direction:
                        others = others * factors[axis_id]
                grad_table[quadrature][corner][direction] = (
                    2.0 * sign_list[direction] * others / 8.0
                )
    return grad_table


def cos_sin(angle):
    square = angle * angle
    cosine = 1.0 / math.factorial(12)
    for power in (10, 8, 6, 4, 2, 0):
        cosine = cosine * square + (-1.0) ** (power // 2) / math.factorial(power)
    sine = 1.0 / math.factorial(13)
    for power in (11, 9, 7, 5, 3, 1):
        sine = sine * square + (-1.0) ** (power // 2) / math.factorial(power)
    return cosine, sine * angle


def quaternion_words(euler_ref):
    cos_one, sin_one = cos_sin(0.5 * euler_ref[0])
    cos_mid, sin_mid = cos_sin(0.5 * euler_ref[1])
    cos_two, sin_two = cos_sin(0.5 * euler_ref[2])
    quaternion = [
        cos_mid * (cos_one * cos_two - sin_one * sin_two),
        sin_mid * (cos_one * cos_two + sin_one * sin_two),
        sin_mid * (sin_one * cos_two - cos_one * sin_two),
        cos_mid * (sin_one * cos_two + cos_one * sin_two),
    ]
    whole = [jnp.round(value * QUANTUM).astype(jnp.int32) for value in quaternion]
    return [
        lax.shift_left(whole[0], 16) | (whole[1] & 0xFFFF),
        lax.shift_left(whole[2], 16) | (whole[3] & 0xFFFF),
    ]


def unpacked(word):
    upper = lax.shift_right_arithmetic(word, 16)
    lower = lax.shift_right_arithmetic(lax.shift_left(word, 16), 16)
    return upper.astype(jnp.float32), lower.astype(jnp.float32)


def looked_up(table_ref, first_row, rows, lane, bits):
    if rows == 1:
        row = jnp.broadcast_to(table_ref[pl.ds(first_row, 1), :], lane.shape)
        return jnp.take_along_axis(row, lane, axis=1, mode="promise_in_bounds")
    half = rows // 2
    level = half.bit_length() - 1
    low = looked_up(table_ref, first_row, half, lane, bits)
    high = looked_up(table_ref, first_row + half, half, lane, bits)
    return jnp.where(bits[level], high, low)


def handover_kernel(
    ids_ref, euler_ref, owner_ref, element_ref, out_ref, table_ref, tile_ref, split_ref, masked_ref
):
    per_octant = ids_ref.shape[0] // 8
    bricks = ids_ref.shape[1]
    table_rows = euler_ref.shape[1]
    owners = out_ref.shape[0]
    words = quaternion_words(euler_ref)
    table_ref[pl.ds(0, table_rows), :] = words[0]
    table_ref[pl.ds(table_rows, table_rows), :] = words[1]

    def tile_sums(tile, carry):
        lanes = pl.ds(pl.multiple_of(tile * LANES, LANES), LANES)
        tile_ref[...] = ids_ref[:, lanes]
        sums = [jnp.zeros((8, LANES), jnp.float32) for pair in range(10)]
        for cell in range(per_octant):
            ids = tile_ref[pl.ds(cell, 8, stride=per_octant), :]
            lane = ids & (LANES - 1)
            row = lax.shift_right_logical(ids, 7)
            bits = [(row & (1 << level)) != 0 for level in range(table_rows.bit_length() - 1)]
            w, x = unpacked(looked_up(table_ref, 0, table_rows, lane, bits))
            y, z = unpacked(looked_up(table_ref, table_rows, table_rows, lane, bits))
            products = [w * w, x * x, y * y, z * z, w * x, w * y, w * z, x * y, x * z, y * z]
            sums = [total + product for total, product in zip(sums, products)]
        scale = 1.0 / (QUANTUM * QUANTUM)
        ww, xx, yy, zz = [value * scale for value in sums[:4]]
        wx, wy, wz, xy, xz, yz = [value * (2.0 * scale) for value in sums[4:]]
        entries = [
            (ww - zz) + (xx - yy),
            xy - wz,
            xz + wy,
            xy + wz,
            (ww - zz) - (xx - yy),
            yz - wx,
            xz - wy,
            yz + wx,
            (ww + zz) - (xx + yy),
        ]
        stacked = jnp.concatenate(entries, axis=0)
        leading = stacked.astype(jnp.bfloat16)
        trailing = (stacked - leading.astype(jnp.float32)).astype(jnp.bfloat16)
        split_ref[:, lanes] = jnp.concatenate([leading, trailing], axis=0)
        return carry

    lax.fori_loop(0, bricks // LANES, tile_sums, 0)

    element = element_ref[...]
    column = lax.broadcasted_iota(jnp.int32, (COLUMNS, bricks), 0)
    chosen = (column == element).astype(jnp.bfloat16)
    split_rows = split_ref.shape[0]
    group = masked_ref.shape[0] // (split_rows + 16)

    def owner_group(step, carry):
        owner = owner_ref[...]
        for member in range(group):
            mask = (owner == step * group + member).astype(jnp.bfloat16)
            first = member * (split_rows + 16)
            masked_ref[pl.ds(first, split_rows), :] = split_ref[...] * mask
            masked_ref[pl.ds(first + split_rows, 16), :] = jnp.broadcast_to(mask, (16, bricks))
        product = lax.dot_general(
            masked_ref[...], chosen, (((1,), (1,)), ((), ())), preferred_element_type=jnp.float32
        )
        for member in range(group):
            first = member * (split_rows + 16)
            half = split_rows // 2
            out_ref[step * group + member, pl.ds(0, half), :] = (
                product[first : first + half] + product[first + half : first + split_rows]
            )
            out_ref[step * group + member, pl.ds(half, 8), :] = product[
                first + split_rows : first + split_rows + 8
            ]
        return carry

    lax.fori_loop(0, owners // group, owner_group, 0)


def handover(grain_ids, euler_angles, owner, element, owners):
    bricks = grain_ids.shape[1]
    table_rows = euler_angles.shape[1] // LANES
    group = 8
    return pl.pallas_call(
        handover_kernel,
        out_shape=jax.ShapeDtypeStruct((owners, ROWS, COLUMNS), jnp.float32),
        scratch_shapes=[
            pltpu.VMEM((2 * table_rows, LANES), jnp.int32),
            pltpu.VMEM((grain_ids.shape[0], LANES), jnp.int32),
            pltpu.VMEM((144, bricks), jnp.bfloat16),
            pltpu.VMEM((group * 160, bricks), jnp.bfloat16),
        ],
        compiler_params=pltpu.CompilerParams(vmem_limit_bytes=48 * 1024 * 1024),
        name="handover",
    )(grain_ids, euler_angles.reshape(3, table_rows, LANES), owner, element)


def three_parts(value):
    first = value.astype(jnp.bfloat16)
    rest = value - first.astype(jnp.float32)
    second = rest.astype(jnp.bfloat16)
    third = (rest - second.astype(jnp.float32)).astype(jnp.bfloat16)
    return first, second, third


def dot_selected(value, selector, contract):
    total = None
    for part in three_parts(value):
        term = lax.dot_general(
            part, selector, (((1,), (contract,)), ((), ())), preferred_element_type=jnp.float32
        )
        total = term if total is None else total + term
    return total


def update_kernel(
    gathered_ref,
    own_ref,
    upper_ref,
    stress_ref,
    resistance_ref,
    weights_ref,
    table_ref,
    stress_out_ref,
    nodal_ref,
):
    elements = stress_ref.shape[2]
    counts = gathered_ref[72:73, 0:elements]
    per_brick = 1.0 / (8.0 * jnp.maximum(counts, 1.0))
    frames = [gathered_ref[8 * k : 8 * k + 8, 0:elements] * per_brick for k in range(9)]

    node = lax.broadcasted_iota(jnp.int32, (COLUMNS, elements), 0)
    element = lax.broadcasted_iota(jnp.int32, (COLUMNS, elements), 1)
    base = element + element // GX
    selectors = [
        (node == base + (step_y * (GX + 1) + step_x)).astype(jnp.bfloat16)
        for step_x in range(2)
        for step_y in range(2)
    ]
    corner = lax.broadcasted_iota(jnp.int32, (24, 1), 0) & 7
    upper_corner = (corner & 1) == 1
    values = jnp.where(
        upper_corner,
        jnp.concatenate([jnp.broadcast_to(upper_ref[c], (8, COLUMNS)) for c in range(3)], axis=0),
        jnp.concatenate([jnp.broadcast_to(own_ref[c], (8, COLUMNS)) for c in range(3)], axis=0),
    )
    corners = jnp.zeros((24, elements), jnp.float32)
    for step in range(4):
        part = jnp.where(corner >> 1 == step, values, 0.0)
        corners = corners + dot_selected(part, selectors[step], 0)
    gradients = []
    for c in range(3):
        product = jnp.dot(
            table_ref[...],
            corners[8 * c : 8 * c + 8],
            precision=lax.Precision.HIGHEST,
            preferred_element_type=jnp.float32,
        )
        gradients.append([product[8 * d : 8 * d + 8] for d in range(3)])
    strain = [
        gradients[0][0],
        gradients[1][1],
        gradients[2][2],
        0.5 * (gradients[1][2] + gradients[2][1]),
        0.5 * (gradients[0][2] + gradients[2][0]),
        0.5 * (gradients[0][1] + gradients[1][0]),
    ]
    volume = strain[0] + strain[1] + strain[2]
    trial = []
    for component in range(6):
        change = 2.0 * SHEAR_MODULUS * strain[component]
        if component < 3:
            change = change + LAMBDA_ELASTIC * volume
        trial.append(stress_ref[component] + change)
    correction = [jnp.zeros_like(trial[0]) for component in range(6)]
    for system in range(12):
        rotated_dir = [
            sum(
                frames[3 * row + axis_id] * SLIP_DIRECTIONS[system][axis_id]
                for axis_id in range(3)
                if SLIP_DIRECTIONS[system][axis_id] != 0.0
            )
            for row in range(3)
        ]
        rotated_normal = [
            sum(frames[3 * row + axis_id] * SLIP_PLANES[system][axis_id] for axis_id in range(3))
            for row in range(3)
        ]
        schmid = [
            rotated_dir[0] * rotated_normal[0],
            rotated_dir[1] * rotated_normal[1],
            rotated_dir[2] * rotated_normal[2],
            0.5 * (rotated_dir[1] * rotated_normal[2] + rotated_dir[2] * rotated_normal[1]),
            0.5 * (rotated_dir[0] * rotated_normal[2] + rotated_dir[2] * rotated_normal[0]),
            0.5 * (rotated_dir[0] * rotated_normal[1] + rotated_dir[1] * rotated_normal[0]),
        ]
        resolved = (
            trial[0] * schmid[0]
            + trial[1] * schmid[1]
            + trial[2] * schmid[2]
            + 2.0 * (trial[3] * schmid[3] + trial[4] * schmid[4] + trial[5] * schmid[5])
        )
        slip_ratio = resolved / resistance_ref[system]
        slip_step = RATE_STEP * slip_ratio * jnp.abs(slip_ratio)
        correction = [
            correction[component] + slip_step * schmid[component] for component in range(6)
        ]
    updated = [
        trial[component] - 2.0 * SHEAR_MODULUS * correction[component] for component in range(6)
    ]
    for component in range(6):
        stress_out_ref[component] = updated[component]
    point_scale = weights_ref[...].astype(jnp.float32) * (1.0 / (FIXED_POINT * 8.0))
    scaled = [value * point_scale for value in updated]
    forces = []
    for rows in [(0, 5, 4), (5, 1, 3), (4, 3, 2)]:
        forces.append(
            lax.dot_general(
                table_ref[...],
                jnp.concatenate([scaled[row] for row in rows], axis=0),
                (((0,), (0,)), ((), ())),
                precision=lax.Precision.HIGHEST,
                preferred_element_type=jnp.float32,
            )
        )
    forces = jnp.concatenate(forces, axis=0)
    nodal = jnp.zeros((24, COLUMNS), jnp.float32)
    for step in range(4):
        part = jnp.where(corner >> 1 == step, forces, 0.0)
        nodal = nodal + dot_selected(part, selectors[step], 1)
    lower = jnp.where(upper_corner, 0.0, nodal)
    above = jnp.where(upper_corner, nodal, 0.0)
    for c in range(3):
        nodal_ref[0, c] = jnp.sum(lower[8 * c : 8 * c + 8], axis=0, keepdims=True)
        nodal_ref[1, c] = jnp.sum(above[8 * c : 8 * c + 8], axis=0, keepdims=True)


def element_update(gathered, own, upper, stress_old, resistance, quad_weights):
    grad_table = shape_gradients()
    table = jnp.asarray(
        [
            [grad_table[quadrature][corner][direction] for corner in range(8)]
            for direction in range(3)
            for quadrature in range(8)
        ],
        dtype=jnp.float32,
    )
    return pl.pallas_call(
        update_kernel,
        out_shape=(
            jax.ShapeDtypeStruct(stress_old.shape, jnp.float32),
            jax.ShapeDtypeStruct((2,) + own.shape, jnp.float32),
        ),
        compiler_params=pltpu.CompilerParams(vmem_limit_bytes=32 * 1024 * 1024),
        name="stress_update",
    )(gathered, own, upper, stress_old, resistance, quad_weights, table)


def body(
    grain_ids,
    euler_angles,
    brick_active,
    brick_owner,
    brick_element,
    displacement,
    stress_old,
    resistance,
    quad_weights,
):
    devices = lax.axis_size("ca") * lax.axis_size("fe")
    bricks = grain_ids.shape[1]
    upper_layer = passed_along(displacement, "fe", -1)
    owner = jnp.where(brick_active > 0, brick_owner[:, 0], -1).reshape(1, bricks)
    partial = handover(grain_ids, euler_angles, owner, brick_element.reshape(1, bricks), devices)
    gathered = lax.psum_scatter(partial, ("ca", "fe"), scatter_dimension=0)
    stress_new, nodal = element_update(
        gathered, displacement, upper_layer, stress_old, resistance, quad_weights
    )
    forces = nodal[0] + passed_along(nodal[1], "fe", 1)
    return (stress_new, forces)


def solution(mesh):
    placed = (
        P(None, ("ca", "fe")),
        P(),
        P(("ca", "fe")),
        P(("ca", "fe"), None),
        P(("ca", "fe")),
        P(None, ("ca", "fe"), None),
        P(None, None, ("ca", "fe")),
        P(None, None, ("ca", "fe")),
        P(None, ("ca", "fe")),
    )
    return jax.shard_map(
        body,
        mesh=mesh,
        in_specs=placed,
        out_specs=(P(None, None, ("ca", "fe")), P(None, ("ca", "fe"), None)),
        check_vma=False,
    )
```

```python
import functools
import math

import jax
import jax.numpy as jnp
from jax import lax
from jax.experimental import pallas as pl
from jax.experimental.pallas import tpu as pltpu
from jax.sharding import PartitionSpec as P

GX = 15
LANES = 128
COLUMNS = 256
ROWS = 72
COUNT_SPAN = 31
SPARE = 11
QUANTUM = float((1 << 20) - 1)

SLIP_PLANES = [
    [value / math.sqrt(3.0) for value in row]
    for row in [[1, 1, 1]] * 3 + [[-1, 1, 1]] * 3 + [[1, -1, 1]] * 3 + [[1, 1, -1]] * 3
]
SLIP_DIRECTIONS = [
    [value / math.sqrt(2.0) for value in row]
    for row in [
        [0, 1, -1],
        [1, 0, -1],
        [1, -1, 0],
        [0, 1, -1],
        [1, 0, 1],
        [1, 1, 0],
        [0, 1, 1],
        [1, 0, -1],
        [1, 1, 0],
        [0, 1, 1],
        [1, 0, 1],
        [1, -1, 0],
    ]
]
LAMBDA_ELASTIC = 1.5
SHEAR_MODULUS = 1.0
RATE_STEP = 0.1
FIXED_POINT = 65536.0


def passed_along(block, axis, distance):
    devices = range(lax.axis_size(axis))
    route = [(i - distance, i) for i in devices if i - distance in devices]
    return lax.ppermute(block, axis, route)


def shape_gradients():
    grad_table = [[[0.0, 0.0, 0.0] for corner in range(8)] for quadrature in range(8)]
    point_offset = 1.0 / math.sqrt(3.0)
    for quadrature in range(8):
        natural = [
            (2 * (quadrature >> shift_bits & 1) - 1) * point_offset for shift_bits in (2, 1, 0)
        ]
        for corner in range(8):
            sign_list = [2 * (corner >> shift_bits & 1) - 1 for shift_bits in (2, 1, 0)]
            factors = [1.0 + sign_list[axis_id] * natural[axis_id] for axis_id in range(3)]
            for direction in range(3):
                others = 1.0
                for axis_id in range(3):
                    if axis_id != direction:
                        others = others * factors[axis_id]
                grad_table[quadrature][corner][direction] = (
                    2.0 * sign_list[direction] * others / 8.0
                )
    return grad_table


def cos_sin(angle):
    square = angle * angle
    cosine = 1.0 / math.factorial(12)
    for power in (10, 8, 6, 4, 2, 0):
        cosine = cosine * square + (-1.0) ** (power // 2) / math.factorial(power)
    sine = 1.0 / math.factorial(13)
    for power in (11, 9, 7, 5, 3, 1):
        sine = sine * square + (-1.0) ** (power // 2) / math.factorial(power)
    return cosine, sine * angle


def rotation_words(euler_ref):
    cos_one, sin_one = cos_sin(0.5 * euler_ref[0])
    cos_mid, sin_mid = cos_sin(0.5 * euler_ref[1])
    cos_two, sin_two = cos_sin(0.5 * euler_ref[2])
    w = cos_mid * (cos_one * cos_two - sin_one * sin_two)
    factor = jnp.where(w < 0.0, -QUANTUM, QUANTUM) / (1.0 + jnp.abs(w))
    x = sin_mid * (cos_one * cos_two + sin_one * sin_two) * factor
    y = sin_mid * (sin_one * cos_two - cos_one * sin_two) * factor
    z = cos_mid * (sin_one * cos_two + cos_one * sin_two) * factor
    x, y, z = [
        jnp.clip(jnp.round(value), -QUANTUM, QUANTUM).astype(jnp.int32) for value in (x, y, z)
    ]
    low = (1 << SPARE) - 1
    return [
        lax.shift_left(x, SPARE) | (lax.shift_right_arithmetic(z, SPARE) & low),
        lax.shift_left(y, SPARE) | (z & low),
    ]


def rotation_products(first, second):
    x = lax.shift_right_arithmetic(first, SPARE).astype(jnp.float32)
    y = lax.shift_right_arithmetic(second, SPARE).astype(jnp.float32)
    z = (
        lax.shift_right_arithmetic(lax.shift_left(first, 32 - SPARE), 32 - 2 * SPARE)
        | (second & ((1 << SPARE) - 1))
    ).astype(jnp.float32)
    square = x * x + y * y + z * z
    scale = 2.0 / (1.0 + square * (1.0 / (QUANTUM * QUANTUM)))
    w = scale - 1.0
    x, y, z = x * scale, y * scale, z * scale
    return [x * x, y * y, z * z, x * y, x * z, y * z, w * x, w * y, w * z]


def looked_up(table_ref, first_row, rows, lane, bits):
    if rows == 1:
        row = jnp.broadcast_to(table_ref[pl.ds(first_row, 1), :], lane.shape)
        return jnp.take_along_axis(row, lane, axis=1, mode="promise_in_bounds")
    half = rows // 2
    level = half.bit_length() - 1
    low = looked_up(table_ref, first_row, half, lane, bits)
    high = looked_up(table_ref, first_row + half, half, lane, bits)
    return jnp.where(bits[level], high, low)


def count_row(element):
    return lax.shift_right_logical(element * (65536 // COUNT_SPAN + 1), 16)


def handover_kernel(
    ids_ref,
    euler_ref,
    place_ref,
    element_ref,
    keep_ref,
    send_ref,
    table_ref,
    tile_ref,
    split_ref,
    masked_ref,
):
    per_octant = ids_ref.shape[0] // 8
    bricks = ids_ref.shape[1]
    table_rows = euler_ref.shape[1]
    half_places = keep_ref.shape[0]
    words = rotation_words(euler_ref)
    table_ref[pl.ds(0, table_rows), :] = words[0]
    table_ref[pl.ds(table_rows, table_rows), :] = words[1]

    def tile_sums(tile, carry):
        lanes = pl.ds(pl.multiple_of(tile * LANES, LANES), LANES)
        tile_ref[...] = ids_ref[:, lanes]
        sums = [jnp.zeros((8, LANES), jnp.float32) for pair in range(9)]
        for cell in range(per_octant):
            ids = tile_ref[pl.ds(cell, 8, stride=per_octant), :]
            lane = ids & (LANES - 1)
            row = lax.shift_right_logical(ids, 7)
            bits = [(row & (1 << level)) != 0 for level in range(table_rows.bit_length() - 1)]
            first = looked_up(table_ref, 0, table_rows, lane, bits)
            second = looked_up(table_ref, table_rows, table_rows, lane, bits)
            sums = [
                total + product
                for total, product in zip(sums, rotation_products(first, second))
            ]
        vector = 2.0 / (QUANTUM * QUANTUM)
        xx, yy, zz, xy, xz, yz = [value * vector for value in sums[:6]]
        wx, wy, wz = [value * (2.0 / QUANTUM) for value in sums[6:]]
        entries = [
            per_octant - (yy + zz),
            xy - wz,
            xz + wy,
            xy + wz,
            per_octant - (xx + zz),
            yz - wx,
            xz - wy,
            yz + wx,
            per_octant - (xx + yy),
        ]
        stacked = jnp.concatenate(entries, axis=0)
        leading = stacked.astype(jnp.bfloat16)
        trailing = (stacked - leading.astype(jnp.float32)).astype(jnp.bfloat16)
        split_ref[pl.ds(0, 2 * ROWS), lanes] = jnp.concatenate([leading, trailing], axis=0)
        return carry

    lax.fori_loop(0, bricks // LANES, tile_sums, 0)

    element = element_ref[...]
    column = lax.broadcasted_iota(jnp.int32, (COLUMNS, bricks), 0)
    row_of = count_row(element)
    chosen = (
        (column == element) | (column == element - row_of * COUNT_SPAN + (COLUMNS - COUNT_SPAN))
    ).astype(jnp.bfloat16)
    split_ref[pl.ds(2 * ROWS, 16), :] = (
        lax.broadcasted_iota(jnp.int32, (16, bricks), 0) == row_of
    ).astype(jnp.bfloat16)
    split_rows = split_ref.shape[0]
    group = masked_ref.shape[0] // split_rows
    in_counts = lax.broadcasted_iota(jnp.int32, (8, COLUMNS), 1) >= COLUMNS - COUNT_SPAN

    for base, out_ref in ((0, keep_ref), (half_places, send_ref)):

        def place_group(step, carry):
            place = place_ref[...] - base
            for member in range(group):
                mask = (place == step * group + member).astype(jnp.bfloat16)
                masked_ref[pl.ds(member * split_rows, split_rows), :] = split_ref[...] * mask
            product = lax.dot_general(
                masked_ref[...],
                chosen,
                (((1,), (1,)), ((), ())),
                preferred_element_type=jnp.float32,
            )
            for member in range(group):
                first = member * split_rows
                total = product[first : first + ROWS] + product[first + ROWS : first + 2 * ROWS]
                counts = product[first + 2 * ROWS : first + 2 * ROWS + 8]
                out_ref[step * group + member, pl.ds(0, 8), :] = jnp.where(
                    in_counts, counts, total[:8]
                )
                out_ref[step * group + member, pl.ds(8, ROWS - 8), :] = total[8:]
            return carry

        lax.fori_loop(0, half_places // group, place_group, 0)


def handover(grain_ids, euler_angles, place, element, places):
    bricks = grain_ids.shape[1]
    table_rows = euler_angles.shape[1] // LANES
    group = 8
    half = jax.ShapeDtypeStruct((places // 2, ROWS, COLUMNS), jnp.float32)
    return pl.pallas_call(
        handover_kernel,
        out_shape=(half, half),
        scratch_shapes=[
            pltpu.VMEM((2 * table_rows, LANES), jnp.int32),
            pltpu.VMEM((grain_ids.shape[0], LANES), jnp.int32),
            pltpu.VMEM((2 * ROWS + 16, bricks), jnp.bfloat16),
            pltpu.VMEM((group * (2 * ROWS + 16), bricks), jnp.bfloat16),
        ],
        compiler_params=pltpu.CompilerParams(vmem_limit_bytes=48 * 1024 * 1024),
        cost_estimate=pl.CostEstimate(
            flops=2 * 160 * places * bricks * COLUMNS,
            bytes_accessed=100 * 1024 * 1024,
            transcendentals=0,
        ),
        name="handover",
    )(grain_ids, euler_angles.reshape(3, table_rows, LANES), place, element)


def three_parts(value):
    first = value.astype(jnp.bfloat16)
    rest = value - first.astype(jnp.float32)
    second = rest.astype(jnp.bfloat16)
    third = (rest - second.astype(jnp.float32)).astype(jnp.bfloat16)
    return first, second, third


def dot_selected(value, selector, contract):
    total = None
    for part in three_parts(value):
        term = lax.dot_general(
            part, selector, (((1,), (contract,)), ((), ())), preferred_element_type=jnp.float32
        )
        total = term if total is None else total + term
    return total


def update_kernel(
    gathered_ref,
    own_ref,
    upper_ref,
    stress_ref,
    resistance_ref,
    weights_ref,
    table_ref,
    stress_out_ref,
    nodal_ref,
):
    elements = stress_ref.shape[2]
    gathered = gathered_ref[0]
    for source in range(1, gathered_ref.shape[0]):
        gathered = gathered + gathered_ref[source]
    element_row = lax.broadcasted_iota(jnp.int32, (8, elements), 1)
    count_at = lax.broadcasted_iota(jnp.int32, (COLUMNS, elements), 1)
    count_at = count_at - count_row(count_at) * COUNT_SPAN + (COLUMNS - COUNT_SPAN)
    spread = dot_selected(
        gathered[:8],
        (lax.broadcasted_iota(jnp.int32, (COLUMNS, elements), 0) == count_at).astype(jnp.bfloat16),
        0,
    )
    in_row = count_row(element_row) == lax.broadcasted_iota(jnp.int32, (8, elements), 0)
    counts = jnp.sum(jnp.where(in_row, spread, 0.0), axis=0, keepdims=True)
    per_brick = 1.0 / (8.0 * jnp.maximum(counts, 1.0))
    frames = [gathered[8 * k : 8 * k + 8, 0:elements] * per_brick for k in range(9)]

    node = lax.broadcasted_iota(jnp.int32, (COLUMNS, elements), 0)
    element = lax.broadcasted_iota(jnp.int32, (COLUMNS, elements), 1)
    base = element + element // GX
    selectors = [
        (node == base + (step_y * (GX + 1) + step_x)).astype(jnp.bfloat16)
        for step_x in range(2)
        for step_y in range(2)
    ]
    corner = lax.broadcasted_iota(jnp.int32, (24, 1), 0) & 7
    upper_corner = (corner & 1) == 1
    values = jnp.where(
        upper_corner,
        jnp.concatenate([jnp.broadcast_to(upper_ref[c], (8, COLUMNS)) for c in range(3)], axis=0),
        jnp.concatenate([jnp.broadcast_to(own_ref[c], (8, COLUMNS)) for c in range(3)], axis=0),
    )
    corners = jnp.zeros((24, elements), jnp.float32)
    for step in range(4):
        part = jnp.where(corner >> 1 == step, values, 0.0)
        corners = corners + dot_selected(part, selectors[step], 0)
    gradients = []
    for c in range(3):
        product = jnp.dot(
            table_ref[...],
            corners[8 * c : 8 * c + 8],
            precision=lax.Precision.HIGHEST,
            preferred_element_type=jnp.float32,
        )
        gradients.append([product[8 * d : 8 * d + 8] for d in range(3)])
    strain = [
        gradients[0][0],
        gradients[1][1],
        gradients[2][2],
        0.5 * (gradients[1][2] + gradients[2][1]),
        0.5 * (gradients[0][2] + gradients[2][0]),
        0.5 * (gradients[0][1] + gradients[1][0]),
    ]
    volume = strain[0] + strain[1] + strain[2]
    trial = []
    for component in range(6):
        change = 2.0 * SHEAR_MODULUS * strain[component]
        if component < 3:
            change = change + LAMBDA_ELASTIC * volume
        trial.append(stress_ref[component] + change)
    correction = [jnp.zeros_like(trial[0]) for component in range(6)]
    for system in range(12):
        rotated_dir = [
            sum(
                frames[3 * row + axis_id] * SLIP_DIRECTIONS[system][axis_id]
                for axis_id in range(3)
                if SLIP_DIRECTIONS[system][axis_id] != 0.0
            )
            for row in range(3)
        ]
        rotated_normal = [
            sum(frames[3 * row + axis_id] * SLIP_PLANES[system][axis_id] for axis_id in range(3))
            for row in range(3)
        ]
        schmid = [
            rotated_dir[0] * rotated_normal[0],
            rotated_dir[1] * rotated_normal[1],
            rotated_dir[2] * rotated_normal[2],
            0.5 * (rotated_dir[1] * rotated_normal[2] + rotated_dir[2] * rotated_normal[1]),
            0.5 * (rotated_dir[0] * rotated_normal[2] + rotated_dir[2] * rotated_normal[0]),
            0.5 * (rotated_dir[0] * rotated_normal[1] + rotated_dir[1] * rotated_normal[0]),
        ]
        resolved = (
            trial[0] * schmid[0]
            + trial[1] * schmid[1]
            + trial[2] * schmid[2]
            + 2.0 * (trial[3] * schmid[3] + trial[4] * schmid[4] + trial[5] * schmid[5])
        )
        slip_ratio = resolved / resistance_ref[system]
        slip_step = RATE_STEP * slip_ratio * jnp.abs(slip_ratio)
        correction = [
            correction[component] + slip_step * schmid[component] for component in range(6)
        ]
    updated = [
        trial[component] - 2.0 * SHEAR_MODULUS * correction[component] for component in range(6)
    ]
    for component in range(6):
        stress_out_ref[component] = updated[component]
    point_scale = weights_ref[...].astype(jnp.float32) * (1.0 / (FIXED_POINT * 8.0))
    scaled = [value * point_scale for value in updated]
    forces = []
    for rows in [(0, 5, 4), (5, 1, 3), (4, 3, 2)]:
        forces.append(
            lax.dot_general(
                table_ref[...],
                jnp.concatenate([scaled[row] for row in rows], axis=0),
                (((0,), (0,)), ((), ())),
                precision=lax.Precision.HIGHEST,
                preferred_element_type=jnp.float32,
            )
        )
    forces = jnp.concatenate(forces, axis=0)
    nodal = jnp.zeros((24, COLUMNS), jnp.float32)
    for step in range(4):
        part = jnp.where(corner >> 1 == step, forces, 0.0)
        nodal = nodal + dot_selected(part, selectors[step], 1)
    lower = jnp.where(upper_corner, 0.0, nodal)
    above = jnp.where(upper_corner, nodal, 0.0)
    for c in range(3):
        nodal_ref[0, c] = jnp.sum(lower[8 * c : 8 * c + 8], axis=0, keepdims=True)
        nodal_ref[1, c] = jnp.sum(above[8 * c : 8 * c + 8], axis=0, keepdims=True)


def element_update(gathered, own, upper, stress_old, resistance, quad_weights):
    grad_table = shape_gradients()
    table = jnp.asarray(
        [
            [grad_table[quadrature][corner][direction] for corner in range(8)]
            for direction in range(3)
            for quadrature in range(8)
        ],
        dtype=jnp.float32,
    )
    return pl.pallas_call(
        update_kernel,
        out_shape=(
            jax.ShapeDtypeStruct(stress_old.shape, jnp.float32),
            jax.ShapeDtypeStruct((2,) + own.shape, jnp.float32),
        ),
        compiler_params=pltpu.CompilerParams(vmem_limit_bytes=32 * 1024 * 1024),
        name="stress_update",
    )(gathered, own, upper, stress_old, resistance, quad_weights, table)


def body(
    grain_ids,
    euler_angles,
    brick_active,
    brick_owner,
    brick_element,
    displacement,
    stress_old,
    resistance,
    quad_weights,
):
    groups, members = lax.axis_size("ca"), lax.axis_size("fe")
    bricks = grain_ids.shape[1]
    upper_layer = passed_along(displacement, "fe", -1)
    owner = brick_owner[:, 0]
    owner_ca, owner_fe = owner // members, owner % members
    other_core = (owner_ca + lax.axis_index("ca")) & 1
    place = ((other_core * (groups // 2) + owner_ca // 2) * members) + owner_fe
    place = jnp.where(brick_active > 0, place, -1).reshape(1, bricks)
    keep, send = handover(
        grain_ids, euler_angles, place, brick_element.reshape(1, bricks), groups * members
    )
    keep = keep + lax.ppermute(send, "ca", [(i, i ^ 1) for i in range(groups)])
    same_core = [
        [(2 * pair + core) * members + member for pair in range(groups // 2) for member in range(members)]
        for core in range(2)
    ]
    gathered = lax.all_to_all(
        keep, ("ca", "fe"), split_axis=0, concat_axis=0, axis_index_groups=same_core, tiled=True
    )
    stress_new, nodal = element_update(
        gathered, displacement, upper_layer, stress_old, resistance, quad_weights
    )
    forces = nodal[0] + passed_along(nodal[1], "fe", 1)
    return (stress_new, forces)


def solution(mesh):
    placed = (
        P(None, ("ca", "fe")),
        P(),
        P(("ca", "fe")),
        P(("ca", "fe"), None),
        P(("ca", "fe")),
        P(None, ("ca", "fe"), None),
        P(None, None, ("ca", "fe")),
        P(None, None, ("ca", "fe")),
        P(None, ("ca", "fe")),
    )
    return jax.shard_map(
        body,
        mesh=mesh,
        in_specs=placed,
        out_specs=(P(None, None, ("ca", "fe")), P(None, ("ca", "fe"), None)),
        check_vma=False,
    )
```

```python
import functools
import functools
import math

import jax
import jax.numpy as jnp
from jax import lax
from jax.experimental import pallas as pl
from jax.experimental.pallas import tpu as pltpu
from jax.sharding import PartitionSpec as P

GX = 15
LANES = 128
COLUMNS = 256
CHUNKS = ((0, 4), (4, 2), (6, 2))
SPARE = 11
QUANTUM = float((1 << 20) - 1)

SLIP_PLANES = [
    [value / math.sqrt(3.0) for value in row]
    for row in [[1, 1, 1]] * 3 + [[-1, 1, 1]] * 3 + [[1, -1, 1]] * 3 + [[1, 1, -1]] * 3
]
SLIP_DIRECTIONS = [
    [value / math.sqrt(2.0) for value in row]
    for row in [
        [0, 1, -1],
        [1, 0, -1],
        [1, -1, 0],
        [0, 1, -1],
        [1, 0, 1],
        [1, 1, 0],
        [0, 1, 1],
        [1, 0, -1],
        [1, 1, 0],
        [0, 1, 1],
        [1, 0, 1],
        [1, -1, 0],
    ]
]
LAMBDA_ELASTIC = 1.5
SHEAR_MODULUS = 1.0
RATE_STEP = 0.1
FIXED_POINT = 65536.0


def passed_along(block, axis, distance):
    devices = range(lax.axis_size(axis))
    route = [(i - distance, i) for i in devices if i - distance in devices]
    return lax.ppermute(block, axis, route)


def shape_gradients():
    grad_table = [[[0.0, 0.0, 0.0] for corner in range(8)] for quadrature in range(8)]
    point_offset = 1.0 / math.sqrt(3.0)
    for quadrature in range(8):
        natural = [
            (2 * (quadrature >> shift_bits & 1) - 1) * point_offset for shift_bits in (2, 1, 0)
        ]
        for corner in range(8):
            sign_list = [2 * (corner >> shift_bits & 1) - 1 for shift_bits in (2, 1, 0)]
            factors = [1.0 + sign_list[axis_id] * natural[axis_id] for axis_id in range(3)]
            for direction in range(3):
                others = 1.0
                for axis_id in range(3):
                    if axis_id != direction:
                        others = others * factors[axis_id]
                grad_table[quadrature][corner][direction] = (
                    2.0 * sign_list[direction] * others / 8.0
                )
    return grad_table


def cos_sin(angle):
    square = angle * angle
    cosine = 1.0 / math.factorial(12)
    for power in (10, 8, 6, 4, 2, 0):
        cosine = cosine * square + (-1.0) ** (power // 2) / math.factorial(power)
    sine = 1.0 / math.factorial(13)
    for power in (11, 9, 7, 5, 3, 1):
        sine = sine * square + (-1.0) ** (power // 2) / math.factorial(power)
    return cosine, sine * angle


def rotation_words(euler):
    cos_one, sin_one = cos_sin(0.5 * euler[0 : 0 + 1])
    cos_mid, sin_mid = cos_sin(0.5 * euler[1 : 1 + 1])
    cos_two, sin_two = cos_sin(0.5 * euler[2 : 2 + 1])
    w = cos_mid * (cos_one * cos_two - sin_one * sin_two)
    factor = jnp.where(w < 0.0, -QUANTUM, QUANTUM) / (1.0 + jnp.abs(w))
    x = sin_mid * (cos_one * cos_two + sin_one * sin_two) * factor
    y = sin_mid * (sin_one * cos_two - cos_one * sin_two) * factor
    z = cos_mid * (sin_one * cos_two + cos_one * sin_two) * factor
    x, y, z = [
        jnp.clip(jnp.round(value), -QUANTUM, QUANTUM).astype(jnp.int32) for value in (x, y, z)
    ]
    low = (1 << SPARE) - 1
    return [
        lax.shift_left(x, SPARE) | (lax.shift_right_arithmetic(z, SPARE) & low),
        lax.shift_left(y, SPARE) | (z & low),
    ]


def rotation_products(first, second):
    x = lax.shift_right_arithmetic(first, SPARE).astype(jnp.float32)
    y = lax.shift_right_arithmetic(second, SPARE).astype(jnp.float32)
    z = (
        lax.shift_right_arithmetic(lax.shift_left(first, 32 - SPARE), 32 - 2 * SPARE)
        | (second & ((1 << SPARE) - 1))
    ).astype(jnp.float32)
    square = x * x + y * y + z * z
    scale = 2.0 / (1.0 + square * (1.0 / (QUANTUM * QUANTUM)))
    w = scale - 1.0
    x, y, z = x * scale, y * scale, z * scale
    return [x * x, y * y, z * z, x * y, x * z, y * z, w * x, w * y, w * z]


def looked_up(table_ref, first_row, rows, lane, bits):
    if rows == 1:
        row = jnp.broadcast_to(table_ref[pl.ds(first_row, 1), :], lane.shape)
        return jnp.take_along_axis(row, lane, axis=1, mode="promise_in_bounds")
    half = rows // 2
    level = half.bit_length() - 1
    low = looked_up(table_ref, first_row, half, lane, bits)
    high = looked_up(table_ref, first_row + half, half, lane, bits)
    return jnp.where(bits[level], high, low)


def cell_sum_kernel(first, count, *refs):
    if first == 0:
        ids_ref, label_ref, euler_ref, split_ref, label_out_ref, table_ref, tile_ref = refs
    else:
        ids_ref, label_ref, table_ref, split_ref, label_out_ref, tile_ref = refs
    per_octant = ids_ref.shape[0] // 8
    table_rows = table_ref.shape[0] // 2
    label_out_ref[...] = label_ref[...]
    if first == 0:
        words = rotation_words(euler_ref[...])
        for word in range(2):
            for row in range(table_rows):
                table_ref[pl.ds(word * table_rows + row, 1), :] = words[word][
                    :, row * LANES : (row + 1) * LANES
                ]
    groups = tile_ref.shape[0] // 8
    rows_left = count * per_octant - 8 * (groups - 1)

    def tile_sums(tile, carry):
        lanes = pl.ds(pl.multiple_of(tile * LANES, LANES), LANES)
        for octant in range(count):
            tile_ref[pl.ds(octant, per_octant, stride=count), :] = ids_ref[
                pl.ds((first + octant) * per_octant, per_octant), lanes
            ]
        sums = [jnp.zeros((8, LANES), jnp.float32) for pair in range(9)]
        for group in range(groups):
            ids = tile_ref[pl.ds(8 * group, 8), :]
            lane = ids & (LANES - 1)
            row = lax.shift_right_logical(ids, 7)
            bits = [(row & (1 << level)) != 0 for level in range(table_rows.bit_length() - 1)]
            leading = looked_up(table_ref, 0, table_rows, lane, bits)
            trailing = looked_up(table_ref, table_rows, table_rows, lane, bits)
            products = rotation_products(leading, trailing)
            if group == groups - 1 and rows_left < 8:
                there = lax.broadcasted_iota(jnp.int32, (8, LANES), 0) < rows_left
                products = [jnp.where(there, product, 0.0) for product in products]
            sums = [total + product for total, product in zip(sums, products)]
        sums = [
            sum(total[count * part : count * (part + 1)] for part in range(8 // count))
            for total in sums
        ]
        vector = 2.0 / (QUANTUM * QUANTUM)
        xx, yy, zz, xy, xz, yz = [value * vector for value in sums[:6]]
        wx, wy, wz = [value * (2.0 / QUANTUM) for value in sums[6:]]
        entries = [
            per_octant - (yy + zz),
            xy - wz,
            xz + wy,
            xy + wz,
            per_octant - (xx + zz),
            yz - wx,
            xz - wy,
            yz + wx,
            per_octant - (xx + yy),
            jnp.ones((split_ref.shape[0] // 2 - 9 * count, LANES), jnp.float32),
        ]
        stacked = jnp.concatenate(entries, axis=0)
        leading = stacked.astype(jnp.bfloat16).astype(jnp.float32)
        split_ref[:, lanes] = jnp.concatenate([leading, stacked - leading], axis=0).astype(
            jnp.bfloat16
        )
        return carry

    lax.fori_loop(0, ids_ref.shape[1] // LANES, tile_sums, 0)


def brick_sum_kernel(split_ref, label_ref, keep_ref, send_ref, label_out_ref, place_ref, masked_ref):
    bricks = split_ref.shape[1]
    half_places = keep_ref.shape[0]
    labels = label_ref[...]
    label_out_ref[...] = labels
    place_ref[...] = jnp.where(
        labels < 0, -1, place_of(lax.shift_right_arithmetic(labels, COLUMNS.bit_length() - 1))
    )
    column = lax.broadcasted_iota(jnp.int32, (COLUMNS, bricks), 0)
    chosen = (column == labels & (COLUMNS - 1)).astype(jnp.bfloat16)
    split_rows = split_ref.shape[0]
    half_rows = split_rows // 2
    members = masked_ref.shape[0] // split_rows
    for base, out_ref in ((half_places, send_ref), (0, keep_ref)):

        def place_group(step, carry):
            place = place_ref[...] - base
            for member in range(members):
                mask = (place == step * members + member).astype(jnp.bfloat16)
                masked_ref[pl.ds(member * split_rows, split_rows), :] = split_ref[...] * mask
            product = lax.dot_general(
                masked_ref[...],
                chosen,
                (((1,), (1,)), ((), ())),
                preferred_element_type=jnp.float32,
            )
            for member in range(members):
                at = member * split_rows
                out_ref[step * members + member] = (
                    product[at : at + half_rows] + product[at + half_rows : at + split_rows]
                )
            return carry

        lax.fori_loop(0, half_places // members, place_group, 0)


def place_of(owner):
    groups, members = lax.axis_size("ca"), lax.axis_size("fe")
    owner_ca = lax.shift_right_logical(owner, members.bit_length() - 1) ^ lax.axis_index("ca")
    owner_fe = (owner & (members - 1)) ^ lax.axis_index("fe")
    place = (owner_ca & 1) * (groups // 2) + lax.shift_right_logical(owner_ca, 1)
    place = place * 2 + (owner_fe & 1)
    return place * (members // 2) + lax.shift_right_logical(owner_fe, 1)


def cell_sums(first, count, grain_ids, labels, table):
    bricks = grain_ids.shape[1]
    per_octant = grain_ids.shape[0] // 8
    out_shape = [
        jax.ShapeDtypeStruct((2 * padded_rows(count), bricks), jnp.bfloat16),
        jax.ShapeDtypeStruct(labels.shape, jnp.int32),
    ]
    if first == 0:
        grains = table.shape[1]
        out_shape.append(jax.ShapeDtypeStruct((2 * grains // LANES, LANES), jnp.int32))
    return pl.pallas_call(
        functools.partial(cell_sum_kernel, first, count),
        out_shape=out_shape,
        scratch_shapes=[pltpu.VMEM((-(-count * per_octant // 8) * 8, LANES), jnp.int32)],
        compiler_params=pltpu.CompilerParams(vmem_limit_bytes=24 * 1024 * 1024),
        cost_estimate=pl.CostEstimate(
            flops=count * 4 * 10**9, bytes_accessed=count * 10**7, transcendentals=0
        ),
        name="cell_sums",
    )(grain_ids, labels, table)


def padded_rows(count):
    return -(-9 * count // 8) * 8


def brick_sums(split, labels, places):
    rows, bricks = split.shape
    members = min(16, places // 2)
    half = jax.ShapeDtypeStruct((places // 2, rows // 2, COLUMNS), jnp.float32)
    return pl.pallas_call(
        brick_sum_kernel,
        out_shape=[half, half, jax.ShapeDtypeStruct(labels.shape, jnp.int32)],
        scratch_shapes=[
            pltpu.VMEM((1, bricks), jnp.int32),
            pltpu.VMEM((members * rows, bricks), jnp.bfloat16),
        ],
        compiler_params=pltpu.CompilerParams(vmem_limit_bytes=32 * 1024 * 1024),
        cost_estimate=pl.CostEstimate(
            flops=rows * 3 * 10**7, bytes_accessed=rows * 10**5, transcendentals=0
        ),
        name="brick_sums",
    )(split, labels)


def part_sum_kernel(terms, passed, *refs):
    flat = sum(terms)
    outs = refs[flat + passed :]
    for index in range(len(outs) - passed):
        at = row = 0
        for group in terms:
            total = refs[at][index]
            for term in refs[at + 1 : at + group]:
                total = total + term[index]
            at += group
            axis = total.ndim - 2
            where = (slice(None),) * axis + (pl.ds(row, total.shape[axis]),)
            outs[index][where] = total
            row += total.shape[axis]
    for i in range(passed):
        outs[len(outs) - passed + i][...] = refs[flat + i][...]


def part_sum(groups, passed, name):
    shape = groups[0][0].shape
    rows = sum(terms[0].shape[-2] for terms in groups)
    part = jax.ShapeDtypeStruct(shape[1:-2] + (rows, shape[-1]), jnp.float32)
    out = pl.pallas_call(
        functools.partial(part_sum_kernel, [len(terms) for terms in groups], len(passed)),
        out_shape=[part] * shape[0]
        + [jax.ShapeDtypeStruct(array.shape, array.dtype) for array in passed],
        name=name,
    )(*[term for terms in groups for term in terms], *passed)
    return out[: shape[0]], *out[shape[0] :]


def to_relative(block, core, pair, last, rest):
    groups, members = lax.axis_size("ca"), lax.axis_size("fe")
    flip = (2 * pair + core) * members + 2 * rest + last
    return lax.ppermute(block, ("ca", "fe"), [(i, i ^ flip) for i in range(groups * members)])


def across_cores(keep, send):
    pairs, rests = lax.axis_size("ca") // 2, lax.axis_size("fe") // 2
    split = (2 * pairs, rests) + keep.shape[1:]
    return [keep.reshape(split), to_relative(send, 1, 0, 0, 0).reshape(split)]


def across_plane(parts):
    return [parts[0]] + [
        to_relative(parts[index], 0, index // 2, index % 2, 0) for index in range(1, len(parts))
    ]


def across_height(parts):
    return [parts[0]] + [to_relative(parts[rest], 0, 0, 0, rest) for rest in range(1, len(parts))]


def three_parts(value):
    first = value.astype(jnp.bfloat16)
    rest = value - first.astype(jnp.float32)
    second = rest.astype(jnp.bfloat16)
    third = (rest - second.astype(jnp.float32)).astype(jnp.bfloat16)
    return first, second, third


def dot_selected(value, selector, contract):
    total = None
    for part in three_parts(value):
        term = lax.dot_general(
            part, selector, (((1,), (contract,)), ((), ())), preferred_element_type=jnp.float32
        )
        total = term if total is None else total + term
    return total


def update_kernel(sources, *refs):
    own_ref, upper_ref, stress_ref, resistance_ref, weights_ref, table_ref = refs[2 * sources : -2]
    stress_out_ref, nodal_ref = refs[-2:]
    elements = stress_ref.shape[2]
    gathered = [
        sum(ref[:, 0:elements] for ref in refs[at : at + sources]) for at in (0, sources)
    ]
    chunk_sums = [
        gathered[0],
        gathered[1][: padded_rows(CHUNKS[1][1])],
        gathered[1][padded_rows(CHUNKS[1][1]) :],
    ]
    counts = gathered[0][9 * CHUNKS[0][1] : 9 * CHUNKS[0][1] + 1]
    per_brick = 1.0 / (8.0 * jnp.maximum(counts, 1.0))
    frames = [
        jnp.concatenate(
            [
                sums[count * k : count * (k + 1)]
                for sums, (first, count) in zip(chunk_sums, CHUNKS)
            ],
            axis=0,
        )
        * per_brick
        for k in range(9)
    ]

    node = lax.broadcasted_iota(jnp.int32, (COLUMNS, elements), 0)
    element = lax.broadcasted_iota(jnp.int32, (COLUMNS, elements), 1)
    base = element + element // GX
    selectors = [
        (node == base + (step_y * (GX + 1) + step_x)).astype(jnp.bfloat16)
        for step_x in range(2)
        for step_y in range(2)
    ]
    corner = lax.broadcasted_iota(jnp.int32, (24, 1), 0) & 7
    upper_corner = (corner & 1) == 1
    values = jnp.where(
        upper_corner,
        jnp.concatenate([jnp.broadcast_to(upper_ref[c], (8, COLUMNS)) for c in range(3)], axis=0),
        jnp.concatenate([jnp.broadcast_to(own_ref[c], (8, COLUMNS)) for c in range(3)], axis=0),
    )
    corners = jnp.zeros((24, elements), jnp.float32)
    for step in range(4):
        part = jnp.where(corner >> 1 == step, values, 0.0)
        corners = corners + dot_selected(part, selectors[step], 0)
    gradients = []
    for c in range(3):
        product = jnp.dot(
            table_ref[...],
            corners[8 * c : 8 * c + 8],
            precision=lax.Precision.HIGHEST,
            preferred_element_type=jnp.float32,
        )
        gradients.append([product[8 * d : 8 * d + 8] for d in range(3)])
    strain = [
        gradients[0][0],
        gradients[1][1],
        gradients[2][2],
        0.5 * (gradients[1][2] + gradients[2][1]),
        0.5 * (gradients[0][2] + gradients[2][0]),
        0.5 * (gradients[0][1] + gradients[1][0]),
    ]
    volume = strain[0] + strain[1] + strain[2]
    trial = []
    for component in range(6):
        change = 2.0 * SHEAR_MODULUS * strain[component]
        if component < 3:
            change = change + LAMBDA_ELASTIC * volume
        trial.append(stress_ref[component] + change)
    correction = [jnp.zeros_like(trial[0]) for component in range(6)]
    for system in range(12):
        rotated_dir = [
            sum(
                frames[3 * row + axis_id] * SLIP_DIRECTIONS[system][axis_id]
                for axis_id in range(3)
                if SLIP_DIRECTIONS[system][axis_id] != 0.0
            )
            for row in range(3)
        ]
        rotated_normal = [
            sum(frames[3 * row + axis_id] * SLIP_PLANES[system][axis_id] for axis_id in range(3))
            for row in range(3)
        ]
        schmid = [
            rotated_dir[0] * rotated_normal[0],
            rotated_dir[1] * rotated_normal[1],
            rotated_dir[2] * rotated_normal[2],
            0.5 * (rotated_dir[1] * rotated_normal[2] + rotated_dir[2] * rotated_normal[1]),
            0.5 * (rotated_dir[0] * rotated_normal[2] + rotated_dir[2] * rotated_normal[0]),
            0.5 * (rotated_dir[0] * rotated_normal[1] + rotated_dir[1] * rotated_normal[0]),
        ]
        resolved = (
            trial[0] * schmid[0]
            + trial[1] * schmid[1]
            + trial[2] * schmid[2]
            + 2.0 * (trial[3] * schmid[3] + trial[4] * schmid[4] + trial[5] * schmid[5])
        )
        slip_ratio = resolved / resistance_ref[system]
        slip_step = RATE_STEP * slip_ratio * jnp.abs(slip_ratio)
        correction = [
            correction[component] + slip_step * schmid[component] for component in range(6)
        ]
    updated = [
        trial[component] - 2.0 * SHEAR_MODULUS * correction[component] for component in range(6)
    ]
    for component in range(6):
        stress_out_ref[component] = updated[component]
    point_scale = weights_ref[...].astype(jnp.float32) * (1.0 / (FIXED_POINT * 8.0))
    scaled = [value * point_scale for value in updated]
    forces = []
    for rows in [(0, 5, 4), (5, 1, 3), (4, 3, 2)]:
        forces.append(
            lax.dot_general(
                table_ref[...],
                jnp.concatenate([scaled[row] for row in rows], axis=0),
                (((0,), (0,)), ((), ())),
                precision=lax.Precision.HIGHEST,
                preferred_element_type=jnp.float32,
            )
        )
    forces = jnp.concatenate(forces, axis=0)
    nodal = jnp.zeros((24, COLUMNS), jnp.float32)
    for step in range(4):
        part = jnp.where(corner >> 1 == step, forces, 0.0)
        nodal = nodal + dot_selected(part, selectors[step], 1)
    lower = jnp.where(upper_corner, 0.0, nodal)
    above = jnp.where(upper_corner, nodal, 0.0)
    for c in range(3):
        nodal_ref[0, c] = jnp.sum(lower[8 * c : 8 * c + 8], axis=0, keepdims=True)
        nodal_ref[1, c] = jnp.sum(above[8 * c : 8 * c + 8], axis=0, keepdims=True)


def element_update(gathered, own, upper, stress_old, resistance, quad_weights):
    grad_table = shape_gradients()
    table = jnp.asarray(
        [
            [grad_table[quadrature][corner][direction] for corner in range(8)]
            for direction in range(3)
            for quadrature in range(8)
        ],
        dtype=jnp.float32,
    )
    return pl.pallas_call(
        functools.partial(update_kernel, len(gathered) // 2),
        out_shape=(
            jax.ShapeDtypeStruct(stress_old.shape, jnp.float32),
            jax.ShapeDtypeStruct((2,) + own.shape, jnp.float32),
        ),
        compiler_params=pltpu.CompilerParams(vmem_limit_bytes=32 * 1024 * 1024),
        name="stress_update",
    )(*gathered, own, upper, stress_old, resistance, quad_weights, table)


def body(
    grain_ids,
    euler_angles,
    brick_active,
    brick_owner,
    brick_element,
    displacement,
    stress_old,
    resistance,
    quad_weights,
):
    places = lax.axis_size("ca") * lax.axis_size("fe")
    bricks = grain_ids.shape[1]
    upper_layer = passed_along(displacement, "fe", -1)
    labels = jnp.where(
        brick_active > 0, brick_owner[:, 0] * COLUMNS + brick_element, -1
    ).reshape(1, bricks)
    (first_a, count_a), (first_b, count_b), (first_c, count_c) = CHUNKS
    split_a, labels, table = cell_sums(first_a, count_a, grain_ids, labels, euler_angles)
    keep_a, send_a, labels = brick_sums(split_a, labels, places)
    split_b, labels = cell_sums(first_b, count_b, grain_ids, labels, table)
    core_a, labels, upper_layer = part_sum(
        [across_cores(keep_a, send_a)], [labels, upper_layer], "core_sum_a"
    )
    keep_b, send_b, labels = brick_sums(split_b, labels, places)
    split_c, labels = cell_sums(first_c, count_c, grain_ids, labels, table)
    plane_a, labels = part_sum([across_plane(core_a)], [labels], "plane_sum_a")
    core_b, labels = part_sum([across_cores(keep_b, send_b)], [labels], "core_sum_b")
    keep_c, send_c, labels = brick_sums(split_c, labels, places)
    core_c, labels = part_sum([across_cores(keep_c, send_c)], [labels], "core_sum_c")
    plane_bc, labels = part_sum(
        [across_plane(core_b), across_plane(core_c)], [labels], "plane_sum_b_c"
    )
    gathered = across_height(plane_a) + across_height(plane_bc)
    stress_new, nodal = element_update(
        gathered, displacement, upper_layer, stress_old, resistance, quad_weights
    )
    forces = nodal[0] + passed_along(nodal[1], "fe", 1)
    return (stress_new, forces)


def solution(mesh):
    placed = (
        P(None, ("ca", "fe")),
        P(),
        P(("ca", "fe")),
        P(("ca", "fe"), None),
        P(("ca", "fe")),
        P(None, ("ca", "fe"), None),
        P(None, None, ("ca", "fe")),
        P(None, None, ("ca", "fe")),
        P(None, ("ca", "fe")),
    )
    return jax.shard_map(
        body,
        mesh=mesh,
        in_specs=placed,
        out_specs=(P(None, None, ("ca", "fe")), P(None, ("ca", "fe"), None)),
        check_vma=False,
    )
```

```python
import functools
import functools
import math

import jax
import jax.numpy as jnp
from jax import lax
from jax.experimental import pallas as pl
from jax.experimental.pallas import tpu as pltpu
from jax.sharding import PartitionSpec as P

GX = 15
LANES = 128
COLUMNS = 256
CHUNKS = ((0, 4), (4, 4))
SPARE = 11
QUANTUM = float((1 << 20) - 1)

SLIP_PLANES = [
    [value / math.sqrt(3.0) for value in row]
    for row in [[1, 1, 1]] * 3 + [[-1, 1, 1]] * 3 + [[1, -1, 1]] * 3 + [[1, 1, -1]] * 3
]
SLIP_DIRECTIONS = [
    [value / math.sqrt(2.0) for value in row]
    for row in [
        [0, 1, -1],
        [1, 0, -1],
        [1, -1, 0],
        [0, 1, -1],
        [1, 0, 1],
        [1, 1, 0],
        [0, 1, 1],
        [1, 0, -1],
        [1, 1, 0],
        [0, 1, 1],
        [1, 0, 1],
        [1, -1, 0],
    ]
]
LAMBDA_ELASTIC = 1.5
SHEAR_MODULUS = 1.0
RATE_STEP = 0.1
FIXED_POINT = 65536.0


def passed_along(block, axis, distance):
    devices = range(lax.axis_size(axis))
    route = [(i - distance, i) for i in devices if i - distance in devices]
    return lax.ppermute(block, axis, route)


def shape_gradients():
    grad_table = [[[0.0, 0.0, 0.0] for corner in range(8)] for quadrature in range(8)]
    point_offset = 1.0 / math.sqrt(3.0)
    for quadrature in range(8):
        natural = [
            (2 * (quadrature >> shift_bits & 1) - 1) * point_offset for shift_bits in (2, 1, 0)
        ]
        for corner in range(8):
            sign_list = [2 * (corner >> shift_bits & 1) - 1 for shift_bits in (2, 1, 0)]
            factors = [1.0 + sign_list[axis_id] * natural[axis_id] for axis_id in range(3)]
            for direction in range(3):
                others = 1.0
                for axis_id in range(3):
                    if axis_id != direction:
                        others = others * factors[axis_id]
                grad_table[quadrature][corner][direction] = (
                    2.0 * sign_list[direction] * others / 8.0
                )
    return grad_table


def cos_sin(angle):
    square = angle * angle
    cosine = 1.0 / math.factorial(12)
    for power in (10, 8, 6, 4, 2, 0):
        cosine = cosine * square + (-1.0) ** (power // 2) / math.factorial(power)
    sine = 1.0 / math.factorial(13)
    for power in (11, 9, 7, 5, 3, 1):
        sine = sine * square + (-1.0) ** (power // 2) / math.factorial(power)
    return cosine, sine * angle


def rotation_words(euler):
    cos_one, sin_one = cos_sin(0.5 * euler[0 : 0 + 1])
    cos_mid, sin_mid = cos_sin(0.5 * euler[1 : 1 + 1])
    cos_two, sin_two = cos_sin(0.5 * euler[2 : 2 + 1])
    w = cos_mid * (cos_one * cos_two - sin_one * sin_two)
    factor = jnp.where(w < 0.0, -QUANTUM, QUANTUM) / (1.0 + jnp.abs(w))
    x = sin_mid * (cos_one * cos_two + sin_one * sin_two) * factor
    y = sin_mid * (sin_one * cos_two - cos_one * sin_two) * factor
    z = cos_mid * (sin_one * cos_two + cos_one * sin_two) * factor
    x, y, z = [
        jnp.clip(jnp.round(value), -QUANTUM, QUANTUM).astype(jnp.int32) for value in (x, y, z)
    ]
    low = (1 << SPARE) - 1
    return [
        lax.shift_left(x, SPARE) | (lax.shift_right_arithmetic(z, SPARE) & low),
        lax.shift_left(y, SPARE) | (z & low),
    ]


def rotation_products(first, second):
    x = lax.shift_right_arithmetic(first, SPARE).astype(jnp.float32)
    y = lax.shift_right_arithmetic(second, SPARE).astype(jnp.float32)
    z = (
        lax.shift_right_arithmetic(lax.shift_left(first, 32 - SPARE), 32 - 2 * SPARE)
        | (second & ((1 << SPARE) - 1))
    ).astype(jnp.float32)
    square = x * x + y * y + z * z
    scale = 2.0 / (1.0 + square * (1.0 / (QUANTUM * QUANTUM)))
    w = scale - 1.0
    x, y, z = x * scale, y * scale, z * scale
    return [x * x, y * y, z * z, x * y, x * z, y * z, w * x, w * y, w * z]


def looked_up(table_ref, first_row, rows, lane, bits):
    if rows == 1:
        row = jnp.broadcast_to(table_ref[pl.ds(first_row, 1), :], lane.shape[:2])
        return lax.gather(
            row,
            lane,
            lax.GatherDimensionNumbers(
                offset_dims=(),
                collapsed_slice_dims=(1,),
                start_index_map=(1,),
                operand_batching_dims=(0,),
                start_indices_batching_dims=(0,),
            ),
            slice_sizes=(1, 1),
            mode=lax.GatherScatterMode.PROMISE_IN_BOUNDS,
        )
    half = rows // 2
    level = half.bit_length() - 1
    low = looked_up(table_ref, first_row, half, lane, bits)
    high = looked_up(table_ref, first_row + half, half, lane, bits)
    return jnp.where(bits[level], high, low)


def cell_sum_kernel(first, count, *refs):
    if first == 0:
        ids_ref, label_ref, euler_ref, split_ref, label_out_ref, table_ref, tile_ref = refs
    else:
        ids_ref, label_ref, table_ref, split_ref, label_out_ref, tile_ref = refs
    per_octant = ids_ref.shape[0] // 8
    table_rows = table_ref.shape[0] // 2
    label_out_ref[...] = label_ref[...]
    if first == 0:
        words = rotation_words(euler_ref[...])
        for word in range(2):
            for row in range(table_rows):
                table_ref[pl.ds(word * table_rows + row, 1), :] = words[word][
                    :, row * LANES : (row + 1) * LANES
                ]
    groups = tile_ref.shape[0] // 8
    rows_left = count * per_octant - 8 * (groups - 1)

    def tile_sums(tile, carry):
        lanes = pl.ds(pl.multiple_of(tile * LANES, LANES), LANES)
        for octant in range(count):
            tile_ref[pl.ds(octant, per_octant, stride=count), :] = ids_ref[
                pl.ds((first + octant) * per_octant, per_octant), lanes
            ]
        sums = [jnp.zeros((8, LANES), jnp.float32) for pair in range(9)]
        for group in range(groups):
            ids = tile_ref[pl.ds(8 * group, 8), :]
            lane = (ids & (LANES - 1))[:, :, None]
            row = lax.shift_right_logical(ids, 7)
            bits = [(row & (1 << level)) != 0 for level in range(table_rows.bit_length() - 1)]
            leading = looked_up(table_ref, 0, table_rows, lane, bits)
            trailing = looked_up(table_ref, table_rows, table_rows, lane, bits)
            products = rotation_products(leading, trailing)
            if group == groups - 1 and rows_left < 8:
                there = lax.broadcasted_iota(jnp.int32, (8, LANES), 0) < rows_left
                products = [jnp.where(there, product, 0.0) for product in products]
            sums = [total + product for total, product in zip(sums, products)]
        sums = [
            sum(total[count * part : count * (part + 1)] for part in range(8 // count))
            for total in sums
        ]
        vector = 2.0 / (QUANTUM * QUANTUM)
        xx, yy, zz, xy, xz, yz = [value * vector for value in sums[:6]]
        wx, wy, wz = [value * (2.0 / QUANTUM) for value in sums[6:]]
        entries = [
            per_octant - (yy + zz),
            xy - wz,
            xz + wy,
            xy + wz,
            per_octant - (xx + zz),
            yz - wx,
            xz - wy,
            yz + wx,
            per_octant - (xx + yy),
            jnp.ones((split_ref.shape[0] // 2 - 9 * count, LANES), jnp.float32),
        ]
        stacked = jnp.concatenate(entries, axis=0)
        leading = stacked.astype(jnp.bfloat16).astype(jnp.float32)
        split_ref[:, lanes] = jnp.concatenate([leading, stacked - leading], axis=0).astype(
            jnp.bfloat16
        )
        return carry

    lax.fori_loop(0, ids_ref.shape[1] // LANES, tile_sums, 0)


def brick_sum_kernel(split_ref, label_ref, keep_ref, send_ref, label_out_ref, place_ref, masked_ref):
    bricks = split_ref.shape[1]
    half_places = keep_ref.shape[0]
    labels = label_ref[...]
    label_out_ref[...] = labels
    place_ref[...] = jnp.where(
        labels < 0, -1, place_of(lax.shift_right_arithmetic(labels, COLUMNS.bit_length() - 1))
    )
    column = lax.broadcasted_iota(jnp.int32, (COLUMNS, bricks), 0)
    chosen = (column == labels & (COLUMNS - 1)).astype(jnp.bfloat16)
    split_rows = split_ref.shape[0]
    half_rows = split_rows // 2
    members = masked_ref.shape[0] // split_rows
    for base, out_ref in ((half_places, send_ref), (0, keep_ref)):

        def place_group(step, carry):
            place = place_ref[...] - base
            for member in range(members):
                mask = (place == step * members + member).astype(jnp.bfloat16)
                masked_ref[pl.ds(member * split_rows, split_rows), :] = split_ref[...] * mask
            product = lax.dot_general(
                masked_ref[...],
                chosen,
                (((1,), (1,)), ((), ())),
                preferred_element_type=jnp.float32,
            )
            for member in range(members):
                at = member * split_rows
                out_ref[step * members + member] = (
                    product[at : at + half_rows] + product[at + half_rows : at + split_rows]
                )
            return carry

        lax.fori_loop(0, half_places // members, place_group, 0)


def place_of(owner):
    groups, members = lax.axis_size("ca"), lax.axis_size("fe")
    owner_ca = lax.shift_right_logical(owner, members.bit_length() - 1) ^ lax.axis_index("ca")
    owner_fe = (owner & (members - 1)) ^ lax.axis_index("fe")
    place = (owner_ca & 1) * (groups // 2) + lax.shift_right_logical(owner_ca, 1)
    place = place * 2 + (owner_fe & 1)
    return place * (members // 2) + lax.shift_right_logical(owner_fe, 1)


def cell_sums(first, count, grain_ids, labels, table):
    bricks = grain_ids.shape[1]
    per_octant = grain_ids.shape[0] // 8
    out_shape = [
        jax.ShapeDtypeStruct((2 * padded_rows(count), bricks), jnp.bfloat16),
        jax.ShapeDtypeStruct(labels.shape, jnp.int32),
    ]
    if first == 0:
        grains = table.shape[1]
        out_shape.append(jax.ShapeDtypeStruct((2 * grains // LANES, LANES), jnp.int32))
    return pl.pallas_call(
        functools.partial(cell_sum_kernel, first, count),
        out_shape=out_shape,
        scratch_shapes=[pltpu.VMEM((-(-count * per_octant // 8) * 8, LANES), jnp.int32)],
        compiler_params=pltpu.CompilerParams(vmem_limit_bytes=8 * 1024 * 1024),
        cost_estimate=pl.CostEstimate(
            flops=count * 4 * 10**9, bytes_accessed=count * 10**7, transcendentals=0
        ),
        name="cell_sums",
    )(grain_ids, labels, table)


def padded_rows(count):
    return -(-9 * count // 8) * 8


def brick_sums(split, labels, places):
    rows, bricks = split.shape
    members = min(16, places // 2)
    half = jax.ShapeDtypeStruct((places // 2, rows // 2, COLUMNS), jnp.float32)
    return pl.pallas_call(
        brick_sum_kernel,
        out_shape=[half, half, jax.ShapeDtypeStruct(labels.shape, jnp.int32)],
        scratch_shapes=[
            pltpu.VMEM((1, bricks), jnp.int32),
            pltpu.VMEM((members * rows, bricks), jnp.bfloat16),
        ],
        compiler_params=pltpu.CompilerParams(vmem_limit_bytes=24 * 1024 * 1024),
        cost_estimate=pl.CostEstimate(
            flops=rows * 3 * 10**7, bytes_accessed=rows * 10**5, transcendentals=0
        ),
        name="brick_sums",
    )(split, labels)


def part_sum_kernel(terms, passed, *refs):
    flat = sum(terms)
    outs = refs[flat + passed :]
    for index in range(len(outs) - passed):
        at = row = 0
        for group in terms:
            total = refs[at][index]
            for term in refs[at + 1 : at + group]:
                total = total + term[index]
            at += group
            axis = total.ndim - 2
            where = (slice(None),) * axis + (pl.ds(row, total.shape[axis]),)
            outs[index][where] = total
            row += total.shape[axis]
    for i in range(passed):
        outs[len(outs) - passed + i][...] = refs[flat + i][...]


def part_sum(groups, passed, name):
    shape = groups[0][0].shape
    rows = sum(terms[0].shape[-2] for terms in groups)
    part = jax.ShapeDtypeStruct(shape[1:-2] + (rows, shape[-1]), jnp.float32)
    out = pl.pallas_call(
        functools.partial(part_sum_kernel, [len(terms) for terms in groups], len(passed)),
        out_shape=[part] * shape[0]
        + [jax.ShapeDtypeStruct(array.shape, array.dtype) for array in passed],
        compiler_params=pltpu.CompilerParams(vmem_limit_bytes=16 * 1024 * 1024),
        name=name,
    )(*[term for terms in groups for term in terms], *passed)
    return out[: shape[0]], *out[shape[0] :]


def to_relative(block, core, pair, last, rest):
    groups, members = lax.axis_size("ca"), lax.axis_size("fe")
    flip = (2 * pair + core) * members + 2 * rest + last
    return lax.ppermute(block, ("ca", "fe"), [(i, i ^ flip) for i in range(groups * members)])


def across_cores(keep, send):
    pairs, rests = lax.axis_size("ca") // 2, lax.axis_size("fe") // 2
    split = (2 * pairs, rests) + keep.shape[1:]
    return [keep.reshape(split), to_relative(send, 1, 0, 0, 0).reshape(split)]


def across_plane(parts):
    return [parts[0]] + [
        to_relative(parts[index], 0, index // 2, index % 2, 0) for index in range(1, len(parts))
    ]


def across_height(parts):
    return [parts[0]] + [to_relative(parts[rest], 0, 0, 0, rest) for rest in range(1, len(parts))]


def three_parts(value):
    first = value.astype(jnp.bfloat16)
    rest = value - first.astype(jnp.float32)
    second = rest.astype(jnp.bfloat16)
    third = (rest - second.astype(jnp.float32)).astype(jnp.bfloat16)
    return first, second, third


def dot_selected(value, selector, contract):
    total = None
    for part in three_parts(value):
        term = lax.dot_general(
            part, selector, (((1,), (contract,)), ((), ())), preferred_element_type=jnp.float32
        )
        total = term if total is None else total + term
    return total


def update_kernel(sources, *refs):
    own_ref, upper_ref, stress_ref, resistance_ref, weights_ref, table_ref = refs[2 * sources : -2]
    stress_out_ref, nodal_ref = refs[-2:]
    elements = stress_ref.shape[2]
    gathered = [
        sum(ref[:, 0:elements] for ref in refs[at : at + sources]) for at in (0, sources)
    ]
    counts = gathered[0][9 * CHUNKS[0][1] : 9 * CHUNKS[0][1] + 1]
    per_brick = 1.0 / (8.0 * jnp.maximum(counts, 1.0))
    frames = [
        jnp.concatenate(
            [
                sums[count * k : count * (k + 1)]
                for sums, (first, count) in zip(gathered, CHUNKS)
            ],
            axis=0,
        )
        * per_brick
        for k in range(9)
    ]

    node = lax.broadcasted_iota(jnp.int32, (COLUMNS, elements), 0)
    element = lax.broadcasted_iota(jnp.int32, (COLUMNS, elements), 1)
    base = element + element // GX
    selectors = [
        (node == base + (step_y * (GX + 1) + step_x)).astype(jnp.bfloat16)
        for step_x in range(2)
        for step_y in range(2)
    ]
    corner = lax.broadcasted_iota(jnp.int32, (24, 1), 0) & 7
    upper_corner = (corner & 1) == 1
    values = jnp.where(
        upper_corner,
        jnp.concatenate([jnp.broadcast_to(upper_ref[c], (8, COLUMNS)) for c in range(3)], axis=0),
        jnp.concatenate([jnp.broadcast_to(own_ref[c], (8, COLUMNS)) for c in range(3)], axis=0),
    )
    corners = jnp.zeros((24, elements), jnp.float32)
    for step in range(4):
        part = jnp.where(corner >> 1 == step, values, 0.0)
        corners = corners + dot_selected(part, selectors[step], 0)
    gradients = []
    for c in range(3):
        product = jnp.dot(
            table_ref[...],
            corners[8 * c : 8 * c + 8],
            precision=lax.Precision.HIGHEST,
            preferred_element_type=jnp.float32,
        )
        gradients.append([product[8 * d : 8 * d + 8] for d in range(3)])
    strain = [
        gradients[0][0],
        gradients[1][1],
        gradients[2][2],
        0.5 * (gradients[1][2] + gradients[2][1]),
        0.5 * (gradients[0][2] + gradients[2][0]),
        0.5 * (gradients[0][1] + gradients[1][0]),
    ]
    volume = strain[0] + strain[1] + strain[2]
    trial = []
    for component in range(6):
        change = 2.0 * SHEAR_MODULUS * strain[component]
        if component < 3:
            change = change + LAMBDA_ELASTIC * volume
        trial.append(stress_ref[component] + change)
    correction = [jnp.zeros_like(trial[0]) for component in range(6)]
    for system in range(12):
        rotated_dir = [
            sum(
                frames[3 * row + axis_id] * SLIP_DIRECTIONS[system][axis_id]
                for axis_id in range(3)
                if SLIP_DIRECTIONS[system][axis_id] != 0.0
            )
            for row in range(3)
        ]
        rotated_normal = [
            sum(frames[3 * row + axis_id] * SLIP_PLANES[system][axis_id] for axis_id in range(3))
            for row in range(3)
        ]
        schmid = [
            rotated_dir[0] * rotated_normal[0],
            rotated_dir[1] * rotated_normal[1],
            rotated_dir[2] * rotated_normal[2],
            0.5 * (rotated_dir[1] * rotated_normal[2] + rotated_dir[2] * rotated_normal[1]),
            0.5 * (rotated_dir[0] * rotated_normal[2] + rotated_dir[2] * rotated_normal[0]),
            0.5 * (rotated_dir[0] * rotated_normal[1] + rotated_dir[1] * rotated_normal[0]),
        ]
        resolved = (
            trial[0] * schmid[0]
            + trial[1] * schmid[1]
            + trial[2] * schmid[2]
            + 2.0 * (trial[3] * schmid[3] + trial[4] * schmid[4] + trial[5] * schmid[5])
        )
        slip_ratio = resolved / resistance_ref[system]
        slip_step = RATE_STEP * slip_ratio * jnp.abs(slip_ratio)
        correction = [
            correction[component] + slip_step * schmid[component] for component in range(6)
        ]
    updated = [
        trial[component] - 2.0 * SHEAR_MODULUS * correction[component] for component in range(6)
    ]
    for component in range(6):
        stress_out_ref[component] = updated[component]
    point_scale = weights_ref[...].astype(jnp.float32) * (1.0 / (FIXED_POINT * 8.0))
    scaled = [value * point_scale for value in updated]
    forces = []
    for rows in [(0, 5, 4), (5, 1, 3), (4, 3, 2)]:
        forces.append(
            lax.dot_general(
                table_ref[...],
                jnp.concatenate([scaled[row] for row in rows], axis=0),
                (((0,), (0,)), ((), ())),
                precision=lax.Precision.HIGHEST,
                preferred_element_type=jnp.float32,
            )
        )
    forces = jnp.concatenate(forces, axis=0)
    nodal = jnp.zeros((24, COLUMNS), jnp.float32)
    for step in range(4):
        part = jnp.where(corner >> 1 == step, forces, 0.0)
        nodal = nodal + dot_selected(part, selectors[step], 1)
    lower = jnp.where(upper_corner, 0.0, nodal)
    above = jnp.where(upper_corner, nodal, 0.0)
    for c in range(3):
        nodal_ref[0, c] = jnp.sum(lower[8 * c : 8 * c + 8], axis=0, keepdims=True)
        nodal_ref[1, c] = jnp.sum(above[8 * c : 8 * c + 8], axis=0, keepdims=True)


def element_update(gathered, own, upper, stress_old, resistance, quad_weights):
    grad_table = shape_gradients()
    table = jnp.asarray(
        [
            [grad_table[quadrature][corner][direction] for corner in range(8)]
            for direction in range(3)
            for quadrature in range(8)
        ],
        dtype=jnp.float32,
    )
    return pl.pallas_call(
        functools.partial(update_kernel, len(gathered) // 2),
        out_shape=(
            jax.ShapeDtypeStruct(stress_old.shape, jnp.float32),
            jax.ShapeDtypeStruct((2,) + own.shape, jnp.float32),
        ),
        compiler_params=pltpu.CompilerParams(vmem_limit_bytes=8 * 1024 * 1024),
        name="stress_update",
    )(*gathered, own, upper, stress_old, resistance, quad_weights, table)


def body(
    grain_ids,
    euler_angles,
    brick_active,
    brick_owner,
    brick_element,
    displacement,
    stress_old,
    resistance,
    quad_weights,
):
    places = lax.axis_size("ca") * lax.axis_size("fe")
    bricks = grain_ids.shape[1]
    upper_layer = passed_along(displacement, "fe", -1)
    owner = lax.optimization_barrier(brick_owner.reshape(bricks))
    labels = jnp.where(brick_active > 0, owner * COLUMNS + brick_element, -1).reshape(1, bricks)
    (first_a, count_a), (first_b, count_b) = CHUNKS
    split_a, labels, table = cell_sums(first_a, count_a, grain_ids, labels, euler_angles)
    keep_a, send_a, labels = brick_sums(split_a, labels, places)
    split_b, labels = cell_sums(first_b, count_b, grain_ids, labels, table)
    core_a, labels = part_sum([across_cores(keep_a, send_a)], [labels], "core_sum_a")
    keep_b, send_b, labels = brick_sums(split_b, labels, places)
    core_b, labels = part_sum([across_cores(keep_b, send_b)], [labels], "core_sum_b")
    plane_a, labels = part_sum([across_plane(core_a)], [labels], "plane_sum_a")
    plane_b, labels = part_sum([across_plane(core_b)], [labels], "plane_sum_b")
    gathered = across_height(plane_a) + across_height(plane_b)
    stress_new, nodal = element_update(
        gathered, displacement, upper_layer, stress_old, resistance, quad_weights
    )
    forces = nodal[0] + passed_along(nodal[1], "fe", 1)
    return (stress_new, forces)


def solution(mesh):
    placed = (
        P(None, ("ca", "fe")),
        P(),
        P(("ca", "fe")),
        P(("ca", "fe"), None),
        P(("ca", "fe")),
        P(None, ("ca", "fe"), None),
        P(None, None, ("ca", "fe")),
        P(None, None, ("ca", "fe")),
        P(None, ("ca", "fe")),
    )
    return jax.shard_map(
        body,
        mesh=mesh,
        in_specs=placed,
        out_specs=(P(None, None, ("ca", "fe")), P(None, ("ca", "fe"), None)),
        check_vma=False,
    )
```

```python
import functools
import functools
import math

import jax
import jax.numpy as jnp
from jax import lax
from jax.experimental import pallas as pl
from jax.experimental.pallas import tpu as pltpu
from jax.sharding import PartitionSpec as P

GX = 15
LANES = 128
COLUMNS = 256
CHUNKS = ((0, 4), (4, 4))
SPARE = 11
QUANTUM = float((1 << 20) - 1)

SLIP_PLANES = [
    [value / math.sqrt(3.0) for value in row]
    for row in [[1, 1, 1]] * 3 + [[-1, 1, 1]] * 3 + [[1, -1, 1]] * 3 + [[1, 1, -1]] * 3
]
SLIP_DIRECTIONS = [
    [value / math.sqrt(2.0) for value in row]
    for row in [
        [0, 1, -1],
        [1, 0, -1],
        [1, -1, 0],
        [0, 1, -1],
        [1, 0, 1],
        [1, 1, 0],
        [0, 1, 1],
        [1, 0, -1],
        [1, 1, 0],
        [0, 1, 1],
        [1, 0, 1],
        [1, -1, 0],
    ]
]
LAMBDA_ELASTIC = 1.5
SHEAR_MODULUS = 1.0
RATE_STEP = 0.1
FIXED_POINT = 65536.0


def passed_along(block, axis, distance):
    devices = range(lax.axis_size(axis))
    route = [(i - distance, i) for i in devices if i - distance in devices]
    return lax.ppermute(block, axis, route)


def shape_gradients():
    grad_table = [[[0.0, 0.0, 0.0] for corner in range(8)] for quadrature in range(8)]
    point_offset = 1.0 / math.sqrt(3.0)
    for quadrature in range(8):
        natural = [
            (2 * (quadrature >> shift_bits & 1) - 1) * point_offset for shift_bits in (2, 1, 0)
        ]
        for corner in range(8):
            sign_list = [2 * (corner >> shift_bits & 1) - 1 for shift_bits in (2, 1, 0)]
            factors = [1.0 + sign_list[axis_id] * natural[axis_id] for axis_id in range(3)]
            for direction in range(3):
                others = 1.0
                for axis_id in range(3):
                    if axis_id != direction:
                        others = others * factors[axis_id]
                grad_table[quadrature][corner][direction] = (
                    2.0 * sign_list[direction] * others / 8.0
                )
    return grad_table


def cos_sin(angle):
    square = angle * angle
    cosine = 1.0 / math.factorial(12)
    for power in (10, 8, 6, 4, 2, 0):
        cosine = cosine * square + (-1.0) ** (power // 2) / math.factorial(power)
    sine = 1.0 / math.factorial(13)
    for power in (11, 9, 7, 5, 3, 1):
        sine = sine * square + (-1.0) ** (power // 2) / math.factorial(power)
    return cosine, sine * angle


def rotation_words(euler):
    cos_one, sin_one = cos_sin(0.5 * euler[0 : 0 + 1])
    cos_mid, sin_mid = cos_sin(0.5 * euler[1 : 1 + 1])
    cos_two, sin_two = cos_sin(0.5 * euler[2 : 2 + 1])
    w = cos_mid * (cos_one * cos_two - sin_one * sin_two)
    factor = jnp.where(w < 0.0, -QUANTUM, QUANTUM) / (1.0 + jnp.abs(w))
    x = sin_mid * (cos_one * cos_two + sin_one * sin_two) * factor
    y = sin_mid * (sin_one * cos_two - cos_one * sin_two) * factor
    z = cos_mid * (sin_one * cos_two + cos_one * sin_two) * factor
    x, y, z = [
        jnp.clip(jnp.round(value), -QUANTUM, QUANTUM).astype(jnp.int32) for value in (x, y, z)
    ]
    low = (1 << SPARE) - 1
    return [
        lax.shift_left(x, SPARE) | (lax.shift_right_arithmetic(z, SPARE) & low),
        lax.shift_left(y, SPARE) | (z & low),
    ]


def rotation_products(first, second):
    x = lax.shift_right_arithmetic(first, SPARE).astype(jnp.float32)
    y = lax.shift_right_arithmetic(second, SPARE).astype(jnp.float32)
    z = (
        lax.shift_right_arithmetic(lax.shift_left(first, 32 - SPARE), 32 - 2 * SPARE)
        | (second & ((1 << SPARE) - 1))
    ).astype(jnp.float32)
    square = x * x + y * y + z * z
    scale = 2.0 / (1.0 + square * (1.0 / (QUANTUM * QUANTUM)))
    w = scale - 1.0
    x, y, z = x * scale, y * scale, z * scale
    return [x * x, y * y, z * z, x * y, x * z, y * z, w * x, w * y, w * z]


def looked_up(table_ref, first_row, rows, lane, bits):
    if rows == 1:
        return lax.gather(
            table_ref[first_row],
            lane,
            lax.GatherDimensionNumbers(
                offset_dims=(),
                collapsed_slice_dims=(1,),
                start_index_map=(1,),
                operand_batching_dims=(0,),
                start_indices_batching_dims=(0,),
            ),
            slice_sizes=(1, 1),
            mode=lax.GatherScatterMode.PROMISE_IN_BOUNDS,
        )
    half = rows // 2
    level = half.bit_length() - 1
    low = looked_up(table_ref, first_row, half, lane, bits)
    high = looked_up(table_ref, first_row + half, half, lane, bits)
    return jnp.where(bits[level], high, low)


def cell_sum_kernel(first, count, *refs):
    if first == 0:
        ids_ref, label_ref, euler_ref, split_ref, label_out_ref, table_ref, tile_ref = refs
    else:
        ids_ref, label_ref, table_ref, split_ref, label_out_ref, tile_ref = refs
    per_octant = ids_ref.shape[0] // 8
    table_rows = table_ref.shape[0] // 2
    label_out_ref[...] = label_ref[...]
    if first == 0:
        words = rotation_words(euler_ref[...])
        for word in range(2):
            for row in range(table_rows):
                table_ref[word * table_rows + row] = jnp.broadcast_to(
                    words[word][:, row * LANES : (row + 1) * LANES], (8, LANES)
                )
    groups = tile_ref.shape[0] // 8
    rows_left = count * per_octant - 8 * (groups - 1)

    def tile_sums(tile, carry):
        lanes = pl.ds(pl.multiple_of(tile * LANES, LANES), LANES)
        for octant in range(count):
            tile_ref[pl.ds(octant, per_octant, stride=count), :] = ids_ref[
                pl.ds((first + octant) * per_octant, per_octant), lanes
            ]
        sums = [jnp.zeros((8, LANES), jnp.float32) for pair in range(9)]
        for group in range(groups):
            ids = tile_ref[pl.ds(8 * group, 8), :]
            lane = (ids & (LANES - 1))[:, :, None]
            row = lax.shift_right_logical(ids, 7)
            bits = [(row & (1 << level)) != 0 for level in range(table_rows.bit_length() - 1)]
            leading = looked_up(table_ref, 0, table_rows, lane, bits)
            trailing = looked_up(table_ref, table_rows, table_rows, lane, bits)
            products = rotation_products(leading, trailing)
            if group == groups - 1 and rows_left < 8:
                there = lax.broadcasted_iota(jnp.int32, (8, LANES), 0) < rows_left
                products = [jnp.where(there, product, 0.0) for product in products]
            sums = [total + product for total, product in zip(sums, products)]
        sums = [
            sum(total[count * part : count * (part + 1)] for part in range(8 // count))
            for total in sums
        ]
        vector = 2.0 / (QUANTUM * QUANTUM)
        xx, yy, zz, xy, xz, yz = [value * vector for value in sums[:6]]
        wx, wy, wz = [value * (2.0 / QUANTUM) for value in sums[6:]]
        entries = [
            per_octant - (yy + zz),
            xy - wz,
            xz + wy,
            xy + wz,
            per_octant - (xx + zz),
            yz - wx,
            xz - wy,
            yz + wx,
            per_octant - (xx + yy),
            jnp.ones((split_ref.shape[0] // 2 - 9 * count, LANES), jnp.float32),
        ]
        stacked = jnp.concatenate(entries, axis=0)
        leading = stacked.astype(jnp.bfloat16).astype(jnp.float32)
        split_ref[:, lanes] = jnp.concatenate([leading, stacked - leading], axis=0).astype(
            jnp.bfloat16
        )
        return carry

    lax.fori_loop(0, ids_ref.shape[1] // LANES, tile_sums, 0)


def brick_sum_kernel(base, split_ref, label_ref, out_ref, label_out_ref, place_ref, masked_ref):
    bricks = split_ref.shape[1]
    labels = label_ref[...]
    label_out_ref[...] = labels
    place = place_of(lax.shift_right_arithmetic(labels, COLUMNS.bit_length() - 1))
    place_ref[...] = jnp.where(labels < 0, -1, place - base)
    column = lax.broadcasted_iota(jnp.int32, (COLUMNS, bricks), 0)
    chosen = (column == labels & (COLUMNS - 1)).astype(jnp.bfloat16)
    split_rows = split_ref.shape[0]
    half_rows = split_rows // 2
    members = masked_ref.shape[0] // split_rows

    def place_group(step, carry):
        for member in range(members):
            mask = (place_ref[...] == step * members + member).astype(jnp.bfloat16)
            masked_ref[pl.ds(member * split_rows, split_rows), :] = split_ref[...] * mask
        product = lax.dot_general(
            masked_ref[...],
            chosen,
            (((1,), (1,)), ((), ())),
            preferred_element_type=jnp.float32,
        )
        for member in range(members):
            at = member * split_rows
            out_ref[step * members + member] = (
                product[at : at + half_rows] + product[at + half_rows : at + split_rows]
            )
        return carry

    lax.fori_loop(0, out_ref.shape[0] // members, place_group, 0)


def place_of(owner):
    groups, members = lax.axis_size("ca"), lax.axis_size("fe")
    owner_ca = lax.shift_right_logical(owner, members.bit_length() - 1) ^ lax.axis_index("ca")
    owner_fe = (owner & (members - 1)) ^ lax.axis_index("fe")
    place = (owner_ca & 1) * (groups // 2) + lax.shift_right_logical(owner_ca, 1)
    place = place * 2 + (owner_fe & 1)
    return place * (members // 2) + lax.shift_right_logical(owner_fe, 1)


def cell_sums(first, count, grain_ids, labels, table):
    bricks = grain_ids.shape[1]
    per_octant = grain_ids.shape[0] // 8
    out_shape = [
        jax.ShapeDtypeStruct((2 * padded_rows(count), bricks), jnp.bfloat16),
        jax.ShapeDtypeStruct(labels.shape, jnp.int32),
    ]
    if first == 0:
        grains = table.shape[1]
        out_shape.append(jax.ShapeDtypeStruct((2 * grains // LANES, 8, LANES), jnp.int32))
    return pl.pallas_call(
        functools.partial(cell_sum_kernel, first, count),
        out_shape=out_shape,
        scratch_shapes=[pltpu.VMEM((-(-count * per_octant // 8) * 8, LANES), jnp.int32)],
        compiler_params=pltpu.CompilerParams(vmem_limit_bytes=8 * 1024 * 1024),
        cost_estimate=pl.CostEstimate(
            flops=count * 4 * 10**9, bytes_accessed=count * 10**7, transcendentals=0
        ),
        name="cell_sums",
    )(grain_ids, labels, table)


def padded_rows(count):
    return -(-9 * count // 8) * 8


def brick_sums(split, labels, places, base):
    rows, bricks = split.shape
    members = min(16, places)
    return pl.pallas_call(
        functools.partial(brick_sum_kernel, base),
        out_shape=[
            jax.ShapeDtypeStruct((places, rows // 2, COLUMNS), jnp.float32),
            jax.ShapeDtypeStruct(labels.shape, jnp.int32),
        ],
        scratch_shapes=[
            pltpu.VMEM((1, bricks), jnp.int32),
            pltpu.VMEM((members * rows, bricks), jnp.bfloat16),
        ],
        compiler_params=pltpu.CompilerParams(vmem_limit_bytes=24 * 1024 * 1024),
        cost_estimate=pl.CostEstimate(
            flops=rows * 15 * 10**6, bytes_accessed=rows * 5 * 10**4, transcendentals=0
        ),
        name="brick_sums",
    )(split, labels)


def part_sum_kernel(terms, passed, *refs):
    flat = sum(terms)
    outs = refs[flat + passed :]
    for index in range(len(outs) - passed):
        at = row = 0
        for group in terms:
            total = refs[at][index]
            for term in refs[at + 1 : at + group]:
                total = total + term[index]
            at += group
            axis = total.ndim - 2
            where = (slice(None),) * axis + (pl.ds(row, total.shape[axis]),)
            outs[index][where] = total
            row += total.shape[axis]
    for i in range(passed):
        outs[len(outs) - passed + i][...] = refs[flat + i][...]


def part_sum(groups, passed, name):
    shape = groups[0][0].shape
    rows = sum(terms[0].shape[-2] for terms in groups)
    part = jax.ShapeDtypeStruct(shape[1:-2] + (rows, shape[-1]), jnp.float32)
    out = pl.pallas_call(
        functools.partial(part_sum_kernel, [len(terms) for terms in groups], len(passed)),
        out_shape=[part] * shape[0]
        + [jax.ShapeDtypeStruct(array.shape, array.dtype) for array in passed],
        compiler_params=pltpu.CompilerParams(vmem_limit_bytes=16 * 1024 * 1024),
        name=name,
    )(*[term for terms in groups for term in terms], *passed)
    return out[: shape[0]], *out[shape[0] :]


def to_relative(block, core, pair, last, rest):
    groups, members = lax.axis_size("ca"), lax.axis_size("fe")
    flip = (2 * pair + core) * members + 2 * rest + last
    return lax.ppermute(block, ("ca", "fe"), [(i, i ^ flip) for i in range(groups * members)])


def across_cores(keep, send):
    pairs, rests = lax.axis_size("ca") // 2, lax.axis_size("fe") // 2
    split = (2 * pairs, rests) + keep.shape[1:]
    return [keep.reshape(split), to_relative(send, 1, 0, 0, 0).reshape(split)]


def across_plane(parts):
    return [parts[0]] + [
        to_relative(parts[index], 0, index // 2, index % 2, 0) for index in range(1, len(parts))
    ]


def across_height(parts):
    return [parts[0]] + [to_relative(parts[rest], 0, 0, 0, rest) for rest in range(1, len(parts))]


def three_parts(value):
    first = value.astype(jnp.bfloat16)
    rest = value - first.astype(jnp.float32)
    second = rest.astype(jnp.bfloat16)
    third = (rest - second.astype(jnp.float32)).astype(jnp.bfloat16)
    return first, second, third


def dot_selected(value, selector, contract):
    total = None
    for part in three_parts(value):
        term = lax.dot_general(
            part, selector, (((1,), (contract,)), ((), ())), preferred_element_type=jnp.float32
        )
        total = term if total is None else total + term
    return total


def update_kernel(sources, *refs):
    own_ref, layers_ref, stress_ref, resistance_ref, weights_ref, table_ref = refs[2 * sources : -2]
    stress_out_ref, nodal_ref = refs[-2:]
    elements = stress_ref.shape[2]
    gathered = [
        sum(ref[:, 0:elements] for ref in refs[at : at + sources]) for at in (0, sources)
    ]
    counts = gathered[0][9 * CHUNKS[0][1] : 9 * CHUNKS[0][1] + 1]
    per_brick = 1.0 / (8.0 * jnp.maximum(counts, 1.0))
    frames = [
        jnp.concatenate(
            [
                sums[count * k : count * (k + 1)]
                for sums, (first, count) in zip(gathered, CHUNKS)
            ],
            axis=0,
        )
        * per_brick
        for k in range(9)
    ]

    node = lax.broadcasted_iota(jnp.int32, (COLUMNS, elements), 0)
    element = lax.broadcasted_iota(jnp.int32, (COLUMNS, elements), 1)
    base = element + element // GX
    selectors = [
        (node == base + (step_y * (GX + 1) + step_x)).astype(jnp.bfloat16)
        for step_x in range(2)
        for step_y in range(2)
    ]
    corner = lax.broadcasted_iota(jnp.int32, (24, 1), 0) & 7
    upper_corner = (corner & 1) == 1
    above = lax.axis_index("fe") + 1
    clamped = above == layers_ref.shape[0]
    above = jnp.minimum(above, layers_ref.shape[0] - 1)
    free = jnp.where(clamped, 0.0, 1.0)
    values = jnp.where(
        upper_corner,
        jnp.concatenate(
            [jnp.broadcast_to(layers_ref[above, c] * free, (8, COLUMNS)) for c in range(3)], axis=0
        ),
        jnp.concatenate([jnp.broadcast_to(own_ref[c], (8, COLUMNS)) for c in range(3)], axis=0),
    )
    corners = jnp.zeros((24, elements), jnp.float32)
    for step in range(4):
        part = jnp.where(corner >> 1 == step, values, 0.0)
        corners = corners + dot_selected(part, selectors[step], 0)
    gradients = []
    for c in range(3):
        product = jnp.dot(
            table_ref[...],
            corners[8 * c : 8 * c + 8],
            precision=lax.Precision.HIGHEST,
            preferred_element_type=jnp.float32,
        )
        gradients.append([product[8 * d : 8 * d + 8] for d in range(3)])
    strain = [
        gradients[0][0],
        gradients[1][1],
        gradients[2][2],
        0.5 * (gradients[1][2] + gradients[2][1]),
        0.5 * (gradients[0][2] + gradients[2][0]),
        0.5 * (gradients[0][1] + gradients[1][0]),
    ]
    volume = strain[0] + strain[1] + strain[2]
    trial = []
    for component in range(6):
        change = 2.0 * SHEAR_MODULUS * strain[component]
        if component < 3:
            change = change + LAMBDA_ELASTIC * volume
        trial.append(stress_ref[component] + change)
    correction = [jnp.zeros_like(trial[0]) for component in range(6)]
    for system in range(12):
        rotated_dir = [
            sum(
                frames[3 * row + axis_id] * SLIP_DIRECTIONS[system][axis_id]
                for axis_id in range(3)
                if SLIP_DIRECTIONS[system][axis_id] != 0.0
            )
            for row in range(3)
        ]
        rotated_normal = [
            sum(frames[3 * row + axis_id] * SLIP_PLANES[system][axis_id] for axis_id in range(3))
            for row in range(3)
        ]
        schmid = [
            rotated_dir[0] * rotated_normal[0],
            rotated_dir[1] * rotated_normal[1],
            rotated_dir[2] * rotated_normal[2],
            0.5 * (rotated_dir[1] * rotated_normal[2] + rotated_dir[2] * rotated_normal[1]),
            0.5 * (rotated_dir[0] * rotated_normal[2] + rotated_dir[2] * rotated_normal[0]),
            0.5 * (rotated_dir[0] * rotated_normal[1] + rotated_dir[1] * rotated_normal[0]),
        ]
        resolved = (
            trial[0] * schmid[0]
            + trial[1] * schmid[1]
            + trial[2] * schmid[2]
            + 2.0 * (trial[3] * schmid[3] + trial[4] * schmid[4] + trial[5] * schmid[5])
        )
        slip_ratio = resolved / resistance_ref[system]
        slip_step = RATE_STEP * slip_ratio * jnp.abs(slip_ratio)
        correction = [
            correction[component] + slip_step * schmid[component] for component in range(6)
        ]
    updated = [
        trial[component] - 2.0 * SHEAR_MODULUS * correction[component] for component in range(6)
    ]
    for component in range(6):
        stress_out_ref[component] = updated[component]
    point_scale = weights_ref[...].astype(jnp.float32) * (1.0 / (FIXED_POINT * 8.0))
    scaled = [value * point_scale for value in updated]
    forces = []
    for rows in [(0, 5, 4), (5, 1, 3), (4, 3, 2)]:
        forces.append(
            lax.dot_general(
                table_ref[...],
                jnp.concatenate([scaled[row] for row in rows], axis=0),
                (((0,), (0,)), ((), ())),
                precision=lax.Precision.HIGHEST,
                preferred_element_type=jnp.float32,
            )
        )
    forces = jnp.concatenate(forces, axis=0)
    nodal = jnp.zeros((24, COLUMNS), jnp.float32)
    for step in range(4):
        part = jnp.where(corner >> 1 == step, forces, 0.0)
        nodal = nodal + dot_selected(part, selectors[step], 1)
    lower = jnp.where(upper_corner, 0.0, nodal)
    above = jnp.where(upper_corner, nodal, 0.0)
    for c in range(3):
        nodal_ref[0, c] = jnp.sum(lower[8 * c : 8 * c + 8], axis=0, keepdims=True)
        nodal_ref[1, c] = jnp.sum(above[8 * c : 8 * c + 8], axis=0, keepdims=True)


def element_update(gathered, own, layers, stress_old, resistance, quad_weights):
    grad_table = shape_gradients()
    table = jnp.asarray(
        [
            [grad_table[quadrature][corner][direction] for corner in range(8)]
            for direction in range(3)
            for quadrature in range(8)
        ],
        dtype=jnp.float32,
    )
    return pl.pallas_call(
        functools.partial(update_kernel, len(gathered) // 2),
        out_shape=(
            jax.ShapeDtypeStruct(stress_old.shape, jnp.float32),
            jax.ShapeDtypeStruct((2,) + own.shape, jnp.float32),
        ),
        compiler_params=pltpu.CompilerParams(vmem_limit_bytes=8 * 1024 * 1024),
        name="stress_update",
    )(*gathered, own, layers, stress_old, resistance, quad_weights, table)


def body(
    grain_ids,
    euler_angles,
    brick_active,
    brick_owner,
    brick_element,
    displacement,
    stress_old,
    resistance,
    quad_weights,
):
    half = lax.axis_size("ca") * lax.axis_size("fe") // 2
    bricks = grain_ids.shape[1]
    layers = lax.all_gather(displacement, "fe")
    owner = lax.optimization_barrier(brick_owner.reshape(bricks))
    labels = jnp.where(brick_active > 0, owner * COLUMNS + brick_element, -1).reshape(1, bricks)
    (first_a, count_a), (first_b, count_b) = CHUNKS
    split, labels, table = cell_sums(first_a, count_a, grain_ids, labels, euler_angles)
    send, labels = brick_sums(split, labels, half, half)
    keep, labels = brick_sums(split, labels, half, 0)
    core_a, labels = part_sum([across_cores(keep, send)], [labels], "core_sum_a")
    split, labels = cell_sums(first_b, count_b, grain_ids, labels, table)
    plane_a, labels, layers = part_sum([across_plane(core_a)], [labels, layers], "plane_sum_a")
    send, labels = brick_sums(split, labels, half, half)
    keep, labels = brick_sums(split, labels, half, 0)
    core_b, labels = part_sum([across_cores(keep, send)], [labels], "core_sum_b")
    plane_b, labels = part_sum([across_plane(core_b)], [labels], "plane_sum_b")
    gathered = across_height(plane_a) + across_height(plane_b)
    stress_new, nodal = element_update(
        gathered, displacement, layers, stress_old, resistance, quad_weights
    )
    forces = nodal[0] + passed_along(nodal[1], "fe", 1)
    return (stress_new, forces)


def solution(mesh):
    placed = (
        P(None, ("ca", "fe")),
        P(),
        P(("ca", "fe")),
        P(("ca", "fe"), None),
        P(("ca", "fe")),
        P(None, ("ca", "fe"), None),
        P(None, None, ("ca", "fe")),
        P(None, None, ("ca", "fe")),
        P(None, ("ca", "fe")),
    )
    return jax.shard_map(
        body,
        mesh=mesh,
        in_specs=placed,
        out_specs=(P(None, None, ("ca", "fe")), P(None, ("ca", "fe"), None)),
        check_vma=False,
    )
```

```python
import functools
import functools
import math

import jax
import jax.numpy as jnp
from jax import lax
from jax.experimental import pallas as pl
from jax.experimental.pallas import tpu as pltpu
from jax.sharding import PartitionSpec as P

GX = 15
LANES = 128
COLUMNS = 256
CHUNKS = ((0, 4), (4, 4))
QUANTUM = float((1 << 17) - 1)

SLIP_PLANES = [
    [value / math.sqrt(3.0) for value in row]
    for row in [[1, 1, 1]] * 3 + [[-1, 1, 1]] * 3 + [[1, -1, 1]] * 3 + [[1, 1, -1]] * 3
]
SLIP_DIRECTIONS = [
    [value / math.sqrt(2.0) for value in row]
    for row in [
        [0, 1, -1],
        [1, 0, -1],
        [1, -1, 0],
        [0, 1, -1],
        [1, 0, 1],
        [1, 1, 0],
        [0, 1, 1],
        [1, 0, -1],
        [1, 1, 0],
        [0, 1, 1],
        [1, 0, 1],
        [1, -1, 0],
    ]
]
LAMBDA_ELASTIC = 1.5
SHEAR_MODULUS = 1.0
RATE_STEP = 0.1
FIXED_POINT = 65536.0


def passed_along(block, axis, distance):
    devices = range(lax.axis_size(axis))
    route = [(i - distance, i) for i in devices if i - distance in devices]
    return lax.ppermute(block, axis, route)


def shape_gradients():
    grad_table = [[[0.0, 0.0, 0.0] for corner in range(8)] for quadrature in range(8)]
    point_offset = 1.0 / math.sqrt(3.0)
    for quadrature in range(8):
        natural = [
            (2 * (quadrature >> shift_bits & 1) - 1) * point_offset for shift_bits in (2, 1, 0)
        ]
        for corner in range(8):
            sign_list = [2 * (corner >> shift_bits & 1) - 1 for shift_bits in (2, 1, 0)]
            factors = [1.0 + sign_list[axis_id] * natural[axis_id] for axis_id in range(3)]
            for direction in range(3):
                others = 1.0
                for axis_id in range(3):
                    if axis_id != direction:
                        others = others * factors[axis_id]
                grad_table[quadrature][corner][direction] = (
                    2.0 * sign_list[direction] * others / 8.0
                )
    return grad_table


def cos_sin(angle):
    square = angle * angle
    cosine = 1.0 / math.factorial(12)
    for power in (10, 8, 6, 4, 2, 0):
        cosine = cosine * square + (-1.0) ** (power // 2) / math.factorial(power)
    sine = 1.0 / math.factorial(13)
    for power in (11, 9, 7, 5, 3, 1):
        sine = sine * square + (-1.0) ** (power // 2) / math.factorial(power)
    return cosine, sine * angle


def rotation_words(euler):
    cos_one, sin_one = cos_sin(0.5 * euler[0 : 0 + 1])
    cos_mid, sin_mid = cos_sin(0.5 * euler[1 : 1 + 1])
    cos_two, sin_two = cos_sin(0.5 * euler[2 : 2 + 1])
    w = cos_mid * (cos_one * cos_two - sin_one * sin_two)
    factor = jnp.where(w < 0.0, -QUANTUM, QUANTUM) / (1.0 + jnp.abs(w))
    x = sin_mid * (cos_one * cos_two + sin_one * sin_two) * factor
    y = sin_mid * (sin_one * cos_two - cos_one * sin_two) * factor
    z = cos_mid * (sin_one * cos_two + cos_one * sin_two) * factor
    x, y, z = [
        jnp.clip(jnp.round(value), -QUANTUM, QUANTUM).astype(jnp.int32) for value in (x, y, z)
    ]
    return [
        (lax.shift_left(x, 14) | (lax.shift_right_arithmetic(y, 4) & 0x3FFF), 32),
        (lax.shift_left(y & 0xF, 12) | (lax.shift_right_arithmetic(z, 6) & 0xFFF), 16),
        (lax.shift_right_arithmetic(z, 2) & 0xF, 4),
        (z & 0x3, 2),
    ]


def fill_table(table_ref, euler):
    at = 0
    for field, width in rotation_words(euler):
        rows = field.shape[1] // LANES
        shared = 32 // width
        for first in range(0, rows, shared):
            word = field[:, first * LANES : (first + 1) * LANES]
            for other in range(1, shared):
                row = field[:, (first + other) * LANES : (first + other + 1) * LANES]
                word = word | lax.shift_left(row, other * width)
            table_ref[at] = jnp.broadcast_to(word, (8, LANES))
            at += 1


def looked_up(table_ref, first_row, rows, lane, bits):
    if rows == 1:
        return lax.gather(
            table_ref[first_row],
            lane,
            lax.GatherDimensionNumbers(
                offset_dims=(),
                collapsed_slice_dims=(1,),
                start_index_map=(1,),
                operand_batching_dims=(0,),
                start_indices_batching_dims=(0,),
            ),
            slice_sizes=(1, 1),
            mode=lax.GatherScatterMode.PROMISE_IN_BOUNDS,
        )
    half = rows // 2
    level = half.bit_length() - 1
    low = looked_up(table_ref, first_row, half, lane, bits)
    high = looked_up(table_ref, first_row + half, half, lane, bits)
    return jnp.where(bits[level], high, low)


def rotation_products(table_ref, table_rows, ids):
    lane = (ids & (LANES - 1))[:, :, None]
    row = lax.shift_right_logical(ids, 7)
    bits = [(row & (1 << level)) != 0 for level in range(table_rows.bit_length() - 1)]
    fields = []
    at = 0
    for width in (32, 16, 4, 2):
        shared = 32 // width
        skipped = shared.bit_length() - 1
        rows = table_rows // shared
        field = looked_up(table_ref, at, rows, lane, bits[skipped:])
        if shared > 1:
            field = lax.shift_right_logical(field, (row & (shared - 1)) * width)
        fields.append(field)
        at += rows
    first, second, third, fourth = fields
    x = lax.shift_right_arithmetic(first, 14).astype(jnp.float32)
    y = lax.shift_right_arithmetic(lax.shift_left(first, 18), 14) | (
        lax.shift_right_logical(second, 12) & 0xF
    )
    z = lax.shift_right_arithmetic(lax.shift_left(second, 20), 14) | (
        lax.shift_left(third & 0xF, 2) | (fourth & 0x3)
    )
    y, z = y.astype(jnp.float32), z.astype(jnp.float32)
    square = x * x + y * y + z * z
    scale = 2.0 / (1.0 + square * (1.0 / (QUANTUM * QUANTUM)))
    w = scale - 1.0
    x, y, z = x * scale, y * scale, z * scale
    return [x * x, y * y, z * z, x * y, x * z, y * z, w * x, w * y, w * z]


def cell_sum_kernel(first, count, *refs):
    if first == 0:
        ids_ref, label_ref, euler_ref, split_ref, label_out_ref, table_ref, tile_ref = refs
    else:
        ids_ref, label_ref, table_ref, split_ref, label_out_ref, tile_ref = refs
    per_octant = ids_ref.shape[0] // 8
    table_rows = table_ref.shape[0] * 16 // 27
    label_out_ref[...] = label_ref[...]
    if first == 0:
        fill_table(table_ref, euler_ref[...])
    groups = tile_ref.shape[0] // 8
    rows_left = count * per_octant - 8 * (groups - 1)

    def tile_sums(tile, carry):
        lanes = pl.ds(pl.multiple_of(tile * LANES, LANES), LANES)
        for octant in range(count):
            tile_ref[pl.ds(octant, per_octant, stride=count), :] = ids_ref[
                pl.ds((first + octant) * per_octant, per_octant), lanes
            ]
        sums = [jnp.zeros((8, LANES), jnp.float32) for pair in range(9)]
        for group in range(groups):
            ids = tile_ref[pl.ds(8 * group, 8), :]
            products = rotation_products(table_ref, table_rows, ids)
            if group == groups - 1 and rows_left < 8:
                there = lax.broadcasted_iota(jnp.int32, (8, LANES), 0) < rows_left
                products = [jnp.where(there, product, 0.0) for product in products]
            sums = [total + product for total, product in zip(sums, products)]
        sums = [
            sum(total[count * part : count * (part + 1)] for part in range(8 // count))
            for total in sums
        ]
        vector = 2.0 / (QUANTUM * QUANTUM)
        xx, yy, zz, xy, xz, yz = [value * vector for value in sums[:6]]
        wx, wy, wz = [value * (2.0 / QUANTUM) for value in sums[6:]]
        entries = [
            per_octant - (yy + zz),
            xy - wz,
            xz + wy,
            xy + wz,
            per_octant - (xx + zz),
            yz - wx,
            xz - wy,
            yz + wx,
            per_octant - (xx + yy),
            jnp.ones((split_ref.shape[0] // 2 - 9 * count, LANES), jnp.float32),
        ]
        stacked = jnp.concatenate(entries, axis=0)
        leading = stacked.astype(jnp.bfloat16).astype(jnp.float32)
        split_ref[:, lanes] = jnp.concatenate([leading, stacked - leading], axis=0).astype(
            jnp.bfloat16
        )
        return carry

    lax.fori_loop(0, ids_ref.shape[1] // LANES, tile_sums, 0)


def brick_sum_kernel(base, split_ref, label_ref, out_ref, label_out_ref, place_ref, masked_ref):
    bricks = split_ref.shape[1]
    labels = label_ref[...]
    label_out_ref[...] = labels
    place = place_of(lax.shift_right_arithmetic(labels, COLUMNS.bit_length() - 1))
    place_ref[...] = jnp.where(labels < 0, -1, place - base)
    column = lax.broadcasted_iota(jnp.int32, (COLUMNS, bricks), 0)
    chosen = (column == labels & (COLUMNS - 1)).astype(jnp.bfloat16)
    split_rows = split_ref.shape[0]
    half_rows = split_rows // 2
    members = masked_ref.shape[0] // split_rows

    def place_group(step, carry):
        for member in range(members):
            mask = (place_ref[...] == step * members + member).astype(jnp.bfloat16)
            masked_ref[pl.ds(member * split_rows, split_rows), :] = split_ref[...] * mask
        product = lax.dot_general(
            masked_ref[...],
            chosen,
            (((1,), (1,)), ((), ())),
            preferred_element_type=jnp.float32,
        )
        for member in range(members):
            at = member * split_rows
            out_ref[step * members + member] = (
                product[at : at + half_rows] + product[at + half_rows : at + split_rows]
            )
        return carry

    lax.fori_loop(0, out_ref.shape[0] // members, place_group, 0)


def place_of(owner):
    groups, members = lax.axis_size("ca"), lax.axis_size("fe")
    owner_ca = lax.shift_right_logical(owner, members.bit_length() - 1)
    owner_fe = owner & (members - 1)
    place = ((owner_ca ^ lax.axis_index("ca")) & 1) * (groups // 2)
    place = place + lax.shift_right_logical(owner_ca, 1)
    place = place * 2 + (owner_fe & 1)
    return place * (members // 2) + lax.shift_right_logical(owner_fe, 1)


def cell_sums(first, count, grain_ids, labels, table):
    bricks = grain_ids.shape[1]
    per_octant = grain_ids.shape[0] // 8
    out_shape = [
        jax.ShapeDtypeStruct((2 * padded_rows(count), bricks), jnp.bfloat16),
        jax.ShapeDtypeStruct(labels.shape, jnp.int32),
    ]
    if first == 0:
        grains = table.shape[1]
        out_shape.append(jax.ShapeDtypeStruct((27 * grains // LANES // 16, 8, LANES), jnp.int32))
    return pl.pallas_call(
        functools.partial(cell_sum_kernel, first, count),
        out_shape=out_shape,
        scratch_shapes=[pltpu.VMEM((-(-count * per_octant // 8) * 8, LANES), jnp.int32)],
        compiler_params=pltpu.CompilerParams(vmem_limit_bytes=8 * 1024 * 1024),
        cost_estimate=pl.CostEstimate(
            flops=count * 4 * 10**9, bytes_accessed=count * 10**7, transcendentals=0
        ),
        name="cell_sums",
    )(grain_ids, labels, table)


def padded_rows(count):
    return -(-9 * count // 8) * 8


def brick_sums(split, labels, places, base):
    rows, bricks = split.shape
    members = min(16, places)
    return pl.pallas_call(
        functools.partial(brick_sum_kernel, base),
        out_shape=[
            jax.ShapeDtypeStruct((places, rows // 2, COLUMNS), jnp.float32),
            jax.ShapeDtypeStruct(labels.shape, jnp.int32),
        ],
        scratch_shapes=[
            pltpu.VMEM((1, bricks), jnp.int32),
            pltpu.VMEM((members * rows, bricks), jnp.bfloat16),
        ],
        compiler_params=pltpu.CompilerParams(vmem_limit_bytes=24 * 1024 * 1024),
        cost_estimate=pl.CostEstimate(
            flops=rows * 15 * 10**6, bytes_accessed=rows * 5 * 10**4, transcendentals=0
        ),
        name="brick_sums",
    )(split, labels)


def core_sum_kernel(kept_ref, received_ref, own_ref, label_ref, out_ref, label_out_ref):
    out_ref[...] = kept_ref[...] + received_ref[...]
    for c in range(3):
        row = out_ref.shape[2] - 3 + c
        out_ref[:, :, row : row + 1, :] = jnp.broadcast_to(
            own_ref[c][None, None], out_ref.shape[:2] + (1, COLUMNS)
        )
    label_out_ref[...] = label_ref[...]


def core_sum(kept, received, own, labels, name):
    pairs, rests = lax.axis_size("ca") // 2, lax.axis_size("fe") // 2
    shape = (2 * pairs, rests) + kept.shape[1:]
    return pl.pallas_call(
        core_sum_kernel,
        out_shape=[
            jax.ShapeDtypeStruct(shape, jnp.float32),
            jax.ShapeDtypeStruct(labels.shape, jnp.int32),
        ],
        compiler_params=pltpu.CompilerParams(vmem_limit_bytes=16 * 1024 * 1024),
        name=name,
    )(kept.reshape(shape), received.reshape(shape), own, labels)


def plane_sum_kernel(received_ref, label_ref, out_ref, label_out_ref):
    total = received_ref[0]
    for source in range(1, received_ref.shape[0]):
        total = total + received_ref[source]
    out_ref[...] = total
    neighbour = (lax.axis_index("ca") // 2 * 2 + (lax.axis_index("fe") & 1)) ^ 1
    rows = pl.ds(out_ref.shape[1] - 3, 3)
    out_ref[:, rows, :] = received_ref[neighbour, :, rows, :]
    label_out_ref[...] = label_ref[...]


def plane_sum(received, labels, name):
    return pl.pallas_call(
        plane_sum_kernel,
        out_shape=[
            jax.ShapeDtypeStruct(received.shape[1:], jnp.float32),
            jax.ShapeDtypeStruct(labels.shape, jnp.int32),
        ],
        compiler_params=pltpu.CompilerParams(vmem_limit_bytes=16 * 1024 * 1024),
        name=name,
    )(received, labels)


def across_cores(block):
    groups = lax.axis_size("ca")
    return lax.ppermute(block, "ca", [(i, i ^ 1) for i in range(groups)])


def across(blocks, groups):
    return lax.all_to_all(
        blocks, ("ca", "fe"), split_axis=0, concat_axis=0, axis_index_groups=groups, tiled=True
    )


def device_groups():
    pairs, rests = lax.axis_size("ca") // 2, lax.axis_size("fe") // 2
    number = lambda pair, core, last, rest: ((2 * pair + core) * rests + rest) * 2 + last
    planes = [
        [number(pair, core, last, rest) for pair in range(pairs) for last in range(2)]
        for core in range(2)
        for rest in range(rests)
    ]
    heights = [
        [number(pair, core, last, rest) for rest in range(rests)]
        for pair in range(pairs)
        for core in range(2)
        for last in range(2)
    ]
    return planes, heights


def three_parts(value):
    first = value.astype(jnp.bfloat16)
    rest = value - first.astype(jnp.float32)
    second = rest.astype(jnp.bfloat16)
    third = (rest - second.astype(jnp.float32)).astype(jnp.bfloat16)
    return first, second, third


def dot_selected(value, selector, contract):
    total = None
    for part in three_parts(value):
        term = lax.dot_general(
            part, selector, (((1,), (contract,)), ((), ())), preferred_element_type=jnp.float32
        )
        total = term if total is None else total + term
    return total


def update_kernel(
    first_ref,
    second_ref,
    own_ref,
    stress_ref,
    resistance_ref,
    weights_ref,
    table_ref,
    stress_out_ref,
    nodal_ref,
):
    elements = stress_ref.shape[2]
    gathered = [
        sum(ref[source, :, 0:elements] for source in range(ref.shape[0]))
        for ref in (first_ref, second_ref)
    ]
    counts = gathered[0][9 * CHUNKS[0][1] : 9 * CHUNKS[0][1] + 1]
    per_brick = 1.0 / (8.0 * jnp.maximum(counts, 1.0))
    frames = [
        jnp.concatenate(
            [
                sums[count * k : count * (k + 1)]
                for sums, (first, count) in zip(gathered, CHUNKS)
            ],
            axis=0,
        )
        * per_brick
        for k in range(9)
    ]

    node = lax.broadcasted_iota(jnp.int32, (COLUMNS, elements), 0)
    element = lax.broadcasted_iota(jnp.int32, (COLUMNS, elements), 1)
    base = element + element // GX
    selectors = [
        (node == base + (step_y * (GX + 1) + step_x)).astype(jnp.bfloat16)
        for step_x in range(2)
        for step_y in range(2)
    ]
    corner = lax.broadcasted_iota(jnp.int32, (24, 1), 0) & 7
    upper_corner = (corner & 1) == 1
    above = lax.axis_index("fe") // 2 + (lax.axis_index("fe") & 1)
    heights, rows = first_ref.shape[:2]
    free = jnp.where(above == heights, 0.0, 1.0)
    above = jnp.minimum(above, heights - 1)
    upper = first_ref[above, rows - 3 : rows, :] * free
    values = jnp.where(
        upper_corner,
        jnp.concatenate(
            [jnp.broadcast_to(upper[c : c + 1], (8, COLUMNS)) for c in range(3)], axis=0
        ),
        jnp.concatenate([jnp.broadcast_to(own_ref[c], (8, COLUMNS)) for c in range(3)], axis=0),
    )
    corners = jnp.zeros((24, elements), jnp.float32)
    for step in range(4):
        part = jnp.where(corner >> 1 == step, values, 0.0)
        corners = corners + dot_selected(part, selectors[step], 0)
    gradients = []
    for c in range(3):
        product = jnp.dot(
            table_ref[...],
            corners[8 * c : 8 * c + 8],
            precision=lax.Precision.HIGHEST,
            preferred_element_type=jnp.float32,
        )
        gradients.append([product[8 * d : 8 * d + 8] for d in range(3)])
    strain = [
        gradients[0][0],
        gradients[1][1],
        gradients[2][2],
        0.5 * (gradients[1][2] + gradients[2][1]),
        0.5 * (gradients[0][2] + gradients[2][0]),
        0.5 * (gradients[0][1] + gradients[1][0]),
    ]
    volume = strain[0] + strain[1] + strain[2]
    trial = []
    for component in range(6):
        change = 2.0 * SHEAR_MODULUS * strain[component]
        if component < 3:
            change = change + LAMBDA_ELASTIC * volume
        trial.append(stress_ref[component] + change)
    correction = [jnp.zeros_like(trial[0]) for component in range(6)]
    for system in range(12):
        rotated_dir = [
            sum(
                frames[3 * row + axis_id] * SLIP_DIRECTIONS[system][axis_id]
                for axis_id in range(3)
                if SLIP_DIRECTIONS[system][axis_id] != 0.0
            )
            for row in range(3)
        ]
        rotated_normal = [
            sum(frames[3 * row + axis_id] * SLIP_PLANES[system][axis_id] for axis_id in range(3))
            for row in range(3)
        ]
        schmid = [
            rotated_dir[0] * rotated_normal[0],
            rotated_dir[1] * rotated_normal[1],
            rotated_dir[2] * rotated_normal[2],
            0.5 * (rotated_dir[1] * rotated_normal[2] + rotated_dir[2] * rotated_normal[1]),
            0.5 * (rotated_dir[0] * rotated_normal[2] + rotated_dir[2] * rotated_normal[0]),
            0.5 * (rotated_dir[0] * rotated_normal[1] + rotated_dir[1] * rotated_normal[0]),
        ]
        resolved = (
            trial[0] * schmid[0]
            + trial[1] * schmid[1]
            + trial[2] * schmid[2]
            + 2.0 * (trial[3] * schmid[3] + trial[4] * schmid[4] + trial[5] * schmid[5])
        )
        slip_ratio = resolved / resistance_ref[system]
        slip_step = RATE_STEP * slip_ratio * jnp.abs(slip_ratio)
        correction = [
            correction[component] + slip_step * schmid[component] for component in range(6)
        ]
    updated = [
        trial[component] - 2.0 * SHEAR_MODULUS * correction[component] for component in range(6)
    ]
    for component in range(6):
        stress_out_ref[component] = updated[component]
    point_scale = weights_ref[...].astype(jnp.float32) * (1.0 / (FIXED_POINT * 8.0))
    scaled = [value * point_scale for value in updated]
    forces = []
    for rows in [(0, 5, 4), (5, 1, 3), (4, 3, 2)]:
        forces.append(
            lax.dot_general(
                table_ref[...],
                jnp.concatenate([scaled[row] for row in rows], axis=0),
                (((0,), (0,)), ((), ())),
                precision=lax.Precision.HIGHEST,
                preferred_element_type=jnp.float32,
            )
        )
    forces = jnp.concatenate(forces, axis=0)
    nodal = jnp.zeros((24, COLUMNS), jnp.float32)
    for step in range(4):
        part = jnp.where(corner >> 1 == step, forces, 0.0)
        nodal = nodal + dot_selected(part, selectors[step], 1)
    lower = jnp.where(upper_corner, 0.0, nodal)
    above = jnp.where(upper_corner, nodal, 0.0)
    for c in range(3):
        nodal_ref[0, c] = jnp.sum(lower[8 * c : 8 * c + 8], axis=0, keepdims=True)
        nodal_ref[1, c] = jnp.sum(above[8 * c : 8 * c + 8], axis=0, keepdims=True)


def element_update(first, second, own, stress_old, resistance, quad_weights):
    grad_table = shape_gradients()
    table = jnp.asarray(
        [
            [grad_table[quadrature][corner][direction] for corner in range(8)]
            for direction in range(3)
            for quadrature in range(8)
        ],
        dtype=jnp.float32,
    )
    return pl.pallas_call(
        update_kernel,
        out_shape=(
            jax.ShapeDtypeStruct(stress_old.shape, jnp.float32),
            jax.ShapeDtypeStruct((2,) + own.shape, jnp.float32),
        ),
        compiler_params=pltpu.CompilerParams(vmem_limit_bytes=8 * 1024 * 1024),
        name="stress_update",
    )(first, second, own, stress_old, resistance, quad_weights, table)


def body(
    grain_ids,
    euler_angles,
    brick_active,
    brick_owner,
    brick_element,
    displacement,
    stress_old,
    resistance,
    quad_weights,
):
    half = lax.axis_size("ca") * lax.axis_size("fe") // 2
    bricks = grain_ids.shape[1]
    owner = lax.optimization_barrier(brick_owner.reshape(bricks))
    labels = jnp.where(brick_active > 0, owner * COLUMNS + brick_element, -1).reshape(1, bricks)
    (first_a, count_a), (first_b, count_b) = CHUNKS
    split, labels, table = cell_sums(first_a, count_a, grain_ids, labels, euler_angles)
    send, labels = brick_sums(split, labels, half, half)
    keep, labels = brick_sums(split, labels, half, 0)
    planes, heights = device_groups()
    core_a, labels = core_sum(keep, across_cores(send), displacement, labels, "core_sum_a")
    split, labels = cell_sums(first_b, count_b, grain_ids, labels, table)
    plane_a, labels = plane_sum(across(core_a, planes), labels, "plane_sum_a")
    send, labels = brick_sums(split, labels, half, half)
    keep, labels = brick_sums(split, labels, half, 0)
    core_b, labels = core_sum(keep, across_cores(send), displacement, labels, "core_sum_b")
    plane_b, labels = plane_sum(across(core_b, planes), labels, "plane_sum_b")
    stress_new, nodal = element_update(
        across(plane_a, heights),
        across(plane_b, heights),
        displacement,
        stress_old,
        resistance,
        quad_weights,
    )
    forces = nodal[0] + passed_along(nodal[1], "fe", 1)
    return (stress_new, forces)


def solution(mesh):
    placed = (
        P(None, ("ca", "fe")),
        P(),
        P(("ca", "fe")),
        P(("ca", "fe"), None),
        P(("ca", "fe")),
        P(None, ("ca", "fe"), None),
        P(None, None, ("ca", "fe")),
        P(None, None, ("ca", "fe")),
        P(None, ("ca", "fe")),
    )
    return jax.shard_map(
        body,
        mesh=mesh,
        in_specs=placed,
        out_specs=(P(None, None, ("ca", "fe")), P(None, ("ca", "fe"), None)),
        check_vma=False,
    )
```

```python
import functools
import functools
import math

import jax
import jax.numpy as jnp
from jax import lax
from jax.experimental import pallas as pl
from jax.experimental.pallas import tpu as pltpu
from jax.sharding import PartitionSpec as P

GX = 15
LANES = 128
COLUMNS = 256
CHUNKS = ((0, 6), (6, 2))
QUANTUM = float((1 << 17) - 1)

SLIP_PLANES = [
    [value / math.sqrt(3.0) for value in row]
    for row in [[1, 1, 1]] * 3 + [[-1, 1, 1]] * 3 + [[1, -1, 1]] * 3 + [[1, 1, -1]] * 3
]
SLIP_DIRECTIONS = [
    [value / math.sqrt(2.0) for value in row]
    for row in [
        [0, 1, -1],
        [1, 0, -1],
        [1, -1, 0],
        [0, 1, -1],
        [1, 0, 1],
        [1, 1, 0],
        [0, 1, 1],
        [1, 0, -1],
        [1, 1, 0],
        [0, 1, 1],
        [1, 0, 1],
        [1, -1, 0],
    ]
]
LAMBDA_ELASTIC = 1.5
SHEAR_MODULUS = 1.0
RATE_STEP = 0.1
FIXED_POINT = 65536.0


def passed_along(block, axis, distance):
    devices = range(lax.axis_size(axis))
    route = [(i - distance, i) for i in devices if i - distance in devices]
    return lax.ppermute(block, axis, route)


def shape_gradients():
    grad_table = [[[0.0, 0.0, 0.0] for corner in range(8)] for quadrature in range(8)]
    point_offset = 1.0 / math.sqrt(3.0)
    for quadrature in range(8):
        natural = [
            (2 * (quadrature >> shift_bits & 1) - 1) * point_offset for shift_bits in (2, 1, 0)
        ]
        for corner in range(8):
            sign_list = [2 * (corner >> shift_bits & 1) - 1 for shift_bits in (2, 1, 0)]
            factors = [1.0 + sign_list[axis_id] * natural[axis_id] for axis_id in range(3)]
            for direction in range(3):
                others = 1.0
                for axis_id in range(3):
                    if axis_id != direction:
                        others = others * factors[axis_id]
                grad_table[quadrature][corner][direction] = (
                    2.0 * sign_list[direction] * others / 8.0
                )
    return grad_table


def cos_sin(angle):
    square = angle * angle
    cosine = 1.0 / math.factorial(12)
    for power in (10, 8, 6, 4, 2, 0):
        cosine = cosine * square + (-1.0) ** (power // 2) / math.factorial(power)
    sine = 1.0 / math.factorial(13)
    for power in (11, 9, 7, 5, 3, 1):
        sine = sine * square + (-1.0) ** (power // 2) / math.factorial(power)
    return cosine, sine * angle


def rotation_words(euler):
    cos_one, sin_one = cos_sin(0.5 * euler[0 : 0 + 1])
    cos_mid, sin_mid = cos_sin(0.5 * euler[1 : 1 + 1])
    cos_two, sin_two = cos_sin(0.5 * euler[2 : 2 + 1])
    w = cos_mid * (cos_one * cos_two - sin_one * sin_two)
    factor = jnp.where(w < 0.0, -QUANTUM, QUANTUM) / (1.0 + jnp.abs(w))
    x = sin_mid * (cos_one * cos_two + sin_one * sin_two) * factor
    y = sin_mid * (sin_one * cos_two - cos_one * sin_two) * factor
    z = cos_mid * (sin_one * cos_two + cos_one * sin_two) * factor
    x, y, z = [
        jnp.clip(jnp.round(value), -QUANTUM, QUANTUM).astype(jnp.int32) for value in (x, y, z)
    ]
    return [
        (lax.shift_left(x, 14) | (lax.shift_right_arithmetic(y, 4) & 0x3FFF), 32),
        (lax.shift_left(y & 0xF, 12) | (lax.shift_right_arithmetic(z, 6) & 0xFFF), 16),
        (lax.shift_right_arithmetic(z, 2) & 0xF, 4),
        (z & 0x3, 2),
    ]


def fill_table(table_ref, euler):
    at = 0
    for field, width in rotation_words(euler):
        rows = field.shape[1] // LANES
        shared = 32 // width
        for first in range(0, rows, shared):
            word = field[:, first * LANES : (first + 1) * LANES]
            for other in range(1, shared):
                row = field[:, (first + other) * LANES : (first + other + 1) * LANES]
                word = word | lax.shift_left(row, other * width)
            table_ref[at] = jnp.broadcast_to(word, (8, LANES))
            at += 1


def looked_up(table_ref, first_row, rows, lane, bits):
    if rows == 1:
        return lax.gather(
            table_ref[first_row],
            lane,
            lax.GatherDimensionNumbers(
                offset_dims=(),
                collapsed_slice_dims=(1,),
                start_index_map=(1,),
                operand_batching_dims=(0,),
                start_indices_batching_dims=(0,),
            ),
            slice_sizes=(1, 1),
            mode=lax.GatherScatterMode.PROMISE_IN_BOUNDS,
        )
    half = rows // 2
    level = half.bit_length() - 1
    low = looked_up(table_ref, first_row, half, lane, bits)
    high = looked_up(table_ref, first_row + half, half, lane, bits)
    return jnp.where(bits[level], high, low)


def rotation_products(table_ref, table_rows, ids):
    lane = (ids & (LANES - 1))[:, :, None]
    row = lax.shift_right_logical(ids, 7)
    bits = [(row & (1 << level)) != 0 for level in range(table_rows.bit_length() - 1)]
    fields = []
    at = 0
    for width in (32, 16, 4, 2):
        shared = 32 // width
        skipped = shared.bit_length() - 1
        rows = table_rows // shared
        field = looked_up(table_ref, at, rows, lane, bits[skipped:])
        if shared > 1:
            field = lax.shift_right_logical(field, (row & (shared - 1)) * width)
        fields.append(field)
        at += rows
    first, second, third, fourth = fields
    x = lax.shift_right_arithmetic(first, 14).astype(jnp.float32)
    y = lax.shift_right_arithmetic(lax.shift_left(first, 18), 14) | (
        lax.shift_right_logical(second, 12) & 0xF
    )
    z = lax.shift_right_arithmetic(lax.shift_left(second, 20), 14) | (
        lax.shift_left(third & 0xF, 2) | (fourth & 0x3)
    )
    y, z = y.astype(jnp.float32), z.astype(jnp.float32)
    square = x * x + y * y + z * z
    scale = 2.0 / (1.0 + square * (1.0 / (QUANTUM * QUANTUM)))
    w = scale - 1.0
    x, y, z = x * scale, y * scale, z * scale
    return [x * x, y * y, z * z, x * y, x * z, y * z, w * x, w * y, w * z]


def cell_sum_kernel(first, count, *refs):
    if first == 0:
        ids_ref, label_ref, euler_ref, split_ref, label_out_ref, table_ref, tile_ref = refs
    else:
        ids_ref, label_ref, table_ref, split_ref, label_out_ref, tile_ref = refs
    per_octant = ids_ref.shape[0] // 8
    table_rows = table_ref.shape[0] * 16 // 27
    label_out_ref[...] = label_ref[...]
    if first == 0:
        fill_table(table_ref, euler_ref[...])
    groups = tile_ref.shape[0] // 8
    rows_left = count * per_octant - 8 * (groups - 1)
    turns = count // math.gcd(count, 8)

    def tile_sums(tile, carry):
        lanes = pl.ds(pl.multiple_of(tile * LANES, LANES), LANES)
        for octant in range(count):
            tile_ref[pl.ds(octant, per_octant, stride=count), :] = ids_ref[
                pl.ds((first + octant) * per_octant, per_octant), lanes
            ]
        sums = [[jnp.zeros((8, LANES), jnp.float32)] * 9 for turn in range(turns)]
        for group in range(groups):
            ids = tile_ref[pl.ds(8 * group, 8), :]
            products = rotation_products(table_ref, table_rows, ids)
            if group == groups - 1 and rows_left < 8:
                there = lax.broadcasted_iota(jnp.int32, (8, LANES), 0) < rows_left
                products = [jnp.where(there, product, 0.0) for product in products]
            sums[group % turns] = [
                total + product for total, product in zip(sums[group % turns], products)
            ]
        sums = [jnp.concatenate(turned, axis=0) for turned in zip(*sums)]
        sums = [
            sum(total[count * part : count * (part + 1)] for part in range(8 * turns // count))
            for total in sums
        ]
        vector = 2.0 / (QUANTUM * QUANTUM)
        xx, yy, zz, xy, xz, yz = [value * vector for value in sums[:6]]
        wx, wy, wz = [value * (2.0 / QUANTUM) for value in sums[6:]]
        entries = [
            per_octant - (yy + zz),
            xy - wz,
            xz + wy,
            xy + wz,
            per_octant - (xx + zz),
            yz - wx,
            xz - wy,
            yz + wx,
            per_octant - (xx + yy),
            jnp.ones((split_ref.shape[0] // 2 - 9 * count, LANES), jnp.float32),
        ]
        stacked = jnp.concatenate(entries, axis=0)
        leading = stacked.astype(jnp.bfloat16).astype(jnp.float32)
        split_ref[:, lanes] = jnp.concatenate([leading, stacked - leading], axis=0).astype(
            jnp.bfloat16
        )
        return carry

    lax.fori_loop(0, ids_ref.shape[1] // LANES, tile_sums, 0, unroll=2)


def across_cores(block):
    groups = lax.axis_size("ca")
    return lax.ppermute(block, "ca", [(i, i ^ 1) for i in range(groups)])


def brick_sum_kernel(base, split_ref, label_ref, out_ref, label_out_ref, place_ref, masked_ref):
    bricks = split_ref.shape[1]
    labels = label_ref[...]
    label_out_ref[...] = labels
    place = place_of(lax.shift_right_arithmetic(labels, COLUMNS.bit_length() - 1))
    place_ref[...] = jnp.where(labels < 0, -1, place - base)
    column = lax.broadcasted_iota(jnp.int32, (COLUMNS, bricks), 0)
    chosen = (column == labels & (COLUMNS - 1)).astype(jnp.bfloat16)
    split_rows = split_ref.shape[0]
    half_rows = split_rows // 2
    members = masked_ref.shape[0] // split_rows

    def place_group(step, carry):
        for member in range(members):
            mask = (place_ref[...] == step * members + member).astype(jnp.bfloat16)
            masked_ref[pl.ds(member * split_rows, split_rows), :] = split_ref[...] * mask
        product = lax.dot_general(
            masked_ref[...],
            chosen,
            (((1,), (1,)), ((), ())),
            preferred_element_type=jnp.float32,
        )
        for member in range(members):
            at = member * split_rows
            out_ref[step * members + member] = (
                product[at : at + half_rows] + product[at + half_rows : at + split_rows]
            )
        return carry

    lax.fori_loop(0, out_ref.shape[0] // members, place_group, 0)


def place_of(owner):
    groups, members = lax.axis_size("ca"), lax.axis_size("fe")
    owner_ca = lax.shift_right_logical(owner, members.bit_length() - 1) ^ lax.axis_index("ca")
    owner_fe = (owner & (members - 1)) ^ lax.axis_index("fe")
    place = (owner_ca & 1) * (groups // 2) + lax.shift_right_logical(owner_ca, 1)
    place = place * 2 + (owner_fe & 1)
    return place * (members // 2) + lax.shift_right_logical(owner_fe, 1)


def cell_sums(first, count, grain_ids, labels, table):
    bricks = grain_ids.shape[1]
    per_octant = grain_ids.shape[0] // 8
    out_shape = [
        jax.ShapeDtypeStruct((2 * padded_rows(count), bricks), jnp.bfloat16),
        jax.ShapeDtypeStruct(labels.shape, jnp.int32),
    ]
    if first == 0:
        grains = table.shape[1]
        out_shape.append(jax.ShapeDtypeStruct((27 * grains // LANES // 16, 8, LANES), jnp.int32))
    return pl.pallas_call(
        functools.partial(cell_sum_kernel, first, count),
        out_shape=out_shape,
        scratch_shapes=[pltpu.VMEM((-(-count * per_octant // 8) * 8, LANES), jnp.int32)],
        compiler_params=pltpu.CompilerParams(vmem_limit_bytes=8 * 1024 * 1024),
        cost_estimate=pl.CostEstimate(
            flops=count * 4 * 10**9, bytes_accessed=count * 10**7, transcendentals=0
        ),
        name="cell_sums",
    )(grain_ids, labels, table)


def padded_rows(count):
    return -(-9 * count // 8) * 8


def brick_sums(split, labels, places, base):
    rows, bricks = split.shape
    members = min(16, places)
    return pl.pallas_call(
        functools.partial(brick_sum_kernel, base),
        out_shape=[
            jax.ShapeDtypeStruct((places, rows // 2, COLUMNS), jnp.float32),
            jax.ShapeDtypeStruct(labels.shape, jnp.int32),
        ],
        scratch_shapes=[
            pltpu.VMEM((1, bricks), jnp.int32),
            pltpu.VMEM((members * rows, bricks), jnp.bfloat16),
        ],
        compiler_params=pltpu.CompilerParams(vmem_limit_bytes=24 * 1024 * 1024),
        cost_estimate=pl.CostEstimate(
            flops=rows * 15 * 10**6, bytes_accessed=rows * 5 * 10**4, transcendentals=0
        ),
        name="brick_sums",
    )(split, labels)


def core_sum_kernel(spare, kept_ref, received_ref, own_ref, label_ref, *out_refs):
    for index, out_ref in enumerate(out_refs[:-1]):
        out_ref[...] = kept_ref[index] + received_ref[index]
        for c in range(spare):
            row = out_ref.shape[1] - spare + c
            out_ref[:, row : row + 1, :] = jnp.broadcast_to(
                own_ref[c][None], (out_ref.shape[0], 1, COLUMNS)
            )
    out_refs[-1][...] = label_ref[...]


def core_sum(kept, received, own, labels, spare, name):
    pairs, rests = lax.axis_size("ca") // 2, lax.axis_size("fe") // 2
    shape = (2 * pairs, rests) + kept.shape[1:]
    *parts, labels = pl.pallas_call(
        functools.partial(core_sum_kernel, spare),
        out_shape=[jax.ShapeDtypeStruct(shape[1:], jnp.float32)] * shape[0]
        + [jax.ShapeDtypeStruct(labels.shape, jnp.int32)],
        compiler_params=pltpu.CompilerParams(vmem_limit_bytes=16 * 1024 * 1024),
        name=name,
    )(kept.reshape(shape), received.reshape(shape), own, labels)
    return parts, labels


def plane_sum_kernel(sources, first_ref, *refs):
    second, outs = refs[:sources], refs[sources:]
    rows = first_ref.shape[1]
    for height, out_ref in enumerate(outs):
        out_ref[0:rows, :] = first_ref[height]
        out_ref[rows:, :] = sum(ref[height] for ref in second)
        out_ref[out_ref.shape[0] - 3 :, :] = second[1][height, second[1].shape[1] - 3 :, :]


def plane_sum(first, second):
    heights, rows, columns = first.shape
    part = jax.ShapeDtypeStruct((rows + second[0].shape[1], columns), jnp.float32)
    return pl.pallas_call(
        functools.partial(plane_sum_kernel, len(second)),
        out_shape=[part] * heights,
        compiler_params=pltpu.CompilerParams(vmem_limit_bytes=16 * 1024 * 1024),
        name="plane_sum",
    )(first, *second)


def first_plane_sum_kernel(*refs):
    *part_refs, label_ref, out_ref, label_out_ref = refs
    out_ref[...] = sum(ref[...] for ref in part_refs)
    label_out_ref[...] = label_ref[...]


def first_plane_sum(parts, labels):
    return pl.pallas_call(
        first_plane_sum_kernel,
        out_shape=[
            jax.ShapeDtypeStruct(parts[0].shape, jnp.float32),
            jax.ShapeDtypeStruct(labels.shape, jnp.int32),
        ],
        compiler_params=pltpu.CompilerParams(vmem_limit_bytes=16 * 1024 * 1024),
        name="first_plane_sum",
    )(*parts, labels)


def to_relative(block, core, pair, last, rest):
    groups, members = lax.axis_size("ca"), lax.axis_size("fe")
    flip = (2 * pair + core) * members + 2 * rest + last
    return lax.ppermute(block, ("ca", "fe"), [(i, i ^ flip) for i in range(groups * members)])


def across_plane(parts):
    return [parts[0]] + [
        to_relative(parts[index], 0, index // 2, index % 2, 0) for index in range(1, len(parts))
    ]


def across_height(parts):
    return [parts[0]] + [to_relative(parts[rest], 0, 0, 0, rest) for rest in range(1, len(parts))]


def three_parts(value):
    first = value.astype(jnp.bfloat16)
    rest = value - first.astype(jnp.float32)
    second = rest.astype(jnp.bfloat16)
    third = (rest - second.astype(jnp.float32)).astype(jnp.bfloat16)
    return first, second, third


def dot_selected(value, selector, contract):
    total = None
    for part in three_parts(value):
        term = lax.dot_general(
            part, selector, (((1,), (contract,)), ((), ())), preferred_element_type=jnp.float32
        )
        total = term if total is None else total + term
    return total


def update_kernel(heights, *refs):
    gathered_refs = refs[:heights]
    own_ref, stress_ref, resistance_ref, weights_ref, table_ref = refs[heights:-2]
    stress_out_ref, nodal_ref = refs[-2:]
    elements = stress_ref.shape[2]
    gathered = sum(ref[:, 0:elements] for ref in gathered_refs)
    starts = [0, padded_rows(CHUNKS[0][1])]
    counted = starts[1] + 9 * CHUNKS[1][1]
    counts = gathered[counted : counted + 1]
    per_brick = 1.0 / (8.0 * jnp.maximum(counts, 1.0))
    frames = [
        jnp.concatenate(
            [
                gathered[start + count * k : start + count * (k + 1)]
                for start, (first, count) in zip(starts, CHUNKS)
            ],
            axis=0,
        )
        * per_brick
        for k in range(9)
    ]

    node = lax.broadcasted_iota(jnp.int32, (COLUMNS, elements), 0)
    element = lax.broadcasted_iota(jnp.int32, (COLUMNS, elements), 1)
    base = element + element // GX
    selectors = [
        (node == base + (step_y * (GX + 1) + step_x)).astype(jnp.bfloat16)
        for step_x in range(2)
        for step_y in range(2)
    ]
    corner = lax.broadcasted_iota(jnp.int32, (24, 1), 0) & 7
    upper_corner = (corner & 1) == 1
    height = lax.axis_index("fe") // 2
    above = height + (lax.axis_index("fe") & 1)
    upper = jnp.zeros((3, COLUMNS), jnp.float32)
    for flip, ref in enumerate(gathered_refs):
        wanted = (height ^ flip) == above
        upper = upper + jnp.where(wanted, ref[ref.shape[0] - 3 :, :], 0.0)
    values = jnp.where(
        upper_corner,
        jnp.concatenate(
            [jnp.broadcast_to(upper[c : c + 1], (8, COLUMNS)) for c in range(3)], axis=0
        ),
        jnp.concatenate([jnp.broadcast_to(own_ref[c], (8, COLUMNS)) for c in range(3)], axis=0),
    )
    corners = jnp.zeros((24, elements), jnp.float32)
    for step in range(4):
        part = jnp.where(corner >> 1 == step, values, 0.0)
        corners = corners + dot_selected(part, selectors[step], 0)
    gradients = []
    for c in range(3):
        product = jnp.dot(
            table_ref[...],
            corners[8 * c : 8 * c + 8],
            precision=lax.Precision.HIGHEST,
            preferred_element_type=jnp.float32,
        )
        gradients.append([product[8 * d : 8 * d + 8] for d in range(3)])
    strain = [
        gradients[0][0],
        gradients[1][1],
        gradients[2][2],
        0.5 * (gradients[1][2] + gradients[2][1]),
        0.5 * (gradients[0][2] + gradients[2][0]),
        0.5 * (gradients[0][1] + gradients[1][0]),
    ]
    volume = strain[0] + strain[1] + strain[2]
    trial = []
    for component in range(6):
        change = 2.0 * SHEAR_MODULUS * strain[component]
        if component < 3:
            change = change + LAMBDA_ELASTIC * volume
        trial.append(stress_ref[component] + change)
    correction = [jnp.zeros_like(trial[0]) for component in range(6)]
    for system in range(12):
        rotated_dir = [
            sum(
                frames[3 * row + axis_id] * SLIP_DIRECTIONS[system][axis_id]
                for axis_id in range(3)
                if SLIP_DIRECTIONS[system][axis_id] != 0.0
            )
            for row in range(3)
        ]
        rotated_normal = [
            sum(frames[3 * row + axis_id] * SLIP_PLANES[system][axis_id] for axis_id in range(3))
            for row in range(3)
        ]
        schmid = [
            rotated_dir[0] * rotated_normal[0],
            rotated_dir[1] * rotated_normal[1],
            rotated_dir[2] * rotated_normal[2],
            0.5 * (rotated_dir[1] * rotated_normal[2] + rotated_dir[2] * rotated_normal[1]),
            0.5 * (rotated_dir[0] * rotated_normal[2] + rotated_dir[2] * rotated_normal[0]),
            0.5 * (rotated_dir[0] * rotated_normal[1] + rotated_dir[1] * rotated_normal[0]),
        ]
        resolved = (
            trial[0] * schmid[0]
            + trial[1] * schmid[1]
            + trial[2] * schmid[2]
            + 2.0 * (trial[3] * schmid[3] + trial[4] * schmid[4] + trial[5] * schmid[5])
        )
        slip_ratio = resolved / resistance_ref[system]
        slip_step = RATE_STEP * slip_ratio * jnp.abs(slip_ratio)
        correction = [
            correction[component] + slip_step * schmid[component] for component in range(6)
        ]
    updated = [
        trial[component] - 2.0 * SHEAR_MODULUS * correction[component] for component in range(6)
    ]
    for component in range(6):
        stress_out_ref[component] = updated[component]
    point_scale = weights_ref[...].astype(jnp.float32) * (1.0 / (FIXED_POINT * 8.0))
    scaled = [value * point_scale for value in updated]
    forces = []
    for rows in [(0, 5, 4), (5, 1, 3), (4, 3, 2)]:
        forces.append(
            lax.dot_general(
                table_ref[...],
                jnp.concatenate([scaled[row] for row in rows], axis=0),
                (((0,), (0,)), ((), ())),
                precision=lax.Precision.HIGHEST,
                preferred_element_type=jnp.float32,
            )
        )
    forces = jnp.concatenate(forces, axis=0)
    nodal = jnp.zeros((24, COLUMNS), jnp.float32)
    for step in range(4):
        part = jnp.where(corner >> 1 == step, forces, 0.0)
        nodal = nodal + dot_selected(part, selectors[step], 1)
    lower = jnp.where(upper_corner, 0.0, nodal)
    above = jnp.where(upper_corner, nodal, 0.0)
    for c in range(3):
        nodal_ref[0, c] = jnp.sum(lower[8 * c : 8 * c + 8], axis=0, keepdims=True)
        nodal_ref[1, c] = jnp.sum(above[8 * c : 8 * c + 8], axis=0, keepdims=True)


def element_update(gathered, own, stress_old, resistance, quad_weights):
    grad_table = shape_gradients()
    table = jnp.asarray(
        [
            [grad_table[quadrature][corner][direction] for corner in range(8)]
            for direction in range(3)
            for quadrature in range(8)
        ],
        dtype=jnp.float32,
    )
    return pl.pallas_call(
        functools.partial(update_kernel, len(gathered)),
        out_shape=(
            jax.ShapeDtypeStruct(stress_old.shape, jnp.float32),
            jax.ShapeDtypeStruct((2,) + own.shape, jnp.float32),
        ),
        compiler_params=pltpu.CompilerParams(vmem_limit_bytes=8 * 1024 * 1024),
        name="stress_update",
    )(*gathered, own, stress_old, resistance, quad_weights, table)


def body(
    grain_ids,
    euler_angles,
    brick_active,
    brick_owner,
    brick_element,
    displacement,
    stress_old,
    resistance,
    quad_weights,
):
    half = lax.axis_size("ca") * lax.axis_size("fe") // 2
    bricks = grain_ids.shape[1]
    owner = lax.optimization_barrier(brick_owner.reshape(bricks))
    labels = jnp.where(brick_active > 0, owner * COLUMNS + brick_element, -1).reshape(1, bricks)
    (first_a, count_a), (first_b, count_b) = CHUNKS
    split, labels, table = cell_sums(first_a, count_a, grain_ids, labels, euler_angles)
    send, labels = brick_sums(split, labels, half, half)
    keep, labels = brick_sums(split, labels, half, 0)
    core_a, labels = core_sum(keep, across_cores(send), displacement, labels, 0, "core_sum_a")
    split, labels = cell_sums(first_b, count_b, grain_ids, labels, table)
    plane_a, labels = first_plane_sum(across_plane(core_a), labels)
    send, labels = brick_sums(split, labels, half, half)
    keep, labels = brick_sums(split, labels, half, 0)
    core_b, labels = core_sum(keep, across_cores(send), displacement, labels, 3, "core_sum_b")
    gathered = plane_sum(plane_a, across_plane(core_b))
    stress_new, nodal = element_update(
        across_height(gathered), displacement, stress_old, resistance, quad_weights
    )
    forces = nodal[0] + passed_along(nodal[1], "fe", 1)
    return (stress_new, forces)


def solution(mesh):
    placed = (
        P(None, ("ca", "fe")),
        P(),
        P(("ca", "fe")),
        P(("ca", "fe"), None),
        P(("ca", "fe")),
        P(None, ("ca", "fe"), None),
        P(None, None, ("ca", "fe")),
        P(None, None, ("ca", "fe")),
        P(None, ("ca", "fe")),
    )
    return jax.shard_map(
        body,
        mesh=mesh,
        in_specs=placed,
        out_specs=(P(None, None, ("ca", "fe")), P(None, ("ca", "fe"), None)),
        check_vma=False,
    )
```

```python
import functools
import functools
import math

import jax
import jax.numpy as jnp
from jax import lax
from jax.experimental import pallas as pl
from jax.experimental.pallas import tpu as pltpu
from jax.sharding import PartitionSpec as P

GX = 15
LANES = 128
COLUMNS = 256
CHUNKS = ((0, 6), (6, 2))
FIELDS = (32, 16, 2, 1)
QUANTUM = float((1 << 16) - 1)

SLIP_PLANES = [
    [value / math.sqrt(3.0) for value in row]
    for row in [[1, 1, 1]] * 3 + [[-1, 1, 1]] * 3 + [[1, -1, 1]] * 3 + [[1, 1, -1]] * 3
]
SLIP_DIRECTIONS = [
    [value / math.sqrt(2.0) for value in row]
    for row in [
        [0, 1, -1],
        [1, 0, -1],
        [1, -1, 0],
        [0, 1, -1],
        [1, 0, 1],
        [1, 1, 0],
        [0, 1, 1],
        [1, 0, -1],
        [1, 1, 0],
        [0, 1, 1],
        [1, 0, 1],
        [1, -1, 0],
    ]
]
LAMBDA_ELASTIC = 1.5
SHEAR_MODULUS = 1.0
RATE_STEP = 0.1
FIXED_POINT = 65536.0


def passed_along(block, axis, distance):
    devices = range(lax.axis_size(axis))
    route = [(i - distance, i) for i in devices if i - distance in devices]
    return lax.ppermute(block, axis, route)


def shape_gradients():
    grad_table = [[[0.0, 0.0, 0.0] for corner in range(8)] for quadrature in range(8)]
    point_offset = 1.0 / math.sqrt(3.0)
    for quadrature in range(8):
        natural = [
            (2 * (quadrature >> shift_bits & 1) - 1) * point_offset for shift_bits in (2, 1, 0)
        ]
        for corner in range(8):
            sign_list = [2 * (corner >> shift_bits & 1) - 1 for shift_bits in (2, 1, 0)]
            factors = [1.0 + sign_list[axis_id] * natural[axis_id] for axis_id in range(3)]
            for direction in range(3):
                others = 1.0
                for axis_id in range(3):
                    if axis_id != direction:
                        others = others * factors[axis_id]
                grad_table[quadrature][corner][direction] = (
                    2.0 * sign_list[direction] * others / 8.0
                )
    return grad_table


def cos_sin(angle):
    square = angle * angle
    cosine = 1.0 / math.factorial(12)
    for power in (10, 8, 6, 4, 2, 0):
        cosine = cosine * square + (-1.0) ** (power // 2) / math.factorial(power)
    sine = 1.0 / math.factorial(13)
    for power in (11, 9, 7, 5, 3, 1):
        sine = sine * square + (-1.0) ** (power // 2) / math.factorial(power)
    return cosine, sine * angle


def rotation_words(euler):
    cos_one, sin_one = cos_sin(0.5 * euler[0 : 0 + 1])
    cos_mid, sin_mid = cos_sin(0.5 * euler[1 : 1 + 1])
    cos_two, sin_two = cos_sin(0.5 * euler[2 : 2 + 1])
    w = cos_mid * (cos_one * cos_two - sin_one * sin_two)
    factor = jnp.where(w < 0.0, -QUANTUM, QUANTUM) / (1.0 + jnp.abs(w))
    x = sin_mid * (cos_one * cos_two + sin_one * sin_two) * factor
    y = sin_mid * (sin_one * cos_two - cos_one * sin_two) * factor
    z = cos_mid * (sin_one * cos_two + cos_one * sin_two) * factor
    x, y, z = [
        jnp.clip(jnp.round(value), -QUANTUM, QUANTUM).astype(jnp.int32) for value in (x, y, z)
    ]
    return [
        lax.shift_left(x, 15) | (lax.shift_right_arithmetic(y, 2) & 0x7FFF),
        lax.shift_left(y & 0x3, 14) | (lax.shift_right_arithmetic(z, 3) & 0x3FFF),
        lax.shift_right_arithmetic(z, 1) & 0x3,
        z & 0x1,
    ]


def table_kernel(euler_ref, table_ref):
    at = 0
    for field, width in zip(rotation_words(euler_ref[...]), FIELDS):
        rows = field.shape[1] // LANES
        shared = 32 // width
        for first in range(0, rows, shared):
            word = field[:, first * LANES : (first + 1) * LANES]
            for other in range(1, shared):
                row = field[:, (first + other) * LANES : (first + other + 1) * LANES]
                word = word | lax.shift_left(row, other * width)
            table_ref[at] = jnp.broadcast_to(word, (8, LANES))
            at += 1


def rotation_table(euler_angles):
    height = euler_angles.shape[1] // LANES * sum(FIELDS) // 32
    return pl.pallas_call(
        table_kernel,
        out_shape=jax.ShapeDtypeStruct((height, 8, LANES), jnp.int32),
        compiler_params=pltpu.CompilerParams(vmem_limit_bytes=8 * 1024 * 1024),
        name="rotation_table",
    )(euler_angles)


def looked_up(table_ref, first_row, rows, lane, bits):
    if rows == 1:
        return lax.gather(
            table_ref[first_row],
            lane,
            lax.GatherDimensionNumbers(
                offset_dims=(),
                collapsed_slice_dims=(1,),
                start_index_map=(1,),
                operand_batching_dims=(0,),
                start_indices_batching_dims=(0,),
            ),
            slice_sizes=(1, 1),
            mode=lax.GatherScatterMode.PROMISE_IN_BOUNDS,
        )
    half = rows // 2
    level = half.bit_length() - 1
    low = looked_up(table_ref, first_row, half, lane, bits)
    high = looked_up(table_ref, first_row + half, half, lane, bits)
    return jnp.where(bits[level], high, low)


def rotation_products(table_ref, table_rows, ids):
    lane = (ids & (LANES - 1))[:, :, None]
    row = lax.shift_right_logical(ids, 7)
    bits = [(row & (1 << level)) != 0 for level in range(table_rows.bit_length() - 1)]
    fields = []
    at = 0
    for width in FIELDS:
        shared = 32 // width
        skipped = shared.bit_length() - 1
        rows = table_rows // shared
        field = looked_up(table_ref, at, rows, lane, bits[skipped:])
        if shared > 1:
            field = lax.shift_right_logical(field, (row & (shared - 1)) * width)
        fields.append(field)
        at += rows
    first, second, third, fourth = fields
    x = lax.shift_right_arithmetic(first, 15).astype(jnp.float32)
    y = lax.shift_right_arithmetic(lax.shift_left(first, 17), 15) | (
        lax.shift_right_logical(second, 14) & 0x3
    )
    z = lax.shift_right_arithmetic(lax.shift_left(second, 18), 15) | (
        lax.shift_left(third & 0x3, 1) | (fourth & 0x1)
    )
    y, z = y.astype(jnp.float32), z.astype(jnp.float32)
    square = x * x + y * y + z * z
    scale = 2.0 / (1.0 + square * (1.0 / (QUANTUM * QUANTUM)))
    w = scale - 1.0
    x, y, z = x * scale, y * scale, z * scale
    return [x * x, y * y, z * z, x * y, x * z, y * z, w * x, w * y, w * z]


def cell_sum_kernel(
    first,
    count,
    ids_ref,
    label_ref,
    table_ref,
    split_ref,
    out_ref,
    label_out_ref,
    tile_ref,
    place_ref,
    masked_ref,
):
    per_octant = ids_ref.shape[0] // 8
    table_rows = table_ref.shape[0] * 32 // sum(FIELDS)
    label_out_ref[...] = label_ref[...]
    groups = tile_ref.shape[0] // 8
    rows_left = count * per_octant - 8 * (groups - 1)
    turns = count // math.gcd(count, 8)

    def tile_sums(tile, carry):
        lanes = pl.ds(pl.multiple_of(tile * LANES, LANES), LANES)
        for octant in range(count):
            tile_ref[pl.ds(octant, per_octant, stride=count), :] = ids_ref[
                pl.ds((first + octant) * per_octant, per_octant), lanes
            ]
        sums = [[jnp.zeros((8, LANES), jnp.float32)] * 9 for turn in range(turns)]
        for group in range(groups):
            ids = tile_ref[pl.ds(8 * group, 8), :]
            products = rotation_products(table_ref, table_rows, ids)
            if group == groups - 1 and rows_left < 8:
                there = lax.broadcasted_iota(jnp.int32, (8, LANES), 0) < rows_left
                products = [jnp.where(there, product, 0.0) for product in products]
            sums[group % turns] = [
                total + product for total, product in zip(sums[group % turns], products)
            ]
        sums = [jnp.concatenate(turned, axis=0) for turned in zip(*sums)]
        sums = [
            sum(total[count * part : count * (part + 1)] for part in range(8 * turns // count))
            for total in sums
        ]
        vector = 2.0 / (QUANTUM * QUANTUM)
        xx, yy, zz, xy, xz, yz = [value * vector for value in sums[:6]]
        wx, wy, wz = [value * (2.0 / QUANTUM) for value in sums[6:]]
        entries = [
            per_octant - (yy + zz),
            xy - wz,
            xz + wy,
            xy + wz,
            per_octant - (xx + zz),
            yz - wx,
            xz - wy,
            yz + wx,
            per_octant - (xx + yy),
            jnp.ones((split_ref.shape[0] // 2 - 9 * count, LANES), jnp.float32),
        ]
        stacked = jnp.concatenate(entries, axis=0)
        leading = stacked.astype(jnp.bfloat16).astype(jnp.float32)
        split_ref[:, lanes] = jnp.concatenate([leading, stacked - leading], axis=0).astype(
            jnp.bfloat16
        )
        return carry

    lax.fori_loop(0, ids_ref.shape[1] // LANES, tile_sums, 0, unroll=2)
    sum_bricks(out_ref.shape[0], split_ref, label_ref, out_ref, place_ref, masked_ref)


def across_cores(block):
    groups = lax.axis_size("ca")
    return lax.ppermute(block, "ca", [(i, i ^ 1) for i in range(groups)])


def brick_sum_kernel(split_ref, label_ref, out_ref, label_out_ref, place_ref, masked_ref):
    label_out_ref[...] = label_ref[...]
    sum_bricks(0, split_ref, label_ref, out_ref, place_ref, masked_ref)


def sum_bricks(base, split_ref, label_ref, out_ref, place_ref, masked_ref):
    bricks = split_ref.shape[1]
    labels = label_ref[...]
    place = place_of(lax.shift_right_arithmetic(labels, COLUMNS.bit_length() - 1))
    place_ref[...] = jnp.where(labels < 0, -1, place - base)
    column = lax.broadcasted_iota(jnp.int32, (COLUMNS, bricks), 0)
    chosen = (column == labels & (COLUMNS - 1)).astype(jnp.bfloat16)
    split_rows = split_ref.shape[0]
    half_rows = split_rows // 2
    members = masked_ref.shape[0] // split_rows

    def place_group(step, carry):
        for member in range(members):
            mask = (place_ref[...] == step * members + member).astype(jnp.bfloat16)
            masked_ref[pl.ds(member * split_rows, split_rows), :] = split_ref[...] * mask
        product = lax.dot_general(
            masked_ref[...],
            chosen,
            (((1,), (1,)), ((), ())),
            preferred_element_type=jnp.float32,
        )
        for member in range(members):
            at = member * split_rows
            out_ref[step * members + member] = (
                product[at : at + half_rows] + product[at + half_rows : at + split_rows]
            )
        return carry

    lax.fori_loop(0, out_ref.shape[0] // members, place_group, 0)


def place_of(owner):
    groups, members = lax.axis_size("ca"), lax.axis_size("fe")
    owner_ca = lax.shift_right_logical(owner, members.bit_length() - 1) ^ lax.axis_index("ca")
    owner_fe = (owner & (members - 1)) ^ lax.axis_index("fe")
    place = (owner_ca & 1) * (groups // 2) + lax.shift_right_logical(owner_ca, 1)
    place = place * 2 + (owner_fe & 1)
    return place * (members // 2) + lax.shift_right_logical(owner_fe, 1)


def cell_sums(first, count, grain_ids, labels, table, places):
    bricks = grain_ids.shape[1]
    tile_rows = -(-count * (grain_ids.shape[0] // 8) // 8) * 8
    rows = padded_rows(count)
    return pl.pallas_call(
        functools.partial(cell_sum_kernel, first, count),
        out_shape=[
            jax.ShapeDtypeStruct((2 * rows, bricks), jnp.bfloat16),
            jax.ShapeDtypeStruct((places, rows, COLUMNS), jnp.float32),
            jax.ShapeDtypeStruct(labels.shape, jnp.int32),
        ],
        scratch_shapes=[pltpu.VMEM((tile_rows, LANES), jnp.int32)]
        + brick_scratch(rows, bricks, places),
        compiler_params=pltpu.CompilerParams(vmem_limit_bytes=28 * 1024 * 1024),
        cost_estimate=pl.CostEstimate(
            flops=count * 4 * 10**9, bytes_accessed=count * 10**7, transcendentals=0
        ),
        name="cell_sums",
    )(grain_ids, labels, table)


def padded_rows(count):
    return -(-9 * count // 8) * 8


def brick_scratch(rows, bricks, places):
    return [
        pltpu.VMEM((1, bricks), jnp.int32),
        pltpu.VMEM((min(16, places) * 2 * rows, bricks), jnp.bfloat16),
    ]


def brick_sums(split, labels, places):
    rows, bricks = split.shape
    return pl.pallas_call(
        brick_sum_kernel,
        out_shape=[
            jax.ShapeDtypeStruct((places, rows // 2, COLUMNS), jnp.float32),
            jax.ShapeDtypeStruct(labels.shape, jnp.int32),
        ],
        scratch_shapes=brick_scratch(rows // 2, bricks, places),
        compiler_params=pltpu.CompilerParams(vmem_limit_bytes=24 * 1024 * 1024),
        cost_estimate=pl.CostEstimate(
            flops=rows * 15 * 10**6, bytes_accessed=rows * 5 * 10**4, transcendentals=0
        ),
        name="brick_sums",
    )(split, labels)


def core_sum_kernel(spare, kept_ref, received_ref, own_ref, label_ref, *out_refs):
    for index, out_ref in enumerate(out_refs[:-1]):
        out_ref[...] = kept_ref[index] + received_ref[index]
        for c in range(spare):
            row = out_ref.shape[1] - spare + c
            out_ref[:, row : row + 1, :] = jnp.broadcast_to(
                own_ref[c][None], (out_ref.shape[0], 1, COLUMNS)
            )
    out_refs[-1][...] = label_ref[...]


def core_sum(kept, received, own, labels, spare, name):
    pairs, rests = lax.axis_size("ca") // 2, lax.axis_size("fe") // 2
    shape = (2 * pairs, rests) + kept.shape[1:]
    *parts, labels = pl.pallas_call(
        functools.partial(core_sum_kernel, spare),
        out_shape=[jax.ShapeDtypeStruct(shape[1:], jnp.float32)] * shape[0]
        + [jax.ShapeDtypeStruct(labels.shape, jnp.int32)],
        compiler_params=pltpu.CompilerParams(vmem_limit_bytes=16 * 1024 * 1024),
        name=name,
    )(kept.reshape(shape), received.reshape(shape), own, labels)
    return parts, labels


def plane_sum_kernel(spare, sources, *refs):
    for height, out_ref in enumerate(refs[sources + 1 : -1]):
        out_ref[...] = sum(ref[height] for ref in refs[:sources])
        if spare:
            rows = pl.ds(out_ref.shape[0] - spare, spare)
            out_ref[rows, :] = refs[1][height, rows, :]
    refs[-1][...] = refs[sources][...]


def plane_sum(parts, labels, spare, name):
    part = jax.ShapeDtypeStruct(parts[0].shape[1:], jnp.float32)
    *parts, labels = pl.pallas_call(
        functools.partial(plane_sum_kernel, spare, len(parts)),
        out_shape=[part] * parts[0].shape[0] + [jax.ShapeDtypeStruct(labels.shape, jnp.int32)],
        compiler_params=pltpu.CompilerParams(vmem_limit_bytes=16 * 1024 * 1024),
        name=name,
    )(*parts, labels)
    return parts, labels


def to_relative(block, core, pair, last, rest):
    groups, members = lax.axis_size("ca"), lax.axis_size("fe")
    flip = (2 * pair + core) * members + 2 * rest + last
    return lax.ppermute(block, ("ca", "fe"), [(i, i ^ flip) for i in range(groups * members)])


def across_plane(parts):
    return [parts[0]] + [
        to_relative(parts[index], 0, index // 2, index % 2, 0) for index in range(1, len(parts))
    ]


def across_height(parts):
    return [parts[0]] + [to_relative(parts[rest], 0, 0, 0, rest) for rest in range(1, len(parts))]


def three_parts(value):
    first = value.astype(jnp.bfloat16)
    rest = value - first.astype(jnp.float32)
    second = rest.astype(jnp.bfloat16)
    third = (rest - second.astype(jnp.float32)).astype(jnp.bfloat16)
    return first, second, third


def dot_selected(value, selector, contract):
    total = None
    for part in three_parts(value):
        term = lax.dot_general(
            part, selector, (((1,), (contract,)), ((), ())), preferred_element_type=jnp.float32
        )
        total = term if total is None else total + term
    return total


def update_kernel(heights, *refs):
    first_refs, second_refs = refs[:heights], refs[heights : 2 * heights]
    own_ref, stress_ref, resistance_ref, weights_ref, table_ref = refs[2 * heights : -2]
    stress_out_ref, nodal_ref = refs[-2:]
    elements = stress_ref.shape[2]
    gathered = [
        sum(ref[:, 0:elements] for ref in chunk_refs) for chunk_refs in (first_refs, second_refs)
    ]
    counted = 9 * CHUNKS[1][1]
    counts = gathered[1][counted : counted + 1]
    per_brick = 1.0 / (8.0 * jnp.maximum(counts, 1.0))
    frames = [
        jnp.concatenate(
            [
                sums[count * k : count * (k + 1)]
                for sums, (first, count) in zip(gathered, CHUNKS)
            ],
            axis=0,
        )
        * per_brick
        for k in range(9)
    ]

    node = lax.broadcasted_iota(jnp.int32, (COLUMNS, elements), 0)
    element = lax.broadcasted_iota(jnp.int32, (COLUMNS, elements), 1)
    base = element + element // GX
    selectors = [
        (node == base + (step_y * (GX + 1) + step_x)).astype(jnp.bfloat16)
        for step_x in range(2)
        for step_y in range(2)
    ]
    corner = lax.broadcasted_iota(jnp.int32, (24, 1), 0) & 7
    upper_corner = (corner & 1) == 1
    height = lax.axis_index("fe") // 2
    above = height + (lax.axis_index("fe") & 1)
    upper = jnp.zeros((3, COLUMNS), jnp.float32)
    for flip, ref in enumerate(second_refs):
        wanted = (height ^ flip) == above
        upper = upper + jnp.where(wanted, ref[ref.shape[0] - 3 :, :], 0.0)
    values = jnp.where(
        upper_corner,
        jnp.concatenate(
            [jnp.broadcast_to(upper[c : c + 1], (8, COLUMNS)) for c in range(3)], axis=0
        ),
        jnp.concatenate([jnp.broadcast_to(own_ref[c], (8, COLUMNS)) for c in range(3)], axis=0),
    )
    corners = jnp.zeros((24, elements), jnp.float32)
    for step in range(4):
        part = jnp.where(corner >> 1 == step, values, 0.0)
        corners = corners + dot_selected(part, selectors[step], 0)
    gradients = []
    for c in range(3):
        product = jnp.dot(
            table_ref[...],
            corners[8 * c : 8 * c + 8],
            precision=lax.Precision.HIGHEST,
            preferred_element_type=jnp.float32,
        )
        gradients.append([product[8 * d : 8 * d + 8] for d in range(3)])
    strain = [
        gradients[0][0],
        gradients[1][1],
        gradients[2][2],
        0.5 * (gradients[1][2] + gradients[2][1]),
        0.5 * (gradients[0][2] + gradients[2][0]),
        0.5 * (gradients[0][1] + gradients[1][0]),
    ]
    volume = strain[0] + strain[1] + strain[2]
    trial = []
    for component in range(6):
        change = 2.0 * SHEAR_MODULUS * strain[component]
        if component < 3:
            change = change + LAMBDA_ELASTIC * volume
        trial.append(stress_ref[component] + change)
    correction = [jnp.zeros_like(trial[0]) for component in range(6)]
    for system in range(12):
        rotated_dir = [
            sum(
                frames[3 * row + axis_id] * SLIP_DIRECTIONS[system][axis_id]
                for axis_id in range(3)
                if SLIP_DIRECTIONS[system][axis_id] != 0.0
            )
            for row in range(3)
        ]
        rotated_normal = [
            sum(frames[3 * row + axis_id] * SLIP_PLANES[system][axis_id] for axis_id in range(3))
            for row in range(3)
        ]
        schmid = [
            rotated_dir[0] * rotated_normal[0],
            rotated_dir[1] * rotated_normal[1],
            rotated_dir[2] * rotated_normal[2],
            0.5 * (rotated_dir[1] * rotated_normal[2] + rotated_dir[2] * rotated_normal[1]),
            0.5 * (rotated_dir[0] * rotated_normal[2] + rotated_dir[2] * rotated_normal[0]),
            0.5 * (rotated_dir[0] * rotated_normal[1] + rotated_dir[1] * rotated_normal[0]),
        ]
        resolved = (
            trial[0] * schmid[0]
            + trial[1] * schmid[1]
            + trial[2] * schmid[2]
            + 2.0 * (trial[3] * schmid[3] + trial[4] * schmid[4] + trial[5] * schmid[5])
        )
        slip_ratio = resolved / resistance_ref[system]
        slip_step = RATE_STEP * slip_ratio * jnp.abs(slip_ratio)
        correction = [
            correction[component] + slip_step * schmid[component] for component in range(6)
        ]
    updated = [
        trial[component] - 2.0 * SHEAR_MODULUS * correction[component] for component in range(6)
    ]
    for component in range(6):
        stress_out_ref[component] = updated[component]
    point_scale = weights_ref[...].astype(jnp.float32) * (1.0 / (FIXED_POINT * 8.0))
    scaled = [value * point_scale for value in updated]
    forces = []
    for rows in [(0, 5, 4), (5, 1, 3), (4, 3, 2)]:
        forces.append(
            lax.dot_general(
                table_ref[...],
                jnp.concatenate([scaled[row] for row in rows], axis=0),
                (((0,), (0,)), ((), ())),
                precision=lax.Precision.HIGHEST,
                preferred_element_type=jnp.float32,
            )
        )
    forces = jnp.concatenate(forces, axis=0)
    nodal = jnp.zeros((24, COLUMNS), jnp.float32)
    for step in range(4):
        part = jnp.where(corner >> 1 == step, forces, 0.0)
        nodal = nodal + dot_selected(part, selectors[step], 1)
    lower = jnp.where(upper_corner, 0.0, nodal)
    above = jnp.where(upper_corner, nodal, 0.0)
    for c in range(3):
        nodal_ref[0, c] = jnp.sum(lower[8 * c : 8 * c + 8], axis=0, keepdims=True)
        nodal_ref[1, c] = jnp.sum(above[8 * c : 8 * c + 8], axis=0, keepdims=True)


def element_update(first, second, own, stress_old, resistance, quad_weights):
    grad_table = shape_gradients()
    table = jnp.asarray(
        [
            [grad_table[quadrature][corner][direction] for corner in range(8)]
            for direction in range(3)
            for quadrature in range(8)
        ],
        dtype=jnp.float32,
    )
    return pl.pallas_call(
        functools.partial(update_kernel, len(first)),
        out_shape=(
            jax.ShapeDtypeStruct(stress_old.shape, jnp.float32),
            jax.ShapeDtypeStruct((2,) + own.shape, jnp.float32),
        ),
        compiler_params=pltpu.CompilerParams(vmem_limit_bytes=8 * 1024 * 1024),
        name="stress_update",
    )(*first, *second, own, stress_old, resistance, quad_weights, table)


def body(
    grain_ids,
    euler_angles,
    brick_active,
    brick_owner,
    brick_element,
    displacement,
    stress_old,
    resistance,
    quad_weights,
):
    half = lax.axis_size("ca") * lax.axis_size("fe") // 2
    bricks = grain_ids.shape[1]
    owner = lax.optimization_barrier(brick_owner.reshape(bricks))
    labels = jnp.where(brick_active > 0, owner * COLUMNS + brick_element, -1).reshape(1, bricks)
    (first_a, count_a), (first_b, count_b) = CHUNKS
    table = rotation_table(euler_angles)
    split, send, labels = cell_sums(first_a, count_a, grain_ids, labels, table, half)
    keep, labels = brick_sums(split, labels, half)
    core_a, labels = core_sum(keep, across_cores(send), displacement, labels, 0, "core_sum_a")
    split, send, labels = cell_sums(first_b, count_b, grain_ids, labels, table, half)
    plane_a, labels = plane_sum(across_plane(core_a), labels, 0, "plane_sum_a")
    keep, labels = brick_sums(split, labels, half)
    core_b, labels = core_sum(keep, across_cores(send), displacement, labels, 3, "core_sum_b")
    plane_b, labels = plane_sum(across_plane(core_b), labels, 3, "plane_sum_b")
    stress_new, nodal = element_update(
        across_height(plane_a),
        across_height(plane_b),
        displacement,
        stress_old,
        resistance,
        quad_weights,
    )
    forces = nodal[0] + passed_along(nodal[1], "fe", 1)
    return (stress_new, forces)


def solution(mesh):
    placed = (
        P(None, ("ca", "fe")),
        P(),
        P(("ca", "fe")),
        P(("ca", "fe"), None),
        P(("ca", "fe")),
        P(None, ("ca", "fe"), None),
        P(None, None, ("ca", "fe")),
        P(None, None, ("ca", "fe")),
        P(None, ("ca", "fe")),
    )
    return jax.shard_map(
        body,
        mesh=mesh,
        in_specs=placed,
        out_specs=(P(None, None, ("ca", "fe")), P(None, ("ca", "fe"), None)),
        check_vma=False,
    )
```

```python
import functools
import functools
import math

import jax
import jax.numpy as jnp
from jax import lax
from jax.experimental import pallas as pl
from jax.experimental.pallas import tpu as pltpu
from jax.sharding import PartitionSpec as P

GX = 15
LANES = 128
COLUMNS = 256
CHUNKS = ((0, 6), (6, 2))
FIELDS = (32, 16, 2, 1)
QUANTUM = float((1 << 16) - 1)

SLIP_PLANES = [
    [value / math.sqrt(3.0) for value in row]
    for row in [[1, 1, 1]] * 3 + [[-1, 1, 1]] * 3 + [[1, -1, 1]] * 3 + [[1, 1, -1]] * 3
]
SLIP_DIRECTIONS = [
    [value / math.sqrt(2.0) for value in row]
    for row in [
        [0, 1, -1],
        [1, 0, -1],
        [1, -1, 0],
        [0, 1, -1],
        [1, 0, 1],
        [1, 1, 0],
        [0, 1, 1],
        [1, 0, -1],
        [1, 1, 0],
        [0, 1, 1],
        [1, 0, 1],
        [1, -1, 0],
    ]
]
LAMBDA_ELASTIC = 1.5
SHEAR_MODULUS = 1.0
RATE_STEP = 0.1
FIXED_POINT = 65536.0


def passed_along(block, axis, distance):
    devices = range(lax.axis_size(axis))
    route = [(i - distance, i) for i in devices if i - distance in devices]
    return lax.ppermute(block, axis, route)


def shape_gradients():
    grad_table = [[[0.0, 0.0, 0.0] for corner in range(8)] for quadrature in range(8)]
    point_offset = 1.0 / math.sqrt(3.0)
    for quadrature in range(8):
        natural = [
            (2 * (quadrature >> shift_bits & 1) - 1) * point_offset for shift_bits in (2, 1, 0)
        ]
        for corner in range(8):
            sign_list = [2 * (corner >> shift_bits & 1) - 1 for shift_bits in (2, 1, 0)]
            factors = [1.0 + sign_list[axis_id] * natural[axis_id] for axis_id in range(3)]
            for direction in range(3):
                others = 1.0
                for axis_id in range(3):
                    if axis_id != direction:
                        others = others * factors[axis_id]
                grad_table[quadrature][corner][direction] = (
                    2.0 * sign_list[direction] * others / 8.0
                )
    return grad_table


def cos_sin(angle):
    square = angle * angle
    cosine = 1.0 / math.factorial(12)
    for power in (10, 8, 6, 4, 2, 0):
        cosine = cosine * square + (-1.0) ** (power // 2) / math.factorial(power)
    sine = 1.0 / math.factorial(13)
    for power in (11, 9, 7, 5, 3, 1):
        sine = sine * square + (-1.0) ** (power // 2) / math.factorial(power)
    return cosine, sine * angle


def rotation_words(euler):
    cos_one, sin_one = cos_sin(0.5 * euler[0 : 0 + 1])
    cos_mid, sin_mid = cos_sin(0.5 * euler[1 : 1 + 1])
    cos_two, sin_two = cos_sin(0.5 * euler[2 : 2 + 1])
    w = cos_mid * (cos_one * cos_two - sin_one * sin_two)
    factor = jnp.where(w < 0.0, -QUANTUM, QUANTUM) / (1.0 + jnp.abs(w))
    x = sin_mid * (cos_one * cos_two + sin_one * sin_two) * factor
    y = sin_mid * (sin_one * cos_two - cos_one * sin_two) * factor
    z = cos_mid * (sin_one * cos_two + cos_one * sin_two) * factor
    x, y, z = [
        jnp.clip(jnp.round(value), -QUANTUM, QUANTUM).astype(jnp.int32) for value in (x, y, z)
    ]
    return [
        lax.shift_left(x, 15) | (lax.shift_right_arithmetic(y, 2) & 0x7FFF),
        lax.shift_left(y & 0x3, 14) | (lax.shift_right_arithmetic(z, 3) & 0x3FFF),
        lax.shift_right_arithmetic(z, 1) & 0x3,
        z & 0x1,
    ]


def table_kernel(euler_ref, table_ref):
    at = 0
    for field, width in zip(rotation_words(euler_ref[...]), FIELDS):
        rows = field.shape[1] // LANES
        shared = 32 // width
        for first in range(0, rows, shared):
            word = field[:, first * LANES : (first + 1) * LANES]
            for other in range(1, shared):
                row = field[:, (first + other) * LANES : (first + other + 1) * LANES]
                word = word | lax.shift_left(row, other * width)
            table_ref[at] = jnp.broadcast_to(word, (8, LANES))
            at += 1


def rotation_table(euler_angles):
    height = euler_angles.shape[1] // LANES * sum(FIELDS) // 32
    return pl.pallas_call(
        table_kernel,
        out_shape=jax.ShapeDtypeStruct((height, 8, LANES), jnp.int32),
        compiler_params=pltpu.CompilerParams(vmem_limit_bytes=8 * 1024 * 1024),
        cost_estimate=pl.CostEstimate(flops=10**6, bytes_accessed=10**7, transcendentals=0),
        name="rotation_table",
    )(euler_angles)


def looked_up(table_ref, first_row, rows, lane, bits):
    if rows == 1:
        return lax.gather(
            table_ref[first_row],
            lane,
            lax.GatherDimensionNumbers(
                offset_dims=(),
                collapsed_slice_dims=(1,),
                start_index_map=(1,),
                operand_batching_dims=(0,),
                start_indices_batching_dims=(0,),
            ),
            slice_sizes=(1, 1),
            mode=lax.GatherScatterMode.PROMISE_IN_BOUNDS,
        )
    half = rows // 2
    level = half.bit_length() - 1
    low = looked_up(table_ref, first_row, half, lane, bits)
    high = looked_up(table_ref, first_row + half, half, lane, bits)
    return jnp.where(bits[level], high, low)


def rotation_products(table_ref, table_rows, ids):
    lane = (ids & (LANES - 1))[:, :, None]
    row = lax.shift_right_logical(ids, 7)
    bits = [(row & (1 << level)) != 0 for level in range(table_rows.bit_length() - 1)]
    fields = []
    at = 0
    for width in FIELDS:
        shared = 32 // width
        skipped = shared.bit_length() - 1
        rows = table_rows // shared
        field = looked_up(table_ref, at, rows, lane, bits[skipped:])
        if shared > 1:
            field = lax.shift_right_logical(field, (row & (shared - 1)) * width)
        fields.append(field)
        at += rows
    first, second, third, fourth = fields
    x = lax.shift_right_arithmetic(first, 15).astype(jnp.float32)
    y = lax.shift_right_arithmetic(lax.shift_left(first, 17), 15) | (
        lax.shift_right_logical(second, 14) & 0x3
    )
    z = lax.shift_right_arithmetic(lax.shift_left(second, 18), 15) | (
        lax.shift_left(third & 0x3, 1) | (fourth & 0x1)
    )
    y, z = y.astype(jnp.float32), z.astype(jnp.float32)
    square = x * x + y * y + z * z
    scale = 2.0 / (1.0 + square * (1.0 / (QUANTUM * QUANTUM)))
    w = scale - 1.0
    x, y, z = x * scale, y * scale, z * scale
    return [x * x, y * y, z * z, x * y, x * z, y * z, w * x, w * y, w * z]


def cell_sum_kernel(
    octants,
    per_octant,
    ids_ref,
    label_ref,
    table_ref,
    split_ref,
    out_ref,
    label_out_ref,
    *refs,
):
    first, count = octants
    start = ids_ref.shape[0] - (8 - first) * per_octant
    tile_ref, place_ref, masked_ref = refs[-3:]
    if len(refs) > 3:
        refs[0][...] = ids_ref[pl.ds(ids_ref.shape[0] - refs[0].shape[0], refs[0].shape[0]), :]
    table_rows = table_ref.shape[0] * 32 // sum(FIELDS)
    label_out_ref[...] = label_ref[...]
    groups = tile_ref.shape[0] // 8
    rows_left = count * per_octant - 8 * (groups - 1)
    turns = count // math.gcd(count, 8)

    def tile_sums(tile, carry):
        lanes = pl.ds(pl.multiple_of(tile * LANES, LANES), LANES)
        for octant in range(count):
            tile_ref[pl.ds(octant, per_octant, stride=count), :] = ids_ref[
                pl.ds(start + octant * per_octant, per_octant), lanes
            ]
        sums = [[jnp.zeros((8, LANES), jnp.float32)] * 9 for turn in range(turns)]
        for group in range(groups):
            ids = tile_ref[pl.ds(8 * group, 8), :]
            products = rotation_products(table_ref, table_rows, ids)
            if group == groups - 1 and rows_left < 8:
                there = lax.broadcasted_iota(jnp.int32, (8, LANES), 0) < rows_left
                products = [jnp.where(there, product, 0.0) for product in products]
            sums[group % turns] = [
                total + product for total, product in zip(sums[group % turns], products)
            ]
        sums = [jnp.concatenate(turned, axis=0) for turned in zip(*sums)]
        sums = [
            sum(total[count * part : count * (part + 1)] for part in range(8 * turns // count))
            for total in sums
        ]
        vector = 2.0 / (QUANTUM * QUANTUM)
        xx, yy, zz, xy, xz, yz = [value * vector for value in sums[:6]]
        wx, wy, wz = [value * (2.0 / QUANTUM) for value in sums[6:]]
        entries = [
            per_octant - (yy + zz),
            xy - wz,
            xz + wy,
            xy + wz,
            per_octant - (xx + zz),
            yz - wx,
            xz - wy,
            yz + wx,
            per_octant - (xx + yy),
            jnp.ones((split_ref.shape[0] // 2 - 9 * count, LANES), jnp.float32),
        ]
        stacked = jnp.concatenate(entries, axis=0)
        leading = stacked.astype(jnp.bfloat16).astype(jnp.float32)
        split_ref[:, lanes] = jnp.concatenate([leading, stacked - leading], axis=0).astype(
            jnp.bfloat16
        )
        return carry

    lax.fori_loop(0, ids_ref.shape[1] // LANES, tile_sums, 0, unroll=2)
    sum_bricks(out_ref.shape[0], split_ref, label_ref, out_ref, place_ref, masked_ref)


def across_cores(block):
    groups = lax.axis_size("ca")
    return lax.ppermute(block, "ca", [(i, i ^ 1) for i in range(groups)])


def brick_sum_kernel(split_ref, label_ref, out_ref, label_out_ref, place_ref, masked_ref):
    label_out_ref[...] = label_ref[...]
    sum_bricks(0, split_ref, label_ref, out_ref, place_ref, masked_ref)


def sum_bricks(base, split_ref, label_ref, out_ref, place_ref, masked_ref):
    bricks = split_ref.shape[1]
    labels = label_ref[...]
    place = place_of(lax.shift_right_arithmetic(labels, COLUMNS.bit_length() - 1))
    place_ref[...] = jnp.where(labels < 0, -1, place - base)
    column = lax.broadcasted_iota(jnp.int32, (COLUMNS, bricks), 0)
    chosen = (column == labels & (COLUMNS - 1)).astype(jnp.bfloat16)
    split_rows = split_ref.shape[0]
    half_rows = split_rows // 2
    members = masked_ref.shape[0] // split_rows

    def place_group(step, carry):
        for member in range(members):
            mask = (place_ref[...] == step * members + member).astype(jnp.bfloat16)
            masked_ref[pl.ds(member * split_rows, split_rows), :] = split_ref[...] * mask
        product = lax.dot_general(
            masked_ref[...],
            chosen,
            (((1,), (1,)), ((), ())),
            preferred_element_type=jnp.float32,
        )
        for member in range(members):
            at = member * split_rows
            out_ref[step * members + member] = (
                product[at : at + half_rows] + product[at + half_rows : at + split_rows]
            )
        return carry

    lax.fori_loop(0, out_ref.shape[0] // members, place_group, 0)


def place_of(owner):
    groups, members = lax.axis_size("ca"), lax.axis_size("fe")
    owner_ca = lax.shift_right_logical(owner, members.bit_length() - 1) ^ lax.axis_index("ca")
    owner_fe = (owner & (members - 1)) ^ lax.axis_index("fe")
    place = (owner_ca & 1) * (groups // 2) + lax.shift_right_logical(owner_ca, 1)
    place = place * 2 + (owner_fe & 1)
    return place * (members // 2) + lax.shift_right_logical(owner_fe, 1)


def cell_sums(octants, per_octant, ids, labels, table, places):
    first, count = octants
    bricks = ids.shape[1]
    rows = padded_rows(count)
    out_shape = [
        jax.ShapeDtypeStruct((2 * rows, bricks), jnp.bfloat16),
        jax.ShapeDtypeStruct((places, rows, COLUMNS), jnp.float32),
        jax.ShapeDtypeStruct(labels.shape, jnp.int32),
    ]
    left = 8 - first - count
    if left:
        out_shape.append(jax.ShapeDtypeStruct((-(-left * per_octant // 8) * 8, bricks), jnp.int32))
    return pl.pallas_call(
        functools.partial(cell_sum_kernel, octants, per_octant),
        out_shape=out_shape,
        scratch_shapes=[pltpu.VMEM((-(-count * per_octant // 8) * 8, LANES), jnp.int32)]
        + brick_scratch(rows, bricks, places),
        compiler_params=pltpu.CompilerParams(vmem_limit_bytes=28 * 1024 * 1024),
        cost_estimate=pl.CostEstimate(
            flops=count * 4 * 10**9, bytes_accessed=count * 10**7, transcendentals=0
        ),
        name="cell_sums",
    )(ids, labels, table)


def padded_rows(count):
    return -(-9 * count // 8) * 8


def brick_scratch(rows, bricks, places):
    return [
        pltpu.VMEM((1, bricks), jnp.int32),
        pltpu.VMEM((min(16, places) * 2 * rows, bricks), jnp.bfloat16),
    ]


def brick_sums(split, labels, places):
    rows, bricks = split.shape
    return pl.pallas_call(
        brick_sum_kernel,
        out_shape=[
            jax.ShapeDtypeStruct((places, rows // 2, COLUMNS), jnp.float32),
            jax.ShapeDtypeStruct(labels.shape, jnp.int32),
        ],
        scratch_shapes=brick_scratch(rows // 2, bricks, places),
        compiler_params=pltpu.CompilerParams(vmem_limit_bytes=24 * 1024 * 1024),
        cost_estimate=pl.CostEstimate(
            flops=rows * 15 * 10**6, bytes_accessed=rows * 5 * 10**4, transcendentals=0
        ),
        name="brick_sums",
    )(split, labels)


def core_sum_kernel(spare, kept_ref, received_ref, own_ref, label_ref, *out_refs):
    for index, out_ref in enumerate(out_refs[:-1]):
        out_ref[...] = kept_ref[index] + received_ref[index]
        for c in range(spare):
            row = out_ref.shape[1] - spare + c
            out_ref[:, row : row + 1, :] = jnp.broadcast_to(
                own_ref[c][None], (out_ref.shape[0], 1, COLUMNS)
            )
    out_refs[-1][...] = label_ref[...]


def core_sum(kept, received, own, labels, spare, name):
    pairs, rests = lax.axis_size("ca") // 2, lax.axis_size("fe") // 2
    shape = (2 * pairs, rests) + kept.shape[1:]
    *parts, labels = pl.pallas_call(
        functools.partial(core_sum_kernel, spare),
        out_shape=[jax.ShapeDtypeStruct(shape[1:], jnp.float32)] * shape[0]
        + [jax.ShapeDtypeStruct(labels.shape, jnp.int32)],
        compiler_params=pltpu.CompilerParams(vmem_limit_bytes=16 * 1024 * 1024),
        name=name,
    )(kept.reshape(shape), received.reshape(shape), own, labels)
    return parts, labels


def plane_sum_kernel(spare, sources, passed, *refs):
    outs = refs[sources + passed :]
    for height, out_ref in enumerate(outs[: len(outs) - passed]):
        out_ref[...] = sum(ref[height] for ref in refs[:sources])
        if spare:
            rows = pl.ds(out_ref.shape[0] - spare, spare)
            out_ref[rows, :] = refs[1][height, rows, :]
    for i in range(passed):
        outs[len(outs) - passed + i][...] = refs[sources + i][...]


def plane_sum(parts, passed, spare, name):
    part = jax.ShapeDtypeStruct(parts[0].shape[1:], jnp.float32)
    out = pl.pallas_call(
        functools.partial(plane_sum_kernel, spare, len(parts), len(passed)),
        out_shape=[part] * parts[0].shape[0]
        + [jax.ShapeDtypeStruct(array.shape, array.dtype) for array in passed],
        compiler_params=pltpu.CompilerParams(vmem_limit_bytes=16 * 1024 * 1024),
        name=name,
    )(*parts, *passed)
    return out[: parts[0].shape[0]], *out[parts[0].shape[0] :]


def to_relative(block, core, pair, last, rest):
    groups, members = lax.axis_size("ca"), lax.axis_size("fe")
    flip = (2 * pair + core) * members + 2 * rest + last
    return lax.ppermute(block, ("ca", "fe"), [(i, i ^ flip) for i in range(groups * members)])


def across_plane(parts):
    return [parts[0]] + [
        to_relative(parts[index], 0, index // 2, index % 2, 0) for index in range(1, len(parts))
    ]


def across_height(parts):
    return [parts[0]] + [to_relative(parts[rest], 0, 0, 0, rest) for rest in range(1, len(parts))]


def three_parts(value):
    first = value.astype(jnp.bfloat16)
    rest = value - first.astype(jnp.float32)
    second = rest.astype(jnp.bfloat16)
    third = (rest - second.astype(jnp.float32)).astype(jnp.bfloat16)
    return first, second, third


def dot_selected(value, selector, contract):
    total = None
    for part in three_parts(value):
        term = lax.dot_general(
            part, selector, (((1,), (contract,)), ((), ())), preferred_element_type=jnp.float32
        )
        total = term if total is None else total + term
    return total


def update_kernel(heights, *refs):
    first_refs, second_refs = refs[:heights], refs[heights : 2 * heights]
    own_ref, stress_ref, resistance_ref, weights_ref, table_ref = refs[2 * heights : -2]
    stress_out_ref, nodal_ref = refs[-2:]
    elements = stress_ref.shape[2]
    gathered = [
        sum(ref[:, 0:elements] for ref in chunk_refs) for chunk_refs in (first_refs, second_refs)
    ]
    counted = 9 * CHUNKS[1][1]
    counts = gathered[1][counted : counted + 1]
    per_brick = 1.0 / (8.0 * jnp.maximum(counts, 1.0))
    frames = [
        jnp.concatenate(
            [
                sums[count * k : count * (k + 1)]
                for sums, (first, count) in zip(gathered, CHUNKS)
            ],
            axis=0,
        )
        * per_brick
        for k in range(9)
    ]

    node = lax.broadcasted_iota(jnp.int32, (COLUMNS, elements), 0)
    element = lax.broadcasted_iota(jnp.int32, (COLUMNS, elements), 1)
    base = element + element // GX
    selectors = [
        (node == base + (step_y * (GX + 1) + step_x)).astype(jnp.bfloat16)
        for step_x in range(2)
        for step_y in range(2)
    ]
    corner = lax.broadcasted_iota(jnp.int32, (24, 1), 0) & 7
    upper_corner = (corner & 1) == 1
    height = lax.axis_index("fe") // 2
    above = height + (lax.axis_index("fe") & 1)
    upper = jnp.zeros((3, COLUMNS), jnp.float32)
    for flip, ref in enumerate(second_refs):
        wanted = (height ^ flip) == above
        upper = upper + jnp.where(wanted, ref[ref.shape[0] - 3 :, :], 0.0)
    values = jnp.where(
        upper_corner,
        jnp.concatenate(
            [jnp.broadcast_to(upper[c : c + 1], (8, COLUMNS)) for c in range(3)], axis=0
        ),
        jnp.concatenate([jnp.broadcast_to(own_ref[c], (8, COLUMNS)) for c in range(3)], axis=0),
    )
    corners = jnp.zeros((24, elements), jnp.float32)
    for step in range(4):
        part = jnp.where(corner >> 1 == step, values, 0.0)
        corners = corners + dot_selected(part, selectors[step], 0)
    gradients = []
    for c in range(3):
        product = jnp.dot(
            table_ref[...],
            corners[8 * c : 8 * c + 8],
            precision=lax.Precision.HIGHEST,
            preferred_element_type=jnp.float32,
        )
        gradients.append([product[8 * d : 8 * d + 8] for d in range(3)])
    strain = [
        gradients[0][0],
        gradients[1][1],
        gradients[2][2],
        0.5 * (gradients[1][2] + gradients[2][1]),
        0.5 * (gradients[0][2] + gradients[2][0]),
        0.5 * (gradients[0][1] + gradients[1][0]),
    ]
    volume = strain[0] + strain[1] + strain[2]
    trial = []
    for component in range(6):
        change = 2.0 * SHEAR_MODULUS * strain[component]
        if component < 3:
            change = change + LAMBDA_ELASTIC * volume
        trial.append(stress_ref[component] + change)
    correction = [jnp.zeros_like(trial[0]) for component in range(6)]
    for system in range(12):
        rotated_dir = [
            sum(
                frames[3 * row + axis_id] * SLIP_DIRECTIONS[system][axis_id]
                for axis_id in range(3)
                if SLIP_DIRECTIONS[system][axis_id] != 0.0
            )
            for row in range(3)
        ]
        rotated_normal = [
            sum(frames[3 * row + axis_id] * SLIP_PLANES[system][axis_id] for axis_id in range(3))
            for row in range(3)
        ]
        schmid = [
            rotated_dir[0] * rotated_normal[0],
            rotated_dir[1] * rotated_normal[1],
            rotated_dir[2] * rotated_normal[2],
            0.5 * (rotated_dir[1] * rotated_normal[2] + rotated_dir[2] * rotated_normal[1]),
            0.5 * (rotated_dir[0] * rotated_normal[2] + rotated_dir[2] * rotated_normal[0]),
            0.5 * (rotated_dir[0] * rotated_normal[1] + rotated_dir[1] * rotated_normal[0]),
        ]
        resolved = (
            trial[0] * schmid[0]
            + trial[1] * schmid[1]
            + trial[2] * schmid[2]
            + 2.0 * (trial[3] * schmid[3] + trial[4] * schmid[4] + trial[5] * schmid[5])
        )
        slip_ratio = resolved / resistance_ref[system]
        slip_step = RATE_STEP * slip_ratio * jnp.abs(slip_ratio)
        correction = [
            correction[component] + slip_step * schmid[component] for component in range(6)
        ]
    updated = [
        trial[component] - 2.0 * SHEAR_MODULUS * correction[component] for component in range(6)
    ]
    for component in range(6):
        stress_out_ref[component] = updated[component]
    point_scale = weights_ref[...].astype(jnp.float32) * (1.0 / (FIXED_POINT * 8.0))
    scaled = [value * point_scale for value in updated]
    forces = []
    for rows in [(0, 5, 4), (5, 1, 3), (4, 3, 2)]:
        forces.append(
            lax.dot_general(
                table_ref[...],
                jnp.concatenate([scaled[row] for row in rows], axis=0),
                (((0,), (0,)), ((), ())),
                precision=lax.Precision.HIGHEST,
                preferred_element_type=jnp.float32,
            )
        )
    forces = jnp.concatenate(forces, axis=0)
    nodal = jnp.zeros((24, COLUMNS), jnp.float32)
    for step in range(4):
        part = jnp.where(corner >> 1 == step, forces, 0.0)
        nodal = nodal + dot_selected(part, selectors[step], 1)
    lower = jnp.where(upper_corner, 0.0, nodal)
    above = jnp.where(upper_corner, nodal, 0.0)
    for c in range(3):
        nodal_ref[0, c] = jnp.sum(lower[8 * c : 8 * c + 8], axis=0, keepdims=True)
        nodal_ref[1, c] = jnp.sum(above[8 * c : 8 * c + 8], axis=0, keepdims=True)


def element_update(first, second, own, stress_old, resistance, quad_weights):
    grad_table = shape_gradients()
    table = jnp.asarray(
        [
            [grad_table[quadrature][corner][direction] for corner in range(8)]
            for direction in range(3)
            for quadrature in range(8)
        ],
        dtype=jnp.float32,
    )
    return pl.pallas_call(
        functools.partial(update_kernel, len(first)),
        out_shape=(
            jax.ShapeDtypeStruct(stress_old.shape, jnp.float32),
            jax.ShapeDtypeStruct((2,) + own.shape, jnp.float32),
        ),
        compiler_params=pltpu.CompilerParams(vmem_limit_bytes=8 * 1024 * 1024),
        name="stress_update",
    )(*first, *second, own, stress_old, resistance, quad_weights, table)


def body(
    grain_ids,
    euler_angles,
    brick_active,
    brick_owner,
    brick_element,
    displacement,
    stress_old,
    resistance,
    quad_weights,
):
    half = lax.axis_size("ca") * lax.axis_size("fe") // 2
    bricks = grain_ids.shape[1]
    owner = lax.optimization_barrier(brick_owner.reshape(bricks))
    labels = jnp.where(brick_active > 0, owner * COLUMNS + brick_element, -1).reshape(1, bricks)
    per_octant = grain_ids.shape[0] // 8
    table = rotation_table(euler_angles)
    split, send, labels, ids = cell_sums(CHUNKS[0], per_octant, grain_ids, labels, table, half)
    keep, labels = brick_sums(split, labels, half)
    core_a, labels = core_sum(keep, across_cores(send), displacement, labels, 0, "core_sum_a")
    split, send, labels = cell_sums(CHUNKS[1], per_octant, ids, labels, table, half)
    plane_a, labels, send = plane_sum(across_plane(core_a), [labels, send], 0, "plane_sum_a")
    keep, labels = brick_sums(split, labels, half)
    core_b, labels = core_sum(keep, across_cores(send), displacement, labels, 3, "core_sum_b")
    (plane_b,) = plane_sum(across_plane(core_b), [], 3, "plane_sum_b")
    stress_new, nodal = element_update(
        across_height(plane_a),
        across_height(plane_b),
        displacement,
        stress_old,
        resistance,
        quad_weights,
    )
    forces = nodal[0] + passed_along(nodal[1], "fe", 1)
    return (stress_new, forces)


def solution(mesh):
    placed = (
        P(None, ("ca", "fe")),
        P(),
        P(("ca", "fe")),
        P(("ca", "fe"), None),
        P(("ca", "fe")),
        P(None, ("ca", "fe"), None),
        P(None, None, ("ca", "fe")),
        P(None, None, ("ca", "fe")),
        P(None, ("ca", "fe")),
    )
    return jax.shard_map(
        body,
        mesh=mesh,
        in_specs=placed,
        out_specs=(P(None, None, ("ca", "fe")), P(None, ("ca", "fe"), None)),
        check_vma=False,
    )
```

```python
import functools
import functools
import math

import jax
import jax.numpy as jnp
from jax import lax
from jax.experimental import pallas as pl
from jax.experimental.pallas import tpu as pltpu
from jax.sharding import PartitionSpec as P

GX = 15
LANES = 128
COLUMNS = 256
CHUNKS = ((0, 6), (6, 2))
QUANTUM = float((1 << 15) - 1)

SLIP_PLANES = [
    [value / math.sqrt(3.0) for value in row]
    for row in [[1, 1, 1]] * 3 + [[-1, 1, 1]] * 3 + [[1, -1, 1]] * 3 + [[1, 1, -1]] * 3
]
SLIP_DIRECTIONS = [
    [value / math.sqrt(2.0) for value in row]
    for row in [
        [0, 1, -1],
        [1, 0, -1],
        [1, -1, 0],
        [0, 1, -1],
        [1, 0, 1],
        [1, 1, 0],
        [0, 1, 1],
        [1, 0, -1],
        [1, 1, 0],
        [0, 1, 1],
        [1, 0, 1],
        [1, -1, 0],
    ]
]
LAMBDA_ELASTIC = 1.5
SHEAR_MODULUS = 1.0
RATE_STEP = 0.1
FIXED_POINT = 65536.0


def passed_along(block, axis, distance):
    devices = range(lax.axis_size(axis))
    route = [(i - distance, i) for i in devices if i - distance in devices]
    return lax.ppermute(block, axis, route)


def shape_gradients():
    grad_table = [[[0.0, 0.0, 0.0] for corner in range(8)] for quadrature in range(8)]
    point_offset = 1.0 / math.sqrt(3.0)
    for quadrature in range(8):
        natural = [
            (2 * (quadrature >> shift_bits & 1) - 1) * point_offset for shift_bits in (2, 1, 0)
        ]
        for corner in range(8):
            sign_list = [2 * (corner >> shift_bits & 1) - 1 for shift_bits in (2, 1, 0)]
            factors = [1.0 + sign_list[axis_id] * natural[axis_id] for axis_id in range(3)]
            for direction in range(3):
                others = 1.0
                for axis_id in range(3):
                    if axis_id != direction:
                        others = others * factors[axis_id]
                grad_table[quadrature][corner][direction] = (
                    2.0 * sign_list[direction] * others / 8.0
                )
    return grad_table


def cos_sin(angle):
    square = angle * angle
    cosine = 1.0 / math.factorial(12)
    for power in (10, 8, 6, 4, 2, 0):
        cosine = cosine * square + (-1.0) ** (power // 2) / math.factorial(power)
    sine = 1.0 / math.factorial(13)
    for power in (11, 9, 7, 5, 3, 1):
        sine = sine * square + (-1.0) ** (power // 2) / math.factorial(power)
    return cosine, sine * angle


def rotation_words(euler):
    cos_one, sin_one = cos_sin(0.5 * euler[0 : 0 + 1])
    cos_mid, sin_mid = cos_sin(0.5 * euler[1 : 1 + 1])
    cos_two, sin_two = cos_sin(0.5 * euler[2 : 2 + 1])
    w = cos_mid * (cos_one * cos_two - sin_one * sin_two)
    factor = jnp.where(w < 0.0, -QUANTUM, QUANTUM) / (1.0 + jnp.abs(w))
    x = sin_mid * (cos_one * cos_two + sin_one * sin_two) * factor
    y = sin_mid * (sin_one * cos_two - cos_one * sin_two) * factor
    z = cos_mid * (sin_one * cos_two + cos_one * sin_two) * factor
    x, y, z = [
        jnp.clip(jnp.round(value), -QUANTUM, QUANTUM).astype(jnp.int32) for value in (x, y, z)
    ]
    return [lax.shift_left(x, 16) | (y & 0xFFFF), z & 0xFFFF]


def table_kernel(euler_ref, table_ref):
    both, third = rotation_words(euler_ref[...])
    rows = both.shape[1] // LANES
    for row in range(rows):
        table_ref[row] = jnp.broadcast_to(both[:, row * LANES : (row + 1) * LANES], (8, LANES))
    for row in range(0, rows, 2):
        word = third[:, row * LANES : (row + 1) * LANES] | lax.shift_left(
            third[:, (row + 1) * LANES : (row + 2) * LANES], 16
        )
        table_ref[rows + row // 2] = jnp.broadcast_to(word, (8, LANES))


def rotation_table(euler_angles):
    height = euler_angles.shape[1] // LANES * 3 // 2
    return pl.pallas_call(
        table_kernel,
        out_shape=jax.ShapeDtypeStruct((height, 8, LANES), jnp.int32),
        compiler_params=pltpu.CompilerParams(vmem_limit_bytes=8 * 1024 * 1024),
        cost_estimate=pl.CostEstimate(flops=10**6, bytes_accessed=10**7, transcendentals=0),
        name="rotation_table",
    )(euler_angles)


def looked_up(table_ref, first_row, rows, lane, bits):
    if rows == 1:
        return lax.gather(
            table_ref[first_row],
            lane,
            lax.GatherDimensionNumbers(
                offset_dims=(),
                collapsed_slice_dims=(1,),
                start_index_map=(1,),
                operand_batching_dims=(0,),
                start_indices_batching_dims=(0,),
            ),
            slice_sizes=(1, 1),
            mode=lax.GatherScatterMode.PROMISE_IN_BOUNDS,
        )
    half = rows // 2
    level = half.bit_length() - 1
    low = looked_up(table_ref, first_row, half, lane, bits)
    high = looked_up(table_ref, first_row + half, half, lane, bits)
    return jnp.where(bits[level], high, low)


def rotation_products(table_ref, table_rows, ids):
    lane = (ids & (LANES - 1))[:, :, None]
    row = lax.shift_right_logical(ids, 7)
    bits = [(row & (1 << level)) != 0 for level in range(table_rows.bit_length() - 1)]
    both = looked_up(table_ref, 0, table_rows, lane, bits)
    third = looked_up(table_ref, table_rows, table_rows // 2, lane, bits[1:])
    third = lax.shift_left(third, lax.shift_left((row & 1) ^ 1, 4))
    x = lax.shift_right_arithmetic(both, 16).astype(jnp.float32)
    y = lax.shift_right_arithmetic(lax.shift_left(both, 16), 16).astype(jnp.float32)
    z = lax.shift_right_arithmetic(third, 16).astype(jnp.float32)
    square = x * x + y * y + z * z
    scale = 2.0 / (1.0 + square * (1.0 / (QUANTUM * QUANTUM)))
    w = scale - 1.0
    x, y, z = x * scale, y * scale, z * scale
    return [x * x, y * y, z * z, x * y, x * z, y * z, w * x, w * y, w * z]


ENTRIES = (
    ((1, -1.0), (2, -1.0)),
    ((3, 1.0), (8, -1.0)),
    ((4, 1.0), (7, 1.0)),
    ((3, 1.0), (8, 1.0)),
    ((0, -1.0), (2, -1.0)),
    ((5, 1.0), (6, -1.0)),
    ((4, 1.0), (7, -1.0)),
    ((5, 1.0), (6, 1.0)),
    ((0, -1.0), (1, -1.0)),
)


def remainder(value, divisor):
    return value - value // divisor * divisor


def cell_sum_kernel(
    octants,
    per_octant,
    ids_ref,
    label_ref,
    table_ref,
    split_ref,
    out_ref,
    label_out_ref,
    *refs,
):
    first, count = octants
    start = ids_ref.shape[0] - (8 - first) * per_octant
    tile_ref, raw_ref, place_ref, masked_ref = refs[-4:]
    if len(refs) > 4:
        refs[0][...] = ids_ref[pl.ds(ids_ref.shape[0] - refs[0].shape[0], refs[0].shape[0]), :]
    table_rows = table_ref.shape[0] * 2 // 3
    label_out_ref[...] = label_ref[...]
    groups = tile_ref.shape[1] // 8
    rows_left = count * per_octant - 8 * (groups - 1)
    turns = count // math.gcd(count, 8)
    rows = out_ref.shape[1]
    width = masked_ref.shape[1]
    pairs = ids_ref.shape[1] // width

    out_row = lax.broadcasted_iota(jnp.int32, (rows, raw_ref.shape[0]), 0)
    raw_row = lax.broadcasted_iota(jnp.int32, (rows, raw_ref.shape[0]), 1)
    entry, product = out_row // count, raw_row // (8 * turns)
    fold = jnp.zeros(out_row.shape, jnp.float32)
    for index, terms in enumerate(ENTRIES):
        for other, sign in terms:
            fold = jnp.where((entry == index) & (product == other), sign, fold)
    fold = jnp.where(remainder(out_row, count) == remainder(raw_row, count), fold, 0.0)
    fold = fold.astype(jnp.bfloat16)
    row = lax.broadcasted_iota(jnp.int32, (rows, width), 0)
    diagonal = (row // count == 0) | (row // count == 4) | (row // count == 8)
    constant = jnp.where(diagonal, float(per_octant), jnp.where(row < 9 * count, 0.0, 1.0))

    def lanes_of(pair):
        return pl.ds(pl.multiple_of(pair * width, width), width)

    def look_up(pair):
        for tile in range(width // LANES):
            lanes = pl.ds(pl.multiple_of(pair * width + tile * LANES, LANES), LANES)
            for octant in range(count):
                tile_ref[tile, pl.ds(octant, per_octant, stride=count), :] = ids_ref[
                    pl.ds(start + octant * per_octant, per_octant), lanes
                ]
            sums = [[jnp.zeros((8, LANES), jnp.float32)] * 9 for turn in range(turns)]
            for group in range(groups):
                ids = tile_ref[tile, pl.ds(8 * group, 8), :]
                products = rotation_products(table_ref, table_rows, ids)
                if group == groups - 1 and rows_left < 8:
                    there = lax.broadcasted_iota(jnp.int32, (8, LANES), 0) < rows_left
                    products = [jnp.where(there, value, 0.0) for value in products]
                sums[group % turns] = [
                    total + value for total, value in zip(sums[group % turns], products)
                ]
            scales = [2.0 / (QUANTUM * QUANTUM)] * 6 + [2.0 / QUANTUM] * 3
            raw_ref[:, lanes] = jnp.concatenate(
                [sums[turn][index] * scales[index] for index in range(9) for turn in range(turns)],
                axis=0,
            )

    def fold_entries(pair):
        lanes = lanes_of(pair)
        total = constant
        for part in three_parts(raw_ref[:, lanes]):
            total = total + jnp.dot(fold, part, preferred_element_type=jnp.float32)
        leading = total.astype(jnp.bfloat16).astype(jnp.float32)
        split_ref[:, lanes] = jnp.concatenate([leading, total - leading], axis=0).astype(
            jnp.bfloat16
        )

    def add_bricks(pair, counted):
        lanes = lanes_of(pair)
        column = lax.broadcasted_iota(jnp.int32, (COLUMNS, width), 0)
        chosen = (column == label_ref[:, lanes] & (COLUMNS - 1)).astype(jnp.bfloat16)
        place = jnp.where(counted, place_ref[:, lanes], -1)
        add_places(split_ref, lanes, place, chosen, out_ref, masked_ref)

    place_ref[...] = relative_places(label_ref[...], out_ref.shape[0])
    out_ref[...] = jnp.zeros(out_ref.shape, jnp.float32)
    raw_ref[:, pl.ds(0, width)] = jnp.zeros((raw_ref.shape[0], width), jnp.float32)
    split_ref[:, pl.ds(0, width)] = jnp.zeros((split_ref.shape[0], width), jnp.bfloat16)

    def step(pair, carry):
        add_bricks(jnp.maximum(pair - 2, 0), pair >= 2)
        fold_entries(jnp.maximum(pair - 1, 0))
        look_up(pair)
        return carry

    lax.fori_loop(0, pairs, step, 0)
    add_bricks(pairs - 2, True)
    fold_entries(pairs - 1)
    add_bricks(pairs - 1, True)


def relative_places(labels, base):
    place = place_of(lax.shift_right_arithmetic(labels, COLUMNS.bit_length() - 1))
    return jnp.where(labels < 0, -1, place - base)


def add_places(split_ref, lanes, place, chosen, out_ref, masked_ref):
    split_rows = split_ref.shape[0]
    half_rows = split_rows // 2
    members = masked_ref.shape[0] // split_rows
    for first in range(0, out_ref.shape[0], members):
        split = split_ref[:, lanes]
        for member in range(members):
            mask = (place == first + member).astype(jnp.bfloat16)
            masked_ref[pl.ds(member * split_rows, split_rows), :] = split * mask
        product = lax.dot_general(
            masked_ref[...],
            chosen,
            (((1,), (1,)), ((), ())),
            preferred_element_type=jnp.float32,
        )
        for member in range(members):
            at = member * split_rows
            out_ref[first + member] += (
                product[at : at + half_rows] + product[at + half_rows : at + split_rows]
            )


def across_cores(block):
    groups = lax.axis_size("ca")
    return lax.ppermute(block, "ca", [(i, i ^ 1) for i in range(groups)])


def brick_sum_kernel(split_ref, label_ref, out_ref, label_out_ref, place_ref, masked_ref):
    labels = label_ref[...]
    label_out_ref[...] = labels
    place_ref[...] = relative_places(labels, 0)
    bricks = split_ref.shape[1]
    column = lax.broadcasted_iota(jnp.int32, (COLUMNS, bricks), 0)
    chosen = (column == labels & (COLUMNS - 1)).astype(jnp.bfloat16)
    split_rows = split_ref.shape[0]
    half_rows = split_rows // 2
    members = masked_ref.shape[0] // split_rows

    def place_group(step, carry):
        for member in range(members):
            mask = (place_ref[...] == step * members + member).astype(jnp.bfloat16)
            masked_ref[pl.ds(member * split_rows, split_rows), :] = split_ref[...] * mask
        product = lax.dot_general(
            masked_ref[...],
            chosen,
            (((1,), (1,)), ((), ())),
            preferred_element_type=jnp.float32,
        )
        for member in range(members):
            at = member * split_rows
            out_ref[step * members + member] = (
                product[at : at + half_rows] + product[at + half_rows : at + split_rows]
            )
        return carry

    lax.fori_loop(0, out_ref.shape[0] // members, place_group, 0)


def place_of(owner):
    groups, members = lax.axis_size("ca"), lax.axis_size("fe")
    owner_ca = lax.shift_right_logical(owner, members.bit_length() - 1) ^ lax.axis_index("ca")
    owner_fe = (owner & (members - 1)) ^ lax.axis_index("fe")
    place = (owner_ca & 1) * (groups // 2) + lax.shift_right_logical(owner_ca, 1)
    place = place * 2 + (owner_fe & 1)
    return place * (members // 2) + lax.shift_right_logical(owner_fe, 1)


def cell_sums(octants, per_octant, ids, labels, table, places):
    first, count = octants
    bricks = ids.shape[1]
    rows = padded_rows(count)
    out_shape = [
        jax.ShapeDtypeStruct((2 * rows, bricks), jnp.bfloat16),
        jax.ShapeDtypeStruct((places, rows, COLUMNS), jnp.float32),
        jax.ShapeDtypeStruct(labels.shape, jnp.int32),
    ]
    left = 8 - first - count
    if left:
        out_shape.append(jax.ShapeDtypeStruct((-(-left * per_octant // 8) * 8, bricks), jnp.int32))
    return pl.pallas_call(
        functools.partial(cell_sum_kernel, octants, per_octant),
        out_shape=out_shape,
        scratch_shapes=[
            pltpu.VMEM((2, -(-count * per_octant // 8) * 8, LANES), jnp.int32),
            pltpu.VMEM((72 * (count // math.gcd(count, 8)), bricks), jnp.float32),
        ]
        + brick_scratch(rows, bricks, places, 2 * LANES),
        compiler_params=pltpu.CompilerParams(vmem_limit_bytes=28 * 1024 * 1024),
        cost_estimate=pl.CostEstimate(
            flops=count * 4 * 10**9, bytes_accessed=count * 10**7, transcendentals=0
        ),
        name="cell_sums",
    )(ids, labels, table)


def padded_rows(count):
    return -(-9 * count // 8) * 8


def brick_scratch(rows, bricks, places, width):
    return [
        pltpu.VMEM((1, bricks), jnp.int32),
        pltpu.VMEM((min(16, places) * 2 * rows, width), jnp.bfloat16),
    ]


def brick_sums(split, labels, places):
    rows, bricks = split.shape
    return pl.pallas_call(
        brick_sum_kernel,
        out_shape=[
            jax.ShapeDtypeStruct((places, rows // 2, COLUMNS), jnp.float32),
            jax.ShapeDtypeStruct(labels.shape, jnp.int32),
        ],
        scratch_shapes=brick_scratch(rows // 2, bricks, places, bricks),
        compiler_params=pltpu.CompilerParams(vmem_limit_bytes=24 * 1024 * 1024),
        cost_estimate=pl.CostEstimate(
            flops=rows * 15 * 10**6, bytes_accessed=rows * 5 * 10**4, transcendentals=0
        ),
        name="brick_sums",
    )(split, labels)


def core_sum_kernel(spare, kept_ref, received_ref, own_ref, label_ref, *out_refs):
    for index, out_ref in enumerate(out_refs[:-2]):
        out_ref[...] = kept_ref[index] + received_ref[index]
        for c in range(spare):
            row = out_ref.shape[1] - spare + c
            out_ref[:, row : row + 1, :] = jnp.broadcast_to(
                own_ref[c][None], (out_ref.shape[0], 1, COLUMNS)
            )
    out_refs[-2][...] = label_ref[...]
    out_refs[-1][...] = own_ref[...]


def core_sum(kept, received, own, labels, spare, name):
    pairs, rests = lax.axis_size("ca") // 2, lax.axis_size("fe") // 2
    shape = (2 * pairs, rests) + kept.shape[1:]
    *parts, labels, own = pl.pallas_call(
        functools.partial(core_sum_kernel, spare),
        out_shape=[jax.ShapeDtypeStruct(shape[1:], jnp.float32)] * shape[0]
        + [
            jax.ShapeDtypeStruct(labels.shape, jnp.int32),
            jax.ShapeDtypeStruct(own.shape, jnp.float32),
        ],
        compiler_params=pltpu.CompilerParams(vmem_limit_bytes=16 * 1024 * 1024),
        name=name,
    )(kept.reshape(shape), received.reshape(shape), own, labels)
    return parts, labels, own


def plane_sum_kernel(spare, sources, passed, *refs):
    outs = refs[sources + passed :]
    height = 0
    for out_ref in outs[: len(outs) - passed]:
        heights = pl.ds(height, out_ref.shape[0])
        out_ref[...] = sum(ref[heights] for ref in refs[:sources])
        if spare:
            rows = pl.ds(out_ref.shape[1] - spare, spare)
            out_ref[:, rows, :] = refs[1][heights, rows, :]
        height += out_ref.shape[0]
    for i in range(passed):
        outs[len(outs) - passed + i][...] = refs[sources + i][...]


def plane_sum(parts, passed, spare, cuts, name):
    rest = parts[0].shape[1:]
    out = pl.pallas_call(
        functools.partial(plane_sum_kernel, spare, len(parts), len(passed)),
        out_shape=[jax.ShapeDtypeStruct((cut,) + rest, jnp.float32) for cut in cuts]
        + [jax.ShapeDtypeStruct(array.shape, array.dtype) for array in passed],
        compiler_params=pltpu.CompilerParams(vmem_limit_bytes=16 * 1024 * 1024),
        name=name,
    )(*parts, *passed)
    return out[: len(cuts)], *out[len(cuts) :]


def to_relative(block, core, pair, last, rest):
    groups, members = lax.axis_size("ca"), lax.axis_size("fe")
    flip = (2 * pair + core) * members + 2 * rest + last
    return lax.ppermute(block, ("ca", "fe"), [(i, i ^ flip) for i in range(groups * members)])


def across_plane(parts):
    return [parts[0]] + [
        to_relative(parts[index], 0, index // 2, index % 2, 0) for index in range(1, len(parts))
    ]


def across_height(parts):
    return [parts[0]] + [to_relative(parts[rest], 0, 0, 0, rest) for rest in range(1, len(parts))]


def three_parts(value):
    first = value.astype(jnp.bfloat16)
    rest = value - first.astype(jnp.float32)
    second = rest.astype(jnp.bfloat16)
    third = (rest - second.astype(jnp.float32)).astype(jnp.bfloat16)
    return first, second, third


def dot_selected(value, selector, contract):
    total = None
    for part in three_parts(value):
        term = lax.dot_general(
            part, selector, (((1,), (contract,)), ((), ())), preferred_element_type=jnp.float32
        )
        total = term if total is None else total + term
    return total


def update_kernel(firsts, seconds, *refs):
    first_refs, second_refs = refs[:firsts], refs[firsts : firsts + seconds]
    own_ref, stress_ref, resistance_ref, weights_ref, table_ref = refs[firsts + seconds : -2]
    stress_out_ref, nodal_ref = refs[-2:]
    elements = stress_ref.shape[2]
    gathered = [
        sum(ref[0, :, 0:elements] for ref in chunk_refs)
        for chunk_refs in (first_refs, second_refs)
    ]
    counted = 9 * CHUNKS[1][1]
    counts = gathered[1][counted : counted + 1]
    per_brick = 1.0 / (8.0 * jnp.maximum(counts, 1.0))
    frames = [
        jnp.concatenate(
            [
                sums[count * k : count * (k + 1)]
                for sums, (first, count) in zip(gathered, CHUNKS)
            ],
            axis=0,
        )
        * per_brick
        for k in range(9)
    ]

    node = lax.broadcasted_iota(jnp.int32, (COLUMNS, elements), 0)
    element = lax.broadcasted_iota(jnp.int32, (COLUMNS, elements), 1)
    base = element + element // GX
    selectors = [
        (node == base + (step_y * (GX + 1) + step_x)).astype(jnp.bfloat16)
        for step_x in range(2)
        for step_y in range(2)
    ]
    corner = lax.broadcasted_iota(jnp.int32, (24, 1), 0) & 7
    upper_corner = (corner & 1) == 1
    height = lax.axis_index("fe") // 2
    above = height + (lax.axis_index("fe") & 1)
    upper = jnp.zeros((3, COLUMNS), jnp.float32)
    for flip, ref in enumerate(second_refs):
        wanted = (height ^ flip) == above
        upper = upper + jnp.where(wanted, ref[0, ref.shape[1] - 3 :, :], 0.0)
    values = jnp.where(
        upper_corner,
        jnp.concatenate(
            [jnp.broadcast_to(upper[c : c + 1], (8, COLUMNS)) for c in range(3)], axis=0
        ),
        jnp.concatenate([jnp.broadcast_to(own_ref[c], (8, COLUMNS)) for c in range(3)], axis=0),
    )
    corners = jnp.zeros((24, elements), jnp.float32)
    for step in range(4):
        part = jnp.where(corner >> 1 == step, values, 0.0)
        corners = corners + dot_selected(part, selectors[step], 0)
    gradients = []
    for c in range(3):
        product = jnp.dot(
            table_ref[...],
            corners[8 * c : 8 * c + 8],
            precision=lax.Precision.HIGHEST,
            preferred_element_type=jnp.float32,
        )
        gradients.append([product[8 * d : 8 * d + 8] for d in range(3)])
    strain = [
        gradients[0][0],
        gradients[1][1],
        gradients[2][2],
        0.5 * (gradients[1][2] + gradients[2][1]),
        0.5 * (gradients[0][2] + gradients[2][0]),
        0.5 * (gradients[0][1] + gradients[1][0]),
    ]
    volume = strain[0] + strain[1] + strain[2]
    trial = []
    for component in range(6):
        change = 2.0 * SHEAR_MODULUS * strain[component]
        if component < 3:
            change = change + LAMBDA_ELASTIC * volume
        trial.append(stress_ref[component] + change)
    correction = [jnp.zeros_like(trial[0]) for component in range(6)]
    for system in range(12):
        rotated_dir = [
            sum(
                frames[3 * row + axis_id] * SLIP_DIRECTIONS[system][axis_id]
                for axis_id in range(3)
                if SLIP_DIRECTIONS[system][axis_id] != 0.0
            )
            for row in range(3)
        ]
        rotated_normal = [
            sum(frames[3 * row + axis_id] * SLIP_PLANES[system][axis_id] for axis_id in range(3))
            for row in range(3)
        ]
        schmid = [
            rotated_dir[0] * rotated_normal[0],
            rotated_dir[1] * rotated_normal[1],
            rotated_dir[2] * rotated_normal[2],
            0.5 * (rotated_dir[1] * rotated_normal[2] + rotated_dir[2] * rotated_normal[1]),
            0.5 * (rotated_dir[0] * rotated_normal[2] + rotated_dir[2] * rotated_normal[0]),
            0.5 * (rotated_dir[0] * rotated_normal[1] + rotated_dir[1] * rotated_normal[0]),
        ]
        resolved = (
            trial[0] * schmid[0]
            + trial[1] * schmid[1]
            + trial[2] * schmid[2]
            + 2.0 * (trial[3] * schmid[3] + trial[4] * schmid[4] + trial[5] * schmid[5])
        )
        slip_ratio = resolved / resistance_ref[system]
        slip_step = RATE_STEP * slip_ratio * jnp.abs(slip_ratio)
        correction = [
            correction[component] + slip_step * schmid[component] for component in range(6)
        ]
    updated = [
        trial[component] - 2.0 * SHEAR_MODULUS * correction[component] for component in range(6)
    ]
    for component in range(6):
        stress_out_ref[component] = updated[component]
    point_scale = weights_ref[...].astype(jnp.float32) * (1.0 / (FIXED_POINT * 8.0))
    scaled = [value * point_scale for value in updated]
    forces = []
    for rows in [(0, 5, 4), (5, 1, 3), (4, 3, 2)]:
        forces.append(
            lax.dot_general(
                table_ref[...],
                jnp.concatenate([scaled[row] for row in rows], axis=0),
                (((0,), (0,)), ((), ())),
                precision=lax.Precision.HIGHEST,
                preferred_element_type=jnp.float32,
            )
        )
    forces = jnp.concatenate(forces, axis=0)
    nodal = jnp.zeros((24, COLUMNS), jnp.float32)
    for step in range(4):
        part = jnp.where(corner >> 1 == step, forces, 0.0)
        nodal = nodal + dot_selected(part, selectors[step], 1)
    lower = jnp.where(upper_corner, 0.0, nodal)
    above = jnp.where(upper_corner, nodal, 0.0)
    for c in range(3):
        nodal_ref[0, c] = jnp.sum(lower[8 * c : 8 * c + 8], axis=0, keepdims=True)
        nodal_ref[1, c] = jnp.sum(above[8 * c : 8 * c + 8], axis=0, keepdims=True)


def element_update(first, second, own, stress_old, resistance, quad_weights):
    grad_table = shape_gradients()
    table = jnp.asarray(
        [
            [grad_table[quadrature][corner][direction] for corner in range(8)]
            for direction in range(3)
            for quadrature in range(8)
        ],
        dtype=jnp.float32,
    )
    return pl.pallas_call(
        functools.partial(update_kernel, len(first), len(second)),
        out_shape=(
            jax.ShapeDtypeStruct(stress_old.shape, jnp.float32),
            jax.ShapeDtypeStruct((2,) + own.shape, jnp.float32),
        ),
        compiler_params=pltpu.CompilerParams(vmem_limit_bytes=8 * 1024 * 1024),
        name="stress_update",
    )(*first, *second, own, stress_old, resistance, quad_weights, table)


def body(
    grain_ids,
    euler_angles,
    brick_active,
    brick_owner,
    brick_element,
    displacement,
    stress_old,
    resistance,
    quad_weights,
):
    half = lax.axis_size("ca") * lax.axis_size("fe") // 2
    bricks = grain_ids.shape[1]
    owner = lax.optimization_barrier(brick_owner.reshape(bricks))
    labels = jnp.where(brick_active > 0, owner * COLUMNS + brick_element, -1).reshape(1, bricks)
    per_octant = grain_ids.shape[0] // 8
    table = rotation_table(euler_angles)
    split, send, labels, ids = cell_sums(CHUNKS[0], per_octant, grain_ids, labels, table, half)
    keep, labels = brick_sums(split, labels, half)
    core_a, labels, own = core_sum(
        keep, across_cores(send), displacement, labels, 0, "core_sum_a"
    )
    split, send, labels = cell_sums(CHUNKS[1], per_octant, ids, labels, table, half)
    heights = lax.axis_size("fe") // 2
    flip = heights // 2
    (kept, sent), labels, send = plane_sum(
        across_plane(core_a), [labels, send], 0, [flip, flip], "plane_sum_a"
    )
    received = to_relative(sent, 0, 0, 0, flip)
    keep, labels = brick_sums(split, labels, half)
    core_b, labels, own = core_sum(keep, across_cores(send), own, labels, 3, "core_sum_b")
    plane_b = across_plane(core_b)
    while flip > 1:
        flip //= 2
        (kept, sent), labels = plane_sum(
            [kept, received], [labels], 0, [flip, flip], "height_sum_a"
        )
        received = to_relative(sent, 0, 0, 0, flip)
    plane_b, labels = plane_sum(plane_b, [labels], 3, [1] * heights, "plane_sum_b")
    stress_new, nodal = element_update(
        [kept, received],
        across_height(plane_b),
        displacement,
        stress_old,
        resistance,
        quad_weights,
    )
    forces = nodal[0] + passed_along(nodal[1], "fe", 1)
    return (stress_new, forces)


def solution(mesh):
    placed = (
        P(None, ("ca", "fe")),
        P(),
        P(("ca", "fe")),
        P(("ca", "fe"), None),
        P(("ca", "fe")),
        P(None, ("ca", "fe"), None),
        P(None, None, ("ca", "fe")),
        P(None, None, ("ca", "fe")),
        P(None, ("ca", "fe")),
    )
    return jax.shard_map(
        body,
        mesh=mesh,
        in_specs=placed,
        out_specs=(P(None, None, ("ca", "fe")), P(None, ("ca", "fe"), None)),
        check_vma=False,
    )
```

```python
import functools
import functools
import math

import jax
import jax.numpy as jnp
from jax import lax
from jax.experimental import pallas as pl
from jax.experimental.pallas import tpu as pltpu
from jax.sharding import PartitionSpec as P

GX = 15
LANES = 128
COLUMNS = 256
CHUNKS = ((0, 6), (6, 2))
QUANTUM = float((1 << 15) - 1)

SLIP_PLANES = [
    [value / math.sqrt(3.0) for value in row]
    for row in [[1, 1, 1]] * 3 + [[-1, 1, 1]] * 3 + [[1, -1, 1]] * 3 + [[1, 1, -1]] * 3
]
SLIP_DIRECTIONS = [
    [value / math.sqrt(2.0) for value in row]
    for row in [
        [0, 1, -1],
        [1, 0, -1],
        [1, -1, 0],
        [0, 1, -1],
        [1, 0, 1],
        [1, 1, 0],
        [0, 1, 1],
        [1, 0, -1],
        [1, 1, 0],
        [0, 1, 1],
        [1, 0, 1],
        [1, -1, 0],
    ]
]
LAMBDA_ELASTIC = 1.5
SHEAR_MODULUS = 1.0
RATE_STEP = 0.1
FIXED_POINT = 65536.0


def passed_along(block, axis, distance):
    devices = range(lax.axis_size(axis))
    route = [(i - distance, i) for i in devices if i - distance in devices]
    return lax.ppermute(block, axis, route)


def shape_gradients():
    grad_table = [[[0.0, 0.0, 0.0] for corner in range(8)] for quadrature in range(8)]
    point_offset = 1.0 / math.sqrt(3.0)
    for quadrature in range(8):
        natural = [
            (2 * (quadrature >> shift_bits & 1) - 1) * point_offset for shift_bits in (2, 1, 0)
        ]
        for corner in range(8):
            sign_list = [2 * (corner >> shift_bits & 1) - 1 for shift_bits in (2, 1, 0)]
            factors = [1.0 + sign_list[axis_id] * natural[axis_id] for axis_id in range(3)]
            for direction in range(3):
                others = 1.0
                for axis_id in range(3):
                    if axis_id != direction:
                        others = others * factors[axis_id]
                grad_table[quadrature][corner][direction] = (
                    2.0 * sign_list[direction] * others / 8.0
                )
    return grad_table


def cos_sin(angle):
    square = angle * angle
    cosine = 1.0 / math.factorial(12)
    for power in (10, 8, 6, 4, 2, 0):
        cosine = cosine * square + (-1.0) ** (power // 2) / math.factorial(power)
    sine = 1.0 / math.factorial(13)
    for power in (11, 9, 7, 5, 3, 1):
        sine = sine * square + (-1.0) ** (power // 2) / math.factorial(power)
    return cosine, sine * angle


def rotation_words(euler):
    cos_one, sin_one = cos_sin(0.5 * euler[0 : 0 + 1])
    cos_mid, sin_mid = cos_sin(0.5 * euler[1 : 1 + 1])
    cos_two, sin_two = cos_sin(0.5 * euler[2 : 2 + 1])
    w = cos_mid * (cos_one * cos_two - sin_one * sin_two)
    factor = jnp.where(w < 0.0, -QUANTUM, QUANTUM) / (1.0 + jnp.abs(w))
    x = sin_mid * (cos_one * cos_two + sin_one * sin_two) * factor
    y = sin_mid * (sin_one * cos_two - cos_one * sin_two) * factor
    z = cos_mid * (sin_one * cos_two + cos_one * sin_two) * factor
    x, y, z = [
        jnp.clip(jnp.round(value), -QUANTUM, QUANTUM).astype(jnp.int32) for value in (x, y, z)
    ]
    return [lax.shift_left(x, 16) | (y & 0xFFFF), z & 0xFFFF]


def table_kernel(euler_ref, table_ref):
    both, third = rotation_words(euler_ref[...])
    rows = both.shape[1] // LANES
    for row in range(rows):
        table_ref[row] = jnp.broadcast_to(both[:, row * LANES : (row + 1) * LANES], (8, LANES))
    for row in range(0, rows, 2):
        word = third[:, row * LANES : (row + 1) * LANES] | lax.shift_left(
            third[:, (row + 1) * LANES : (row + 2) * LANES], 16
        )
        table_ref[rows + row // 2] = jnp.broadcast_to(word, (8, LANES))


def rotation_table(euler_angles):
    height = euler_angles.shape[1] // LANES * 3 // 2
    return pl.pallas_call(
        table_kernel,
        out_shape=jax.ShapeDtypeStruct((height, 8, LANES), jnp.int32),
        compiler_params=pltpu.CompilerParams(vmem_limit_bytes=8 * 1024 * 1024),
        cost_estimate=pl.CostEstimate(flops=10**6, bytes_accessed=10**7, transcendentals=0),
        name="rotation_table",
    )(euler_angles)


def looked_up(table_ref, first_row, rows, lane, bits):
    if rows == 1:
        return lax.gather(
            table_ref[first_row],
            lane,
            lax.GatherDimensionNumbers(
                offset_dims=(),
                collapsed_slice_dims=(1,),
                start_index_map=(1,),
                operand_batching_dims=(0,),
                start_indices_batching_dims=(0,),
            ),
            slice_sizes=(1, 1),
            mode=lax.GatherScatterMode.PROMISE_IN_BOUNDS,
        )
    half = rows // 2
    level = half.bit_length() - 1
    low = looked_up(table_ref, first_row, half, lane, bits)
    high = looked_up(table_ref, first_row + half, half, lane, bits)
    return jnp.where(bits[level], high, low)


def rotation_coordinates(table_ref, table_rows, ids):
    lane = (ids & (LANES - 1))[:, :, None]
    row = lax.shift_right_logical(ids, 7)
    bits = [(row & (1 << level)) != 0 for level in range(table_rows.bit_length() - 1)]
    both = looked_up(table_ref, 0, table_rows, lane, bits)
    third = looked_up(table_ref, table_rows, table_rows // 2, lane, bits[1:])
    return both, lax.shift_left(third, lax.shift_left((row & 1) ^ 1, 4))


def rotation_products(both, third):
    x = lax.shift_right_arithmetic(both, 16).astype(jnp.float32)
    y = lax.shift_right_arithmetic(lax.shift_left(both, 16), 16).astype(jnp.float32)
    z = lax.shift_right_arithmetic(third, 16).astype(jnp.float32)
    length = (x * x + y * y + z * z) * (0.5 / (QUANTUM * QUANTUM)) + 0.5
    scale = pl.reciprocal(length, approx=True)
    scale = scale * (2.0 - length * scale)
    w = scale - 1.0
    x, y, z = x * scale, y * scale, z * scale
    return [x * x, y * y, z * z, x * y, x * z, y * z, w * x, w * y, w * z]


ENTRIES = (
    ((1, -1.0), (2, -1.0)),
    ((3, 1.0), (8, -1.0)),
    ((4, 1.0), (7, 1.0)),
    ((3, 1.0), (8, 1.0)),
    ((0, -1.0), (2, -1.0)),
    ((5, 1.0), (6, -1.0)),
    ((4, 1.0), (7, -1.0)),
    ((5, 1.0), (6, 1.0)),
    ((0, -1.0), (1, -1.0)),
)


def remainder(value, divisor):
    return value - value // divisor * divisor


def cell_sum_kernel(
    octants,
    per_octant,
    ids_ref,
    label_ref,
    table_ref,
    *refs,
):
    first, count = octants
    start = ids_ref.shape[0] - (8 - first) * per_octant
    tile_ref, raw_ref, place_ref, masked_ref = refs[-4:]
    if first + count < 8:
        label_out_ref, send_ref, split_ref, rest_ref = refs[:-4]
        label_out_ref[...] = label_ref[...]
        rest_ref[...] = ids_ref[pl.ds(ids_ref.shape[0] - rest_ref.shape[0], rest_ref.shape[0]), :]
        targets = [(send_ref.shape[0], send_ref)]
    else:
        send_ref, keep_ref, split_ref = refs[:-4]
        targets = [(send_ref.shape[0], send_ref), (0, keep_ref)]
    table_rows = table_ref.shape[0] * 2 // 3
    groups = tile_ref.shape[1] // 8
    rows_left = count * per_octant - 8 * (groups - 1)
    turns = count // math.gcd(count, 8)
    rows = send_ref.shape[1]
    width = masked_ref.shape[1]
    pairs = ids_ref.shape[1] // width

    out_row = lax.broadcasted_iota(jnp.int32, (rows, raw_ref.shape[0]), 0)
    raw_row = lax.broadcasted_iota(jnp.int32, (rows, raw_ref.shape[0]), 1)
    entry, product = out_row // count, raw_row // (8 * turns)
    fold = jnp.zeros(out_row.shape, jnp.float32)
    for index, terms in enumerate(ENTRIES):
        for other, sign in terms:
            fold = jnp.where((entry == index) & (product == other), sign, fold)
    fold = jnp.where(remainder(out_row, count) == remainder(raw_row, count), fold, 0.0)
    fold = fold.astype(jnp.bfloat16)
    row = lax.broadcasted_iota(jnp.int32, (rows, width), 0)
    diagonal = (row // count == 0) | (row // count == 4) | (row // count == 8)
    constant = jnp.where(diagonal, float(per_octant), jnp.where(row < 9 * count, 0.0, 1.0))

    def lanes_of(pair):
        return pl.ds(pl.multiple_of(pair * width, width), width)

    def look_up(pair):
        for tile in range(width // LANES):
            lanes = pl.ds(pl.multiple_of(pair * width + tile * LANES, LANES), LANES)
            for octant in range(count):
                tile_ref[tile, pl.ds(octant, per_octant, stride=count), :] = ids_ref[
                    pl.ds(start + octant * per_octant, per_octant), lanes
                ]
            sums = [[jnp.zeros((8, LANES), jnp.float32)] * 9 for turn in range(turns)]
            found = None
            for group in range(groups + 1):
                last = found
                if group < groups:
                    ids = tile_ref[tile, pl.ds(8 * group, 8), :]
                    found = rotation_coordinates(table_ref, table_rows, ids)
                if group == 0:
                    continue
                products = rotation_products(*last)
                if group == groups and rows_left < 8:
                    there = lax.broadcasted_iota(jnp.int32, (8, LANES), 0) < rows_left
                    products = [jnp.where(there, value, 0.0) for value in products]
                turn = (group - 1) % turns
                sums[turn] = [total + value for total, value in zip(sums[turn], products)]
            scales = [2.0 / (QUANTUM * QUANTUM)] * 6 + [2.0 / QUANTUM] * 3
            raw_ref[:, lanes] = jnp.concatenate(
                [sums[turn][index] * scales[index] for index in range(9) for turn in range(turns)],
                axis=0,
            )

    def fold_entries(pair):
        lanes = lanes_of(pair)
        total = constant
        for part in three_parts(raw_ref[:, lanes]):
            total = total + jnp.dot(fold, part, preferred_element_type=jnp.float32)
        leading = total.astype(jnp.bfloat16).astype(jnp.float32)
        split_ref[:, lanes] = jnp.concatenate([leading, total - leading], axis=0).astype(
            jnp.bfloat16
        )

    def add_bricks(pair, counted):
        lanes = lanes_of(pair)
        column = lax.broadcasted_iota(jnp.int32, (COLUMNS, width), 0)
        chosen = (column == label_ref[:, lanes] & (COLUMNS - 1)).astype(jnp.bfloat16)
        place = jnp.where(counted, place_ref[:, lanes], -1)
        for base, out_ref in targets:
            add_places(split_ref, lanes, place - base, chosen, out_ref, masked_ref)

    place_ref[...] = relative_places(label_ref[...])
    for base, out_ref in targets:
        out_ref[...] = jnp.zeros(out_ref.shape, jnp.float32)
    raw_ref[:, pl.ds(0, width)] = jnp.zeros((raw_ref.shape[0], width), jnp.float32)
    split_ref[:, pl.ds(0, width)] = jnp.zeros((split_ref.shape[0], width), jnp.bfloat16)

    def step(pair, carry):
        add_bricks(jnp.maximum(pair - 2, 0), pair >= 2)
        fold_entries(jnp.maximum(pair - 1, 0))
        look_up(pair)
        return carry

    lax.fori_loop(0, pairs, step, 0, unroll=2)
    add_bricks(pairs - 2, True)
    fold_entries(pairs - 1)
    add_bricks(pairs - 1, True)


def relative_places(labels):
    place = place_of(lax.shift_right_arithmetic(labels, COLUMNS.bit_length() - 1))
    return jnp.where(labels < 0, -1, place)


def add_places(split_ref, lanes, place, chosen, out_ref, masked_ref):
    split_rows = split_ref.shape[0]
    half_rows = split_rows // 2
    members = masked_ref.shape[0] // split_rows
    for first in range(0, out_ref.shape[0], members):
        split = split_ref[:, lanes]
        for member in range(members):
            mask = (place == first + member).astype(jnp.bfloat16)
            masked_ref[pl.ds(member * split_rows, split_rows), :] = split * mask
        product = lax.dot_general(
            masked_ref[...],
            chosen,
            (((1,), (1,)), ((), ())),
            preferred_element_type=jnp.float32,
        )
        for member in range(members):
            at = member * split_rows
            out_ref[first + member] += (
                product[at : at + half_rows] + product[at + half_rows : at + split_rows]
            )


def across_cores(block):
    groups = lax.axis_size("ca")
    return lax.ppermute(block, "ca", [(i, i ^ 1) for i in range(groups)])


def brick_sum_kernel(split_ref, label_ref, out_ref, label_out_ref, place_ref, masked_ref):
    labels = label_ref[...]
    label_out_ref[...] = labels
    place_ref[...] = relative_places(labels)
    bricks = split_ref.shape[1]
    column = lax.broadcasted_iota(jnp.int32, (COLUMNS, bricks), 0)
    chosen = (column == labels & (COLUMNS - 1)).astype(jnp.bfloat16)
    split_rows = split_ref.shape[0]
    half_rows = split_rows // 2
    members = masked_ref.shape[0] // split_rows

    def place_group(step, carry):
        for member in range(members):
            mask = (place_ref[...] == step * members + member).astype(jnp.bfloat16)
            masked_ref[pl.ds(member * split_rows, split_rows), :] = split_ref[...] * mask
        product = lax.dot_general(
            masked_ref[...],
            chosen,
            (((1,), (1,)), ((), ())),
            preferred_element_type=jnp.float32,
        )
        for member in range(members):
            at = member * split_rows
            out_ref[step * members + member] = (
                product[at : at + half_rows] + product[at + half_rows : at + split_rows]
            )
        return carry

    lax.fori_loop(0, out_ref.shape[0] // members, place_group, 0)


def place_of(owner):
    groups, members = lax.axis_size("ca"), lax.axis_size("fe")
    owner_ca = lax.shift_right_logical(owner, members.bit_length() - 1) ^ lax.axis_index("ca")
    owner_fe = (owner & (members - 1)) ^ lax.axis_index("fe")
    place = (owner_ca & 1) * (groups // 2) + lax.shift_right_logical(owner_ca, 1)
    place = place * 2 + (owner_fe & 1)
    return place * (members // 2) + lax.shift_right_logical(owner_fe, 1)


def cell_sums(octants, per_octant, ids, labels, table, places):
    first, count = octants
    bricks = ids.shape[1]
    rows = padded_rows(count)
    half = jax.ShapeDtypeStruct((places, rows, COLUMNS), jnp.float32)
    split = jax.ShapeDtypeStruct((2 * rows, bricks), jnp.bfloat16)
    scratch = []
    left = 8 - first - count
    if left:
        out_shape = [
            jax.ShapeDtypeStruct(labels.shape, jnp.int32),
            half,
            split,
            jax.ShapeDtypeStruct((-(-left * per_octant // 8) * 8, bricks), jnp.int32),
        ]
    else:
        out_shape = [half, half]
        scratch.append(pltpu.VMEM(split.shape, split.dtype))
    return pl.pallas_call(
        functools.partial(cell_sum_kernel, octants, per_octant),
        out_shape=out_shape,
        scratch_shapes=scratch
        + [
            pltpu.VMEM((2, -(-count * per_octant // 8) * 8, LANES), jnp.int32),
            pltpu.VMEM((72 * (count // math.gcd(count, 8)), bricks), jnp.float32),
        ]
        + brick_scratch(rows, bricks, places, 2 * LANES),
        compiler_params=pltpu.CompilerParams(vmem_limit_bytes=28 * 1024 * 1024),
        cost_estimate=pl.CostEstimate(
            flops=count * 4 * 10**9, bytes_accessed=count * 10**7, transcendentals=0
        ),
        name="cell_sums",
    )(ids, labels, table)


def padded_rows(count):
    return -(-9 * count // 8) * 8


def brick_scratch(rows, bricks, places, width):
    return [
        pltpu.VMEM((1, bricks), jnp.int32),
        pltpu.VMEM((min(16, places) * 2 * rows, width), jnp.bfloat16),
    ]


def brick_sums(split, labels, places):
    rows, bricks = split.shape
    return pl.pallas_call(
        brick_sum_kernel,
        out_shape=[
            jax.ShapeDtypeStruct((places, rows // 2, COLUMNS), jnp.float32),
            jax.ShapeDtypeStruct(labels.shape, jnp.int32),
        ],
        scratch_shapes=brick_scratch(rows // 2, bricks, places, bricks),
        compiler_params=pltpu.CompilerParams(vmem_limit_bytes=24 * 1024 * 1024),
        cost_estimate=pl.CostEstimate(
            flops=rows * 15 * 10**6, bytes_accessed=rows * 5 * 10**4, transcendentals=0
        ),
        name="brick_sums",
    )(split, labels)


def core_sum_kernel(passed, kept_ref, received_ref, *refs):
    outs = refs[passed:]
    for index, out_ref in enumerate(outs[: len(outs) - passed]):
        out_ref[...] = kept_ref[index] + received_ref[index]
    for i in range(passed):
        outs[len(outs) - passed + i][...] = refs[i][...]


def last_core_sum_kernel(kept_ref, received_ref, own_ref, *outs):
    for index, out_ref in enumerate(outs):
        out_ref[...] = kept_ref[index] + received_ref[index]
        for c in range(3):
            row = out_ref.shape[1] - 3 + c
            out_ref[:, row : row + 1, :] = jnp.broadcast_to(
                own_ref[c][None], (out_ref.shape[0], 1, COLUMNS)
            )


def last_core_sum(kept, received, own):
    pairs, rests = lax.axis_size("ca") // 2, lax.axis_size("fe") // 2
    shape = (2 * pairs, rests) + kept.shape[1:]
    return pl.pallas_call(
        last_core_sum_kernel,
        out_shape=[jax.ShapeDtypeStruct(shape[1:], jnp.float32)] * shape[0],
        compiler_params=pltpu.CompilerParams(vmem_limit_bytes=16 * 1024 * 1024),
        name="core_sum_b",
    )(kept.reshape(shape), received.reshape(shape), own)


def core_sum(kept, received, passed, name):
    pairs, rests = lax.axis_size("ca") // 2, lax.axis_size("fe") // 2
    shape = (2 * pairs, rests) + kept.shape[1:]
    out = pl.pallas_call(
        functools.partial(core_sum_kernel, len(passed)),
        out_shape=[jax.ShapeDtypeStruct(shape[1:], jnp.float32)] * shape[0]
        + [jax.ShapeDtypeStruct(array.shape, array.dtype) for array in passed],
        compiler_params=pltpu.CompilerParams(vmem_limit_bytes=16 * 1024 * 1024),
        name=name,
    )(kept.reshape(shape), received.reshape(shape), *passed)
    return out[: shape[0]], *out[shape[0] :]


def plane_sum_kernel(sources, passed, *refs):
    outs = refs[sources + passed :]
    height = 0
    for out_ref in outs[: len(outs) - passed]:
        out_ref[...] = sum(ref[pl.ds(height, out_ref.shape[0])] for ref in refs[:sources])
        height += out_ref.shape[0]
    for i in range(passed):
        outs[len(outs) - passed + i][...] = refs[sources + i][...]


def plane_sum(parts, passed, cuts, name):
    rest = parts[0].shape[1:]
    out = pl.pallas_call(
        functools.partial(plane_sum_kernel, len(parts), len(passed)),
        out_shape=[jax.ShapeDtypeStruct((cut,) + rest, jnp.float32) for cut in cuts]
        + [jax.ShapeDtypeStruct(array.shape, array.dtype) for array in passed],
        compiler_params=pltpu.CompilerParams(vmem_limit_bytes=16 * 1024 * 1024),
        name=name,
    )(*parts, *passed)
    return out[: len(cuts)], *out[len(cuts) :]


def last_sum_kernel(sources, spare, kept_ref, received_ref, *refs):
    parts, outs = refs[:sources], refs[sources:]
    rows = kept_ref.shape[1]
    outs[0][...] = kept_ref[0] + received_ref[0]
    outs[2][0:rows, :] = kept_ref[1] + received_ref[1]
    for height, out_ref in enumerate(outs[1:]):
        first = out_ref.shape[0] - parts[0].shape[1]
        out_ref[first:, :] = sum(ref[height] for ref in parts)
        out_ref[out_ref.shape[0] - spare :, :] = parts[1][height, parts[1].shape[1] - spare :, :]


def last_sum(kept, received, parts, spare):
    heights, rows, columns = parts[0].shape
    part = jax.ShapeDtypeStruct((rows, columns), jnp.float32)
    both = jax.ShapeDtypeStruct((kept.shape[1] + rows, columns), jnp.float32)
    return pl.pallas_call(
        functools.partial(last_sum_kernel, len(parts), spare),
        out_shape=[jax.ShapeDtypeStruct(kept.shape[1:], jnp.float32), part, both]
        + [part] * (heights - 2),
        compiler_params=pltpu.CompilerParams(vmem_limit_bytes=16 * 1024 * 1024),
        name="last_sum",
    )(kept, received, *parts)


def to_relative(block, core, pair, last, rest):
    groups, members = lax.axis_size("ca"), lax.axis_size("fe")
    flip = (2 * pair + core) * members + 2 * rest + last
    return lax.ppermute(block, ("ca", "fe"), [(i, i ^ flip) for i in range(groups * members)])


def across_plane(parts):
    return [parts[0]] + [
        to_relative(parts[index], 0, index // 2, index % 2, 0) for index in range(1, len(parts))
    ]


def across_height(parts):
    return [parts[0]] + [to_relative(parts[rest], 0, 0, 0, rest) for rest in range(1, len(parts))]


def three_parts(value):
    first = value.astype(jnp.bfloat16)
    rest = value - first.astype(jnp.float32)
    second = rest.astype(jnp.bfloat16)
    third = (rest - second.astype(jnp.float32)).astype(jnp.bfloat16)
    return first, second, third


def dot_selected(value, selector, contract):
    total = None
    for part in three_parts(value):
        term = lax.dot_general(
            part, selector, (((1,), (contract,)), ((), ())), preferred_element_type=jnp.float32
        )
        total = term if total is None else total + term
    return total


def update_kernel(heights, *refs):
    first_ref, second_refs = refs[0], refs[1 : 1 + heights]
    own_ref, stress_ref, resistance_ref, weights_ref, table_ref = refs[1 + heights : -2]
    stress_out_ref, nodal_ref = refs[-2:]
    elements = stress_ref.shape[2]
    rows, second_rows = first_ref.shape[0], second_refs[0].shape[0]
    gathered = [
        first_ref[:, 0:elements] + second_refs[1][0:rows, 0:elements],
        sum(ref[ref.shape[0] - second_rows :, 0:elements] for ref in second_refs),
    ]
    counted = 9 * CHUNKS[1][1]
    counts = gathered[1][counted : counted + 1]
    per_brick = 1.0 / (8.0 * jnp.maximum(counts, 1.0))
    frames = [
        jnp.concatenate(
            [
                sums[count * k : count * (k + 1)]
                for sums, (first, count) in zip(gathered, CHUNKS)
            ],
            axis=0,
        )
        * per_brick
        for k in range(9)
    ]

    node = lax.broadcasted_iota(jnp.int32, (COLUMNS, elements), 0)
    element = lax.broadcasted_iota(jnp.int32, (COLUMNS, elements), 1)
    base = element + element // GX
    selectors = [
        (node == base + (step_y * (GX + 1) + step_x)).astype(jnp.bfloat16)
        for step_x in range(2)
        for step_y in range(2)
    ]
    corner = lax.broadcasted_iota(jnp.int32, (24, 1), 0) & 7
    upper_corner = (corner & 1) == 1
    height = lax.axis_index("fe") // 2
    above = height + (lax.axis_index("fe") & 1)
    upper = jnp.zeros((3, COLUMNS), jnp.float32)
    for flip, ref in enumerate(second_refs):
        wanted = (height ^ flip) == above
        upper = upper + jnp.where(wanted, ref[ref.shape[0] - 3 :, :], 0.0)
    values = jnp.where(
        upper_corner,
        jnp.concatenate(
            [jnp.broadcast_to(upper[c : c + 1], (8, COLUMNS)) for c in range(3)], axis=0
        ),
        jnp.concatenate([jnp.broadcast_to(own_ref[c], (8, COLUMNS)) for c in range(3)], axis=0),
    )
    corners = jnp.zeros((24, elements), jnp.float32)
    for step in range(4):
        part = jnp.where(corner >> 1 == step, values, 0.0)
        corners = corners + dot_selected(part, selectors[step], 0)
    gradients = []
    for c in range(3):
        product = jnp.dot(
            table_ref[...],
            corners[8 * c : 8 * c + 8],
            precision=lax.Precision.HIGHEST,
            preferred_element_type=jnp.float32,
        )
        gradients.append([product[8 * d : 8 * d + 8] for d in range(3)])
    strain = [
        gradients[0][0],
        gradients[1][1],
        gradients[2][2],
        0.5 * (gradients[1][2] + gradients[2][1]),
        0.5 * (gradients[0][2] + gradients[2][0]),
        0.5 * (gradients[0][1] + gradients[1][0]),
    ]
    volume = strain[0] + strain[1] + strain[2]
    trial = []
    for component in range(6):
        change = 2.0 * SHEAR_MODULUS * strain[component]
        if component < 3:
            change = change + LAMBDA_ELASTIC * volume
        trial.append(stress_ref[component] + change)
    correction = [jnp.zeros_like(trial[0]) for component in range(6)]
    for system in range(12):
        rotated_dir = [
            sum(
                frames[3 * row + axis_id] * SLIP_DIRECTIONS[system][axis_id]
                for axis_id in range(3)
                if SLIP_DIRECTIONS[system][axis_id] != 0.0
            )
            for row in range(3)
        ]
        rotated_normal = [
            sum(frames[3 * row + axis_id] * SLIP_PLANES[system][axis_id] for axis_id in range(3))
            for row in range(3)
        ]
        schmid = [
            rotated_dir[0] * rotated_normal[0],
            rotated_dir[1] * rotated_normal[1],
            rotated_dir[2] * rotated_normal[2],
            0.5 * (rotated_dir[1] * rotated_normal[2] + rotated_dir[2] * rotated_normal[1]),
            0.5 * (rotated_dir[0] * rotated_normal[2] + rotated_dir[2] * rotated_normal[0]),
            0.5 * (rotated_dir[0] * rotated_normal[1] + rotated_dir[1] * rotated_normal[0]),
        ]
        resolved = (
            trial[0] * schmid[0]
            + trial[1] * schmid[1]
            + trial[2] * schmid[2]
            + 2.0 * (trial[3] * schmid[3] + trial[4] * schmid[4] + trial[5] * schmid[5])
        )
        slip_ratio = resolved / resistance_ref[system]
        slip_step = RATE_STEP * slip_ratio * jnp.abs(slip_ratio)
        correction = [
            correction[component] + slip_step * schmid[component] for component in range(6)
        ]
    updated = [
        trial[component] - 2.0 * SHEAR_MODULUS * correction[component] for component in range(6)
    ]
    for component in range(6):
        stress_out_ref[component] = updated[component]
    point_scale = weights_ref[...].astype(jnp.float32) * (1.0 / (FIXED_POINT * 8.0))
    scaled = [value * point_scale for value in updated]
    forces = []
    for rows in [(0, 5, 4), (5, 1, 3), (4, 3, 2)]:
        forces.append(
            lax.dot_general(
                table_ref[...],
                jnp.concatenate([scaled[row] for row in rows], axis=0),
                (((0,), (0,)), ((), ())),
                precision=lax.Precision.HIGHEST,
                preferred_element_type=jnp.float32,
            )
        )
    forces = jnp.concatenate(forces, axis=0)
    nodal = jnp.zeros((24, COLUMNS), jnp.float32)
    for step in range(4):
        part = jnp.where(corner >> 1 == step, forces, 0.0)
        nodal = nodal + dot_selected(part, selectors[step], 1)
    lower = jnp.where(upper_corner, 0.0, nodal)
    above = jnp.where(upper_corner, nodal, 0.0)
    for c in range(3):
        nodal_ref[0, c] = jnp.sum(lower[8 * c : 8 * c + 8], axis=0, keepdims=True)
        nodal_ref[1, c] = jnp.sum(above[8 * c : 8 * c + 8], axis=0, keepdims=True)


def element_update(first, second, own, stress_old, resistance, quad_weights):
    grad_table = shape_gradients()
    table = jnp.asarray(
        [
            [grad_table[quadrature][corner][direction] for corner in range(8)]
            for direction in range(3)
            for quadrature in range(8)
        ],
        dtype=jnp.float32,
    )
    return pl.pallas_call(
        functools.partial(update_kernel, len(second)),
        out_shape=(
            jax.ShapeDtypeStruct(stress_old.shape, jnp.float32),
            jax.ShapeDtypeStruct((2,) + own.shape, jnp.float32),
        ),
        compiler_params=pltpu.CompilerParams(vmem_limit_bytes=8 * 1024 * 1024),
        name="stress_update",
    )(first, *second, own, stress_old, resistance, quad_weights, table)


def body(
    grain_ids,
    euler_angles,
    brick_active,
    brick_owner,
    brick_element,
    displacement,
    stress_old,
    resistance,
    quad_weights,
):
    half = lax.axis_size("ca") * lax.axis_size("fe") // 2
    bricks = grain_ids.shape[1]
    owner = lax.optimization_barrier(brick_owner.reshape(bricks))
    labels = jnp.where(brick_active > 0, owner * COLUMNS + brick_element, -1).reshape(1, bricks)
    per_octant = grain_ids.shape[0] // 8
    table = rotation_table(euler_angles)
    labels, send, split, ids = cell_sums(CHUNKS[0], per_octant, grain_ids, labels, table, half)
    keep, labels = brick_sums(split, labels, half)
    core_a, labels, own = core_sum(
        keep, across_cores(send), [labels, displacement], "core_sum_a"
    )
    send, keep = cell_sums(CHUNKS[1], per_octant, ids, labels, table, half)
    flip = lax.axis_size("fe") // 4
    (kept, sent), own, send = plane_sum(
        across_plane(core_a), [own, send], [flip, flip], "plane_sum_a"
    )
    received = to_relative(sent, 0, 0, 0, flip)
    core_b = last_core_sum(keep, across_cores(send), own)
    while flip > 2:
        flip //= 2
        (kept, sent) = plane_sum([kept, received], [], [flip, flip], "height_sum_a")[0]
        received = to_relative(sent, 0, 0, 0, flip)
    first, *second = last_sum(kept, received, across_plane(core_b), 3)
    stress_new, nodal = element_update(
        first, across_height(second), displacement, stress_old, resistance, quad_weights
    )
    forces = nodal[0] + passed_along(nodal[1], "fe", 1)
    return (stress_new, forces)


def solution(mesh):
    placed = (
        P(None, ("ca", "fe")),
        P(),
        P(("ca", "fe")),
        P(("ca", "fe"), None),
        P(("ca", "fe")),
        P(None, ("ca", "fe"), None),
        P(None, None, ("ca", "fe")),
        P(None, None, ("ca", "fe")),
        P(None, ("ca", "fe")),
    )
    return jax.shard_map(
        body,
        mesh=mesh,
        in_specs=placed,
        out_specs=(P(None, None, ("ca", "fe")), P(None, ("ca", "fe"), None)),
        check_vma=False,
    )
```

```python
import functools
import functools
import math

import jax
import jax.numpy as jnp
from jax import lax
from jax.experimental import pallas as pl
from jax.experimental.pallas import tpu as pltpu
from jax.sharding import PartitionSpec as P

GX = 15
LANES = 128
COLUMNS = 256
CHUNKS = ((0, 6), (6, 2))
QUANTUM = float((1 << 15) - 1)

SLIP_PLANES = [
    [value / math.sqrt(3.0) for value in row]
    for row in [[1, 1, 1]] * 3 + [[-1, 1, 1]] * 3 + [[1, -1, 1]] * 3 + [[1, 1, -1]] * 3
]
SLIP_DIRECTIONS = [
    [value / math.sqrt(2.0) for value in row]
    for row in [
        [0, 1, -1],
        [1, 0, -1],
        [1, -1, 0],
        [0, 1, -1],
        [1, 0, 1],
        [1, 1, 0],
        [0, 1, 1],
        [1, 0, -1],
        [1, 1, 0],
        [0, 1, 1],
        [1, 0, 1],
        [1, -1, 0],
    ]
]
LAMBDA_ELASTIC = 1.5
SHEAR_MODULUS = 1.0
RATE_STEP = 0.1
FIXED_POINT = 65536.0


def passed_along(block, axis, distance):
    devices = range(lax.axis_size(axis))
    route = [(i - distance, i) for i in devices if i - distance in devices]
    return lax.ppermute(block, axis, route)


def shape_gradients():
    grad_table = [[[0.0, 0.0, 0.0] for corner in range(8)] for quadrature in range(8)]
    point_offset = 1.0 / math.sqrt(3.0)
    for quadrature in range(8):
        natural = [
            (2 * (quadrature >> shift_bits & 1) - 1) * point_offset for shift_bits in (2, 1, 0)
        ]
        for corner in range(8):
            sign_list = [2 * (corner >> shift_bits & 1) - 1 for shift_bits in (2, 1, 0)]
            factors = [1.0 + sign_list[axis_id] * natural[axis_id] for axis_id in range(3)]
            for direction in range(3):
                others = 1.0
                for axis_id in range(3):
                    if axis_id != direction:
                        others = others * factors[axis_id]
                grad_table[quadrature][corner][direction] = (
                    2.0 * sign_list[direction] * others / 8.0
                )
    return grad_table


def cos_sin(angle):
    square = angle * angle
    cosine = 1.0 / math.factorial(12)
    for power in (10, 8, 6, 4, 2, 0):
        cosine = cosine * square + (-1.0) ** (power // 2) / math.factorial(power)
    sine = 1.0 / math.factorial(13)
    for power in (11, 9, 7, 5, 3, 1):
        sine = sine * square + (-1.0) ** (power // 2) / math.factorial(power)
    return cosine, sine * angle


def rotation_coordinates(euler):
    cos_one, sin_one = cos_sin(0.5 * euler[0 : 0 + 1])
    cos_mid, sin_mid = cos_sin(0.5 * euler[1 : 1 + 1])
    cos_two, sin_two = cos_sin(0.5 * euler[2 : 2 + 1])
    w = cos_mid * (cos_one * cos_two - sin_one * sin_two)
    factor = jnp.where(w < 0.0, -QUANTUM, QUANTUM) / (1.0 + jnp.abs(w))
    x = sin_mid * (cos_one * cos_two + sin_one * sin_two) * factor
    y = sin_mid * (sin_one * cos_two - cos_one * sin_two) * factor
    z = cos_mid * (sin_one * cos_two + cos_one * sin_two) * factor
    x, y, z = [
        jnp.clip(jnp.round(value), -QUANTUM, QUANTUM).astype(jnp.int32) for value in (x, y, z)
    ]
    return [x, y, z]


def table_kernel(euler_ref, table_ref):
    at = 0
    for coordinate in rotation_coordinates(euler_ref[...]):
        for row in range(0, coordinate.shape[1] // LANES, 2):
            low = coordinate[:, row * LANES : (row + 1) * LANES]
            high = coordinate[:, (row + 1) * LANES : (row + 2) * LANES]
            table_ref[at] = jnp.broadcast_to(lax.shift_left(high, 16) | (low & 0xFFFF), (8, LANES))
            at += 1


def rotation_table(euler_angles):
    height = euler_angles.shape[1] // LANES * 3 // 2
    return pl.pallas_call(
        table_kernel,
        out_shape=jax.ShapeDtypeStruct((height, 8, LANES), jnp.int32),
        compiler_params=pltpu.CompilerParams(vmem_limit_bytes=8 * 1024 * 1024),
        cost_estimate=pl.CostEstimate(flops=10**6, bytes_accessed=10**7, transcendentals=0),
        name="rotation_table",
    )(euler_angles)


def looked_up(table_ref, first_row, rows, lane, bits):
    if rows == 1:
        return lax.gather(
            table_ref[first_row],
            lane,
            lax.GatherDimensionNumbers(
                offset_dims=(),
                collapsed_slice_dims=(1,),
                start_index_map=(1,),
                operand_batching_dims=(0,),
                start_indices_batching_dims=(0,),
            ),
            slice_sizes=(1, 1),
            mode=lax.GatherScatterMode.PROMISE_IN_BOUNDS,
        )
    half = rows // 2
    level = half.bit_length() - 1
    low = looked_up(table_ref, first_row, half, lane, bits)
    high = looked_up(table_ref, first_row + half, half, lane, bits)
    return jnp.where(bits[level], high, low)


def looked_up_words(table_ref, ids):
    lane = (ids & (LANES - 1))[:, :, None]
    row = lax.shift_right_logical(ids, 7)
    words = table_ref.shape[0] // 3
    bits = [(row & (2 << level)) != 0 for level in range(words.bit_length() - 1)]
    shift = lax.shift_left((row & 1) ^ 1, 4)
    return [
        lax.shift_left(looked_up(table_ref, words * axis, words, lane, bits), shift)
        for axis in range(3)
    ]


def rotation_products(words):
    x, y, z = [lax.shift_right_arithmetic(word, 16).astype(jnp.float32) for word in words]
    length = (x * x + y * y + z * z) * (0.5 / (QUANTUM * QUANTUM)) + 0.5
    scale = pl.reciprocal(length, approx=True)
    scale = scale * (2.0 - length * scale)
    w = scale - 1.0
    x, y, z = x * scale, y * scale, z * scale
    return [x * x, y * y, z * z, x * y, x * z, y * z, w * x, w * y, w * z]


ENTRIES = (
    ((1, -1.0), (2, -1.0)),
    ((3, 1.0), (8, -1.0)),
    ((4, 1.0), (7, 1.0)),
    ((3, 1.0), (8, 1.0)),
    ((0, -1.0), (2, -1.0)),
    ((5, 1.0), (6, -1.0)),
    ((4, 1.0), (7, -1.0)),
    ((5, 1.0), (6, 1.0)),
    ((0, -1.0), (1, -1.0)),
)


def remainder(value, divisor):
    return value - value // divisor * divisor


def cell_sum_kernel(
    octants,
    per_octant,
    ids_ref,
    label_ref,
    table_ref,
    *refs,
):
    first, count = octants
    start = ids_ref.shape[0] - (8 - first) * per_octant
    tile_ref, raw_ref, place_ref, masked_ref = refs[-4:]
    if first + count < 8:
        label_out_ref, send_ref, split_ref, rest_ref = refs[:-4]
        label_out_ref[...] = label_ref[...]
        rest_ref[...] = ids_ref[pl.ds(ids_ref.shape[0] - rest_ref.shape[0], rest_ref.shape[0]), :]
        targets = [(send_ref.shape[0], send_ref)]
    else:
        send_ref, keep_ref, split_ref = refs[:-4]
        targets = [(send_ref.shape[0], send_ref), (0, keep_ref)]
    groups = tile_ref.shape[1] // 8
    rows_left = count * per_octant - 8 * (groups - 1)
    turns = count // math.gcd(count, 8)
    rows = send_ref.shape[1]
    width = masked_ref.shape[1]
    pairs = ids_ref.shape[1] // width

    out_row = lax.broadcasted_iota(jnp.int32, (rows, raw_ref.shape[0]), 0)
    raw_row = lax.broadcasted_iota(jnp.int32, (rows, raw_ref.shape[0]), 1)
    entry, product = out_row // count, raw_row // (8 * turns)
    fold = jnp.zeros(out_row.shape, jnp.float32)
    for index, terms in enumerate(ENTRIES):
        for other, sign in terms:
            fold = jnp.where((entry == index) & (product == other), sign, fold)
    fold = jnp.where(remainder(out_row, count) == remainder(raw_row, count), fold, 0.0)
    fold = fold.astype(jnp.bfloat16)
    row = lax.broadcasted_iota(jnp.int32, (rows, width), 0)
    diagonal = (row // count == 0) | (row // count == 4) | (row // count == 8)
    constant = jnp.where(diagonal, float(per_octant), jnp.where(row < 9 * count, 0.0, 1.0))

    def lanes_of(pair):
        return pl.ds(pl.multiple_of(pair * width, width), width)

    def look_up(pair):
        for tile in range(width // LANES):
            lanes = pl.ds(pl.multiple_of(pair * width + tile * LANES, LANES), LANES)
            for octant in range(count):
                tile_ref[tile, pl.ds(octant, per_octant, stride=count), :] = ids_ref[
                    pl.ds(start + octant * per_octant, per_octant), lanes
                ]
            sums = [[jnp.zeros((8, LANES), jnp.float32)] * 9 for turn in range(turns)]
            found = None
            for group in range(groups + 1):
                last = found
                if group < groups:
                    ids = tile_ref[tile, pl.ds(8 * group, 8), :]
                    found = looked_up_words(table_ref, ids)
                if group == 0:
                    continue
                products = rotation_products(last)
                if group == groups and rows_left < 8:
                    there = lax.broadcasted_iota(jnp.int32, (8, LANES), 0) < rows_left
                    products = [jnp.where(there, value, 0.0) for value in products]
                turn = (group - 1) % turns
                sums[turn] = [total + value for total, value in zip(sums[turn], products)]
            scales = [2.0 / (QUANTUM * QUANTUM)] * 6 + [2.0 / QUANTUM] * 3
            raw_ref[:, lanes] = jnp.concatenate(
                [sums[turn][index] * scales[index] for index in range(9) for turn in range(turns)],
                axis=0,
            )

    def fold_entries(pair):
        lanes = lanes_of(pair)
        total = constant
        for part in three_parts(raw_ref[:, lanes]):
            total = total + jnp.dot(fold, part, preferred_element_type=jnp.float32)
        leading = total.astype(jnp.bfloat16).astype(jnp.float32)
        split_ref[:, lanes] = jnp.concatenate([leading, total - leading], axis=0).astype(
            jnp.bfloat16
        )

    def add_bricks(pair, counted):
        lanes = lanes_of(pair)
        column = lax.broadcasted_iota(jnp.int32, (COLUMNS, width), 0)
        chosen = (column == label_ref[:, lanes] & (COLUMNS - 1)).astype(jnp.bfloat16)
        place = jnp.where(counted, place_ref[:, lanes], -1)
        for base, out_ref in targets:
            add_places(split_ref, lanes, place - base, chosen, out_ref, masked_ref)

    place_ref[...] = relative_places(label_ref[...])
    for base, out_ref in targets:
        out_ref[...] = jnp.zeros(out_ref.shape, jnp.float32)
    raw_ref[:, pl.ds(0, width)] = jnp.zeros((raw_ref.shape[0], width), jnp.float32)
    split_ref[:, pl.ds(0, width)] = jnp.zeros((split_ref.shape[0], width), jnp.bfloat16)

    def step(pair, carry):
        add_bricks(jnp.maximum(pair - 2, 0), pair >= 2)
        fold_entries(jnp.maximum(pair - 1, 0))
        look_up(pair)
        return carry

    lax.fori_loop(0, pairs, step, 0, unroll=2)
    add_bricks(pairs - 2, True)
    fold_entries(pairs - 1)
    add_bricks(pairs - 1, True)


def relative_places(labels):
    place = place_of(lax.shift_right_arithmetic(labels, COLUMNS.bit_length() - 1))
    return jnp.where(labels < 0, -1, place)


def add_places(split_ref, lanes, place, chosen, out_ref, masked_ref):
    split_rows = split_ref.shape[0]
    half_rows = split_rows // 2
    members = masked_ref.shape[0] // split_rows
    for first in range(0, out_ref.shape[0], members):
        split = split_ref[:, lanes]
        for member in range(members):
            mask = (place == first + member).astype(jnp.bfloat16)
            masked_ref[pl.ds(member * split_rows, split_rows), :] = split * mask
        product = lax.dot_general(
            masked_ref[...],
            chosen,
            (((1,), (1,)), ((), ())),
            preferred_element_type=jnp.float32,
        )
        for member in range(members):
            at = member * split_rows
            out_ref[first + member] += (
                product[at : at + half_rows] + product[at + half_rows : at + split_rows]
            )


def across_cores(block):
    groups = lax.axis_size("ca")
    return lax.ppermute(block, "ca", [(i, i ^ 1) for i in range(groups)])


def brick_sum_kernel(split_ref, label_ref, out_ref, label_out_ref, place_ref, masked_ref):
    labels = label_ref[...]
    label_out_ref[...] = labels
    place_ref[...] = relative_places(labels)
    bricks = split_ref.shape[1]
    column = lax.broadcasted_iota(jnp.int32, (COLUMNS, bricks), 0)
    chosen = (column == labels & (COLUMNS - 1)).astype(jnp.bfloat16)
    split_rows = split_ref.shape[0]
    half_rows = split_rows // 2
    members = masked_ref.shape[0] // split_rows

    def place_group(step, carry):
        for member in range(members):
            mask = (place_ref[...] == step * members + member).astype(jnp.bfloat16)
            masked_ref[pl.ds(member * split_rows, split_rows), :] = split_ref[...] * mask
        product = lax.dot_general(
            masked_ref[...],
            chosen,
            (((1,), (1,)), ((), ())),
            preferred_element_type=jnp.float32,
        )
        for member in range(members):
            at = member * split_rows
            out_ref[step * members + member] = (
                product[at : at + half_rows] + product[at + half_rows : at + split_rows]
            )
        return carry

    lax.fori_loop(0, out_ref.shape[0] // members, place_group, 0)


def place_of(owner):
    groups, members = lax.axis_size("ca"), lax.axis_size("fe")
    owner_ca = lax.shift_right_logical(owner, members.bit_length() - 1) ^ lax.axis_index("ca")
    owner_fe = (owner & (members - 1)) ^ lax.axis_index("fe")
    place = (owner_ca & 1) * (groups // 2) + lax.shift_right_logical(owner_ca, 1)
    place = place * 2 + (owner_fe & 1)
    return place * (members // 2) + lax.shift_right_logical(owner_fe, 1)


def cell_sums(octants, per_octant, ids, labels, table, places):
    first, count = octants
    bricks = ids.shape[1]
    rows = padded_rows(count)
    half = jax.ShapeDtypeStruct((places, rows, COLUMNS), jnp.float32)
    split = jax.ShapeDtypeStruct((2 * rows, bricks), jnp.bfloat16)
    scratch = []
    left = 8 - first - count
    if left:
        out_shape = [
            jax.ShapeDtypeStruct(labels.shape, jnp.int32),
            half,
            split,
            jax.ShapeDtypeStruct((-(-left * per_octant // 8) * 8, bricks), jnp.int32),
        ]
    else:
        out_shape = [half, half]
        scratch.append(pltpu.VMEM(split.shape, split.dtype))
    return pl.pallas_call(
        functools.partial(cell_sum_kernel, octants, per_octant),
        out_shape=out_shape,
        scratch_shapes=scratch
        + [
            pltpu.VMEM((2, -(-count * per_octant // 8) * 8, LANES), jnp.int32),
            pltpu.VMEM((72 * (count // math.gcd(count, 8)), bricks), jnp.float32),
        ]
        + brick_scratch(rows, bricks, places, 2 * LANES),
        compiler_params=pltpu.CompilerParams(vmem_limit_bytes=28 * 1024 * 1024),
        cost_estimate=pl.CostEstimate(
            flops=count * 4 * 10**9, bytes_accessed=count * 10**7, transcendentals=0
        ),
        name="cell_sums",
    )(ids, labels, table)


def padded_rows(count):
    return -(-9 * count // 8) * 8


def brick_scratch(rows, bricks, places, width):
    return [
        pltpu.VMEM((1, bricks), jnp.int32),
        pltpu.VMEM((min(16, places) * 2 * rows, width), jnp.bfloat16),
    ]


def brick_sums(split, labels, places):
    rows, bricks = split.shape
    return pl.pallas_call(
        brick_sum_kernel,
        out_shape=[
            jax.ShapeDtypeStruct((places, rows // 2, COLUMNS), jnp.float32),
            jax.ShapeDtypeStruct(labels.shape, jnp.int32),
        ],
        scratch_shapes=brick_scratch(rows // 2, bricks, places, bricks),
        compiler_params=pltpu.CompilerParams(vmem_limit_bytes=24 * 1024 * 1024),
        cost_estimate=pl.CostEstimate(
            flops=rows * 15 * 10**6, bytes_accessed=rows * 5 * 10**4, transcendentals=0
        ),
        name="brick_sums",
    )(split, labels)


def core_sum_kernel(passed, kept_ref, received_ref, *refs):
    outs = refs[passed:]
    for index, out_ref in enumerate(outs[: len(outs) - passed]):
        out_ref[...] = kept_ref[index] + received_ref[index]
    for i in range(passed):
        outs[len(outs) - passed + i][...] = refs[i][...]


def last_core_sum_kernel(kept_ref, received_ref, own_ref, *outs):
    for index, out_ref in enumerate(outs):
        out_ref[...] = kept_ref[index] + received_ref[index]
        for c in range(3):
            row = out_ref.shape[1] - 3 + c
            out_ref[:, row : row + 1, :] = jnp.broadcast_to(
                own_ref[c][None], (out_ref.shape[0], 1, COLUMNS)
            )


def last_core_sum(kept, received, own):
    pairs, rests = lax.axis_size("ca") // 2, lax.axis_size("fe") // 2
    shape = (2 * pairs, rests) + kept.shape[1:]
    return pl.pallas_call(
        last_core_sum_kernel,
        out_shape=[jax.ShapeDtypeStruct(shape[1:], jnp.float32)] * shape[0],
        compiler_params=pltpu.CompilerParams(vmem_limit_bytes=16 * 1024 * 1024),
        name="core_sum_b",
    )(kept.reshape(shape), received.reshape(shape), own)


def core_sum(kept, received, passed, name):
    pairs, rests = lax.axis_size("ca") // 2, lax.axis_size("fe") // 2
    shape = (2 * pairs, rests) + kept.shape[1:]
    out = pl.pallas_call(
        functools.partial(core_sum_kernel, len(passed)),
        out_shape=[jax.ShapeDtypeStruct(shape[1:], jnp.float32)] * shape[0]
        + [jax.ShapeDtypeStruct(array.shape, array.dtype) for array in passed],
        compiler_params=pltpu.CompilerParams(vmem_limit_bytes=16 * 1024 * 1024),
        name=name,
    )(kept.reshape(shape), received.reshape(shape), *passed)
    return out[: shape[0]], *out[shape[0] :]


def plane_sum_kernel(sources, passed, *refs):
    outs = refs[sources + passed :]
    height = 0
    for out_ref in outs[: len(outs) - passed]:
        out_ref[...] = sum(ref[pl.ds(height, out_ref.shape[0])] for ref in refs[:sources])
        height += out_ref.shape[0]
    for i in range(passed):
        outs[len(outs) - passed + i][...] = refs[sources + i][...]


def plane_sum(parts, passed, cuts, name):
    rest = parts[0].shape[1:]
    out = pl.pallas_call(
        functools.partial(plane_sum_kernel, len(parts), len(passed)),
        out_shape=[jax.ShapeDtypeStruct((cut,) + rest, jnp.float32) for cut in cuts]
        + [jax.ShapeDtypeStruct(array.shape, array.dtype) for array in passed],
        compiler_params=pltpu.CompilerParams(vmem_limit_bytes=16 * 1024 * 1024),
        name=name,
    )(*parts, *passed)
    return out[: len(cuts)], *out[len(cuts) :]


def last_sum_kernel(sources, spare, kept_ref, received_ref, *refs):
    parts, outs = refs[:sources], refs[sources:]
    rows = kept_ref.shape[1]
    outs[0][...] = kept_ref[0] + received_ref[0]
    outs[2][0:rows, :] = kept_ref[1] + received_ref[1]
    for height, out_ref in enumerate(outs[1:]):
        first = out_ref.shape[0] - parts[0].shape[1]
        out_ref[first:, :] = sum(ref[height] for ref in parts)
        out_ref[out_ref.shape[0] - spare :, :] = parts[-1][height, -spare:, :]


def last_sum(kept, received, parts, spare):
    heights, rows, columns = parts[0].shape
    part = jax.ShapeDtypeStruct((rows, columns), jnp.float32)
    both = jax.ShapeDtypeStruct((kept.shape[1] + rows, columns), jnp.float32)
    return pl.pallas_call(
        functools.partial(last_sum_kernel, len(parts), spare),
        out_shape=[jax.ShapeDtypeStruct(kept.shape[1:], jnp.float32), part, both]
        + [part] * (heights - 2),
        compiler_params=pltpu.CompilerParams(vmem_limit_bytes=16 * 1024 * 1024),
        name="last_sum",
    )(kept, received, *parts)


def to_relative(block, core, pair, last, rest):
    groups, members = lax.axis_size("ca"), lax.axis_size("fe")
    flip = (2 * pair + core) * members + 2 * rest + last
    return lax.ppermute(block, ("ca", "fe"), [(i, i ^ flip) for i in range(groups * members)])


def across_plane(parts):
    return [parts[0]] + [
        to_relative(parts[index], 0, index // 2, index % 2, 0)
        for index in range(len(parts) - 1, 0, -1)
    ]


def across_height(parts):
    return [parts[0]] + [to_relative(parts[rest], 0, 0, 0, rest) for rest in range(1, len(parts))]


def three_parts(value):
    first = value.astype(jnp.bfloat16)
    rest = value - first.astype(jnp.float32)
    second = rest.astype(jnp.bfloat16)
    third = (rest - second.astype(jnp.float32)).astype(jnp.bfloat16)
    return first, second, third


def dot_selected(value, selector, contract):
    total = None
    for part in three_parts(value):
        term = lax.dot_general(
            part, selector, (((1,), (contract,)), ((), ())), preferred_element_type=jnp.float32
        )
        total = term if total is None else total + term
    return total


def update_kernel(heights, *refs):
    first_ref, second_refs = refs[0], refs[1 : 1 + heights]
    own_ref, stress_ref, resistance_ref, weights_ref, table_ref = refs[1 + heights : -2]
    stress_out_ref, nodal_ref = refs[-2:]
    elements = stress_ref.shape[2]
    rows, second_rows = first_ref.shape[0], second_refs[0].shape[0]
    gathered = [
        first_ref[:, 0:elements] + second_refs[1][0:rows, 0:elements],
        sum(ref[ref.shape[0] - second_rows :, 0:elements] for ref in second_refs),
    ]
    counted = 9 * CHUNKS[1][1]
    counts = gathered[1][counted : counted + 1]
    per_brick = 1.0 / (8.0 * jnp.maximum(counts, 1.0))
    frames = [
        jnp.concatenate(
            [
                sums[count * k : count * (k + 1)]
                for sums, (first, count) in zip(gathered, CHUNKS)
            ],
            axis=0,
        )
        * per_brick
        for k in range(9)
    ]

    node = lax.broadcasted_iota(jnp.int32, (COLUMNS, elements), 0)
    element = lax.broadcasted_iota(jnp.int32, (COLUMNS, elements), 1)
    base = element + element // GX
    selectors = [
        (node == base + (step_y * (GX + 1) + step_x)).astype(jnp.bfloat16)
        for step_x in range(2)
        for step_y in range(2)
    ]
    corner = lax.broadcasted_iota(jnp.int32, (24, 1), 0) & 7
    upper_corner = (corner & 1) == 1
    height = lax.axis_index("fe") // 2
    above = height + (lax.axis_index("fe") & 1)
    upper = jnp.zeros((3, COLUMNS), jnp.float32)
    for flip, ref in enumerate(second_refs):
        wanted = (height ^ flip) == above
        upper = upper + jnp.where(wanted, ref[ref.shape[0] - 3 :, :], 0.0)
    values = jnp.where(
        upper_corner,
        jnp.concatenate(
            [jnp.broadcast_to(upper[c : c + 1], (8, COLUMNS)) for c in range(3)], axis=0
        ),
        jnp.concatenate([jnp.broadcast_to(own_ref[c], (8, COLUMNS)) for c in range(3)], axis=0),
    )
    corners = jnp.zeros((24, elements), jnp.float32)
    for step in range(4):
        part = jnp.where(corner >> 1 == step, values, 0.0)
        corners = corners + dot_selected(part, selectors[step], 0)
    gradients = []
    for c in range(3):
        product = jnp.dot(
            table_ref[...],
            corners[8 * c : 8 * c + 8],
            precision=lax.Precision.HIGHEST,
            preferred_element_type=jnp.float32,
        )
        gradients.append([product[8 * d : 8 * d + 8] for d in range(3)])
    strain = [
        gradients[0][0],
        gradients[1][1],
        gradients[2][2],
        0.5 * (gradients[1][2] + gradients[2][1]),
        0.5 * (gradients[0][2] + gradients[2][0]),
        0.5 * (gradients[0][1] + gradients[1][0]),
    ]
    volume = strain[0] + strain[1] + strain[2]
    trial = []
    for component in range(6):
        change = 2.0 * SHEAR_MODULUS * strain[component]
        if component < 3:
            change = change + LAMBDA_ELASTIC * volume
        trial.append(stress_ref[component] + change)
    correction = [jnp.zeros_like(trial[0]) for component in range(6)]
    for system in range(12):
        rotated_dir = [
            sum(
                frames[3 * row + axis_id] * SLIP_DIRECTIONS[system][axis_id]
                for axis_id in range(3)
                if SLIP_DIRECTIONS[system][axis_id] != 0.0
            )
            for row in range(3)
        ]
        rotated_normal = [
            sum(frames[3 * row + axis_id] * SLIP_PLANES[system][axis_id] for axis_id in range(3))
            for row in range(3)
        ]
        schmid = [
            rotated_dir[0] * rotated_normal[0],
            rotated_dir[1] * rotated_normal[1],
            rotated_dir[2] * rotated_normal[2],
            0.5 * (rotated_dir[1] * rotated_normal[2] + rotated_dir[2] * rotated_normal[1]),
            0.5 * (rotated_dir[0] * rotated_normal[2] + rotated_dir[2] * rotated_normal[0]),
            0.5 * (rotated_dir[0] * rotated_normal[1] + rotated_dir[1] * rotated_normal[0]),
        ]
        resolved = (
            trial[0] * schmid[0]
            + trial[1] * schmid[1]
            + trial[2] * schmid[2]
            + 2.0 * (trial[3] * schmid[3] + trial[4] * schmid[4] + trial[5] * schmid[5])
        )
        slip_ratio = resolved / resistance_ref[system]
        slip_step = RATE_STEP * slip_ratio * jnp.abs(slip_ratio)
        correction = [
            correction[component] + slip_step * schmid[component] for component in range(6)
        ]
    updated = [
        trial[component] - 2.0 * SHEAR_MODULUS * correction[component] for component in range(6)
    ]
    for component in range(6):
        stress_out_ref[component] = updated[component]
    point_scale = weights_ref[...].astype(jnp.float32) * (1.0 / (FIXED_POINT * 8.0))
    scaled = [value * point_scale for value in updated]
    forces = []
    for rows in [(0, 5, 4), (5, 1, 3), (4, 3, 2)]:
        forces.append(
            lax.dot_general(
                table_ref[...],
                jnp.concatenate([scaled[row] for row in rows], axis=0),
                (((0,), (0,)), ((), ())),
                precision=lax.Precision.HIGHEST,
                preferred_element_type=jnp.float32,
            )
        )
    forces = jnp.concatenate(forces, axis=0)
    nodal = jnp.zeros((24, COLUMNS), jnp.float32)
    for step in range(4):
        part = jnp.where(corner >> 1 == step, forces, 0.0)
        nodal = nodal + dot_selected(part, selectors[step], 1)
    lower = jnp.where(upper_corner, 0.0, nodal)
    above = jnp.where(upper_corner, nodal, 0.0)
    for c in range(3):
        nodal_ref[0, c] = jnp.sum(lower[8 * c : 8 * c + 8], axis=0, keepdims=True)
        nodal_ref[1, c] = jnp.sum(above[8 * c : 8 * c + 8], axis=0, keepdims=True)


def element_update(first, second, own, stress_old, resistance, quad_weights):
    grad_table = shape_gradients()
    table = jnp.asarray(
        [
            [grad_table[quadrature][corner][direction] for corner in range(8)]
            for direction in range(3)
            for quadrature in range(8)
        ],
        dtype=jnp.float32,
    )
    return pl.pallas_call(
        functools.partial(update_kernel, len(second)),
        out_shape=(
            jax.ShapeDtypeStruct(stress_old.shape, jnp.float32),
            jax.ShapeDtypeStruct((2,) + own.shape, jnp.float32),
        ),
        compiler_params=pltpu.CompilerParams(vmem_limit_bytes=8 * 1024 * 1024),
        name="stress_update",
    )(first, *second, own, stress_old, resistance, quad_weights, table)


def body(
    grain_ids,
    euler_angles,
    brick_active,
    brick_owner,
    brick_element,
    displacement,
    stress_old,
    resistance,
    quad_weights,
):
    half = lax.axis_size("ca") * lax.axis_size("fe") // 2
    bricks = grain_ids.shape[1]
    owner = lax.optimization_barrier(brick_owner.reshape(bricks))
    labels = jnp.where(brick_active > 0, owner * COLUMNS + brick_element, -1).reshape(1, bricks)
    per_octant = grain_ids.shape[0] // 8
    table = rotation_table(euler_angles)
    labels, send, split, ids = cell_sums(CHUNKS[0], per_octant, grain_ids, labels, table, half)
    keep, labels = brick_sums(split, labels, half)
    core_a, labels, own = core_sum(
        keep, across_cores(send), [labels, displacement], "core_sum_a"
    )
    send, keep = cell_sums(CHUNKS[1], per_octant, ids, labels, table, half)
    flip = lax.axis_size("fe") // 4
    (kept, sent), own, send = plane_sum(
        across_plane(core_a), [own, send], [flip, flip], "plane_sum_a"
    )
    received = to_relative(sent, 0, 0, 0, flip)
    core_b = last_core_sum(keep, across_cores(send), own)
    while flip > 2:
        flip //= 2
        (kept, sent) = plane_sum([kept, received], [], [flip, flip], "height_sum_a")[0]
        received = to_relative(sent, 0, 0, 0, flip)
    first, *second = last_sum(kept, received, across_plane(core_b), 3)
    stress_new, nodal = element_update(
        first, across_height(second), displacement, stress_old, resistance, quad_weights
    )
    forces = nodal[0] + passed_along(nodal[1], "fe", 1)
    return (stress_new, forces)


def solution(mesh):
    placed = (
        P(None, ("ca", "fe")),
        P(),
        P(("ca", "fe")),
        P(("ca", "fe"), None),
        P(("ca", "fe")),
        P(None, ("ca", "fe"), None),
        P(None, None, ("ca", "fe")),
        P(None, None, ("ca", "fe")),
        P(None, ("ca", "fe")),
    )
    return jax.shard_map(
        body,
        mesh=mesh,
        in_specs=placed,
        out_specs=(P(None, None, ("ca", "fe")), P(None, ("ca", "fe"), None)),
        check_vma=False,
    )
```

```python
import functools
import functools
import math

import jax
import jax.numpy as jnp
from jax import lax
from jax.experimental import pallas as pl
from jax.experimental.pallas import tpu as pltpu
from jax.sharding import PartitionSpec as P

GX = 15
LANES = 128
COLUMNS = 256
CHUNKS = ((0, 4), (4, 4))
QUANTUM = float((1 << 15) - 1)

SLIP_PLANES = [
    [value / math.sqrt(3.0) for value in row]
    for row in [[1, 1, 1]] * 3 + [[-1, 1, 1]] * 3 + [[1, -1, 1]] * 3 + [[1, 1, -1]] * 3
]
SLIP_DIRECTIONS = [
    [value / math.sqrt(2.0) for value in row]
    for row in [
        [0, 1, -1],
        [1, 0, -1],
        [1, -1, 0],
        [0, 1, -1],
        [1, 0, 1],
        [1, 1, 0],
        [0, 1, 1],
        [1, 0, -1],
        [1, 1, 0],
        [0, 1, 1],
        [1, 0, 1],
        [1, -1, 0],
    ]
]
LAMBDA_ELASTIC = 1.5
SHEAR_MODULUS = 1.0
RATE_STEP = 0.1
FIXED_POINT = 65536.0


def passed_along(block, axis, distance):
    devices = range(lax.axis_size(axis))
    route = [(i - distance, i) for i in devices if i - distance in devices]
    return lax.ppermute(block, axis, route)


def shape_gradients():
    grad_table = [[[0.0, 0.0, 0.0] for corner in range(8)] for quadrature in range(8)]
    point_offset = 1.0 / math.sqrt(3.0)
    for quadrature in range(8):
        natural = [
            (2 * (quadrature >> shift_bits & 1) - 1) * point_offset for shift_bits in (2, 1, 0)
        ]
        for corner in range(8):
            sign_list = [2 * (corner >> shift_bits & 1) - 1 for shift_bits in (2, 1, 0)]
            factors = [1.0 + sign_list[axis_id] * natural[axis_id] for axis_id in range(3)]
            for direction in range(3):
                others = 1.0
                for axis_id in range(3):
                    if axis_id != direction:
                        others = others * factors[axis_id]
                grad_table[quadrature][corner][direction] = (
                    2.0 * sign_list[direction] * others / 8.0
                )
    return grad_table


def cos_sin(angle):
    square = angle * angle
    cosine = 1.0 / math.factorial(12)
    for power in (10, 8, 6, 4, 2, 0):
        cosine = cosine * square + (-1.0) ** (power // 2) / math.factorial(power)
    sine = 1.0 / math.factorial(13)
    for power in (11, 9, 7, 5, 3, 1):
        sine = sine * square + (-1.0) ** (power // 2) / math.factorial(power)
    return cosine, sine * angle


def rotation_coordinates(euler):
    cos_one, sin_one = cos_sin(0.5 * euler[0 : 0 + 1])
    cos_mid, sin_mid = cos_sin(0.5 * euler[1 : 1 + 1])
    cos_two, sin_two = cos_sin(0.5 * euler[2 : 2 + 1])
    w = cos_mid * (cos_one * cos_two - sin_one * sin_two)
    factor = jnp.where(w < 0.0, -QUANTUM, QUANTUM) / (1.0 + jnp.abs(w))
    x = sin_mid * (cos_one * cos_two + sin_one * sin_two) * factor
    y = sin_mid * (sin_one * cos_two - cos_one * sin_two) * factor
    z = cos_mid * (sin_one * cos_two + cos_one * sin_two) * factor
    x, y, z = [
        jnp.clip(jnp.round(value), -QUANTUM, QUANTUM).astype(jnp.int32) for value in (x, y, z)
    ]
    return [x, y, z]


def table_kernel(euler_ref, table_ref):
    at = 0
    for coordinate in rotation_coordinates(euler_ref[...]):
        for row in range(0, coordinate.shape[1] // LANES, 2):
            low = coordinate[:, row * LANES : (row + 1) * LANES]
            high = coordinate[:, (row + 1) * LANES : (row + 2) * LANES]
            table_ref[at] = jnp.broadcast_to(lax.shift_left(high, 16) | (low & 0xFFFF), (8, LANES))
            at += 1


def rotation_table(euler_angles):
    height = euler_angles.shape[1] // LANES * 3 // 2
    return pl.pallas_call(
        table_kernel,
        out_shape=jax.ShapeDtypeStruct((height, 8, LANES), jnp.int32),
        compiler_params=pltpu.CompilerParams(vmem_limit_bytes=8 * 1024 * 1024),
        cost_estimate=pl.CostEstimate(flops=10**6, bytes_accessed=10**7, transcendentals=0),
        name="rotation_table",
    )(euler_angles)


def looked_up(table_ref, first_row, rows, lane, bits):
    if rows == 1:
        return lax.gather(
            table_ref[first_row],
            lane,
            lax.GatherDimensionNumbers(
                offset_dims=(),
                collapsed_slice_dims=(1,),
                start_index_map=(1,),
                operand_batching_dims=(0,),
                start_indices_batching_dims=(0,),
            ),
            slice_sizes=(1, 1),
            mode=lax.GatherScatterMode.PROMISE_IN_BOUNDS,
        )
    half = rows // 2
    level = half.bit_length() - 1
    low = looked_up(table_ref, first_row, half, lane, bits)
    high = looked_up(table_ref, first_row + half, half, lane, bits)
    return jnp.where(bits[level], high, low)


def looked_up_words(table_ref, ids):
    lane = (ids & (LANES - 1))[:, :, None]
    row = lax.shift_right_logical(ids, 7)
    words = table_ref.shape[0] // 3
    bits = [(row & (2 << level)) != 0 for level in range(words.bit_length() - 1)]
    shift = lax.shift_left((row & 1) ^ 1, 4)
    return [
        lax.shift_left(looked_up(table_ref, words * axis, words, lane, bits), shift)
        for axis in range(3)
    ]


def rotation_products(words):
    x, y, z = [lax.shift_right_arithmetic(word, 16).astype(jnp.float32) for word in words]
    length = (x * x + y * y + z * z) * (0.5 / (QUANTUM * QUANTUM)) + 0.5
    scale = pl.reciprocal(length, approx=True)
    scale = scale * (2.0 - length * scale)
    w = scale - 1.0
    x, y, z = x * scale, y * scale, z * scale
    return [x * x, y * y, z * z, x * y, x * z, y * z, w * x, w * y, w * z]


ENTRIES = (
    ((1, -1.0), (2, -1.0)),
    ((3, 1.0), (8, -1.0)),
    ((4, 1.0), (7, 1.0)),
    ((3, 1.0), (8, 1.0)),
    ((0, -1.0), (2, -1.0)),
    ((5, 1.0), (6, -1.0)),
    ((4, 1.0), (7, -1.0)),
    ((5, 1.0), (6, 1.0)),
    ((0, -1.0), (1, -1.0)),
)


def remainder(value, divisor):
    return value - value // divisor * divisor


def cell_sum_kernel(
    octants,
    per_octant,
    ids_ref,
    label_ref,
    table_ref,
    *refs,
):
    first, count = octants
    start = ids_ref.shape[0] - (8 - first) * per_octant
    tile_ref, raw_ref, place_ref, masked_ref = refs[-4:]
    if first + count < 8:
        label_out_ref, send_ref, split_ref, rest_ref = refs[:-4]
        label_out_ref[...] = label_ref[...]
        rest_ref[...] = ids_ref[pl.ds(ids_ref.shape[0] - rest_ref.shape[0], rest_ref.shape[0]), :]
        targets = [(send_ref.shape[0], send_ref)]
    else:
        send_ref, keep_ref, split_ref = refs[:-4]
        targets = [(send_ref.shape[0], send_ref), (0, keep_ref)]
    groups = tile_ref.shape[1] // 8
    rows_left = count * per_octant - 8 * (groups - 1)
    turns = count // math.gcd(count, 8)
    rows = send_ref.shape[1]
    width = masked_ref.shape[1]
    pairs = ids_ref.shape[1] // width

    out_row = lax.broadcasted_iota(jnp.int32, (rows, raw_ref.shape[0]), 0)
    raw_row = lax.broadcasted_iota(jnp.int32, (rows, raw_ref.shape[0]), 1)
    entry, product = out_row // count, raw_row // (8 * turns)
    fold = jnp.zeros(out_row.shape, jnp.float32)
    for index, terms in enumerate(ENTRIES):
        for other, sign in terms:
            fold = jnp.where((entry == index) & (product == other), sign, fold)
    fold = jnp.where(remainder(out_row, count) == remainder(raw_row, count), fold, 0.0)
    fold = fold.astype(jnp.bfloat16)
    row = lax.broadcasted_iota(jnp.int32, (rows, width), 0)
    diagonal = (row // count == 0) | (row // count == 4) | (row // count == 8)
    constant = jnp.where(diagonal, float(per_octant), jnp.where(row < 9 * count, 0.0, 1.0))

    def lanes_of(pair):
        return pl.ds(pl.multiple_of(pair * width, width), width)

    def look_up(pair):
        for tile in range(width // LANES):
            lanes = pl.ds(pl.multiple_of(pair * width + tile * LANES, LANES), LANES)
            for octant in range(count):
                tile_ref[tile, pl.ds(octant, per_octant, stride=count), :] = ids_ref[
                    pl.ds(start + octant * per_octant, per_octant), lanes
                ]
            sums = [[jnp.zeros((8, LANES), jnp.float32)] * 9 for turn in range(turns)]
            found = None
            for group in range(groups + 1):
                last = found
                if group < groups:
                    ids = tile_ref[tile, pl.ds(8 * group, 8), :]
                    found = looked_up_words(table_ref, ids)
                if group == 0:
                    continue
                products = rotation_products(last)
                if group == groups and rows_left < 8:
                    there = lax.broadcasted_iota(jnp.int32, (8, LANES), 0) < rows_left
                    products = [jnp.where(there, value, 0.0) for value in products]
                turn = (group - 1) % turns
                sums[turn] = [total + value for total, value in zip(sums[turn], products)]
            scales = [2.0 / (QUANTUM * QUANTUM)] * 6 + [2.0 / QUANTUM] * 3
            raw_ref[:, lanes] = jnp.concatenate(
                [sums[turn][index] * scales[index] for index in range(9) for turn in range(turns)],
                axis=0,
            )

    def fold_entries(pair):
        lanes = lanes_of(pair)
        total = constant
        for part in three_parts(raw_ref[:, lanes]):
            total = total + jnp.dot(fold, part, preferred_element_type=jnp.float32)
        leading = total.astype(jnp.bfloat16).astype(jnp.float32)
        split_ref[:, lanes] = jnp.concatenate([leading, total - leading], axis=0).astype(
            jnp.bfloat16
        )

    def add_bricks(pair, counted):
        lanes = lanes_of(pair)
        column = lax.broadcasted_iota(jnp.int32, (COLUMNS, width), 0)
        chosen = (column == label_ref[:, lanes] & (COLUMNS - 1)).astype(jnp.bfloat16)
        place = jnp.where(counted, place_ref[:, lanes], -1)
        for base, out_ref in targets:
            add_places(split_ref, lanes, place - base, chosen, out_ref, masked_ref)

    place_ref[...] = relative_places(label_ref[...])
    for base, out_ref in targets:
        out_ref[...] = jnp.zeros(out_ref.shape, jnp.float32)
    raw_ref[:, pl.ds(0, width)] = jnp.zeros((raw_ref.shape[0], width), jnp.float32)
    split_ref[:, pl.ds(0, width)] = jnp.zeros((split_ref.shape[0], width), jnp.bfloat16)

    def step(pair, carry):
        add_bricks(jnp.maximum(pair - 2, 0), pair >= 2)
        fold_entries(jnp.maximum(pair - 1, 0))
        look_up(pair)
        return carry

    lax.fori_loop(0, pairs, step, 0, unroll=2)
    add_bricks(pairs - 2, True)
    fold_entries(pairs - 1)
    add_bricks(pairs - 1, True)


def relative_places(labels):
    place = place_of(lax.shift_right_arithmetic(labels, COLUMNS.bit_length() - 1))
    return jnp.where(labels < 0, -1, place)


def add_places(split_ref, lanes, place, chosen, out_ref, masked_ref):
    split_rows = split_ref.shape[0]
    half_rows = split_rows // 2
    members = masked_ref.shape[0] // split_rows
    for first in range(0, out_ref.shape[0], members):
        split = split_ref[:, lanes]
        for member in range(members):
            mask = (place == first + member).astype(jnp.bfloat16)
            masked_ref[pl.ds(member * split_rows, split_rows), :] = split * mask
        product = lax.dot_general(
            masked_ref[...],
            chosen,
            (((1,), (1,)), ((), ())),
            preferred_element_type=jnp.float32,
        )
        for member in range(members):
            at = member * split_rows
            out_ref[first + member] += (
                product[at : at + half_rows] + product[at + half_rows : at + split_rows]
            )


def across_cores(block):
    groups = lax.axis_size("ca")
    return lax.ppermute(block, "ca", [(i, i ^ 1) for i in range(groups)])


def brick_sum_kernel(split_ref, label_ref, out_ref, label_out_ref, place_ref, masked_ref):
    labels = label_ref[...]
    label_out_ref[...] = labels
    place_ref[...] = relative_places(labels)
    bricks = split_ref.shape[1]
    column = lax.broadcasted_iota(jnp.int32, (COLUMNS, bricks), 0)
    chosen = (column == labels & (COLUMNS - 1)).astype(jnp.bfloat16)
    split_rows = split_ref.shape[0]
    half_rows = split_rows // 2
    members = masked_ref.shape[0] // split_rows

    def place_group(step, carry):
        for member in range(members):
            mask = (place_ref[...] == step * members + member).astype(jnp.bfloat16)
            masked_ref[pl.ds(member * split_rows, split_rows), :] = split_ref[...] * mask
        product = lax.dot_general(
            masked_ref[...],
            chosen,
            (((1,), (1,)), ((), ())),
            preferred_element_type=jnp.float32,
        )
        for member in range(members):
            at = member * split_rows
            out_ref[step * members + member] = (
                product[at : at + half_rows] + product[at + half_rows : at + split_rows]
            )
        return carry

    lax.fori_loop(0, out_ref.shape[0] // members, place_group, 0)


def place_of(owner):
    groups, members = lax.axis_size("ca"), lax.axis_size("fe")
    owner_ca = lax.shift_right_logical(owner, members.bit_length() - 1) ^ lax.axis_index("ca")
    owner_fe = (owner & (members - 1)) ^ lax.axis_index("fe")
    place = (owner_ca & 1) * (groups // 2) + lax.shift_right_logical(owner_ca, 1)
    place = place * 2 + (owner_fe & 1)
    return place * (members // 2) + lax.shift_right_logical(owner_fe, 1)


def cell_sums(octants, per_octant, ids, labels, table, places):
    first, count = octants
    bricks = ids.shape[1]
    rows = padded_rows(count)
    half = jax.ShapeDtypeStruct((places, rows, COLUMNS), jnp.float32)
    split = jax.ShapeDtypeStruct((2 * rows, bricks), jnp.bfloat16)
    scratch = []
    left = 8 - first - count
    if left:
        out_shape = [
            jax.ShapeDtypeStruct(labels.shape, jnp.int32),
            half,
            split,
            jax.ShapeDtypeStruct((-(-left * per_octant // 8) * 8, bricks), jnp.int32),
        ]
    else:
        out_shape = [half, half]
        scratch.append(pltpu.VMEM(split.shape, split.dtype))
    return pl.pallas_call(
        functools.partial(cell_sum_kernel, octants, per_octant),
        out_shape=out_shape,
        scratch_shapes=scratch
        + [
            pltpu.VMEM((2, -(-count * per_octant // 8) * 8, LANES), jnp.int32),
            pltpu.VMEM((72 * (count // math.gcd(count, 8)), bricks), jnp.float32),
        ]
        + brick_scratch(rows, bricks, places, 2 * LANES),
        compiler_params=pltpu.CompilerParams(vmem_limit_bytes=28 * 1024 * 1024),
        cost_estimate=pl.CostEstimate(
            flops=count * 4 * 10**9, bytes_accessed=count * 10**7, transcendentals=0
        ),
        name="cell_sums",
    )(ids, labels, table)


def padded_rows(count):
    return -(-9 * count // 8) * 8


def brick_scratch(rows, bricks, places, width):
    return [
        pltpu.VMEM((1, bricks), jnp.int32),
        pltpu.VMEM((min(16, places) * 2 * rows, width), jnp.bfloat16),
    ]


def brick_sums(split, labels, places):
    rows, bricks = split.shape
    return pl.pallas_call(
        brick_sum_kernel,
        out_shape=[
            jax.ShapeDtypeStruct((places, rows // 2, COLUMNS), jnp.float32),
            jax.ShapeDtypeStruct(labels.shape, jnp.int32),
        ],
        scratch_shapes=brick_scratch(rows // 2, bricks, places, bricks),
        compiler_params=pltpu.CompilerParams(vmem_limit_bytes=24 * 1024 * 1024),
        cost_estimate=pl.CostEstimate(
            flops=rows * 15 * 10**6, bytes_accessed=rows * 5 * 10**4, transcendentals=0
        ),
        name="brick_sums",
    )(split, labels)


def core_sum_kernel(passed, kept_ref, received_ref, *refs):
    outs = refs[passed:]
    for index, out_ref in enumerate(outs[: len(outs) - passed]):
        out_ref[...] = kept_ref[index] + received_ref[index]
    for i in range(passed):
        outs[len(outs) - passed + i][...] = refs[i][...]


def last_core_sum_kernel(kept_ref, received_ref, own_ref, *outs):
    for index, out_ref in enumerate(outs):
        out_ref[...] = kept_ref[index] + received_ref[index]
        for c in range(3):
            row = out_ref.shape[1] - 3 + c
            out_ref[:, row : row + 1, :] = jnp.broadcast_to(
                own_ref[c][None], (out_ref.shape[0], 1, COLUMNS)
            )


def last_core_sum(kept, received, own):
    pairs, rests = lax.axis_size("ca") // 2, lax.axis_size("fe") // 2
    shape = (2 * pairs, rests) + kept.shape[1:]
    return pl.pallas_call(
        last_core_sum_kernel,
        out_shape=[jax.ShapeDtypeStruct(shape[1:], jnp.float32)] * shape[0],
        compiler_params=pltpu.CompilerParams(vmem_limit_bytes=16 * 1024 * 1024),
        name="core_sum_b",
    )(kept.reshape(shape), received.reshape(shape), own)


def core_sum(kept, received, passed, name):
    pairs, rests = lax.axis_size("ca") // 2, lax.axis_size("fe") // 2
    shape = (2 * pairs, rests) + kept.shape[1:]
    out = pl.pallas_call(
        functools.partial(core_sum_kernel, len(passed)),
        out_shape=[jax.ShapeDtypeStruct(shape[1:], jnp.float32)] * shape[0]
        + [jax.ShapeDtypeStruct(array.shape, array.dtype) for array in passed],
        compiler_params=pltpu.CompilerParams(vmem_limit_bytes=16 * 1024 * 1024),
        name=name,
    )(kept.reshape(shape), received.reshape(shape), *passed)
    return out[: shape[0]], *out[shape[0] :]


def plane_sum_kernel(sources, passed, *refs):
    outs = refs[sources + passed :]
    height = 0
    for out_ref in outs[: len(outs) - passed]:
        out_ref[...] = sum(ref[pl.ds(height, out_ref.shape[0])] for ref in refs[:sources])
        height += out_ref.shape[0]
    for i in range(passed):
        outs[len(outs) - passed + i][...] = refs[sources + i][...]


def plane_sum(parts, passed, cuts, name):
    rest = parts[0].shape[1:]
    out = pl.pallas_call(
        functools.partial(plane_sum_kernel, len(parts), len(passed)),
        out_shape=[jax.ShapeDtypeStruct((cut,) + rest, jnp.float32) for cut in cuts]
        + [jax.ShapeDtypeStruct(array.shape, array.dtype) for array in passed],
        compiler_params=pltpu.CompilerParams(vmem_limit_bytes=16 * 1024 * 1024),
        name=name,
    )(*parts, *passed)
    return out[: len(cuts)], *out[len(cuts) :]


def last_sum_kernel(sources, spare, kept_ref, received_ref, *refs):
    parts, outs = refs[:sources], refs[sources:]
    rows = kept_ref.shape[1]
    outs[0][...] = kept_ref[0] + received_ref[0]
    outs[2][0:rows, :] = kept_ref[1] + received_ref[1]
    for height, out_ref in enumerate(outs[1:]):
        first = out_ref.shape[0] - parts[0].shape[1]
        out_ref[first:, :] = sum(ref[height] for ref in parts)
        out_ref[out_ref.shape[0] - spare :, :] = parts[-1][height, -spare:, :]


def last_sum(kept, received, parts, spare):
    heights, rows, columns = parts[0].shape
    part = jax.ShapeDtypeStruct((rows, columns), jnp.float32)
    both = jax.ShapeDtypeStruct((kept.shape[1] + rows, columns), jnp.float32)
    return pl.pallas_call(
        functools.partial(last_sum_kernel, len(parts), spare),
        out_shape=[jax.ShapeDtypeStruct(kept.shape[1:], jnp.float32), part, both]
        + [part] * (heights - 2),
        compiler_params=pltpu.CompilerParams(vmem_limit_bytes=16 * 1024 * 1024),
        name="last_sum",
    )(kept, received, *parts)


def to_relative(block, core, pair, last, rest):
    groups, members = lax.axis_size("ca"), lax.axis_size("fe")
    flip = (2 * pair + core) * members + 2 * rest + last
    return lax.ppermute(block, ("ca", "fe"), [(i, i ^ flip) for i in range(groups * members)])


def across_plane(parts):
    return [parts[0]] + [
        to_relative(parts[index], 0, index // 2, index % 2, 0)
        for index in range(len(parts) - 1, 0, -1)
    ]


def across_height(parts):
    return [parts[0]] + [to_relative(parts[rest], 0, 0, 0, rest) for rest in range(1, len(parts))]


def three_parts(value):
    first = value.astype(jnp.bfloat16)
    rest = value - first.astype(jnp.float32)
    second = rest.astype(jnp.bfloat16)
    third = (rest - second.astype(jnp.float32)).astype(jnp.bfloat16)
    return first, second, third


def dot_selected(value, selector, contract):
    total = None
    for part in three_parts(value):
        term = lax.dot_general(
            part, selector, (((1,), (contract,)), ((), ())), preferred_element_type=jnp.float32
        )
        total = term if total is None else total + term
    return total


def update_kernel(heights, *refs):
    first_ref, second_refs = refs[0], refs[1 : 1 + heights]
    own_ref, stress_ref, resistance_ref, weights_ref, table_ref = refs[1 + heights : -2]
    stress_out_ref, nodal_ref = refs[-2:]
    elements = stress_ref.shape[2]
    rows, second_rows = first_ref.shape[0], second_refs[0].shape[0]
    gathered = [
        first_ref[:, 0:elements] + second_refs[1][0:rows, 0:elements],
        sum(ref[ref.shape[0] - second_rows :, 0:elements] for ref in second_refs),
    ]
    counted = 9 * CHUNKS[1][1]
    counts = gathered[1][counted : counted + 1]
    per_brick = 1.0 / (8.0 * jnp.maximum(counts, 1.0))
    frames = [
        jnp.concatenate(
            [
                sums[count * k : count * (k + 1)]
                for sums, (first, count) in zip(gathered, CHUNKS)
            ],
            axis=0,
        )
        * per_brick
        for k in range(9)
    ]

    node = lax.broadcasted_iota(jnp.int32, (COLUMNS, elements), 0)
    element = lax.broadcasted_iota(jnp.int32, (COLUMNS, elements), 1)
    base = element + element // GX
    selectors = [
        (node == base + (step_y * (GX + 1) + step_x)).astype(jnp.bfloat16)
        for step_x in range(2)
        for step_y in range(2)
    ]
    corner = lax.broadcasted_iota(jnp.int32, (24, 1), 0) & 7
    upper_corner = (corner & 1) == 1
    height = lax.axis_index("fe") // 2
    above = height + (lax.axis_index("fe") & 1)
    upper = jnp.zeros((3, COLUMNS), jnp.float32)
    for flip, ref in enumerate(second_refs):
        wanted = (height ^ flip) == above
        upper = upper + jnp.where(wanted, ref[ref.shape[0] - 3 :, :], 0.0)
    values = jnp.where(
        upper_corner,
        jnp.concatenate(
            [jnp.broadcast_to(upper[c : c + 1], (8, COLUMNS)) for c in range(3)], axis=0
        ),
        jnp.concatenate([jnp.broadcast_to(own_ref[c], (8, COLUMNS)) for c in range(3)], axis=0),
    )
    corners = jnp.zeros((24, elements), jnp.float32)
    for step in range(4):
        part = jnp.where(corner >> 1 == step, values, 0.0)
        corners = corners + dot_selected(part, selectors[step], 0)
    gradients = []
    for c in range(3):
        product = jnp.dot(
            table_ref[...],
            corners[8 * c : 8 * c + 8],
            precision=lax.Precision.HIGHEST,
            preferred_element_type=jnp.float32,
        )
        gradients.append([product[8 * d : 8 * d + 8] for d in range(3)])
    strain = [
        gradients[0][0],
        gradients[1][1],
        gradients[2][2],
        0.5 * (gradients[1][2] + gradients[2][1]),
        0.5 * (gradients[0][2] + gradients[2][0]),
        0.5 * (gradients[0][1] + gradients[1][0]),
    ]
    volume = strain[0] + strain[1] + strain[2]
    trial = []
    for component in range(6):
        change = 2.0 * SHEAR_MODULUS * strain[component]
        if component < 3:
            change = change + LAMBDA_ELASTIC * volume
        trial.append(stress_ref[component] + change)
    correction = [jnp.zeros_like(trial[0]) for component in range(6)]
    for system in range(12):
        rotated_dir = [
            sum(
                frames[3 * row + axis_id] * SLIP_DIRECTIONS[system][axis_id]
                for axis_id in range(3)
                if SLIP_DIRECTIONS[system][axis_id] != 0.0
            )
            for row in range(3)
        ]
        rotated_normal = [
            sum(frames[3 * row + axis_id] * SLIP_PLANES[system][axis_id] for axis_id in range(3))
            for row in range(3)
        ]
        schmid = [
            rotated_dir[0] * rotated_normal[0],
            rotated_dir[1] * rotated_normal[1],
            rotated_dir[2] * rotated_normal[2],
            0.5 * (rotated_dir[1] * rotated_normal[2] + rotated_dir[2] * rotated_normal[1]),
            0.5 * (rotated_dir[0] * rotated_normal[2] + rotated_dir[2] * rotated_normal[0]),
            0.5 * (rotated_dir[0] * rotated_normal[1] + rotated_dir[1] * rotated_normal[0]),
        ]
        resolved = (
            trial[0] * schmid[0]
            + trial[1] * schmid[1]
            + trial[2] * schmid[2]
            + 2.0 * (trial[3] * schmid[3] + trial[4] * schmid[4] + trial[5] * schmid[5])
        )
        slip_ratio = resolved / resistance_ref[system]
        slip_step = RATE_STEP * slip_ratio * jnp.abs(slip_ratio)
        correction = [
            correction[component] + slip_step * schmid[component] for component in range(6)
        ]
    updated = [
        trial[component] - 2.0 * SHEAR_MODULUS * correction[component] for component in range(6)
    ]
    for component in range(6):
        stress_out_ref[component] = updated[component]
    point_scale = weights_ref[...].astype(jnp.float32) * (1.0 / (FIXED_POINT * 8.0))
    scaled = [value * point_scale for value in updated]
    forces = []
    for rows in [(0, 5, 4), (5, 1, 3), (4, 3, 2)]:
        forces.append(
            lax.dot_general(
                table_ref[...],
                jnp.concatenate([scaled[row] for row in rows], axis=0),
                (((0,), (0,)), ((), ())),
                precision=lax.Precision.HIGHEST,
                preferred_element_type=jnp.float32,
            )
        )
    forces = jnp.concatenate(forces, axis=0)
    nodal = jnp.zeros((24, COLUMNS), jnp.float32)
    for step in range(4):
        part = jnp.where(corner >> 1 == step, forces, 0.0)
        nodal = nodal + dot_selected(part, selectors[step], 1)
    lower = jnp.where(upper_corner, 0.0, nodal)
    above = jnp.where(upper_corner, nodal, 0.0)
    for c in range(3):
        nodal_ref[0, c] = jnp.sum(lower[8 * c : 8 * c + 8], axis=0, keepdims=True)
        nodal_ref[1, c] = jnp.sum(above[8 * c : 8 * c + 8], axis=0, keepdims=True)


def element_update(first, second, own, stress_old, resistance, quad_weights):
    grad_table = shape_gradients()
    table = jnp.asarray(
        [
            [grad_table[quadrature][corner][direction] for corner in range(8)]
            for direction in range(3)
            for quadrature in range(8)
        ],
        dtype=jnp.float32,
    )
    return pl.pallas_call(
        functools.partial(update_kernel, len(second)),
        out_shape=(
            jax.ShapeDtypeStruct(stress_old.shape, jnp.float32),
            jax.ShapeDtypeStruct((2,) + own.shape, jnp.float32),
        ),
        compiler_params=pltpu.CompilerParams(vmem_limit_bytes=8 * 1024 * 1024),
        name="stress_update",
    )(first, *second, own, stress_old, resistance, quad_weights, table)


def body(
    grain_ids,
    euler_angles,
    brick_active,
    brick_owner,
    brick_element,
    displacement,
    stress_old,
    resistance,
    quad_weights,
):
    half = lax.axis_size("ca") * lax.axis_size("fe") // 2
    bricks = grain_ids.shape[1]
    owner = lax.optimization_barrier(brick_owner.reshape(bricks))
    labels = jnp.where(brick_active > 0, owner * COLUMNS + brick_element, -1).reshape(1, bricks)
    per_octant = grain_ids.shape[0] // 8
    table = rotation_table(euler_angles)
    labels, send, split, ids = cell_sums(CHUNKS[0], per_octant, grain_ids, labels, table, half)
    keep, labels = brick_sums(split, labels, half)
    core_a, labels, own = core_sum(
        keep, across_cores(send), [labels, displacement], "core_sum_a"
    )
    send, keep = cell_sums(CHUNKS[1], per_octant, ids, labels, table, half)
    flip = lax.axis_size("fe") // 4
    (kept, sent), own, send = plane_sum(
        across_plane(core_a), [own, send], [flip, flip], "plane_sum_a"
    )
    received = to_relative(sent, 0, 0, 0, flip)
    core_b = last_core_sum(keep, across_cores(send), own)
    while flip > 2:
        flip //= 2
        (kept, sent) = plane_sum([kept, received], [], [flip, flip], "height_sum_a")[0]
        received = to_relative(sent, 0, 0, 0, flip)
    first, *second = last_sum(kept, received, across_plane(core_b), 3)
    stress_new, nodal = element_update(
        first, across_height(second), displacement, stress_old, resistance, quad_weights
    )
    forces = nodal[0] + passed_along(nodal[1], "fe", 1)
    return (stress_new, forces)


def solution(mesh):
    placed = (
        P(None, ("ca", "fe")),
        P(),
        P(("ca", "fe")),
        P(("ca", "fe"), None),
        P(("ca", "fe")),
        P(None, ("ca", "fe"), None),
        P(None, None, ("ca", "fe")),
        P(None, None, ("ca", "fe")),
        P(None, ("ca", "fe")),
    )
    return jax.shard_map(
        body,
        mesh=mesh,
        in_specs=placed,
        out_specs=(P(None, None, ("ca", "fe")), P(None, ("ca", "fe"), None)),
        check_vma=False,
    )
```

```python
import functools
import functools
import math

import jax
import jax.numpy as jnp
from jax import lax
from jax.experimental import pallas as pl
from jax.experimental.pallas import tpu as pltpu
from jax.sharding import PartitionSpec as P

GX = 15
LANES = 128
COLUMNS = 256
CHUNKS = ((0, 4), (4, 4))
QUANTUM = float((1 << 15) - 1)

SLIP_PLANES = [
    [value / math.sqrt(3.0) for value in row]
    for row in [[1, 1, 1]] * 3 + [[-1, 1, 1]] * 3 + [[1, -1, 1]] * 3 + [[1, 1, -1]] * 3
]
SLIP_DIRECTIONS = [
    [value / math.sqrt(2.0) for value in row]
    for row in [
        [0, 1, -1],
        [1, 0, -1],
        [1, -1, 0],
        [0, 1, -1],
        [1, 0, 1],
        [1, 1, 0],
        [0, 1, 1],
        [1, 0, -1],
        [1, 1, 0],
        [0, 1, 1],
        [1, 0, 1],
        [1, -1, 0],
    ]
]
LAMBDA_ELASTIC = 1.5
SHEAR_MODULUS = 1.0
RATE_STEP = 0.1
FIXED_POINT = 65536.0


def passed_along(block, axis, distance):
    devices = range(lax.axis_size(axis))
    route = [(i - distance, i) for i in devices if i - distance in devices]
    return lax.ppermute(block, axis, route)


def shape_gradients():
    grad_table = [[[0.0, 0.0, 0.0] for corner in range(8)] for quadrature in range(8)]
    point_offset = 1.0 / math.sqrt(3.0)
    for quadrature in range(8):
        natural = [
            (2 * (quadrature >> shift_bits & 1) - 1) * point_offset for shift_bits in (2, 1, 0)
        ]
        for corner in range(8):
            sign_list = [2 * (corner >> shift_bits & 1) - 1 for shift_bits in (2, 1, 0)]
            factors = [1.0 + sign_list[axis_id] * natural[axis_id] for axis_id in range(3)]
            for direction in range(3):
                others = 1.0
                for axis_id in range(3):
                    if axis_id != direction:
                        others = others * factors[axis_id]
                grad_table[quadrature][corner][direction] = (
                    2.0 * sign_list[direction] * others / 8.0
                )
    return grad_table


def cos_sin(angle):
    square = angle * angle
    cosine = 1.0 / math.factorial(12)
    for power in (10, 8, 6, 4, 2, 0):
        cosine = cosine * square + (-1.0) ** (power // 2) / math.factorial(power)
    sine = 1.0 / math.factorial(13)
    for power in (11, 9, 7, 5, 3, 1):
        sine = sine * square + (-1.0) ** (power // 2) / math.factorial(power)
    return cosine, sine * angle


def rotation_coordinates(euler):
    cos_one, sin_one = cos_sin(0.5 * euler[0 : 0 + 1])
    cos_mid, sin_mid = cos_sin(0.5 * euler[1 : 1 + 1])
    cos_two, sin_two = cos_sin(0.5 * euler[2 : 2 + 1])
    w = cos_mid * (cos_one * cos_two - sin_one * sin_two)
    factor = jnp.where(w < 0.0, -QUANTUM, QUANTUM) / (1.0 + jnp.abs(w))
    x = sin_mid * (cos_one * cos_two + sin_one * sin_two) * factor
    y = sin_mid * (sin_one * cos_two - cos_one * sin_two) * factor
    z = cos_mid * (sin_one * cos_two + cos_one * sin_two) * factor
    x, y, z = [
        jnp.clip(jnp.round(value), -QUANTUM, QUANTUM).astype(jnp.int32) for value in (x, y, z)
    ]
    return [x, y, z]


def table_kernel(euler_ref, table_ref):
    at = 0
    for coordinate in rotation_coordinates(euler_ref[...]):
        for row in range(0, coordinate.shape[1] // LANES, 2):
            low = coordinate[:, row * LANES : (row + 1) * LANES]
            high = coordinate[:, (row + 1) * LANES : (row + 2) * LANES]
            table_ref[at] = jnp.broadcast_to(lax.shift_left(high, 16) | (low & 0xFFFF), (8, LANES))
            at += 1


def rotation_table(euler_angles):
    height = euler_angles.shape[1] // LANES * 3 // 2
    return pl.pallas_call(
        table_kernel,
        out_shape=jax.ShapeDtypeStruct((height, 8, LANES), jnp.int32),
        compiler_params=pltpu.CompilerParams(vmem_limit_bytes=8 * 1024 * 1024),
        cost_estimate=pl.CostEstimate(flops=10**6, bytes_accessed=10**7, transcendentals=0),
        name="rotation_table",
    )(euler_angles)


def looked_up(table_ref, first_row, rows, lane, bits):
    if rows == 1:
        return lax.gather(
            table_ref[first_row],
            lane,
            lax.GatherDimensionNumbers(
                offset_dims=(),
                collapsed_slice_dims=(1,),
                start_index_map=(1,),
                operand_batching_dims=(0,),
                start_indices_batching_dims=(0,),
            ),
            slice_sizes=(1, 1),
            mode=lax.GatherScatterMode.PROMISE_IN_BOUNDS,
        )
    half = rows // 2
    level = half.bit_length() - 1
    low = looked_up(table_ref, first_row, half, lane, bits)
    high = looked_up(table_ref, first_row + half, half, lane, bits)
    return jnp.where(bits[level], high, low)


def looked_up_words(table_ref, ids):
    lane = (ids & (LANES - 1))[:, :, None]
    row = lax.shift_right_logical(ids, 7)
    words = table_ref.shape[0] // 3
    bits = [(row & (2 << level)) != 0 for level in range(words.bit_length() - 1)]
    shift = lax.shift_left((row & 1) ^ 1, 4)
    return [
        lax.shift_left(looked_up(table_ref, words * axis, words, lane, bits), shift)
        for axis in range(3)
    ]


def rotation_products(words):
    x, y, z = [lax.shift_right_arithmetic(word, 16).astype(jnp.float32) for word in words]
    length = (x * x + y * y + z * z) * (0.5 / (QUANTUM * QUANTUM)) + 0.5
    scale = pl.reciprocal(length, approx=True)
    scale = scale * (2.0 - length * scale)
    w = scale - 1.0
    x, y, z = x * scale, y * scale, z * scale
    return [x * x, y * y, z * z, x * y, x * z, y * z, w * x, w * y, w * z]


ENTRIES = (
    ((1, -1.0), (2, -1.0)),
    ((3, 1.0), (8, -1.0)),
    ((4, 1.0), (7, 1.0)),
    ((3, 1.0), (8, 1.0)),
    ((0, -1.0), (2, -1.0)),
    ((5, 1.0), (6, -1.0)),
    ((4, 1.0), (7, -1.0)),
    ((5, 1.0), (6, 1.0)),
    ((0, -1.0), (1, -1.0)),
)


def remainder(value, divisor):
    return value - value // divisor * divisor


def cell_sum_kernel(
    octants,
    per_octant,
    part,
    ids_ref,
    label_ref,
    table_ref,
    *refs,
):
    first, count = octants
    start = ids_ref.shape[0] - (8 - first) * per_octant
    tile_ref, raw_ref, place_ref, masked_ref = refs[-4:]
    if first + count < 8:
        label_out_ref, send_ref, split_ref, rest_ref = refs[:-4]
        label_out_ref[...] = label_ref[...]
        rest_ref[...] = ids_ref[pl.ds(ids_ref.shape[0] - rest_ref.shape[0], rest_ref.shape[0]), :]
        targets = [(send_ref.shape[0], send_ref, None)]
    elif part == 0:
        send_ref, keep_ref, split_ref = refs[:-4]
        targets = [(send_ref.shape[0], send_ref, None), (0, keep_ref, None)]
    else:
        sent_ref, kept_ref, send_ref, keep_ref, split_ref = refs[:-4]
        targets = [(send_ref.shape[0], send_ref, sent_ref), (0, keep_ref, kept_ref)]
    groups = tile_ref.shape[1] // 8
    rows_left = count * per_octant - 8 * (groups - 1)
    turns = count // math.gcd(count, 8)
    rows = send_ref.shape[1]
    width = masked_ref.shape[1]
    pairs = ids_ref.shape[1] // width
    begin, end = (0, pairs) if part is None else (part * pairs // 2, (part + 1) * pairs // 2)

    out_row = lax.broadcasted_iota(jnp.int32, (rows, raw_ref.shape[0]), 0)
    raw_row = lax.broadcasted_iota(jnp.int32, (rows, raw_ref.shape[0]), 1)
    entry, product = out_row // count, raw_row // (8 * turns)
    fold = jnp.zeros(out_row.shape, jnp.float32)
    for index, terms in enumerate(ENTRIES):
        for other, sign in terms:
            fold = jnp.where((entry == index) & (product == other), sign, fold)
    fold = jnp.where(remainder(out_row, count) == remainder(raw_row, count), fold, 0.0)
    fold = fold.astype(jnp.bfloat16)
    row = lax.broadcasted_iota(jnp.int32, (rows, width), 0)
    diagonal = (row // count == 0) | (row // count == 4) | (row // count == 8)
    constant = jnp.where(diagonal, float(per_octant), jnp.where(row < 9 * count, 0.0, 1.0))

    def lanes_of(pair):
        if isinstance(pair, int):
            return pl.ds(pair * width, width)
        return pl.ds(pl.multiple_of(pair * width, width), width)

    def look_up(pair):
        for tile in range(width // LANES):
            lanes = pl.ds(pl.multiple_of(pair * width + tile * LANES, LANES), LANES)
            for octant in range(count):
                tile_ref[tile, pl.ds(octant, per_octant, stride=count), :] = ids_ref[
                    pl.ds(start + octant * per_octant, per_octant), lanes
                ]
            sums = [[jnp.zeros((8, LANES), jnp.float32)] * 9 for turn in range(turns)]
            found = None
            for group in range(groups + 1):
                last = found
                if group < groups:
                    ids = tile_ref[tile, pl.ds(8 * group, 8), :]
                    found = looked_up_words(table_ref, ids)
                if group == 0:
                    continue
                products = rotation_products(last)
                if group == groups and rows_left < 8:
                    there = lax.broadcasted_iota(jnp.int32, (8, LANES), 0) < rows_left
                    products = [jnp.where(there, value, 0.0) for value in products]
                turn = (group - 1) % turns
                sums[turn] = [total + value for total, value in zip(sums[turn], products)]
            scales = [2.0 / (QUANTUM * QUANTUM)] * 6 + [2.0 / QUANTUM] * 3
            raw_ref[:, lanes] = jnp.concatenate(
                [sums[turn][index] * scales[index] for index in range(9) for turn in range(turns)],
                axis=0,
            )

    def fold_entries(pair):
        lanes = lanes_of(pair)
        total = constant
        for part in three_parts(raw_ref[:, lanes]):
            total = total + jnp.dot(fold, part, preferred_element_type=jnp.float32)
        leading = total.astype(jnp.bfloat16).astype(jnp.float32)
        split_ref[:, lanes] = jnp.concatenate([leading, total - leading], axis=0).astype(
            jnp.bfloat16
        )

    def add_bricks(pair, counted):
        lanes = lanes_of(pair)
        column = lax.broadcasted_iota(jnp.int32, (COLUMNS, width), 0)
        chosen = (column == label_ref[:, lanes] & (COLUMNS - 1)).astype(jnp.bfloat16)
        place = jnp.where(counted, place_ref[:, lanes], -1)
        for base, out_ref, earlier_ref in targets:
            add_places(split_ref, lanes, place - base, chosen, out_ref, masked_ref)

    place_ref[...] = relative_places(label_ref[...])
    for base, out_ref, earlier_ref in targets:
        if earlier_ref is None:
            out_ref[...] = jnp.zeros(out_ref.shape, jnp.float32)
        else:
            out_ref[...] = earlier_ref[...]
    raw_ref[:, lanes_of(begin)] = jnp.zeros((raw_ref.shape[0], width), jnp.float32)
    split_ref[:, lanes_of(begin)] = jnp.zeros((split_ref.shape[0], width), jnp.bfloat16)

    def step(pair, carry):
        add_bricks(jnp.maximum(pair - 2, begin), pair >= begin + 2)
        fold_entries(jnp.maximum(pair - 1, begin))
        look_up(pair)
        return carry

    lax.fori_loop(begin, end, step, 0, unroll=2)
    add_bricks(end - 2, True)
    fold_entries(end - 1)
    add_bricks(end - 1, True)


def relative_places(labels):
    place = place_of(lax.shift_right_arithmetic(labels, COLUMNS.bit_length() - 1))
    return jnp.where(labels < 0, -1, place)


def add_places(split_ref, lanes, place, chosen, out_ref, masked_ref):
    split_rows = split_ref.shape[0]
    half_rows = split_rows // 2
    members = masked_ref.shape[0] // split_rows
    for first in range(0, out_ref.shape[0], members):
        split = split_ref[:, lanes]
        for member in range(members):
            mask = (place == first + member).astype(jnp.bfloat16)
            masked_ref[pl.ds(member * split_rows, split_rows), :] = split * mask
        product = lax.dot_general(
            masked_ref[...],
            chosen,
            (((1,), (1,)), ((), ())),
            preferred_element_type=jnp.float32,
        )
        for member in range(members):
            at = member * split_rows
            out_ref[first + member] += (
                product[at : at + half_rows] + product[at + half_rows : at + split_rows]
            )


def across_cores(block):
    groups = lax.axis_size("ca")
    return lax.ppermute(block, "ca", [(i, i ^ 1) for i in range(groups)])


def brick_sum_kernel(split_ref, label_ref, out_ref, label_out_ref, place_ref, masked_ref):
    labels = label_ref[...]
    label_out_ref[...] = labels
    place_ref[...] = relative_places(labels)
    bricks = split_ref.shape[1]
    column = lax.broadcasted_iota(jnp.int32, (COLUMNS, bricks), 0)
    chosen = (column == labels & (COLUMNS - 1)).astype(jnp.bfloat16)
    split_rows = split_ref.shape[0]
    half_rows = split_rows // 2
    members = masked_ref.shape[0] // split_rows

    def place_group(step, carry):
        for member in range(members):
            mask = (place_ref[...] == step * members + member).astype(jnp.bfloat16)
            masked_ref[pl.ds(member * split_rows, split_rows), :] = split_ref[...] * mask
        product = lax.dot_general(
            masked_ref[...],
            chosen,
            (((1,), (1,)), ((), ())),
            preferred_element_type=jnp.float32,
        )
        for member in range(members):
            at = member * split_rows
            out_ref[step * members + member] = (
                product[at : at + half_rows] + product[at + half_rows : at + split_rows]
            )
        return carry

    lax.fori_loop(0, out_ref.shape[0] // members, place_group, 0)


def place_of(owner):
    groups, members = lax.axis_size("ca"), lax.axis_size("fe")
    owner_ca = lax.shift_right_logical(owner, members.bit_length() - 1) ^ lax.axis_index("ca")
    owner_fe = (owner & (members - 1)) ^ lax.axis_index("fe")
    place = (owner_ca & 1) * (groups // 2) + lax.shift_right_logical(owner_ca, 1)
    place = place * 2 + (owner_fe & 1)
    return place * (members // 2) + lax.shift_right_logical(owner_fe, 1)


def cell_sums(octants, per_octant, part, ids, labels, table, places, earlier=()):
    first, count = octants
    bricks = ids.shape[1]
    rows = padded_rows(count)
    half = jax.ShapeDtypeStruct((places, rows, COLUMNS), jnp.float32)
    split = jax.ShapeDtypeStruct((2 * rows, bricks), jnp.bfloat16)
    scratch = []
    left = 8 - first - count
    if left:
        out_shape = [
            jax.ShapeDtypeStruct(labels.shape, jnp.int32),
            half,
            split,
            jax.ShapeDtypeStruct((-(-left * per_octant // 8) * 8, bricks), jnp.int32),
        ]
    else:
        out_shape = [half, half]
        scratch.append(pltpu.VMEM(split.shape, split.dtype))
    return pl.pallas_call(
        functools.partial(cell_sum_kernel, octants, per_octant, part),
        out_shape=out_shape,
        scratch_shapes=scratch
        + [
            pltpu.VMEM((2, -(-count * per_octant // 8) * 8, LANES), jnp.int32),
            pltpu.VMEM((72 * (count // math.gcd(count, 8)), bricks), jnp.float32),
        ]
        + brick_scratch(rows, bricks, places, 2 * LANES),
        compiler_params=pltpu.CompilerParams(vmem_limit_bytes=28 * 1024 * 1024),
        cost_estimate=pl.CostEstimate(
            flops=count * 4 * 10**9, bytes_accessed=count * 10**7, transcendentals=0
        ),
        name="cell_sums",
    )(ids, labels, table, *earlier)


def padded_rows(count):
    return -(-9 * count // 8) * 8


def brick_scratch(rows, bricks, places, width):
    return [
        pltpu.VMEM((1, bricks), jnp.int32),
        pltpu.VMEM((min(16, places) * 2 * rows, width), jnp.bfloat16),
    ]


def brick_sums(split, labels, places):
    rows, bricks = split.shape
    return pl.pallas_call(
        brick_sum_kernel,
        out_shape=[
            jax.ShapeDtypeStruct((places, rows // 2, COLUMNS), jnp.float32),
            jax.ShapeDtypeStruct(labels.shape, jnp.int32),
        ],
        scratch_shapes=brick_scratch(rows // 2, bricks, places, bricks),
        compiler_params=pltpu.CompilerParams(vmem_limit_bytes=24 * 1024 * 1024),
        cost_estimate=pl.CostEstimate(
            flops=rows * 15 * 10**6, bytes_accessed=rows * 5 * 10**4, transcendentals=0
        ),
        name="brick_sums",
    )(split, labels)


def core_sum_kernel(passed, kept_ref, received_ref, *refs):
    outs = refs[passed:]
    for index, out_ref in enumerate(outs[: len(outs) - passed]):
        out_ref[...] = kept_ref[index] + received_ref[index]
    for i in range(passed):
        outs[len(outs) - passed + i][...] = refs[i][...]


def last_core_sum_kernel(kept_ref, received_ref, own_ref, *outs):
    for index, out_ref in enumerate(outs):
        out_ref[...] = kept_ref[index] + received_ref[index]
        for c in range(3):
            row = out_ref.shape[1] - 3 + c
            out_ref[:, row : row + 1, :] = jnp.broadcast_to(
                own_ref[c][None], (out_ref.shape[0], 1, COLUMNS)
            )


def last_core_sum(kept, received, own):
    pairs, rests = lax.axis_size("ca") // 2, lax.axis_size("fe") // 2
    shape = (2 * pairs, rests) + kept.shape[1:]
    return pl.pallas_call(
        last_core_sum_kernel,
        out_shape=[jax.ShapeDtypeStruct(shape[1:], jnp.float32)] * shape[0],
        compiler_params=pltpu.CompilerParams(vmem_limit_bytes=16 * 1024 * 1024),
        name="core_sum_b",
    )(kept.reshape(shape), received.reshape(shape), own)


def core_sum(kept, received, passed, name):
    pairs, rests = lax.axis_size("ca") // 2, lax.axis_size("fe") // 2
    shape = (2 * pairs, rests) + kept.shape[1:]
    out = pl.pallas_call(
        functools.partial(core_sum_kernel, len(passed)),
        out_shape=[jax.ShapeDtypeStruct(shape[1:], jnp.float32)] * shape[0]
        + [jax.ShapeDtypeStruct(array.shape, array.dtype) for array in passed],
        compiler_params=pltpu.CompilerParams(vmem_limit_bytes=16 * 1024 * 1024),
        name=name,
    )(kept.reshape(shape), received.reshape(shape), *passed)
    return out[: shape[0]], *out[shape[0] :]


def plane_sum_kernel(sources, passed, *refs):
    outs = refs[sources + passed :]
    height = 0
    for out_ref in outs[: len(outs) - passed]:
        out_ref[...] = sum(ref[pl.ds(height, out_ref.shape[0])] for ref in refs[:sources])
        height += out_ref.shape[0]
    for i in range(passed):
        outs[len(outs) - passed + i][...] = refs[sources + i][...]


def plane_sum(parts, passed, cuts, name):
    rest = parts[0].shape[1:]
    out = pl.pallas_call(
        functools.partial(plane_sum_kernel, len(parts), len(passed)),
        out_shape=[jax.ShapeDtypeStruct((cut,) + rest, jnp.float32) for cut in cuts]
        + [jax.ShapeDtypeStruct(array.shape, array.dtype) for array in passed],
        compiler_params=pltpu.CompilerParams(vmem_limit_bytes=16 * 1024 * 1024),
        name=name,
    )(*parts, *passed)
    return out[: len(cuts)], *out[len(cuts) :]


def last_sum_kernel(sources, spare, next_ref, *refs):
    parts, outs = refs[:sources], refs[sources:]
    outs[1][0 : next_ref.shape[1], :] = next_ref[0]
    for height, out_ref in enumerate(outs):
        first = out_ref.shape[0] - parts[0].shape[1]
        out_ref[first:, :] = sum(ref[height] for ref in parts)
        out_ref[out_ref.shape[0] - spare :, :] = parts[-1][height, -spare:, :]


def last_sum(next_height, parts, spare):
    heights, rows, columns = parts[0].shape
    part = jax.ShapeDtypeStruct((rows, columns), jnp.float32)
    both = jax.ShapeDtypeStruct((next_height.shape[1] + rows, columns), jnp.float32)
    return pl.pallas_call(
        functools.partial(last_sum_kernel, len(parts), spare),
        out_shape=[part, both] + [part] * (heights - 2),
        compiler_params=pltpu.CompilerParams(vmem_limit_bytes=16 * 1024 * 1024),
        name="last_sum",
    )(next_height, *parts)


def to_relative(block, core, pair, last, rest):
    groups, members = lax.axis_size("ca"), lax.axis_size("fe")
    flip = (2 * pair + core) * members + 2 * rest + last
    return lax.ppermute(block, ("ca", "fe"), [(i, i ^ flip) for i in range(groups * members)])


def across_plane(parts):
    return [parts[0]] + [
        to_relative(parts[index], 0, index // 2, index % 2, 0)
        for index in range(len(parts) - 1, 0, -1)
    ]


def across_height(parts):
    return [parts[0]] + [to_relative(parts[rest], 0, 0, 0, rest) for rest in range(1, len(parts))]


def three_parts(value):
    first = value.astype(jnp.bfloat16)
    rest = value - first.astype(jnp.float32)
    second = rest.astype(jnp.bfloat16)
    third = (rest - second.astype(jnp.float32)).astype(jnp.bfloat16)
    return first, second, third


def dot_selected(value, selector, contract):
    total = None
    for part in three_parts(value):
        term = lax.dot_general(
            part, selector, (((1,), (contract,)), ((), ())), preferred_element_type=jnp.float32
        )
        total = term if total is None else total + term
    return total


def update_kernel(heights, *refs):
    first_ref, second_refs = refs[0], refs[1 : 1 + heights]
    own_ref, stress_ref, resistance_ref, weights_ref, table_ref = refs[1 + heights : -2]
    stress_out_ref, nodal_ref = refs[-2:]
    elements = stress_ref.shape[2]
    rows, second_rows = first_ref.shape[1], second_refs[0].shape[0]
    gathered = [
        first_ref[0, :, 0:elements] + second_refs[1][0:rows, 0:elements],
        sum(ref[ref.shape[0] - second_rows :, 0:elements] for ref in second_refs),
    ]
    counted = 9 * CHUNKS[1][1]
    counts = gathered[1][counted : counted + 1]
    per_brick = 1.0 / (8.0 * jnp.maximum(counts, 1.0))
    frames = [
        jnp.concatenate(
            [
                sums[count * k : count * (k + 1)]
                for sums, (first, count) in zip(gathered, CHUNKS)
            ],
            axis=0,
        )
        * per_brick
        for k in range(9)
    ]

    node = lax.broadcasted_iota(jnp.int32, (COLUMNS, elements), 0)
    element = lax.broadcasted_iota(jnp.int32, (COLUMNS, elements), 1)
    base = element + element // GX
    selectors = [
        (node == base + (step_y * (GX + 1) + step_x)).astype(jnp.bfloat16)
        for step_x in range(2)
        for step_y in range(2)
    ]
    corner = lax.broadcasted_iota(jnp.int32, (24, 1), 0) & 7
    upper_corner = (corner & 1) == 1
    height = lax.axis_index("fe") // 2
    above = height + (lax.axis_index("fe") & 1)
    upper = jnp.zeros((3, COLUMNS), jnp.float32)
    for flip, ref in enumerate(second_refs):
        wanted = (height ^ flip) == above
        upper = upper + jnp.where(wanted, ref[ref.shape[0] - 3 :, :], 0.0)
    values = jnp.where(
        upper_corner,
        jnp.concatenate(
            [jnp.broadcast_to(upper[c : c + 1], (8, COLUMNS)) for c in range(3)], axis=0
        ),
        jnp.concatenate([jnp.broadcast_to(own_ref[c], (8, COLUMNS)) for c in range(3)], axis=0),
    )
    corners = jnp.zeros((24, elements), jnp.float32)
    for step in range(4):
        part = jnp.where(corner >> 1 == step, values, 0.0)
        corners = corners + dot_selected(part, selectors[step], 0)
    gradients = []
    for c in range(3):
        product = jnp.dot(
            table_ref[...],
            corners[8 * c : 8 * c + 8],
            precision=lax.Precision.HIGHEST,
            preferred_element_type=jnp.float32,
        )
        gradients.append([product[8 * d : 8 * d + 8] for d in range(3)])
    strain = [
        gradients[0][0],
        gradients[1][1],
        gradients[2][2],
        0.5 * (gradients[1][2] + gradients[2][1]),
        0.5 * (gradients[0][2] + gradients[2][0]),
        0.5 * (gradients[0][1] + gradients[1][0]),
    ]
    volume = strain[0] + strain[1] + strain[2]
    trial = []
    for component in range(6):
        change = 2.0 * SHEAR_MODULUS * strain[component]
        if component < 3:
            change = change + LAMBDA_ELASTIC * volume
        trial.append(stress_ref[component] + change)
    correction = [jnp.zeros_like(trial[0]) for component in range(6)]
    for system in range(12):
        rotated_dir = [
            sum(
                frames[3 * row + axis_id] * SLIP_DIRECTIONS[system][axis_id]
                for axis_id in range(3)
                if SLIP_DIRECTIONS[system][axis_id] != 0.0
            )
            for row in range(3)
        ]
        rotated_normal = [
            sum(frames[3 * row + axis_id] * SLIP_PLANES[system][axis_id] for axis_id in range(3))
            for row in range(3)
        ]
        schmid = [
            rotated_dir[0] * rotated_normal[0],
            rotated_dir[1] * rotated_normal[1],
            rotated_dir[2] * rotated_normal[2],
            0.5 * (rotated_dir[1] * rotated_normal[2] + rotated_dir[2] * rotated_normal[1]),
            0.5 * (rotated_dir[0] * rotated_normal[2] + rotated_dir[2] * rotated_normal[0]),
            0.5 * (rotated_dir[0] * rotated_normal[1] + rotated_dir[1] * rotated_normal[0]),
        ]
        resolved = (
            trial[0] * schmid[0]
            + trial[1] * schmid[1]
            + trial[2] * schmid[2]
            + 2.0 * (trial[3] * schmid[3] + trial[4] * schmid[4] + trial[5] * schmid[5])
        )
        slip_ratio = resolved / resistance_ref[system]
        slip_step = RATE_STEP * slip_ratio * jnp.abs(slip_ratio)
        correction = [
            correction[component] + slip_step * schmid[component] for component in range(6)
        ]
    updated = [
        trial[component] - 2.0 * SHEAR_MODULUS * correction[component] for component in range(6)
    ]
    for component in range(6):
        stress_out_ref[component] = updated[component]
    point_scale = weights_ref[...].astype(jnp.float32) * (1.0 / (FIXED_POINT * 8.0))
    scaled = [value * point_scale for value in updated]
    forces = []
    for rows in [(0, 5, 4), (5, 1, 3), (4, 3, 2)]:
        forces.append(
            lax.dot_general(
                table_ref[...],
                jnp.concatenate([scaled[row] for row in rows], axis=0),
                (((0,), (0,)), ((), ())),
                precision=lax.Precision.HIGHEST,
                preferred_element_type=jnp.float32,
            )
        )
    forces = jnp.concatenate(forces, axis=0)
    nodal = jnp.zeros((24, COLUMNS), jnp.float32)
    for step in range(4):
        part = jnp.where(corner >> 1 == step, forces, 0.0)
        nodal = nodal + dot_selected(part, selectors[step], 1)
    lower = jnp.where(upper_corner, 0.0, nodal)
    above = jnp.where(upper_corner, nodal, 0.0)
    for c in range(3):
        nodal_ref[0, c] = jnp.sum(lower[8 * c : 8 * c + 8], axis=0, keepdims=True)
        nodal_ref[1, c] = jnp.sum(above[8 * c : 8 * c + 8], axis=0, keepdims=True)


def element_update(first, second, own, stress_old, resistance, quad_weights):
    grad_table = shape_gradients()
    table = jnp.asarray(
        [
            [grad_table[quadrature][corner][direction] for corner in range(8)]
            for direction in range(3)
            for quadrature in range(8)
        ],
        dtype=jnp.float32,
    )
    return pl.pallas_call(
        functools.partial(update_kernel, len(second)),
        out_shape=(
            jax.ShapeDtypeStruct(stress_old.shape, jnp.float32),
            jax.ShapeDtypeStruct((2,) + own.shape, jnp.float32),
        ),
        compiler_params=pltpu.CompilerParams(vmem_limit_bytes=8 * 1024 * 1024),
        name="stress_update",
    )(first, *second, own, stress_old, resistance, quad_weights, table)


def body(
    grain_ids,
    euler_angles,
    brick_active,
    brick_owner,
    brick_element,
    displacement,
    stress_old,
    resistance,
    quad_weights,
):
    half = lax.axis_size("ca") * lax.axis_size("fe") // 2
    bricks = grain_ids.shape[1]
    owner = lax.optimization_barrier(brick_owner.reshape(bricks))
    labels = jnp.where(brick_active > 0, owner * COLUMNS + brick_element, -1).reshape(1, bricks)
    per_octant = grain_ids.shape[0] // 8
    table = rotation_table(euler_angles)
    labels, send, split, ids = cell_sums(
        CHUNKS[0], per_octant, None, grain_ids, labels, table, half
    )
    keep, labels = brick_sums(split, labels, half)
    core_a, labels, own = core_sum(
        keep, across_cores(send), [labels, displacement], "core_sum_a"
    )
    send, keep = cell_sums(CHUNKS[1], per_octant, 0, ids, labels, table, half)
    flip = lax.axis_size("fe") // 4
    (kept, sent), own, send = plane_sum(
        across_plane(core_a), [own, send], [flip, flip], "plane_sum_a"
    )
    received = to_relative(sent, 0, 0, 0, flip)
    send, keep = cell_sums(CHUNKS[1], per_octant, 1, ids, labels, table, half, (send, keep))
    while flip > 1:
        flip //= 2
        (kept, sent), send = plane_sum([kept, received], [send], [flip, flip], "height_sum_a")
        if flip > 1:
            received = to_relative(sent, 0, 0, 0, flip)
    core_b = last_core_sum(keep, across_cores(send), own)
    second = last_sum(sent, across_plane(core_b), 3)
    stress_new, nodal = element_update(
        kept, across_height(second), displacement, stress_old, resistance, quad_weights
    )
    forces = nodal[0] + passed_along(nodal[1], "fe", 1)
    return (stress_new, forces)


def solution(mesh):
    placed = (
        P(None, ("ca", "fe")),
        P(),
        P(("ca", "fe")),
        P(("ca", "fe"), None),
        P(("ca", "fe")),
        P(None, ("ca", "fe"), None),
        P(None, None, ("ca", "fe")),
        P(None, None, ("ca", "fe")),
        P(None, ("ca", "fe")),
    )
    return jax.shard_map(
        body,
        mesh=mesh,
        in_specs=placed,
        out_specs=(P(None, None, ("ca", "fe")), P(None, ("ca", "fe"), None)),
        check_vma=False,
    )
```

```python
import functools
import functools
import math

import jax
import jax.numpy as jnp
from jax import lax
from jax.experimental import pallas as pl
from jax.experimental.pallas import tpu as pltpu
from jax.sharding import PartitionSpec as P

GX = 15
LANES = 128
COLUMNS = 256
CHUNKS = ((0, 5), (5, 3))
QUANTUM = float((1 << 15) - 1)

SLIP_PLANES = [
    [value / math.sqrt(3.0) for value in row]
    for row in [[1, 1, 1]] * 3 + [[-1, 1, 1]] * 3 + [[1, -1, 1]] * 3 + [[1, 1, -1]] * 3
]
SLIP_DIRECTIONS = [
    [value / math.sqrt(2.0) for value in row]
    for row in [
        [0, 1, -1],
        [1, 0, -1],
        [1, -1, 0],
        [0, 1, -1],
        [1, 0, 1],
        [1, 1, 0],
        [0, 1, 1],
        [1, 0, -1],
        [1, 1, 0],
        [0, 1, 1],
        [1, 0, 1],
        [1, -1, 0],
    ]
]
LAMBDA_ELASTIC = 1.5
SHEAR_MODULUS = 1.0
RATE_STEP = 0.1
FIXED_POINT = 65536.0


def passed_along(block, axis, distance):
    devices = range(lax.axis_size(axis))
    route = [(i - distance, i) for i in devices if i - distance in devices]
    return lax.ppermute(block, axis, route)


def shape_gradients():
    grad_table = [[[0.0, 0.0, 0.0] for corner in range(8)] for quadrature in range(8)]
    point_offset = 1.0 / math.sqrt(3.0)
    for quadrature in range(8):
        natural = [
            (2 * (quadrature >> shift_bits & 1) - 1) * point_offset for shift_bits in (2, 1, 0)
        ]
        for corner in range(8):
            sign_list = [2 * (corner >> shift_bits & 1) - 1 for shift_bits in (2, 1, 0)]
            factors = [1.0 + sign_list[axis_id] * natural[axis_id] for axis_id in range(3)]
            for direction in range(3):
                others = 1.0
                for axis_id in range(3):
                    if axis_id != direction:
                        others = others * factors[axis_id]
                grad_table[quadrature][corner][direction] = (
                    2.0 * sign_list[direction] * others / 8.0
                )
    return grad_table


def cos_sin(angle):
    square = angle * angle
    cosine = 1.0 / math.factorial(12)
    for power in (10, 8, 6, 4, 2, 0):
        cosine = cosine * square + (-1.0) ** (power // 2) / math.factorial(power)
    sine = 1.0 / math.factorial(13)
    for power in (11, 9, 7, 5, 3, 1):
        sine = sine * square + (-1.0) ** (power // 2) / math.factorial(power)
    return cosine, sine * angle


def rotation_coordinates(euler):
    cos_one, sin_one = cos_sin(0.5 * euler[0 : 0 + 1])
    cos_mid, sin_mid = cos_sin(0.5 * euler[1 : 1 + 1])
    cos_two, sin_two = cos_sin(0.5 * euler[2 : 2 + 1])
    w = cos_mid * (cos_one * cos_two - sin_one * sin_two)
    factor = jnp.where(w < 0.0, -QUANTUM, QUANTUM) / (1.0 + jnp.abs(w))
    x = sin_mid * (cos_one * cos_two + sin_one * sin_two) * factor
    y = sin_mid * (sin_one * cos_two - cos_one * sin_two) * factor
    z = cos_mid * (sin_one * cos_two + cos_one * sin_two) * factor
    x, y, z = [
        jnp.clip(jnp.round(value), -QUANTUM, QUANTUM).astype(jnp.int32) for value in (x, y, z)
    ]
    return [x, y, z]


def table_kernel(euler_ref, table_ref):
    at = 0
    for coordinate in rotation_coordinates(euler_ref[...]):
        for row in range(0, coordinate.shape[1] // LANES, 2):
            low = coordinate[:, row * LANES : (row + 1) * LANES]
            high = coordinate[:, (row + 1) * LANES : (row + 2) * LANES]
            table_ref[at] = jnp.broadcast_to(lax.shift_left(high, 16) | (low & 0xFFFF), (8, LANES))
            at += 1


def rotation_table(euler_angles):
    height = euler_angles.shape[1] // LANES * 3 // 2
    return pl.pallas_call(
        table_kernel,
        out_shape=jax.ShapeDtypeStruct((height, 8, LANES), jnp.int32),
        compiler_params=pltpu.CompilerParams(vmem_limit_bytes=8 * 1024 * 1024),
        cost_estimate=pl.CostEstimate(flops=10**6, bytes_accessed=10**7, transcendentals=0),
        name="rotation_table",
    )(euler_angles)


def looked_up(table_ref, first_row, rows, lane, bits):
    if rows == 1:
        return lax.gather(
            table_ref[first_row],
            lane,
            lax.GatherDimensionNumbers(
                offset_dims=(),
                collapsed_slice_dims=(1,),
                start_index_map=(1,),
                operand_batching_dims=(0,),
                start_indices_batching_dims=(0,),
            ),
            slice_sizes=(1, 1),
            mode=lax.GatherScatterMode.PROMISE_IN_BOUNDS,
        )
    half = rows // 2
    level = half.bit_length() - 1
    low = looked_up(table_ref, first_row, half, lane, bits)
    high = looked_up(table_ref, first_row + half, half, lane, bits)
    return jnp.where(bits[level], high, low)


def looked_up_words(table_ref, ids):
    lane = (ids & (LANES - 1))[:, :, None]
    row = lax.shift_right_logical(ids, 7)
    words = table_ref.shape[0] // 3
    bits = [(row & (2 << level)) != 0 for level in range(words.bit_length() - 1)]
    shift = lax.shift_left((row & 1) ^ 1, 4)
    return [
        lax.shift_left(looked_up(table_ref, words * axis, words, lane, bits), shift)
        for axis in range(3)
    ]


def rotation_products(words):
    x, y, z = [lax.shift_right_arithmetic(word, 16).astype(jnp.float32) for word in words]
    length = (x * x + y * y + z * z) * (0.5 / (QUANTUM * QUANTUM)) + 0.5
    scale = pl.reciprocal(length, approx=True)
    scale = scale * (2.0 - length * scale)
    w = scale - 1.0
    x, y, z = x * scale, y * scale, z * scale
    return [x * x, y * y, z * z, x * y, x * z, y * z, w * x, w * y, w * z]


ENTRIES = (
    ((1, -1.0), (2, -1.0)),
    ((3, 1.0), (8, -1.0)),
    ((4, 1.0), (7, 1.0)),
    ((3, 1.0), (8, 1.0)),
    ((0, -1.0), (2, -1.0)),
    ((5, 1.0), (6, -1.0)),
    ((4, 1.0), (7, -1.0)),
    ((5, 1.0), (6, 1.0)),
    ((0, -1.0), (1, -1.0)),
)


def remainder(value, divisor):
    return value - value // divisor * divisor


def cell_sum_kernel(
    octants,
    per_octant,
    ids_ref,
    label_ref,
    table_ref,
    *refs,
):
    first, count = octants
    start = ids_ref.shape[0] - (8 - first) * per_octant
    tile_ref, raw_ref, place_ref, masked_ref = refs[-4:]
    if first + count < 8:
        label_out_ref, send_ref, split_ref, rest_ref = refs[:-4]
        label_out_ref[...] = label_ref[...]
        rest_ref[...] = ids_ref[pl.ds(ids_ref.shape[0] - rest_ref.shape[0], rest_ref.shape[0]), :]
        targets = [(send_ref.shape[0], send_ref)]
    else:
        send_ref, keep_ref, split_ref = refs[:-4]
        targets = [(send_ref.shape[0], send_ref), (0, keep_ref)]
    groups = tile_ref.shape[1] // 8
    rows_left = count * per_octant - 8 * (groups - 1)
    turns = count // math.gcd(count, 8)
    rows = send_ref.shape[1]
    width = masked_ref.shape[1]
    pairs = ids_ref.shape[1] // width

    out_row = lax.broadcasted_iota(jnp.int32, (rows, raw_ref.shape[0]), 0)
    raw_row = lax.broadcasted_iota(jnp.int32, (rows, raw_ref.shape[0]), 1)
    entry, product = out_row // count, raw_row // (8 * turns)
    fold = jnp.zeros(out_row.shape, jnp.float32)
    for index, terms in enumerate(ENTRIES):
        for other, sign in terms:
            fold = jnp.where((entry == index) & (product == other), sign, fold)
    fold = jnp.where(remainder(out_row, count) == remainder(raw_row, count), fold, 0.0)
    fold = fold.astype(jnp.bfloat16)
    row = lax.broadcasted_iota(jnp.int32, (rows, width), 0)
    diagonal = (row // count == 0) | (row // count == 4) | (row // count == 8)
    constant = jnp.where(diagonal, float(per_octant), jnp.where(row < 9 * count, 0.0, 1.0))

    def lanes_of(pair):
        return pl.ds(pl.multiple_of(pair * width, width), width)

    def look_up(pair):
        for tile in range(width // LANES):
            lanes = pl.ds(pl.multiple_of(pair * width + tile * LANES, LANES), LANES)
            for octant in range(count):
                tile_ref[tile, pl.ds(octant, per_octant, stride=count), :] = ids_ref[
                    pl.ds(start + octant * per_octant, per_octant), lanes
                ]
            sums = [[jnp.zeros((8, LANES), jnp.float32)] * 9 for turn in range(turns)]
            found = None
            for group in range(groups + 1):
                last = found
                if group < groups:
                    ids = tile_ref[tile, pl.ds(8 * group, 8), :]
                    found = looked_up_words(table_ref, ids)
                if group == 0:
                    continue
                products = rotation_products(last)
                if group == groups and rows_left < 8:
                    there = lax.broadcasted_iota(jnp.int32, (8, LANES), 0) < rows_left
                    products = [jnp.where(there, value, 0.0) for value in products]
                turn = (group - 1) % turns
                sums[turn] = [total + value for total, value in zip(sums[turn], products)]
            scales = [2.0 / (QUANTUM * QUANTUM)] * 6 + [2.0 / QUANTUM] * 3
            raw_ref[:, lanes] = jnp.concatenate(
                [sums[turn][index] * scales[index] for index in range(9) for turn in range(turns)],
                axis=0,
            )

    def fold_entries(pair):
        lanes = lanes_of(pair)
        total = constant
        for part in three_parts(raw_ref[:, lanes]):
            total = total + jnp.dot(fold, part, preferred_element_type=jnp.float32)
        leading = total.astype(jnp.bfloat16).astype(jnp.float32)
        split_ref[:, lanes] = jnp.concatenate([leading, total - leading], axis=0).astype(
            jnp.bfloat16
        )

    def add_bricks(pair, counted):
        lanes = lanes_of(pair)
        column = lax.broadcasted_iota(jnp.int32, (COLUMNS, width), 0)
        chosen = (column == label_ref[:, lanes] & (COLUMNS - 1)).astype(jnp.bfloat16)
        place = jnp.where(counted, place_ref[:, lanes], -1)
        for base, out_ref in targets:
            add_places(split_ref, lanes, place - base, chosen, out_ref, masked_ref)

    place_ref[...] = relative_places(label_ref[...])
    for base, out_ref in targets:
        out_ref[...] = jnp.zeros(out_ref.shape, jnp.float32)
    raw_ref[:, pl.ds(0, width)] = jnp.zeros((raw_ref.shape[0], width), jnp.float32)
    split_ref[:, pl.ds(0, width)] = jnp.zeros((split_ref.shape[0], width), jnp.bfloat16)

    def step(pair, carry):
        add_bricks(jnp.maximum(pair - 2, 0), pair >= 2)
        fold_entries(jnp.maximum(pair - 1, 0))
        look_up(pair)
        return carry

    lax.fori_loop(0, pairs, step, 0, unroll=2)
    add_bricks(pairs - 2, True)
    fold_entries(pairs - 1)
    add_bricks(pairs - 1, True)


def relative_places(labels):
    place = place_of(lax.shift_right_arithmetic(labels, COLUMNS.bit_length() - 1))
    return jnp.where(labels < 0, -1, place)


def add_places(split_ref, lanes, place, chosen, out_ref, masked_ref):
    split_rows = split_ref.shape[0]
    half_rows = split_rows // 2
    members = masked_ref.shape[0] // split_rows
    for first in range(0, out_ref.shape[0], members):
        split = split_ref[:, lanes]
        for member in range(members):
            mask = (place == first + member).astype(jnp.bfloat16)
            masked_ref[pl.ds(member * split_rows, split_rows), :] = split * mask
        product = lax.dot_general(
            masked_ref[...],
            chosen,
            (((1,), (1,)), ((), ())),
            preferred_element_type=jnp.float32,
        )
        for member in range(members):
            at = member * split_rows
            out_ref[first + member] += (
                product[at : at + half_rows] + product[at + half_rows : at + split_rows]
            )


def across_cores(block):
    groups = lax.axis_size("ca")
    return lax.ppermute(block, "ca", [(i, i ^ 1) for i in range(groups)])


def brick_sum_kernel(split_ref, label_ref, out_ref, label_out_ref, place_ref, masked_ref):
    labels = label_ref[...]
    label_out_ref[...] = labels
    place_ref[...] = relative_places(labels)
    bricks = split_ref.shape[1]
    column = lax.broadcasted_iota(jnp.int32, (COLUMNS, bricks), 0)
    chosen = (column == labels & (COLUMNS - 1)).astype(jnp.bfloat16)
    split_rows = split_ref.shape[0]
    half_rows = split_rows // 2
    members = masked_ref.shape[0] // split_rows

    def place_group(step, carry):
        for member in range(members):
            mask = (place_ref[...] == step * members + member).astype(jnp.bfloat16)
            masked_ref[pl.ds(member * split_rows, split_rows), :] = split_ref[...] * mask
        product = lax.dot_general(
            masked_ref[...],
            chosen,
            (((1,), (1,)), ((), ())),
            preferred_element_type=jnp.float32,
        )
        for member in range(members):
            at = member * split_rows
            out_ref[step * members + member] = (
                product[at : at + half_rows] + product[at + half_rows : at + split_rows]
            )
        return carry

    lax.fori_loop(0, out_ref.shape[0] // members, place_group, 0)


def place_of(owner):
    groups, members = lax.axis_size("ca"), lax.axis_size("fe")
    owner_ca = lax.shift_right_logical(owner, members.bit_length() - 1) ^ lax.axis_index("ca")
    owner_fe = (owner & (members - 1)) ^ lax.axis_index("fe")
    place = (owner_ca & 1) * (groups // 2) + lax.shift_right_logical(owner_ca, 1)
    place = place * 2 + (owner_fe & 1)
    return place * (members // 2) + lax.shift_right_logical(owner_fe, 1)


def cell_sums(octants, per_octant, ids, labels, table, places):
    first, count = octants
    bricks = ids.shape[1]
    rows = padded_rows(count)
    half = jax.ShapeDtypeStruct((places, rows, COLUMNS), jnp.float32)
    split = jax.ShapeDtypeStruct((2 * rows, bricks), jnp.bfloat16)
    scratch = []
    left = 8 - first - count
    if left:
        out_shape = [
            jax.ShapeDtypeStruct(labels.shape, jnp.int32),
            half,
            split,
            jax.ShapeDtypeStruct((-(-left * per_octant // 8) * 8, bricks), jnp.int32),
        ]
    else:
        out_shape = [half, half]
        scratch.append(pltpu.VMEM(split.shape, split.dtype))
    return pl.pallas_call(
        functools.partial(cell_sum_kernel, octants, per_octant),
        out_shape=out_shape,
        scratch_shapes=scratch
        + [
            pltpu.VMEM((2, -(-count * per_octant // 8) * 8, LANES), jnp.int32),
            pltpu.VMEM((72 * (count // math.gcd(count, 8)), bricks), jnp.float32),
        ]
        + brick_scratch(rows, bricks, places, 2 * LANES),
        compiler_params=pltpu.CompilerParams(vmem_limit_bytes=28 * 1024 * 1024),
        cost_estimate=pl.CostEstimate(
            flops=count * 4 * 10**9, bytes_accessed=count * 10**7, transcendentals=0
        ),
        name="cell_sums",
    )(ids, labels, table)


def padded_rows(count):
    return -(-9 * count // 8) * 8


def brick_scratch(rows, bricks, places, width):
    return [
        pltpu.VMEM((1, bricks), jnp.int32),
        pltpu.VMEM((min(16, places) * 2 * rows, width), jnp.bfloat16),
    ]


def brick_sums(split, labels, places):
    rows, bricks = split.shape
    return pl.pallas_call(
        brick_sum_kernel,
        out_shape=[
            jax.ShapeDtypeStruct((places, rows // 2, COLUMNS), jnp.float32),
            jax.ShapeDtypeStruct(labels.shape, jnp.int32),
        ],
        scratch_shapes=brick_scratch(rows // 2, bricks, places, bricks),
        compiler_params=pltpu.CompilerParams(vmem_limit_bytes=24 * 1024 * 1024),
        cost_estimate=pl.CostEstimate(
            flops=rows * 15 * 10**6, bytes_accessed=rows * 5 * 10**4, transcendentals=0
        ),
        name="brick_sums",
    )(split, labels)


def core_sum_kernel(passed, kept_ref, received_ref, *refs):
    outs = refs[passed:]
    for index, out_ref in enumerate(outs[: len(outs) - passed]):
        out_ref[...] = kept_ref[index] + received_ref[index]
    for i in range(passed):
        outs[len(outs) - passed + i][...] = refs[i][...]


def last_core_sum_kernel(kept_ref, received_ref, own_ref, *outs):
    for index, out_ref in enumerate(outs):
        out_ref[...] = kept_ref[index] + received_ref[index]
        for c in range(3):
            row = out_ref.shape[1] - 3 + c
            out_ref[:, row : row + 1, :] = jnp.broadcast_to(
                own_ref[c][None], (out_ref.shape[0], 1, COLUMNS)
            )


def last_core_sum(kept, received, own):
    pairs, rests = lax.axis_size("ca") // 2, lax.axis_size("fe") // 2
    shape = (2 * pairs, rests) + kept.shape[1:]
    return pl.pallas_call(
        last_core_sum_kernel,
        out_shape=[jax.ShapeDtypeStruct(shape[1:], jnp.float32)] * shape[0],
        compiler_params=pltpu.CompilerParams(vmem_limit_bytes=16 * 1024 * 1024),
        name="core_sum_b",
    )(kept.reshape(shape), received.reshape(shape), own)


def core_sum(kept, received, passed, name):
    pairs, rests = lax.axis_size("ca") // 2, lax.axis_size("fe") // 2
    shape = (2 * pairs, rests) + kept.shape[1:]
    out = pl.pallas_call(
        functools.partial(core_sum_kernel, len(passed)),
        out_shape=[jax.ShapeDtypeStruct(shape[1:], jnp.float32)] * shape[0]
        + [jax.ShapeDtypeStruct(array.shape, array.dtype) for array in passed],
        compiler_params=pltpu.CompilerParams(vmem_limit_bytes=16 * 1024 * 1024),
        name=name,
    )(kept.reshape(shape), received.reshape(shape), *passed)
    return out[: shape[0]], *out[shape[0] :]


def plane_sum_kernel(sources, passed, *refs):
    outs = refs[sources + passed :]
    height = 0
    for out_ref in outs[: len(outs) - passed]:
        out_ref[...] = sum(ref[pl.ds(height, out_ref.shape[0])] for ref in refs[:sources])
        height += out_ref.shape[0]
    for i in range(passed):
        outs[len(outs) - passed + i][...] = refs[sources + i][...]


def plane_sum(parts, passed, cuts, name):
    rest = parts[0].shape[1:]
    out = pl.pallas_call(
        functools.partial(plane_sum_kernel, len(parts), len(passed)),
        out_shape=[jax.ShapeDtypeStruct((cut,) + rest, jnp.float32) for cut in cuts]
        + [jax.ShapeDtypeStruct(array.shape, array.dtype) for array in passed],
        compiler_params=pltpu.CompilerParams(vmem_limit_bytes=16 * 1024 * 1024),
        name=name,
    )(*parts, *passed)
    return out[: len(cuts)], *out[len(cuts) :]


def last_sum_kernel(sources, spare, kept_ref, received_ref, *refs):
    parts, outs = refs[:sources], refs[sources:]
    rows = kept_ref.shape[1]
    outs[0][...] = kept_ref[0] + received_ref[0]
    outs[2][0:rows, :] = kept_ref[1] + received_ref[1]
    for height, out_ref in enumerate(outs[1:]):
        first = out_ref.shape[0] - parts[0].shape[1]
        out_ref[first:, :] = sum(ref[height] for ref in parts)
        out_ref[out_ref.shape[0] - spare :, :] = parts[-1][height, -spare:, :]


def last_sum(kept, received, parts, spare):
    heights, rows, columns = parts[0].shape
    part = jax.ShapeDtypeStruct((rows, columns), jnp.float32)
    both = jax.ShapeDtypeStruct((kept.shape[1] + rows, columns), jnp.float32)
    return pl.pallas_call(
        functools.partial(last_sum_kernel, len(parts), spare),
        out_shape=[jax.ShapeDtypeStruct(kept.shape[1:], jnp.float32), part, both]
        + [part] * (heights - 2),
        compiler_params=pltpu.CompilerParams(vmem_limit_bytes=16 * 1024 * 1024),
        name="last_sum",
    )(kept, received, *parts)


def to_relative(block, core, pair, last, rest):
    groups, members = lax.axis_size("ca"), lax.axis_size("fe")
    flip = (2 * pair + core) * members + 2 * rest + last
    return lax.ppermute(block, ("ca", "fe"), [(i, i ^ flip) for i in range(groups * members)])


def across_plane(parts):
    return [parts[0]] + [
        to_relative(parts[index], 0, index // 2, index % 2, 0)
        for index in range(len(parts) - 1, 0, -1)
    ]


def across_height(parts):
    return [parts[0]] + [to_relative(parts[rest], 0, 0, 0, rest) for rest in range(1, len(parts))]


def three_parts(value):
    first = value.astype(jnp.bfloat16)
    rest = value - first.astype(jnp.float32)
    second = rest.astype(jnp.bfloat16)
    third = (rest - second.astype(jnp.float32)).astype(jnp.bfloat16)
    return first, second, third


def dot_selected(value, selector, contract):
    total = None
    for part in three_parts(value):
        term = lax.dot_general(
            part, selector, (((1,), (contract,)), ((), ())), preferred_element_type=jnp.float32
        )
        total = term if total is None else total + term
    return total


def update_kernel(heights, *refs):
    first_ref, second_refs = refs[0], refs[1 : 1 + heights]
    own_ref, stress_ref, resistance_ref, weights_ref, table_ref = refs[1 + heights : -2]
    stress_out_ref, nodal_ref = refs[-2:]
    elements = stress_ref.shape[2]
    rows, second_rows = first_ref.shape[0], second_refs[0].shape[0]
    gathered = [
        first_ref[:, 0:elements] + second_refs[1][0:rows, 0:elements],
        sum(ref[ref.shape[0] - second_rows :, 0:elements] for ref in second_refs),
    ]
    counted = 9 * CHUNKS[1][1]
    counts = gathered[1][counted : counted + 1]
    per_brick = 1.0 / (8.0 * jnp.maximum(counts, 1.0))
    frames = [
        jnp.concatenate(
            [
                sums[count * k : count * (k + 1)]
                for sums, (first, count) in zip(gathered, CHUNKS)
            ],
            axis=0,
        )
        * per_brick
        for k in range(9)
    ]

    node = lax.broadcasted_iota(jnp.int32, (COLUMNS, elements), 0)
    element = lax.broadcasted_iota(jnp.int32, (COLUMNS, elements), 1)
    base = element + element // GX
    selectors = [
        (node == base + (step_y * (GX + 1) + step_x)).astype(jnp.bfloat16)
        for step_x in range(2)
        for step_y in range(2)
    ]
    corner = lax.broadcasted_iota(jnp.int32, (24, 1), 0) & 7
    upper_corner = (corner & 1) == 1
    height = lax.axis_index("fe") // 2
    above = height + (lax.axis_index("fe") & 1)
    upper = jnp.zeros((3, COLUMNS), jnp.float32)
    for flip, ref in enumerate(second_refs):
        wanted = (height ^ flip) == above
        upper = upper + jnp.where(wanted, ref[ref.shape[0] - 3 :, :], 0.0)
    values = jnp.where(
        upper_corner,
        jnp.concatenate(
            [jnp.broadcast_to(upper[c : c + 1], (8, COLUMNS)) for c in range(3)], axis=0
        ),
        jnp.concatenate([jnp.broadcast_to(own_ref[c], (8, COLUMNS)) for c in range(3)], axis=0),
    )
    corners = jnp.zeros((24, elements), jnp.float32)
    for step in range(4):
        part = jnp.where(corner >> 1 == step, values, 0.0)
        corners = corners + dot_selected(part, selectors[step], 0)
    gradients = []
    for c in range(3):
        product = jnp.dot(
            table_ref[...],
            corners[8 * c : 8 * c + 8],
            precision=lax.Precision.HIGHEST,
            preferred_element_type=jnp.float32,
        )
        gradients.append([product[8 * d : 8 * d + 8] for d in range(3)])
    strain = [
        gradients[0][0],
        gradients[1][1],
        gradients[2][2],
        0.5 * (gradients[1][2] + gradients[2][1]),
        0.5 * (gradients[0][2] + gradients[2][0]),
        0.5 * (gradients[0][1] + gradients[1][0]),
    ]
    volume = strain[0] + strain[1] + strain[2]
    trial = []
    for component in range(6):
        change = 2.0 * SHEAR_MODULUS * strain[component]
        if component < 3:
            change = change + LAMBDA_ELASTIC * volume
        trial.append(stress_ref[component] + change)
    correction = [jnp.zeros_like(trial[0]) for component in range(6)]
    for system in range(12):
        rotated_dir = [
            sum(
                frames[3 * row + axis_id] * SLIP_DIRECTIONS[system][axis_id]
                for axis_id in range(3)
                if SLIP_DIRECTIONS[system][axis_id] != 0.0
            )
            for row in range(3)
        ]
        rotated_normal = [
            sum(frames[3 * row + axis_id] * SLIP_PLANES[system][axis_id] for axis_id in range(3))
            for row in range(3)
        ]
        schmid = [
            rotated_dir[0] * rotated_normal[0],
            rotated_dir[1] * rotated_normal[1],
            rotated_dir[2] * rotated_normal[2],
            0.5 * (rotated_dir[1] * rotated_normal[2] + rotated_dir[2] * rotated_normal[1]),
            0.5 * (rotated_dir[0] * rotated_normal[2] + rotated_dir[2] * rotated_normal[0]),
            0.5 * (rotated_dir[0] * rotated_normal[1] + rotated_dir[1] * rotated_normal[0]),
        ]
        resolved = (
            trial[0] * schmid[0]
            + trial[1] * schmid[1]
            + trial[2] * schmid[2]
            + 2.0 * (trial[3] * schmid[3] + trial[4] * schmid[4] + trial[5] * schmid[5])
        )
        slip_ratio = resolved / resistance_ref[system]
        slip_step = RATE_STEP * slip_ratio * jnp.abs(slip_ratio)
        correction = [
            correction[component] + slip_step * schmid[component] for component in range(6)
        ]
    updated = [
        trial[component] - 2.0 * SHEAR_MODULUS * correction[component] for component in range(6)
    ]
    for component in range(6):
        stress_out_ref[component] = updated[component]
    point_scale = weights_ref[...].astype(jnp.float32) * (1.0 / (FIXED_POINT * 8.0))
    scaled = [value * point_scale for value in updated]
    forces = []
    for rows in [(0, 5, 4), (5, 1, 3), (4, 3, 2)]:
        forces.append(
            lax.dot_general(
                table_ref[...],
                jnp.concatenate([scaled[row] for row in rows], axis=0),
                (((0,), (0,)), ((), ())),
                precision=lax.Precision.HIGHEST,
                preferred_element_type=jnp.float32,
            )
        )
    forces = jnp.concatenate(forces, axis=0)
    nodal = jnp.zeros((24, COLUMNS), jnp.float32)
    for step in range(4):
        part = jnp.where(corner >> 1 == step, forces, 0.0)
        nodal = nodal + dot_selected(part, selectors[step], 1)
    lower = jnp.where(upper_corner, 0.0, nodal)
    above = jnp.where(upper_corner, nodal, 0.0)
    for c in range(3):
        nodal_ref[0, c] = jnp.sum(lower[8 * c : 8 * c + 8], axis=0, keepdims=True)
        nodal_ref[1, c] = jnp.sum(above[8 * c : 8 * c + 8], axis=0, keepdims=True)


def element_update(first, second, own, stress_old, resistance, quad_weights):
    grad_table = shape_gradients()
    table = jnp.asarray(
        [
            [grad_table[quadrature][corner][direction] for corner in range(8)]
            for direction in range(3)
            for quadrature in range(8)
        ],
        dtype=jnp.float32,
    )
    return pl.pallas_call(
        functools.partial(update_kernel, len(second)),
        out_shape=(
            jax.ShapeDtypeStruct(stress_old.shape, jnp.float32),
            jax.ShapeDtypeStruct((2,) + own.shape, jnp.float32),
        ),
        compiler_params=pltpu.CompilerParams(vmem_limit_bytes=8 * 1024 * 1024),
        name="stress_update",
    )(first, *second, own, stress_old, resistance, quad_weights, table)


def body(
    grain_ids,
    euler_angles,
    brick_active,
    brick_owner,
    brick_element,
    displacement,
    stress_old,
    resistance,
    quad_weights,
):
    half = lax.axis_size("ca") * lax.axis_size("fe") // 2
    bricks = grain_ids.shape[1]
    owner = lax.optimization_barrier(brick_owner.reshape(bricks))
    labels = jnp.where(brick_active > 0, owner * COLUMNS + brick_element, -1).reshape(1, bricks)
    per_octant = grain_ids.shape[0] // 8
    table = rotation_table(euler_angles)
    labels, send, split, ids = cell_sums(CHUNKS[0], per_octant, grain_ids, labels, table, half)
    keep, labels = brick_sums(split, labels, half)
    core_a, labels, own = core_sum(
        keep, across_cores(send), [labels, displacement], "core_sum_a"
    )
    send, keep = cell_sums(CHUNKS[1], per_octant, ids, labels, table, half)
    flip = lax.axis_size("fe") // 4
    (kept, sent), own, send = plane_sum(
        across_plane(core_a), [own, send], [flip, flip], "plane_sum_a"
    )
    received = to_relative(sent, 0, 0, 0, flip)
    core_b = last_core_sum(keep, across_cores(send), own)
    while flip > 2:
        flip //= 2
        (kept, sent) = plane_sum([kept, received], [], [flip, flip], "height_sum_a")[0]
        received = to_relative(sent, 0, 0, 0, flip)
    first, *second = last_sum(kept, received, across_plane(core_b), 3)
    stress_new, nodal = element_update(
        first, across_height(second), displacement, stress_old, resistance, quad_weights
    )
    forces = nodal[0] + passed_along(nodal[1], "fe", 1)
    return (stress_new, forces)


def solution(mesh):
    placed = (
        P(None, ("ca", "fe")),
        P(),
        P(("ca", "fe")),
        P(("ca", "fe"), None),
        P(("ca", "fe")),
        P(None, ("ca", "fe"), None),
        P(None, None, ("ca", "fe")),
        P(None, None, ("ca", "fe")),
        P(None, ("ca", "fe")),
    )
    return jax.shard_map(
        body,
        mesh=mesh,
        in_specs=placed,
        out_specs=(P(None, None, ("ca", "fe")), P(None, ("ca", "fe"), None)),
        check_vma=False,
    )
```

```python
import functools
import functools
import math

import jax
import jax.numpy as jnp
from jax import lax
from jax.experimental import pallas as pl
from jax.experimental.pallas import tpu as pltpu
from jax.sharding import PartitionSpec as P

GX = 15
LANES = 128
COLUMNS = 256
CHUNKS = ((0, 6), (6, 2))
QUANTUM = float((1 << 15) - 1)

SLIP_PLANES = [
    [value / math.sqrt(3.0) for value in row]
    for row in [[1, 1, 1]] * 3 + [[-1, 1, 1]] * 3 + [[1, -1, 1]] * 3 + [[1, 1, -1]] * 3
]
SLIP_DIRECTIONS = [
    [value / math.sqrt(2.0) for value in row]
    for row in [
        [0, 1, -1],
        [1, 0, -1],
        [1, -1, 0],
        [0, 1, -1],
        [1, 0, 1],
        [1, 1, 0],
        [0, 1, 1],
        [1, 0, -1],
        [1, 1, 0],
        [0, 1, 1],
        [1, 0, 1],
        [1, -1, 0],
    ]
]
LAMBDA_ELASTIC = 1.5
SHEAR_MODULUS = 1.0
RATE_STEP = 0.1
FIXED_POINT = 65536.0


def passed_along(block, axis, distance):
    devices = range(lax.axis_size(axis))
    route = [(i - distance, i) for i in devices if i - distance in devices]
    return lax.ppermute(block, axis, route)


def shape_gradients():
    grad_table = [[[0.0, 0.0, 0.0] for corner in range(8)] for quadrature in range(8)]
    point_offset = 1.0 / math.sqrt(3.0)
    for quadrature in range(8):
        natural = [
            (2 * (quadrature >> shift_bits & 1) - 1) * point_offset for shift_bits in (2, 1, 0)
        ]
        for corner in range(8):
            sign_list = [2 * (corner >> shift_bits & 1) - 1 for shift_bits in (2, 1, 0)]
            factors = [1.0 + sign_list[axis_id] * natural[axis_id] for axis_id in range(3)]
            for direction in range(3):
                others = 1.0
                for axis_id in range(3):
                    if axis_id != direction:
                        others = others * factors[axis_id]
                grad_table[quadrature][corner][direction] = (
                    2.0 * sign_list[direction] * others / 8.0
                )
    return grad_table


def cos_sin(angle):
    square = angle * angle
    cosine = 1.0 / math.factorial(12)
    for power in (10, 8, 6, 4, 2, 0):
        cosine = cosine * square + (-1.0) ** (power // 2) / math.factorial(power)
    sine = 1.0 / math.factorial(13)
    for power in (11, 9, 7, 5, 3, 1):
        sine = sine * square + (-1.0) ** (power // 2) / math.factorial(power)
    return cosine, sine * angle


def rotation_coordinates(euler):
    cos_one, sin_one = cos_sin(0.5 * euler[0 : 0 + 1])
    cos_mid, sin_mid = cos_sin(0.5 * euler[1 : 1 + 1])
    cos_two, sin_two = cos_sin(0.5 * euler[2 : 2 + 1])
    w = cos_mid * (cos_one * cos_two - sin_one * sin_two)
    factor = jnp.where(w < 0.0, -QUANTUM, QUANTUM) / (1.0 + jnp.abs(w))
    x = sin_mid * (cos_one * cos_two + sin_one * sin_two) * factor
    y = sin_mid * (sin_one * cos_two - cos_one * sin_two) * factor
    z = cos_mid * (sin_one * cos_two + cos_one * sin_two) * factor
    x, y, z = [
        jnp.clip(jnp.round(value), -QUANTUM, QUANTUM).astype(jnp.int32) for value in (x, y, z)
    ]
    return [x, y, z]


def table_kernel(euler_ref, table_ref):
    at = 0
    for coordinate in rotation_coordinates(euler_ref[...]):
        for row in range(0, coordinate.shape[1] // LANES, 2):
            low = coordinate[:, row * LANES : (row + 1) * LANES]
            high = coordinate[:, (row + 1) * LANES : (row + 2) * LANES]
            table_ref[at] = jnp.broadcast_to(lax.shift_left(high, 16) | (low & 0xFFFF), (8, LANES))
            at += 1


def rotation_table(euler_angles):
    height = euler_angles.shape[1] // LANES * 3 // 2
    return pl.pallas_call(
        table_kernel,
        out_shape=jax.ShapeDtypeStruct((height, 8, LANES), jnp.int32),
        compiler_params=pltpu.CompilerParams(vmem_limit_bytes=8 * 1024 * 1024),
        cost_estimate=pl.CostEstimate(flops=10**6, bytes_accessed=10**7, transcendentals=0),
        name="rotation_table",
    )(euler_angles)


def looked_up(table_ref, first_row, rows, lane, bits):
    if rows == 1:
        return lax.gather(
            table_ref[first_row],
            lane,
            lax.GatherDimensionNumbers(
                offset_dims=(),
                collapsed_slice_dims=(1,),
                start_index_map=(1,),
                operand_batching_dims=(0,),
                start_indices_batching_dims=(0,),
            ),
            slice_sizes=(1, 1),
            mode=lax.GatherScatterMode.PROMISE_IN_BOUNDS,
        )
    half = rows // 2
    level = half.bit_length() - 1
    low = looked_up(table_ref, first_row, half, lane, bits)
    high = looked_up(table_ref, first_row + half, half, lane, bits)
    return jnp.where(bits[level], high, low)


def looked_up_words(table_ref, ids):
    lane = (ids & (LANES - 1))[:, :, None]
    row = lax.shift_right_logical(ids, 7)
    words = table_ref.shape[0] // 3
    bits = [(row & (2 << level)) != 0 for level in range(words.bit_length() - 1)]
    shift = lax.shift_left((row & 1) ^ 1, 4)
    return [
        lax.shift_left(looked_up(table_ref, words * axis, words, lane, bits), shift)
        for axis in range(3)
    ]


def rotation_products(words):
    x, y, z = [lax.shift_right_arithmetic(word, 16).astype(jnp.float32) for word in words]
    length = (x * x + y * y + z * z) * (0.5 / (QUANTUM * QUANTUM)) + 0.5
    scale = pl.reciprocal(length, approx=True)
    scale = scale * (2.0 - length * scale)
    w = scale - 1.0
    x, y, z = x * scale, y * scale, z * scale
    return [x * x, y * y, z * z, x * y, x * z, y * z, w * x, w * y, w * z]


ENTRIES = (
    ((1, -1.0), (2, -1.0)),
    ((3, 1.0), (8, -1.0)),
    ((4, 1.0), (7, 1.0)),
    ((3, 1.0), (8, 1.0)),
    ((0, -1.0), (2, -1.0)),
    ((5, 1.0), (6, -1.0)),
    ((4, 1.0), (7, -1.0)),
    ((5, 1.0), (6, 1.0)),
    ((0, -1.0), (1, -1.0)),
)


def remainder(value, divisor):
    return value - value // divisor * divisor


def cell_sum_kernel(
    octants,
    per_octant,
    ids_ref,
    label_ref,
    table_ref,
    *refs,
):
    first, count = octants
    cells = ids_ref.shape[0] if label_ref is not None else ids_ref.shape[0] - 1
    start = cells - (8 - first) * per_octant
    if label_ref is None:
        label_ref = ids_ref.at[pl.ds(cells, 1), :]
    tile_ref, raw_ref, place_ref, masked_ref = refs[-4:]
    if first + count < 8:
        label_out_ref, send_ref, split_ref, rest_ref = refs[:-4]
        label_out_ref[...] = label_ref[...]
        rest_ref[...] = ids_ref[pl.ds(cells - rest_ref.shape[0], rest_ref.shape[0]), :]
        targets = [(send_ref.shape[0], send_ref)]
    else:
        send_ref, keep_ref, split_ref = refs[:-4]
        targets = [(send_ref.shape[0], send_ref), (0, keep_ref)]
    groups = tile_ref.shape[1] // 8
    rows_left = count * per_octant - 8 * (groups - 1)
    turns = count // math.gcd(count, 8)
    rows = send_ref.shape[1]
    width = masked_ref.shape[1]
    pairs = ids_ref.shape[1] // width

    out_row = lax.broadcasted_iota(jnp.int32, (rows, raw_ref.shape[0]), 0)
    raw_row = lax.broadcasted_iota(jnp.int32, (rows, raw_ref.shape[0]), 1)
    entry, product = out_row // count, raw_row // (8 * turns)
    fold = jnp.zeros(out_row.shape, jnp.float32)
    for index, terms in enumerate(ENTRIES):
        for other, sign in terms:
            fold = jnp.where((entry == index) & (product == other), sign, fold)
    fold = jnp.where(remainder(out_row, count) == remainder(raw_row, count), fold, 0.0)
    fold = fold.astype(jnp.bfloat16)
    row = lax.broadcasted_iota(jnp.int32, (rows, width), 0)
    diagonal = (row // count == 0) | (row // count == 4) | (row // count == 8)
    constant = jnp.where(diagonal, float(per_octant), jnp.where(row < 9 * count, 0.0, 1.0))

    def lanes_of(pair):
        return pl.ds(pl.multiple_of(pair * width, width), width)

    def look_up(pair):
        for tile in range(width // LANES):
            lanes = pl.ds(pl.multiple_of(pair * width + tile * LANES, LANES), LANES)
            for octant in range(count):
                tile_ref[tile, pl.ds(octant, per_octant, stride=count), :] = ids_ref[
                    pl.ds(start + octant * per_octant, per_octant), lanes
                ]
            sums = [[jnp.zeros((8, LANES), jnp.float32)] * 9 for turn in range(turns)]
            found = None
            for group in range(groups + 1):
                last = found
                if group < groups:
                    ids = tile_ref[tile, pl.ds(8 * group, 8), :]
                    found = looked_up_words(table_ref, ids)
                if group == 0:
                    continue
                products = rotation_products(last)
                if group == groups and rows_left < 8:
                    there = lax.broadcasted_iota(jnp.int32, (8, LANES), 0) < rows_left
                    products = [jnp.where(there, value, 0.0) for value in products]
                turn = (group - 1) % turns
                sums[turn] = [total + value for total, value in zip(sums[turn], products)]
            scales = [2.0 / (QUANTUM * QUANTUM)] * 6 + [2.0 / QUANTUM] * 3
            raw_ref[:, lanes] = jnp.concatenate(
                [sums[turn][index] * scales[index] for index in range(9) for turn in range(turns)],
                axis=0,
            )

    def fold_entries(pair):
        lanes = lanes_of(pair)
        total = constant
        for part in three_parts(raw_ref[:, lanes]):
            total = total + jnp.dot(fold, part, preferred_element_type=jnp.float32)
        leading = total.astype(jnp.bfloat16).astype(jnp.float32)
        split_ref[:, lanes] = jnp.concatenate([leading, total - leading], axis=0).astype(
            jnp.bfloat16
        )

    def add_bricks(pair, counted):
        lanes = lanes_of(pair)
        column = lax.broadcasted_iota(jnp.int32, (COLUMNS, width), 0)
        chosen = (column == label_ref[:, lanes] & (COLUMNS - 1)).astype(jnp.bfloat16)
        place = jnp.where(counted, place_ref[:, lanes], -1)
        for base, out_ref in targets:
            add_places(split_ref, lanes, place - base, chosen, out_ref, masked_ref)

    place_ref[...] = relative_places(label_ref[...])
    for base, out_ref in targets:
        out_ref[...] = jnp.zeros(out_ref.shape, jnp.float32)
    raw_ref[:, pl.ds(0, width)] = jnp.zeros((raw_ref.shape[0], width), jnp.float32)

    def step(pair, carry):
        fold_entries(jnp.maximum(pair - 1, 0))
        add_bricks(jnp.maximum(pair - 1, 0), pair >= 1)
        look_up(pair)
        return carry

    lax.fori_loop(0, pairs, step, 0, unroll=2)
    fold_entries(pairs - 1)
    add_bricks(pairs - 1, True)


def relative_places(labels):
    place = place_of(lax.shift_right_arithmetic(labels, COLUMNS.bit_length() - 1))
    return jnp.where(labels < 0, -1, place)


def add_places(split_ref, lanes, place, chosen, out_ref, masked_ref):
    split_rows = split_ref.shape[0]
    half_rows = split_rows // 2
    members = masked_ref.shape[0] // split_rows
    for first in range(0, out_ref.shape[0], members):
        split = split_ref[:, lanes]
        for member in range(members):
            mask = (place == first + member).astype(jnp.bfloat16)
            masked_ref[pl.ds(member * split_rows, split_rows), :] = split * mask
        product = lax.dot_general(
            masked_ref[...],
            chosen,
            (((1,), (1,)), ((), ())),
            preferred_element_type=jnp.float32,
        )
        for member in range(members):
            at = member * split_rows
            out_ref[first + member] += (
                product[at : at + half_rows] + product[at + half_rows : at + split_rows]
            )


def across_cores(block):
    groups = lax.axis_size("ca")
    return lax.ppermute(block, "ca", [(i, i ^ 1) for i in range(groups)])


def brick_sum_kernel(split_ref, label_ref, out_ref, label_out_ref, place_ref, masked_ref):
    labels = label_ref[...]
    label_out_ref[...] = labels
    place_ref[...] = relative_places(labels)
    bricks = split_ref.shape[1]
    column = lax.broadcasted_iota(jnp.int32, (COLUMNS, bricks), 0)
    chosen = (column == labels & (COLUMNS - 1)).astype(jnp.bfloat16)
    split_rows = split_ref.shape[0]
    half_rows = split_rows // 2
    members = masked_ref.shape[0] // split_rows

    def place_group(step, carry):
        for member in range(members):
            mask = (place_ref[...] == step * members + member).astype(jnp.bfloat16)
            masked_ref[pl.ds(member * split_rows, split_rows), :] = split_ref[...] * mask
        product = lax.dot_general(
            masked_ref[...],
            chosen,
            (((1,), (1,)), ((), ())),
            preferred_element_type=jnp.float32,
        )
        for member in range(members):
            at = member * split_rows
            out_ref[step * members + member] = (
                product[at : at + half_rows] + product[at + half_rows : at + split_rows]
            )
        return carry

    lax.fori_loop(0, out_ref.shape[0] // members, place_group, 0)


def place_of(owner):
    groups, members = lax.axis_size("ca"), lax.axis_size("fe")
    owner_ca = lax.shift_right_logical(owner, members.bit_length() - 1) ^ lax.axis_index("ca")
    owner_fe = (owner & (members - 1)) ^ lax.axis_index("fe")
    place = (owner_ca & 1) * (groups // 2) + lax.shift_right_logical(owner_ca, 1)
    place = place * 2 + (owner_fe & 1)
    return place * (members // 2) + lax.shift_right_logical(owner_fe, 1)


def cell_sums(octants, per_octant, ids, labels, table, places):
    first, count = octants
    bricks = ids.shape[1]
    rows = padded_rows(count)
    half = jax.ShapeDtypeStruct((places, rows, COLUMNS), jnp.float32)
    split = jax.ShapeDtypeStruct((2 * rows, bricks), jnp.bfloat16)
    scratch = []
    left = 8 - first - count
    if left:
        out_shape = [
            jax.ShapeDtypeStruct((1, bricks), jnp.int32),
            half,
            split,
            jax.ShapeDtypeStruct((-(-left * per_octant // 8) * 8, bricks), jnp.int32),
        ]
    else:
        out_shape = [half, half]
        scratch.append(pltpu.VMEM(split.shape, split.dtype))
    kernel = functools.partial(cell_sum_kernel, octants, per_octant)
    inputs = (ids, labels, table)
    if labels is None:
        kernel = lambda ids_ref, *refs: cell_sum_kernel(octants, per_octant, ids_ref, None, *refs)
        inputs = (ids, table)
    return pl.pallas_call(
        kernel,
        out_shape=out_shape,
        scratch_shapes=scratch
        + [
            pltpu.VMEM((2, -(-count * per_octant // 8) * 8, LANES), jnp.int32),
            pltpu.VMEM((72 * (count // math.gcd(count, 8)), bricks), jnp.float32),
        ]
        + brick_scratch(rows, bricks, places, 2 * LANES),
        compiler_params=pltpu.CompilerParams(vmem_limit_bytes=28 * 1024 * 1024),
        cost_estimate=pl.CostEstimate(
            flops=count * 4 * 10**9, bytes_accessed=count * 10**7, transcendentals=0
        ),
        name="cell_sums",
    )(*inputs)


def padded_rows(count):
    return -(-9 * count // 8) * 8


def brick_scratch(rows, bricks, places, width):
    return [
        pltpu.VMEM((1, bricks), jnp.int32),
        pltpu.VMEM((min(16, places) * 2 * rows, width), jnp.bfloat16),
    ]


def brick_sums(split, labels, places):
    rows, bricks = split.shape
    return pl.pallas_call(
        brick_sum_kernel,
        out_shape=[
            jax.ShapeDtypeStruct((places, rows // 2, COLUMNS), jnp.float32),
            jax.ShapeDtypeStruct(labels.shape, jnp.int32),
        ],
        scratch_shapes=brick_scratch(rows // 2, bricks, places, bricks),
        compiler_params=pltpu.CompilerParams(vmem_limit_bytes=24 * 1024 * 1024),
        cost_estimate=pl.CostEstimate(
            flops=rows * 15 * 10**6, bytes_accessed=rows * 5 * 10**4, transcendentals=0
        ),
        name="brick_sums",
    )(split, labels)


def core_sum_kernel(passed, kept_ref, received_ref, *refs):
    outs = refs[passed:]
    for index, out_ref in enumerate(outs[: len(outs) - passed]):
        out_ref[...] = kept_ref[index] + received_ref[index]
    for i in range(passed):
        outs[len(outs) - passed + i][...] = refs[i][...]


def last_core_sum_kernel(kept_ref, received_ref, own_ref, *outs):
    for index, out_ref in enumerate(outs):
        out_ref[...] = kept_ref[index] + received_ref[index]
        for c in range(3):
            row = out_ref.shape[1] - 3 + c
            out_ref[:, row : row + 1, :] = jnp.broadcast_to(
                own_ref[c][None], (out_ref.shape[0], 1, COLUMNS)
            )


def last_core_sum(kept, received, own):
    pairs, rests = lax.axis_size("ca") // 2, lax.axis_size("fe") // 2
    shape = (2 * pairs, rests) + kept.shape[1:]
    return pl.pallas_call(
        last_core_sum_kernel,
        out_shape=[jax.ShapeDtypeStruct(shape[1:], jnp.float32)] * shape[0],
        compiler_params=pltpu.CompilerParams(vmem_limit_bytes=16 * 1024 * 1024),
        name="core_sum_b",
    )(kept.reshape(shape), received.reshape(shape), own)


def core_sum(kept, received, passed, name):
    pairs, rests = lax.axis_size("ca") // 2, lax.axis_size("fe") // 2
    shape = (2 * pairs, rests) + kept.shape[1:]
    out = pl.pallas_call(
        functools.partial(core_sum_kernel, len(passed)),
        out_shape=[jax.ShapeDtypeStruct(shape[1:], jnp.float32)] * shape[0]
        + [jax.ShapeDtypeStruct(array.shape, array.dtype) for array in passed],
        compiler_params=pltpu.CompilerParams(vmem_limit_bytes=16 * 1024 * 1024),
        name=name,
    )(kept.reshape(shape), received.reshape(shape), *passed)
    return out[: shape[0]], *out[shape[0] :]


def plane_sum_kernel(sources, passed, *refs):
    outs = refs[sources + passed :]
    height = 0
    for out_ref in outs[: len(outs) - passed]:
        out_ref[...] = sum(ref[pl.ds(height, out_ref.shape[0])] for ref in refs[:sources])
        height += out_ref.shape[0]
    for i in range(passed):
        outs[len(outs) - passed + i][...] = refs[sources + i][...]


def plane_sum(parts, passed, cuts, name):
    rest = parts[0].shape[1:]
    out = pl.pallas_call(
        functools.partial(plane_sum_kernel, len(parts), len(passed)),
        out_shape=[jax.ShapeDtypeStruct((cut,) + rest, jnp.float32) for cut in cuts]
        + [jax.ShapeDtypeStruct(array.shape, array.dtype) for array in passed],
        compiler_params=pltpu.CompilerParams(vmem_limit_bytes=16 * 1024 * 1024),
        name=name,
    )(*parts, *passed)
    return out[: len(cuts)], *out[len(cuts) :]


def last_sum_kernel(sources, spare, kept_ref, received_ref, *refs):
    parts, outs = refs[:sources], refs[sources:]
    rows = kept_ref.shape[1]
    outs[0][...] = kept_ref[0] + received_ref[0]
    outs[2][0:rows, :] = kept_ref[1] + received_ref[1]
    for height, out_ref in enumerate(outs[1:]):
        first = out_ref.shape[0] - parts[0].shape[1]
        out_ref[first:, :] = sum(ref[height] for ref in parts)
        out_ref[out_ref.shape[0] - spare :, :] = parts[-1][height, -spare:, :]


def last_sum(kept, received, parts, spare):
    heights, rows, columns = parts[0].shape
    part = jax.ShapeDtypeStruct((rows, columns), jnp.float32)
    both = jax.ShapeDtypeStruct((kept.shape[1] + rows, columns), jnp.float32)
    return pl.pallas_call(
        functools.partial(last_sum_kernel, len(parts), spare),
        out_shape=[jax.ShapeDtypeStruct(kept.shape[1:], jnp.float32), part, both]
        + [part] * (heights - 2),
        compiler_params=pltpu.CompilerParams(vmem_limit_bytes=16 * 1024 * 1024),
        name="last_sum",
    )(kept, received, *parts)


def to_relative(block, core, pair, last, rest):
    groups, members = lax.axis_size("ca"), lax.axis_size("fe")
    flip = (2 * pair + core) * members + 2 * rest + last
    return lax.ppermute(block, ("ca", "fe"), [(i, i ^ flip) for i in range(groups * members)])


def across_plane(parts):
    return [parts[0]] + [
        to_relative(parts[index], 0, index // 2, index % 2, 0)
        for index in range(len(parts) - 1, 0, -1)
    ]


def across_height(parts):
    return [parts[0]] + [to_relative(parts[rest], 0, 0, 0, rest) for rest in range(1, len(parts))]


def three_parts(value):
    first = value.astype(jnp.bfloat16)
    rest = value - first.astype(jnp.float32)
    second = rest.astype(jnp.bfloat16)
    third = (rest - second.astype(jnp.float32)).astype(jnp.bfloat16)
    return first, second, third


def dot_selected(value, selector, contract):
    total = None
    for part in three_parts(value):
        term = lax.dot_general(
            part, selector, (((1,), (contract,)), ((), ())), preferred_element_type=jnp.float32
        )
        total = term if total is None else total + term
    return total


def update_kernel(heights, *refs):
    first_ref, second_refs = refs[0], refs[1 : 1 + heights]
    own_ref, stress_ref, resistance_ref, weights_ref, table_ref = refs[1 + heights : -2]
    stress_out_ref, nodal_ref = refs[-2:]
    elements = stress_ref.shape[2]
    rows, second_rows = first_ref.shape[0], second_refs[0].shape[0]
    gathered = [
        first_ref[:, 0:elements] + second_refs[1][0:rows, 0:elements],
        sum(ref[ref.shape[0] - second_rows :, 0:elements] for ref in second_refs),
    ]
    counted = 9 * CHUNKS[1][1]
    counts = gathered[1][counted : counted + 1]
    per_brick = 1.0 / (8.0 * jnp.maximum(counts, 1.0))
    frames = [
        jnp.concatenate(
            [
                sums[count * k : count * (k + 1)]
                for sums, (first, count) in zip(gathered, CHUNKS)
            ],
            axis=0,
        )
        * per_brick
        for k in range(9)
    ]

    node = lax.broadcasted_iota(jnp.int32, (COLUMNS, elements), 0)
    element = lax.broadcasted_iota(jnp.int32, (COLUMNS, elements), 1)
    base = element + element // GX
    selectors = [
        (node == base + (step_y * (GX + 1) + step_x)).astype(jnp.bfloat16)
        for step_x in range(2)
        for step_y in range(2)
    ]
    corner = lax.broadcasted_iota(jnp.int32, (24, 1), 0) & 7
    upper_corner = (corner & 1) == 1
    height = lax.axis_index("fe") // 2
    above = height + (lax.axis_index("fe") & 1)
    upper = jnp.zeros((3, COLUMNS), jnp.float32)
    for flip, ref in enumerate(second_refs):
        wanted = (height ^ flip) == above
        upper = upper + jnp.where(wanted, ref[ref.shape[0] - 3 :, :], 0.0)
    values = jnp.where(
        upper_corner,
        jnp.concatenate(
            [jnp.broadcast_to(upper[c : c + 1], (8, COLUMNS)) for c in range(3)], axis=0
        ),
        jnp.concatenate([jnp.broadcast_to(own_ref[c], (8, COLUMNS)) for c in range(3)], axis=0),
    )
    corners = jnp.zeros((24, elements), jnp.float32)
    for step in range(4):
        part = jnp.where(corner >> 1 == step, values, 0.0)
        corners = corners + dot_selected(part, selectors[step], 0)
    gradients = []
    for c in range(3):
        product = jnp.dot(
            table_ref[...],
            corners[8 * c : 8 * c + 8],
            precision=lax.Precision.HIGHEST,
            preferred_element_type=jnp.float32,
        )
        gradients.append([product[8 * d : 8 * d + 8] for d in range(3)])
    strain = [
        gradients[0][0],
        gradients[1][1],
        gradients[2][2],
        0.5 * (gradients[1][2] + gradients[2][1]),
        0.5 * (gradients[0][2] + gradients[2][0]),
        0.5 * (gradients[0][1] + gradients[1][0]),
    ]
    volume = strain[0] + strain[1] + strain[2]
    trial = []
    for component in range(6):
        change = 2.0 * SHEAR_MODULUS * strain[component]
        if component < 3:
            change = change + LAMBDA_ELASTIC * volume
        trial.append(stress_ref[component] + change)
    correction = [jnp.zeros_like(trial[0]) for component in range(6)]
    for system in range(12):
        rotated_dir = [
            sum(
                frames[3 * row + axis_id] * SLIP_DIRECTIONS[system][axis_id]
                for axis_id in range(3)
                if SLIP_DIRECTIONS[system][axis_id] != 0.0
            )
            for row in range(3)
        ]
        rotated_normal = [
            sum(frames[3 * row + axis_id] * SLIP_PLANES[system][axis_id] for axis_id in range(3))
            for row in range(3)
        ]
        schmid = [
            rotated_dir[0] * rotated_normal[0],
            rotated_dir[1] * rotated_normal[1],
            rotated_dir[2] * rotated_normal[2],
            0.5 * (rotated_dir[1] * rotated_normal[2] + rotated_dir[2] * rotated_normal[1]),
            0.5 * (rotated_dir[0] * rotated_normal[2] + rotated_dir[2] * rotated_normal[0]),
            0.5 * (rotated_dir[0] * rotated_normal[1] + rotated_dir[1] * rotated_normal[0]),
        ]
        resolved = (
            trial[0] * schmid[0]
            + trial[1] * schmid[1]
            + trial[2] * schmid[2]
            + 2.0 * (trial[3] * schmid[3] + trial[4] * schmid[4] + trial[5] * schmid[5])
        )
        slip_ratio = resolved / resistance_ref[system]
        slip_step = RATE_STEP * slip_ratio * jnp.abs(slip_ratio)
        correction = [
            correction[component] + slip_step * schmid[component] for component in range(6)
        ]
    updated = [
        trial[component] - 2.0 * SHEAR_MODULUS * correction[component] for component in range(6)
    ]
    for component in range(6):
        stress_out_ref[component] = updated[component]
    point_scale = weights_ref[...].astype(jnp.float32) * (1.0 / (FIXED_POINT * 8.0))
    scaled = [value * point_scale for value in updated]
    forces = []
    for rows in [(0, 5, 4), (5, 1, 3), (4, 3, 2)]:
        forces.append(
            lax.dot_general(
                table_ref[...],
                jnp.concatenate([scaled[row] for row in rows], axis=0),
                (((0,), (0,)), ((), ())),
                precision=lax.Precision.HIGHEST,
                preferred_element_type=jnp.float32,
            )
        )
    forces = jnp.concatenate(forces, axis=0)
    nodal = jnp.zeros((24, COLUMNS), jnp.float32)
    for step in range(4):
        part = jnp.where(corner >> 1 == step, forces, 0.0)
        nodal = nodal + dot_selected(part, selectors[step], 1)
    lower = jnp.where(upper_corner, 0.0, nodal)
    above = jnp.where(upper_corner, nodal, 0.0)
    for c in range(3):
        nodal_ref[0, c] = jnp.sum(lower[8 * c : 8 * c + 8], axis=0, keepdims=True)
        nodal_ref[1, c] = jnp.sum(above[8 * c : 8 * c + 8], axis=0, keepdims=True)


def element_update(first, second, own, stress_old, resistance, quad_weights):
    grad_table = shape_gradients()
    table = jnp.asarray(
        [
            [grad_table[quadrature][corner][direction] for corner in range(8)]
            for direction in range(3)
            for quadrature in range(8)
        ],
        dtype=jnp.float32,
    )
    return pl.pallas_call(
        functools.partial(update_kernel, len(second)),
        out_shape=(
            jax.ShapeDtypeStruct(stress_old.shape, jnp.float32),
            jax.ShapeDtypeStruct((2,) + own.shape, jnp.float32),
        ),
        compiler_params=pltpu.CompilerParams(vmem_limit_bytes=8 * 1024 * 1024),
        name="stress_update",
    )(first, *second, own, stress_old, resistance, quad_weights, table)


def body(
    grain_ids,
    euler_angles,
    brick_active,
    brick_owner,
    brick_element,
    displacement,
    stress_old,
    resistance,
    quad_weights,
):
    half = lax.axis_size("ca") * lax.axis_size("fe") // 2
    bricks = grain_ids.shape[1]
    owner = lax.optimization_barrier(brick_owner.reshape(bricks))
    labels = jnp.where(brick_active > 0, owner * COLUMNS + brick_element, -1).reshape(1, bricks)
    ids = jnp.concatenate([grain_ids, labels], axis=0)
    per_octant = grain_ids.shape[0] // 8
    table = rotation_table(euler_angles)
    labels, send, split, ids = cell_sums(CHUNKS[0], per_octant, ids, None, table, half)
    keep, labels = brick_sums(split, labels, half)
    core_a, labels, own = core_sum(
        keep, across_cores(send), [labels, displacement], "core_sum_a"
    )
    send, keep = cell_sums(CHUNKS[1], per_octant, ids, labels, table, half)
    flip = lax.axis_size("fe") // 4
    (kept, sent), own, send = plane_sum(
        across_plane(core_a), [own, send], [flip, flip], "plane_sum_a"
    )
    received = to_relative(sent, 0, 0, 0, flip)
    core_b = last_core_sum(keep, across_cores(send), own)
    while flip > 2:
        flip //= 2
        (kept, sent) = plane_sum([kept, received], [], [flip, flip], "height_sum_a")[0]
        received = to_relative(sent, 0, 0, 0, flip)
    first, *second = last_sum(kept, received, across_plane(core_b), 3)
    stress_new, nodal = element_update(
        first, across_height(second), displacement, stress_old, resistance, quad_weights
    )
    forces = nodal[0] + passed_along(nodal[1], "fe", 1)
    return (stress_new, forces)


def solution(mesh):
    placed = (
        P(None, ("ca", "fe")),
        P(),
        P(("ca", "fe")),
        P(("ca", "fe"), None),
        P(("ca", "fe")),
        P(None, ("ca", "fe"), None),
        P(None, None, ("ca", "fe")),
        P(None, None, ("ca", "fe")),
        P(None, ("ca", "fe")),
    )
    return jax.shard_map(
        body,
        mesh=mesh,
        in_specs=placed,
        out_specs=(P(None, None, ("ca", "fe")), P(None, ("ca", "fe"), None)),
        check_vma=False,
    )
```

```python
import functools
import functools
import math

import jax
import jax.numpy as jnp
import ml_dtypes
import numpy as np
from jax import lax
from jax.experimental import pallas as pl
from jax.experimental.pallas import tpu as pltpu
from jax.sharding import PartitionSpec as P

GX = 15
LANES = 128
COLUMNS = 256
CHUNKS = ((0, 6), (6, 2))
QUANTUM = float((1 << 15) - 1)

SLIP_PLANES = [
    [value / math.sqrt(3.0) for value in row]
    for row in [[1, 1, 1]] * 3 + [[-1, 1, 1]] * 3 + [[1, -1, 1]] * 3 + [[1, 1, -1]] * 3
]
SLIP_DIRECTIONS = [
    [value / math.sqrt(2.0) for value in row]
    for row in [
        [0, 1, -1],
        [1, 0, -1],
        [1, -1, 0],
        [0, 1, -1],
        [1, 0, 1],
        [1, 1, 0],
        [0, 1, 1],
        [1, 0, -1],
        [1, 1, 0],
        [0, 1, 1],
        [1, 0, 1],
        [1, -1, 0],
    ]
]
LAMBDA_ELASTIC = 1.5
SHEAR_MODULUS = 1.0
RATE_STEP = 0.1
FIXED_POINT = 65536.0


def passed_along(block, axis, distance):
    devices = range(lax.axis_size(axis))
    route = [(i - distance, i) for i in devices if i - distance in devices]
    return lax.ppermute(block, axis, route)


def shape_gradients():
    grad_table = [[[0.0, 0.0, 0.0] for corner in range(8)] for quadrature in range(8)]
    point_offset = 1.0 / math.sqrt(3.0)
    for quadrature in range(8):
        natural = [
            (2 * (quadrature >> shift_bits & 1) - 1) * point_offset for shift_bits in (2, 1, 0)
        ]
        for corner in range(8):
            sign_list = [2 * (corner >> shift_bits & 1) - 1 for shift_bits in (2, 1, 0)]
            factors = [1.0 + sign_list[axis_id] * natural[axis_id] for axis_id in range(3)]
            for direction in range(3):
                others = 1.0
                for axis_id in range(3):
                    if axis_id != direction:
                        others = others * factors[axis_id]
                grad_table[quadrature][corner][direction] = (
                    2.0 * sign_list[direction] * others / 8.0
                )
    return grad_table


def cos_sin(angle):
    square = angle * angle
    cosine = 1.0 / math.factorial(12)
    for power in (10, 8, 6, 4, 2, 0):
        cosine = cosine * square + (-1.0) ** (power // 2) / math.factorial(power)
    sine = 1.0 / math.factorial(13)
    for power in (11, 9, 7, 5, 3, 1):
        sine = sine * square + (-1.0) ** (power // 2) / math.factorial(power)
    return cosine, sine * angle


def rotation_coordinates(euler):
    cos_one, sin_one = cos_sin(0.5 * euler[0 : 0 + 1])
    cos_mid, sin_mid = cos_sin(0.5 * euler[1 : 1 + 1])
    cos_two, sin_two = cos_sin(0.5 * euler[2 : 2 + 1])
    w = cos_mid * (cos_one * cos_two - sin_one * sin_two)
    factor = jnp.where(w < 0.0, -QUANTUM, QUANTUM) / (1.0 + jnp.abs(w))
    x = sin_mid * (cos_one * cos_two + sin_one * sin_two) * factor
    y = sin_mid * (sin_one * cos_two - cos_one * sin_two) * factor
    z = cos_mid * (sin_one * cos_two + cos_one * sin_two) * factor
    x, y, z = [
        jnp.clip(jnp.round(value), -QUANTUM, QUANTUM).astype(jnp.int32) for value in (x, y, z)
    ]
    return [x, y, z]


def table_kernel(euler_ref, table_ref):
    at = 0
    for coordinate in rotation_coordinates(euler_ref[...]):
        for row in range(0, coordinate.shape[1] // LANES, 2):
            low = coordinate[:, row * LANES : (row + 1) * LANES]
            high = coordinate[:, (row + 1) * LANES : (row + 2) * LANES]
            table_ref[at] = jnp.broadcast_to(lax.shift_left(high, 16) | (low & 0xFFFF), (8, LANES))
            at += 1


def rotation_table(euler_angles):
    height = euler_angles.shape[1] // LANES * 3 // 2
    return pl.pallas_call(
        table_kernel,
        out_shape=jax.ShapeDtypeStruct((height, 8, LANES), jnp.int32),
        compiler_params=pltpu.CompilerParams(vmem_limit_bytes=8 * 1024 * 1024),
        cost_estimate=pl.CostEstimate(flops=10**6, bytes_accessed=10**7, transcendentals=0),
        name="rotation_table",
    )(euler_angles)


def looked_up(table_ref, first_row, rows, lane, bits):
    if rows == 1:
        return lax.gather(
            table_ref[first_row],
            lane,
            lax.GatherDimensionNumbers(
                offset_dims=(),
                collapsed_slice_dims=(1,),
                start_index_map=(1,),
                operand_batching_dims=(0,),
                start_indices_batching_dims=(0,),
            ),
            slice_sizes=(1, 1),
            mode=lax.GatherScatterMode.PROMISE_IN_BOUNDS,
        )
    half = rows // 2
    level = half.bit_length() - 1
    low = looked_up(table_ref, first_row, half, lane, bits)
    high = looked_up(table_ref, first_row + half, half, lane, bits)
    return jnp.where(bits[level], high, low)


def looked_up_words(table_ref, ids):
    lane = (ids & (LANES - 1))[:, :, None]
    row = lax.shift_right_logical(ids, 7)
    words = table_ref.shape[0] // 3
    bits = [(row & (2 << level)) != 0 for level in range(words.bit_length() - 1)]
    shift = lax.shift_left((row & 1) ^ 1, 4)
    return [
        lax.shift_left(looked_up(table_ref, words * axis, words, lane, bits), shift)
        for axis in range(3)
    ]


def rotation_products(words):
    x, y, z = [lax.shift_right_arithmetic(word, 16).astype(jnp.float32) for word in words]
    length = (x * x + y * y + z * z) * (0.5 / (QUANTUM * QUANTUM)) + 0.5
    scale = pl.reciprocal(length, approx=True)
    scale = scale * (2.0 - length * scale)
    w = scale - 1.0
    x, y, z = x * scale, y * scale, z * scale
    return [x * x, y * y, z * z, x * y, x * z, y * z, w * x, w * y, w * z]


ENTRIES = (
    ((1, -1.0), (2, -1.0)),
    ((3, 1.0), (8, -1.0)),
    ((4, 1.0), (7, 1.0)),
    ((3, 1.0), (8, 1.0)),
    ((0, -1.0), (2, -1.0)),
    ((5, 1.0), (6, -1.0)),
    ((4, 1.0), (7, -1.0)),
    ((5, 1.0), (6, 1.0)),
    ((0, -1.0), (1, -1.0)),
)


def remainder(value, divisor):
    return value - value // divisor * divisor


def cell_sum_kernel(
    octants,
    per_octant,
    ids_ref,
    label_ref,
    table_ref,
    *refs,
):
    first, count = octants
    start = ids_ref.shape[0] - (8 - first) * per_octant
    tile_ref, raw_ref, place_ref, masked_ref = refs[-4:]
    if first + count < 8:
        label_out_ref, send_ref, split_ref, rest_ref = refs[:-4]
        label_out_ref[...] = label_ref[...]
        rest_ref[...] = ids_ref[pl.ds(ids_ref.shape[0] - rest_ref.shape[0], rest_ref.shape[0]), :]
        targets = [(send_ref.shape[0], send_ref)]
    else:
        send_ref, keep_ref, split_ref = refs[:-4]
        targets = [(send_ref.shape[0], send_ref), (0, keep_ref)]
    groups = tile_ref.shape[1] // 8
    rows_left = count * per_octant - 8 * (groups - 1)
    turns = count // math.gcd(count, 8)
    rows = send_ref.shape[1]
    width = masked_ref.shape[1]
    pairs = ids_ref.shape[1] // width

    out_row = lax.broadcasted_iota(jnp.int32, (rows, raw_ref.shape[0]), 0)
    raw_row = lax.broadcasted_iota(jnp.int32, (rows, raw_ref.shape[0]), 1)
    entry, product = out_row // count, raw_row // (8 * turns)
    fold = jnp.zeros(out_row.shape, jnp.float32)
    for index, terms in enumerate(ENTRIES):
        for other, sign in terms:
            fold = jnp.where((entry == index) & (product == other), sign, fold)
    fold = jnp.where(remainder(out_row, count) == remainder(raw_row, count), fold, 0.0)
    fold = fold.astype(jnp.bfloat16)
    row = lax.broadcasted_iota(jnp.int32, (rows, width), 0)
    diagonal = (row // count == 0) | (row // count == 4) | (row // count == 8)
    constant = jnp.where(diagonal, float(per_octant), jnp.where(row < 9 * count, 0.0, 1.0))

    def lanes_of(pair):
        return pl.ds(pl.multiple_of(pair * width, width), width)

    def look_up(pair):
        for tile in range(width // LANES):
            lanes = pl.ds(pl.multiple_of(pair * width + tile * LANES, LANES), LANES)
            for octant in range(count):
                tile_ref[tile, pl.ds(octant, per_octant, stride=count), :] = ids_ref[
                    pl.ds(start + octant * per_octant, per_octant), lanes
                ]
            sums = [[jnp.zeros((8, LANES), jnp.float32)] * 9 for turn in range(turns)]
            found = None
            for group in range(groups + 1):
                last = found
                if group < groups:
                    ids = tile_ref[tile, pl.ds(8 * group, 8), :]
                    found = looked_up_words(table_ref, ids)
                if group == 0:
                    continue
                products = rotation_products(last)
                if group == groups and rows_left < 8:
                    there = lax.broadcasted_iota(jnp.int32, (8, LANES), 0) < rows_left
                    products = [jnp.where(there, value, 0.0) for value in products]
                turn = (group - 1) % turns
                sums[turn] = [total + value for total, value in zip(sums[turn], products)]
            scales = [2.0 / (QUANTUM * QUANTUM)] * 6 + [2.0 / QUANTUM] * 3
            raw_ref[:, lanes] = jnp.concatenate(
                [sums[turn][index] * scales[index] for index in range(9) for turn in range(turns)],
                axis=0,
            )

    def fold_entries(pair):
        lanes = lanes_of(pair)
        total = constant
        for part in three_parts(raw_ref[:, lanes]):
            total = total + jnp.dot(fold, part, preferred_element_type=jnp.float32)
        leading = total.astype(jnp.bfloat16).astype(jnp.float32)
        split_ref[:, lanes] = jnp.concatenate([leading, total - leading], axis=0).astype(
            jnp.bfloat16
        )

    def add_bricks(pair, counted):
        lanes = lanes_of(pair)
        column = lax.broadcasted_iota(jnp.int32, (COLUMNS, width), 0)
        chosen = (column == label_ref[:, lanes] & (COLUMNS - 1)).astype(jnp.bfloat16)
        place = jnp.where(counted, place_ref[:, lanes], -1)
        for base, out_ref in targets:
            add_places(split_ref, lanes, place - base, chosen, out_ref, masked_ref)

    place_ref[...] = relative_places(label_ref[...])
    for base, out_ref in targets:
        out_ref[...] = jnp.zeros(out_ref.shape, jnp.float32)
    raw_ref[:, pl.ds(0, width)] = jnp.zeros((raw_ref.shape[0], width), jnp.float32)
    split_ref[:, pl.ds(0, width)] = jnp.zeros((split_ref.shape[0], width), jnp.bfloat16)

    def step(pair, carry):
        add_bricks(jnp.maximum(pair - 2, 0), pair >= 2)
        fold_entries(jnp.maximum(pair - 1, 0))
        look_up(pair)
        return carry

    lax.fori_loop(0, pairs, step, 0, unroll=2)
    add_bricks(pairs - 2, True)
    fold_entries(pairs - 1)
    add_bricks(pairs - 1, True)


def relative_places(labels):
    place = place_of(lax.shift_right_arithmetic(labels, COLUMNS.bit_length() - 1))
    return jnp.where(labels < 0, -1, place)


def add_places(split_ref, lanes, place, chosen, out_ref, masked_ref):
    split_rows = split_ref.shape[0]
    half_rows = split_rows // 2
    members = masked_ref.shape[0] // split_rows
    for first in range(0, out_ref.shape[0], members):
        split = split_ref[:, lanes]
        for member in range(members):
            mask = (place == first + member).astype(jnp.bfloat16)
            masked_ref[pl.ds(member * split_rows, split_rows), :] = split * mask
        product = lax.dot_general(
            masked_ref[...],
            chosen,
            (((1,), (1,)), ((), ())),
            preferred_element_type=jnp.float32,
        )
        for member in range(members):
            at = member * split_rows
            out_ref[first + member] += (
                product[at : at + half_rows] + product[at + half_rows : at + split_rows]
            )


def across_cores(block):
    groups = lax.axis_size("ca")
    return lax.ppermute(block, "ca", [(i, i ^ 1) for i in range(groups)])


def brick_sum_kernel(split_ref, label_ref, out_ref, label_out_ref, place_ref, masked_ref):
    labels = label_ref[...]
    label_out_ref[...] = labels
    place_ref[...] = relative_places(labels)
    bricks = split_ref.shape[1]
    column = lax.broadcasted_iota(jnp.int32, (COLUMNS, bricks), 0)
    chosen = (column == labels & (COLUMNS - 1)).astype(jnp.bfloat16)
    split_rows = split_ref.shape[0]
    half_rows = split_rows // 2
    members = masked_ref.shape[0] // split_rows

    def place_group(step, carry):
        for member in range(members):
            mask = (place_ref[...] == step * members + member).astype(jnp.bfloat16)
            masked_ref[pl.ds(member * split_rows, split_rows), :] = split_ref[...] * mask
        product = lax.dot_general(
            masked_ref[...],
            chosen,
            (((1,), (1,)), ((), ())),
            preferred_element_type=jnp.float32,
        )
        for member in range(members):
            at = member * split_rows
            out_ref[step * members + member] = (
                product[at : at + half_rows] + product[at + half_rows : at + split_rows]
            )
        return carry

    lax.fori_loop(0, out_ref.shape[0] // members, place_group, 0)


def place_of(owner):
    groups, members = lax.axis_size("ca"), lax.axis_size("fe")
    owner_ca = lax.shift_right_logical(owner, members.bit_length() - 1) ^ lax.axis_index("ca")
    owner_fe = (owner & (members - 1)) ^ lax.axis_index("fe")
    place = (owner_ca & 1) * (groups // 2) + lax.shift_right_logical(owner_ca, 1)
    place = place * 2 + (owner_fe & 1)
    return place * (members // 2) + lax.shift_right_logical(owner_fe, 1)


def cell_sums(octants, per_octant, ids, labels, table, places):
    first, count = octants
    bricks = ids.shape[1]
    rows = padded_rows(count)
    half = jax.ShapeDtypeStruct((places, rows, COLUMNS), jnp.float32)
    split = jax.ShapeDtypeStruct((2 * rows, bricks), jnp.bfloat16)
    scratch = []
    left = 8 - first - count
    if left:
        out_shape = [
            jax.ShapeDtypeStruct(labels.shape, jnp.int32),
            half,
            split,
            jax.ShapeDtypeStruct((-(-left * per_octant // 8) * 8, bricks), jnp.int32),
        ]
    else:
        out_shape = [half, half]
        scratch.append(pltpu.VMEM(split.shape, split.dtype))
    return pl.pallas_call(
        functools.partial(cell_sum_kernel, octants, per_octant),
        out_shape=out_shape,
        scratch_shapes=scratch
        + [
            pltpu.VMEM((2, -(-count * per_octant // 8) * 8, LANES), jnp.int32),
            pltpu.VMEM((72 * (count // math.gcd(count, 8)), bricks), jnp.float32),
        ]
        + brick_scratch(rows, bricks, places, 2 * LANES),
        compiler_params=pltpu.CompilerParams(vmem_limit_bytes=28 * 1024 * 1024),
        cost_estimate=pl.CostEstimate(
            flops=count * 4 * 10**9, bytes_accessed=count * 10**7, transcendentals=0
        ),
        name="cell_sums",
    )(ids, labels, table)


def padded_rows(count):
    return -(-9 * count // 8) * 8


def brick_scratch(rows, bricks, places, width):
    return [
        pltpu.VMEM((1, bricks), jnp.int32),
        pltpu.VMEM((min(16, places) * 2 * rows, width), jnp.bfloat16),
    ]


def brick_sums(split, labels, places):
    rows, bricks = split.shape
    return pl.pallas_call(
        brick_sum_kernel,
        out_shape=[
            jax.ShapeDtypeStruct((places, rows // 2, COLUMNS), jnp.float32),
            jax.ShapeDtypeStruct(labels.shape, jnp.int32),
        ],
        scratch_shapes=brick_scratch(rows // 2, bricks, places, bricks),
        compiler_params=pltpu.CompilerParams(vmem_limit_bytes=24 * 1024 * 1024),
        cost_estimate=pl.CostEstimate(
            flops=rows * 15 * 10**6, bytes_accessed=rows * 5 * 10**4, transcendentals=0
        ),
        name="brick_sums",
    )(split, labels)


def core_sum_kernel(passed, kept_ref, received_ref, *refs):
    outs = refs[passed:]
    for index, out_ref in enumerate(outs[: len(outs) - passed]):
        out_ref[...] = kept_ref[index] + received_ref[index]
    for i in range(passed):
        outs[len(outs) - passed + i][...] = refs[i][...]


def last_core_sum_kernel(kept_ref, received_ref, own_ref, *outs):
    for index, out_ref in enumerate(outs):
        out_ref[...] = kept_ref[index] + received_ref[index]
        for c in range(3):
            row = out_ref.shape[1] - 3 + c
            out_ref[:, row : row + 1, :] = jnp.broadcast_to(
                own_ref[c][None], (out_ref.shape[0], 1, COLUMNS)
            )


def last_core_sum(kept, received, own):
    pairs, rests = lax.axis_size("ca") // 2, lax.axis_size("fe") // 2
    shape = (2 * pairs, rests) + kept.shape[1:]
    return pl.pallas_call(
        last_core_sum_kernel,
        out_shape=[jax.ShapeDtypeStruct(shape[1:], jnp.float32)] * shape[0],
        compiler_params=pltpu.CompilerParams(vmem_limit_bytes=16 * 1024 * 1024),
        name="core_sum_b",
    )(kept.reshape(shape), received.reshape(shape), own)


def core_sum(kept, received, passed, name):
    pairs, rests = lax.axis_size("ca") // 2, lax.axis_size("fe") // 2
    shape = (2 * pairs, rests) + kept.shape[1:]
    out = pl.pallas_call(
        functools.partial(core_sum_kernel, len(passed)),
        out_shape=[jax.ShapeDtypeStruct(shape[1:], jnp.float32)] * shape[0]
        + [jax.ShapeDtypeStruct(array.shape, array.dtype) for array in passed],
        compiler_params=pltpu.CompilerParams(vmem_limit_bytes=16 * 1024 * 1024),
        name=name,
    )(kept.reshape(shape), received.reshape(shape), *passed)
    return out[: shape[0]], *out[shape[0] :]


def plane_sum_kernel(sources, passed, *refs):
    outs = refs[sources + passed :]
    height = 0
    for out_ref in outs[: len(outs) - passed]:
        out_ref[...] = sum(ref[pl.ds(height, out_ref.shape[0])] for ref in refs[:sources])
        height += out_ref.shape[0]
    for i in range(passed):
        outs[len(outs) - passed + i][...] = refs[sources + i][...]


def plane_sum(parts, passed, cuts, name):
    rest = parts[0].shape[1:]
    out = pl.pallas_call(
        functools.partial(plane_sum_kernel, len(parts), len(passed)),
        out_shape=[jax.ShapeDtypeStruct((cut,) + rest, jnp.float32) for cut in cuts]
        + [jax.ShapeDtypeStruct(array.shape, array.dtype) for array in passed],
        compiler_params=pltpu.CompilerParams(vmem_limit_bytes=16 * 1024 * 1024),
        name=name,
    )(*parts, *passed)
    return out[: len(cuts)], *out[len(cuts) :]


def last_sum_kernel(sources, spare, kept_ref, received_ref, *refs):
    parts, outs = refs[:sources], refs[sources:]
    rows = kept_ref.shape[1]
    outs[0][...] = kept_ref[0] + received_ref[0]
    outs[2][0:rows, :] = kept_ref[1] + received_ref[1]
    for height, out_ref in enumerate(outs[1:]):
        first = out_ref.shape[0] - parts[0].shape[1]
        out_ref[first:, :] = sum(ref[height] for ref in parts)
        out_ref[out_ref.shape[0] - spare :, :] = parts[-1][height, -spare:, :]


def last_sum(kept, received, parts, spare):
    heights, rows, columns = parts[0].shape
    part = jax.ShapeDtypeStruct((rows, columns), jnp.float32)
    both = jax.ShapeDtypeStruct((kept.shape[1] + rows, columns), jnp.float32)
    return pl.pallas_call(
        functools.partial(last_sum_kernel, len(parts), spare),
        out_shape=[jax.ShapeDtypeStruct(kept.shape[1:], jnp.float32), part, both]
        + [part] * (heights - 2),
        compiler_params=pltpu.CompilerParams(vmem_limit_bytes=16 * 1024 * 1024),
        name="last_sum",
    )(kept, received, *parts)


def to_relative(block, core, pair, last, rest):
    groups, members = lax.axis_size("ca"), lax.axis_size("fe")
    flip = (2 * pair + core) * members + 2 * rest + last
    return lax.ppermute(block, ("ca", "fe"), [(i, i ^ flip) for i in range(groups * members)])


def across_plane(parts):
    return [parts[0]] + [
        to_relative(parts[index], 0, index // 2, index % 2, 0)
        for index in range(len(parts) - 1, 0, -1)
    ]


def across_height(parts):
    return [parts[0]] + [to_relative(parts[rest], 0, 0, 0, rest) for rest in range(1, len(parts))]


def three_parts(value):
    first = value.astype(jnp.bfloat16)
    rest = value - first.astype(jnp.float32)
    second = rest.astype(jnp.bfloat16)
    third = (rest - second.astype(jnp.float32)).astype(jnp.bfloat16)
    return first, second, third


def joined(parts, axis):
    whole = jnp.concatenate([part.astype(jnp.float32) for part in parts], axis=axis)
    return whole.astype(jnp.bfloat16)


def six_terms(value):
    first, second, third = three_parts(value)
    return joined([first, second, third, first, second, first], 0)


def six_terms_of(table):
    first = table.astype(ml_dtypes.bfloat16)
    rest = table - first.astype(np.float32)
    second = rest.astype(ml_dtypes.bfloat16)
    third = (rest - second.astype(np.float32)).astype(ml_dtypes.bfloat16)
    terms = np.concatenate([first, first, first, second, second, third], axis=1)
    return np.pad(terms, ((0, -terms.shape[0] % 16), (0, 0)))


def dot_selected(value, selector, contract):
    rows = value.shape[0]
    product = lax.dot_general(
        joined(three_parts(value), 0),
        selector,
        (((1,), (contract,)), ((), ())),
        preferred_element_type=jnp.float32,
    )
    return product[:rows] + product[rows : 2 * rows] + product[2 * rows :]


def update_kernel(heights, *refs):
    first_ref, second_refs = refs[0], refs[1 : 1 + heights]
    own_ref, stress_ref, resistance_ref, weights_ref, table_ref, turned_ref = refs[1 + heights : -2]
    stress_out_ref, nodal_ref = refs[-2:]
    elements = stress_ref.shape[2]
    rows, second_rows = first_ref.shape[0], second_refs[0].shape[0]
    gathered = [
        first_ref[:, 0:elements] + second_refs[1][0:rows, 0:elements],
        sum(ref[ref.shape[0] - second_rows :, 0:elements] for ref in second_refs),
    ]
    counted = 9 * CHUNKS[1][1]
    counts = gathered[1][counted : counted + 1]
    per_brick = 1.0 / (8.0 * jnp.maximum(counts, 1.0))
    frames = [
        jnp.concatenate(
            [
                sums[count * k : count * (k + 1)]
                for sums, (first, count) in zip(gathered, CHUNKS)
            ],
            axis=0,
        )
        * per_brick
        for k in range(9)
    ]

    node = lax.broadcasted_iota(jnp.int32, (COLUMNS, elements), 0)
    element = lax.broadcasted_iota(jnp.int32, (COLUMNS, elements), 1)
    base = element + element // GX
    selectors = [
        (node == base + (step_y * (GX + 1) + step_x)).astype(jnp.bfloat16)
        for step_x in range(2)
        for step_y in range(2)
    ]
    corner = lax.broadcasted_iota(jnp.int32, (24, 1), 0) & 7
    upper_corner = (corner & 1) == 1
    height = lax.axis_index("fe") // 2
    above = height + (lax.axis_index("fe") & 1)
    upper = jnp.zeros((3, COLUMNS), jnp.float32)
    for flip, ref in enumerate(second_refs):
        wanted = (height ^ flip) == above
        upper = upper + jnp.where(wanted, ref[ref.shape[0] - 3 :, :], 0.0)
    values = jnp.where(
        upper_corner,
        jnp.concatenate(
            [jnp.broadcast_to(upper[c : c + 1], (8, COLUMNS)) for c in range(3)], axis=0
        ),
        jnp.concatenate([jnp.broadcast_to(own_ref[c], (8, COLUMNS)) for c in range(3)], axis=0),
    )
    corners = dot_selected(
        jnp.concatenate(
            [jnp.where(corner >> 1 == step, values, 0.0) for step in range(4)], axis=1
        ),
        jnp.concatenate(selectors, axis=0),
        0,
    )
    gradients = []
    for c in range(3):
        product = jnp.dot(
            table_ref[...],
            six_terms(corners[8 * c : 8 * c + 8]),
            preferred_element_type=jnp.float32,
        )
        gradients.append([product[8 * d : 8 * d + 8] for d in range(3)])
    strain = [
        gradients[0][0],
        gradients[1][1],
        gradients[2][2],
        0.5 * (gradients[1][2] + gradients[2][1]),
        0.5 * (gradients[0][2] + gradients[2][0]),
        0.5 * (gradients[0][1] + gradients[1][0]),
    ]
    volume = strain[0] + strain[1] + strain[2]
    trial = []
    for component in range(6):
        change = 2.0 * SHEAR_MODULUS * strain[component]
        if component < 3:
            change = change + LAMBDA_ELASTIC * volume
        trial.append(stress_ref[component] + change)
    correction = [jnp.zeros_like(trial[0]) for component in range(6)]
    for system in range(12):
        rotated_dir = [
            sum(
                frames[3 * row + axis_id] * SLIP_DIRECTIONS[system][axis_id]
                for axis_id in range(3)
                if SLIP_DIRECTIONS[system][axis_id] != 0.0
            )
            for row in range(3)
        ]
        rotated_normal = [
            sum(frames[3 * row + axis_id] * SLIP_PLANES[system][axis_id] for axis_id in range(3))
            for row in range(3)
        ]
        schmid = [
            rotated_dir[0] * rotated_normal[0],
            rotated_dir[1] * rotated_normal[1],
            rotated_dir[2] * rotated_normal[2],
            0.5 * (rotated_dir[1] * rotated_normal[2] + rotated_dir[2] * rotated_normal[1]),
            0.5 * (rotated_dir[0] * rotated_normal[2] + rotated_dir[2] * rotated_normal[0]),
            0.5 * (rotated_dir[0] * rotated_normal[1] + rotated_dir[1] * rotated_normal[0]),
        ]
        resolved = (
            trial[0] * schmid[0]
            + trial[1] * schmid[1]
            + trial[2] * schmid[2]
            + 2.0 * (trial[3] * schmid[3] + trial[4] * schmid[4] + trial[5] * schmid[5])
        )
        slip_ratio = resolved / resistance_ref[system]
        slip_step = RATE_STEP * slip_ratio * jnp.abs(slip_ratio)
        correction = [
            correction[component] + slip_step * schmid[component] for component in range(6)
        ]
    updated = [
        trial[component] - 2.0 * SHEAR_MODULUS * correction[component] for component in range(6)
    ]
    for component in range(6):
        stress_out_ref[component] = updated[component]
    point_scale = weights_ref[...].astype(jnp.float32) * (1.0 / (FIXED_POINT * 8.0))
    scaled = [value * point_scale for value in updated]
    forces = []
    for rows in [(0, 5, 4), (5, 1, 3), (4, 3, 2)]:
        forces.append(
            jnp.dot(
                turned_ref[...],
                six_terms(jnp.concatenate([scaled[row] for row in rows], axis=0)),
                preferred_element_type=jnp.float32,
            )[:8]
        )
    forces = jnp.concatenate(forces, axis=0)
    nodal = jnp.zeros((24, COLUMNS), jnp.float32)
    for step in range(4):
        part = jnp.where(corner >> 1 == step, forces, 0.0)
        nodal = nodal + dot_selected(part, selectors[step], 1)
    lower = jnp.where(upper_corner, 0.0, nodal)
    above = jnp.where(upper_corner, nodal, 0.0)
    for c in range(3):
        nodal_ref[0, c] = jnp.sum(lower[8 * c : 8 * c + 8], axis=0, keepdims=True)
        nodal_ref[1, c] = jnp.sum(above[8 * c : 8 * c + 8], axis=0, keepdims=True)


def element_update(first, second, own, stress_old, resistance, quad_weights):
    grad_table = shape_gradients()
    table = np.asarray(
        [
            [grad_table[quadrature][corner][direction] for corner in range(8)]
            for direction in range(3)
            for quadrature in range(8)
        ],
        dtype=np.float32,
    )
    tables = [jnp.asarray(six_terms_of(part)) for part in (table, table.T)]
    return pl.pallas_call(
        functools.partial(update_kernel, len(second)),
        out_shape=(
            jax.ShapeDtypeStruct(stress_old.shape, jnp.float32),
            jax.ShapeDtypeStruct((2,) + own.shape, jnp.float32),
        ),
        compiler_params=pltpu.CompilerParams(vmem_limit_bytes=8 * 1024 * 1024),
        name="stress_update",
    )(first, *second, own, stress_old, resistance, quad_weights, *tables)


def body(
    grain_ids,
    euler_angles,
    brick_active,
    brick_owner,
    brick_element,
    displacement,
    stress_old,
    resistance,
    quad_weights,
):
    half = lax.axis_size("ca") * lax.axis_size("fe") // 2
    bricks = grain_ids.shape[1]
    owner = lax.optimization_barrier(brick_owner.reshape(bricks))
    labels = jnp.where(brick_active > 0, owner * COLUMNS + brick_element, -1).reshape(1, bricks)
    per_octant = grain_ids.shape[0] // 8
    table = rotation_table(euler_angles)
    labels, send, split, ids = cell_sums(CHUNKS[0], per_octant, grain_ids, labels, table, half)
    keep, labels = brick_sums(split, labels, half)
    core_a, labels, own = core_sum(
        keep, across_cores(send), [labels, displacement], "core_sum_a"
    )
    send, keep = cell_sums(CHUNKS[1], per_octant, ids, labels, table, half)
    flip = lax.axis_size("fe") // 4
    (kept, sent), own, send = plane_sum(
        across_plane(core_a), [own, send], [flip, flip], "plane_sum_a"
    )
    received = to_relative(sent, 0, 0, 0, flip)
    core_b = last_core_sum(keep, across_cores(send), own)
    while flip > 2:
        flip //= 2
        (kept, sent) = plane_sum([kept, received], [], [flip, flip], "height_sum_a")[0]
        received = to_relative(sent, 0, 0, 0, flip)
    first, *second = last_sum(kept, received, across_plane(core_b), 3)
    stress_new, nodal = element_update(
        first, across_height(second), displacement, stress_old, resistance, quad_weights
    )
    forces = nodal[0] + passed_along(nodal[1], "fe", 1)
    return (stress_new, forces)


def solution(mesh):
    placed = (
        P(None, ("ca", "fe")),
        P(),
        P(("ca", "fe")),
        P(("ca", "fe"), None),
        P(("ca", "fe")),
        P(None, ("ca", "fe"), None),
        P(None, None, ("ca", "fe")),
        P(None, None, ("ca", "fe")),
        P(None, ("ca", "fe")),
    )
    return jax.shard_map(
        body,
        mesh=mesh,
        in_specs=placed,
        out_specs=(P(None, None, ("ca", "fe")), P(None, ("ca", "fe"), None)),
        check_vma=False,
    )
```

```python
import functools
import functools
import math

import jax
import jax.numpy as jnp
import ml_dtypes
import numpy as np
from jax import lax
from jax.experimental import pallas as pl
from jax.experimental.pallas import tpu as pltpu
from jax.sharding import PartitionSpec as P

GX = 15
LANES = 128
COLUMNS = 256
CHUNKS = ((0, 6), (6, 2))
QUANTUM = float((1 << 15) - 1)

SLIP_PLANES = [
    [value / math.sqrt(3.0) for value in row]
    for row in [[1, 1, 1]] * 3 + [[-1, 1, 1]] * 3 + [[1, -1, 1]] * 3 + [[1, 1, -1]] * 3
]
SLIP_DIRECTIONS = [
    [value / math.sqrt(2.0) for value in row]
    for row in [
        [0, 1, -1],
        [1, 0, -1],
        [1, -1, 0],
        [0, 1, -1],
        [1, 0, 1],
        [1, 1, 0],
        [0, 1, 1],
        [1, 0, -1],
        [1, 1, 0],
        [0, 1, 1],
        [1, 0, 1],
        [1, -1, 0],
    ]
]
LAMBDA_ELASTIC = 1.5
SHEAR_MODULUS = 1.0
RATE_STEP = 0.1
FIXED_POINT = 65536.0


def passed_along(block, axis, distance):
    devices = range(lax.axis_size(axis))
    route = [(i - distance, i) for i in devices if i - distance in devices]
    return lax.ppermute(block, axis, route)


def shape_gradients():
    grad_table = [[[0.0, 0.0, 0.0] for corner in range(8)] for quadrature in range(8)]
    point_offset = 1.0 / math.sqrt(3.0)
    for quadrature in range(8):
        natural = [
            (2 * (quadrature >> shift_bits & 1) - 1) * point_offset for shift_bits in (2, 1, 0)
        ]
        for corner in range(8):
            sign_list = [2 * (corner >> shift_bits & 1) - 1 for shift_bits in (2, 1, 0)]
            factors = [1.0 + sign_list[axis_id] * natural[axis_id] for axis_id in range(3)]
            for direction in range(3):
                others = 1.0
                for axis_id in range(3):
                    if axis_id != direction:
                        others = others * factors[axis_id]
                grad_table[quadrature][corner][direction] = (
                    2.0 * sign_list[direction] * others / 8.0
                )
    return grad_table


def cos_sin(angle):
    square = angle * angle
    cosine = 1.0 / math.factorial(12)
    for power in (10, 8, 6, 4, 2, 0):
        cosine = cosine * square + (-1.0) ** (power // 2) / math.factorial(power)
    sine = 1.0 / math.factorial(13)
    for power in (11, 9, 7, 5, 3, 1):
        sine = sine * square + (-1.0) ** (power // 2) / math.factorial(power)
    return cosine, sine * angle


def rotation_coordinates(euler):
    cos_one, sin_one = cos_sin(0.5 * euler[0 : 0 + 1])
    cos_mid, sin_mid = cos_sin(0.5 * euler[1 : 1 + 1])
    cos_two, sin_two = cos_sin(0.5 * euler[2 : 2 + 1])
    w = cos_mid * (cos_one * cos_two - sin_one * sin_two)
    factor = jnp.where(w < 0.0, -QUANTUM, QUANTUM) / (1.0 + jnp.abs(w))
    x = sin_mid * (cos_one * cos_two + sin_one * sin_two) * factor
    y = sin_mid * (sin_one * cos_two - cos_one * sin_two) * factor
    z = cos_mid * (sin_one * cos_two + cos_one * sin_two) * factor
    x, y, z = [
        jnp.clip(jnp.round(value), -QUANTUM, QUANTUM).astype(jnp.int32) for value in (x, y, z)
    ]
    return [x, y, z]


def table_kernel(euler_ref, table_ref):
    at = 0
    for coordinate in rotation_coordinates(euler_ref[...]):
        for row in range(0, coordinate.shape[1] // LANES, 2):
            low = coordinate[:, row * LANES : (row + 1) * LANES]
            high = coordinate[:, (row + 1) * LANES : (row + 2) * LANES]
            table_ref[at] = jnp.broadcast_to(lax.shift_left(high, 16) | (low & 0xFFFF), (8, LANES))
            at += 1


def rotation_table(euler_angles):
    height = euler_angles.shape[1] // LANES * 3 // 2
    return pl.pallas_call(
        table_kernel,
        out_shape=jax.ShapeDtypeStruct((height, 8, LANES), jnp.int32),
        compiler_params=pltpu.CompilerParams(vmem_limit_bytes=8 * 1024 * 1024),
        cost_estimate=pl.CostEstimate(flops=10**6, bytes_accessed=10**7, transcendentals=0),
        name="rotation_table",
    )(euler_angles)


def looked_up(table_ref, first_row, rows, lane, bits):
    if rows == 1:
        return lax.gather(
            table_ref[first_row],
            lane,
            lax.GatherDimensionNumbers(
                offset_dims=(),
                collapsed_slice_dims=(1,),
                start_index_map=(1,),
                operand_batching_dims=(0,),
                start_indices_batching_dims=(0,),
            ),
            slice_sizes=(1, 1),
            mode=lax.GatherScatterMode.PROMISE_IN_BOUNDS,
        )
    half = rows // 2
    level = half.bit_length() - 1
    low = looked_up(table_ref, first_row, half, lane, bits)
    high = looked_up(table_ref, first_row + half, half, lane, bits)
    return jnp.where(bits[level], high, low)


def looked_up_words(table_ref, ids):
    lane = (ids & (LANES - 1))[:, :, None]
    row = lax.shift_right_logical(ids, 7)
    words = table_ref.shape[0] // 3
    bits = [(row & (2 << level)) != 0 for level in range(words.bit_length() - 1)]
    shift = lax.shift_left((row & 1) ^ 1, 4)
    return [
        lax.shift_left(looked_up(table_ref, words * axis, words, lane, bits), shift)
        for axis in range(3)
    ]


def rotation_products(words):
    x, y, z = [lax.shift_right_arithmetic(word, 16).astype(jnp.float32) for word in words]
    length = (x * x + y * y + z * z) * (0.5 / (QUANTUM * QUANTUM)) + 0.5
    scale = pl.reciprocal(length, approx=True)
    scale = scale * (2.0 - length * scale)
    w = scale - 1.0
    x, y, z = x * scale, y * scale, z * scale
    return [x * x, y * y, z * z, x * y, x * z, y * z, w * x, w * y, w * z]


ENTRIES = (
    ((1, -1.0), (2, -1.0)),
    ((3, 1.0), (8, -1.0)),
    ((4, 1.0), (7, 1.0)),
    ((3, 1.0), (8, 1.0)),
    ((0, -1.0), (2, -1.0)),
    ((5, 1.0), (6, -1.0)),
    ((4, 1.0), (7, -1.0)),
    ((5, 1.0), (6, 1.0)),
    ((0, -1.0), (1, -1.0)),
)


def remainder(value, divisor):
    return value - value // divisor * divisor


def cell_sum_kernel(
    octants,
    per_octant,
    ids_ref,
    label_ref,
    table_ref,
    *refs,
):
    first, count = octants
    start = ids_ref.shape[0] - (8 - first) * per_octant
    tile_ref, raw_ref, place_ref, masked_ref = refs[-4:]
    if first + count < 8:
        label_out_ref, send_ref, split_ref, rest_ref = refs[:-4]
        label_out_ref[...] = label_ref[...]
        rest_ref[...] = ids_ref[pl.ds(ids_ref.shape[0] - rest_ref.shape[0], rest_ref.shape[0]), :]
        targets = [(send_ref.shape[0], send_ref)]
    else:
        send_ref, keep_ref, split_ref = refs[:-4]
        targets = [(send_ref.shape[0], send_ref), (0, keep_ref)]
    groups = tile_ref.shape[1] // 8
    rows_left = count * per_octant - 8 * (groups - 1)
    turns = count // math.gcd(count, 8)
    rows = send_ref.shape[1]
    width = masked_ref.shape[1]
    pairs = ids_ref.shape[1] // width

    out_row = lax.broadcasted_iota(jnp.int32, (rows, raw_ref.shape[0]), 0)
    raw_row = lax.broadcasted_iota(jnp.int32, (rows, raw_ref.shape[0]), 1)
    entry, product = out_row // count, raw_row // (8 * turns)
    fold = jnp.zeros(out_row.shape, jnp.float32)
    for index, terms in enumerate(ENTRIES):
        for other, sign in terms:
            fold = jnp.where((entry == index) & (product == other), sign, fold)
    fold = jnp.where(remainder(out_row, count) == remainder(raw_row, count), fold, 0.0)
    fold = fold.astype(jnp.bfloat16)
    row = lax.broadcasted_iota(jnp.int32, (rows, width), 0)
    diagonal = (row // count == 0) | (row // count == 4) | (row // count == 8)
    constant = jnp.where(diagonal, float(per_octant), jnp.where(row < 9 * count, 0.0, 1.0))

    def lanes_of(pair):
        return pl.ds(pl.multiple_of(pair * width, width), width)

    def look_up(pair):
        for tile in range(width // LANES):
            lanes = pl.ds(pl.multiple_of(pair * width + tile * LANES, LANES), LANES)
            for octant in range(count):
                tile_ref[tile, pl.ds(octant, per_octant, stride=count), :] = ids_ref[
                    pl.ds(start + octant * per_octant, per_octant), lanes
                ]
            sums = [[jnp.zeros((8, LANES), jnp.float32)] * 9 for turn in range(turns)]
            found = None
            for group in range(groups + 1):
                last = found
                if group < groups:
                    ids = tile_ref[tile, pl.ds(8 * group, 8), :]
                    found = looked_up_words(table_ref, ids)
                if group == 0:
                    continue
                products = rotation_products(last)
                if group == groups and rows_left < 8:
                    there = lax.broadcasted_iota(jnp.int32, (8, LANES), 0) < rows_left
                    products = [jnp.where(there, value, 0.0) for value in products]
                turn = (group - 1) % turns
                sums[turn] = [total + value for total, value in zip(sums[turn], products)]
            scales = [2.0 / (QUANTUM * QUANTUM)] * 6 + [2.0 / QUANTUM] * 3
            raw_ref[:, lanes] = jnp.concatenate(
                [sums[turn][index] * scales[index] for index in range(9) for turn in range(turns)],
                axis=0,
            )

    def fold_entries(pair):
        lanes = lanes_of(pair)
        total = constant
        for part in three_parts(raw_ref[:, lanes]):
            total = total + jnp.dot(fold, part, preferred_element_type=jnp.float32)
        leading = total.astype(jnp.bfloat16).astype(jnp.float32)
        split_ref[:, lanes] = jnp.concatenate([leading, total - leading], axis=0).astype(
            jnp.bfloat16
        )

    def add_bricks(pair, counted):
        lanes = lanes_of(pair)
        column = lax.broadcasted_iota(jnp.int32, (COLUMNS, width), 0)
        chosen = (column == label_ref[:, lanes] & (COLUMNS - 1)).astype(jnp.bfloat16)
        place = jnp.where(counted, place_ref[:, lanes], -1)
        for base, out_ref in targets:
            add_places(split_ref, lanes, place - base, chosen, out_ref, masked_ref)

    place_ref[...] = relative_places(label_ref[...])
    for base, out_ref in targets:
        out_ref[...] = jnp.zeros(out_ref.shape, jnp.float32)
    raw_ref[:, pl.ds(0, width)] = jnp.zeros((raw_ref.shape[0], width), jnp.float32)
    split_ref[:, pl.ds(0, width)] = jnp.zeros((split_ref.shape[0], width), jnp.bfloat16)

    def step(pair, carry):
        add_bricks(jnp.maximum(pair - 2, 0), pair >= 2)
        fold_entries(jnp.maximum(pair - 1, 0))
        look_up(pair)
        return carry

    lax.fori_loop(0, pairs, step, 0, unroll=2)
    add_bricks(pairs - 2, True)
    fold_entries(pairs - 1)
    add_bricks(pairs - 1, True)


def relative_places(labels):
    place = place_of(lax.shift_right_arithmetic(labels, COLUMNS.bit_length() - 1))
    return jnp.where(labels < 0, -1, place)


def add_places(split_ref, lanes, place, chosen, out_ref, masked_ref):
    split_rows = split_ref.shape[0]
    half_rows = split_rows // 2
    members = masked_ref.shape[0] // split_rows
    for first in range(0, out_ref.shape[0], members):
        split = split_ref[:, lanes]
        for member in range(members):
            mask = (place == first + member).astype(jnp.bfloat16)
            masked_ref[pl.ds(member * split_rows, split_rows), :] = split * mask
        product = lax.dot_general(
            masked_ref[...],
            chosen,
            (((1,), (1,)), ((), ())),
            preferred_element_type=jnp.float32,
        )
        for member in range(members):
            at = member * split_rows
            out_ref[first + member] += (
                product[at : at + half_rows] + product[at + half_rows : at + split_rows]
            )


def across_cores(block):
    groups = lax.axis_size("ca")
    return lax.ppermute(block, "ca", [(i, i ^ 1) for i in range(groups)])


def brick_sum_kernel(split_ref, label_ref, out_ref, label_out_ref, place_ref, masked_ref):
    labels = label_ref[...]
    label_out_ref[...] = labels
    place_ref[...] = relative_places(labels)
    bricks = split_ref.shape[1]
    column = lax.broadcasted_iota(jnp.int32, (COLUMNS, bricks), 0)
    chosen = (column == labels & (COLUMNS - 1)).astype(jnp.bfloat16)
    split_rows = split_ref.shape[0]
    half_rows = split_rows // 2
    members = masked_ref.shape[0] // split_rows

    def place_group(step, carry):
        for member in range(members):
            mask = (place_ref[...] == step * members + member).astype(jnp.bfloat16)
            masked_ref[pl.ds(member * split_rows, split_rows), :] = split_ref[...] * mask
        product = lax.dot_general(
            masked_ref[...],
            chosen,
            (((1,), (1,)), ((), ())),
            preferred_element_type=jnp.float32,
        )
        for member in range(members):
            at = member * split_rows
            out_ref[step * members + member] = (
                product[at : at + half_rows] + product[at + half_rows : at + split_rows]
            )
        return carry

    lax.fori_loop(0, out_ref.shape[0] // members, place_group, 0)


def place_of(owner):
    groups, members = lax.axis_size("ca"), lax.axis_size("fe")
    owner_ca = lax.shift_right_logical(owner, members.bit_length() - 1) ^ lax.axis_index("ca")
    owner_fe = (owner & (members - 1)) ^ lax.axis_index("fe")
    place = (owner_ca & 1) * (groups // 2) + lax.shift_right_logical(owner_ca, 1)
    place = place * 2 + (owner_fe & 1)
    return place * (members // 2) + lax.shift_right_logical(owner_fe, 1)


def cell_sums(octants, per_octant, ids, labels, table, places):
    first, count = octants
    bricks = ids.shape[1]
    rows = padded_rows(count)
    half = jax.ShapeDtypeStruct((places, rows, COLUMNS), jnp.float32)
    split = jax.ShapeDtypeStruct((2 * rows, bricks), jnp.bfloat16)
    scratch = []
    left = 8 - first - count
    if left:
        out_shape = [
            jax.ShapeDtypeStruct(labels.shape, jnp.int32),
            half,
            split,
            jax.ShapeDtypeStruct((-(-left * per_octant // 8) * 8, bricks), jnp.int32),
        ]
    else:
        out_shape = [half, half]
        scratch.append(pltpu.VMEM(split.shape, split.dtype))
    return pl.pallas_call(
        functools.partial(cell_sum_kernel, octants, per_octant),
        out_shape=out_shape,
        scratch_shapes=scratch
        + [
            pltpu.VMEM((2, -(-count * per_octant // 8) * 8, LANES), jnp.int32),
            pltpu.VMEM((72 * (count // math.gcd(count, 8)), bricks), jnp.float32),
        ]
        + brick_scratch(rows, bricks, places, 2 * LANES),
        compiler_params=pltpu.CompilerParams(vmem_limit_bytes=28 * 1024 * 1024),
        cost_estimate=pl.CostEstimate(
            flops=count * 4 * 10**9, bytes_accessed=count * 10**7, transcendentals=0
        ),
        name="cell_sums",
    )(ids, labels, table)


def padded_rows(count):
    return -(-9 * count // 8) * 8


def brick_scratch(rows, bricks, places, width):
    return [
        pltpu.VMEM((1, bricks), jnp.int32),
        pltpu.VMEM((min(16, places) * 2 * rows, width), jnp.bfloat16),
    ]


def brick_sums(split, labels, places):
    rows, bricks = split.shape
    return pl.pallas_call(
        brick_sum_kernel,
        out_shape=[
            jax.ShapeDtypeStruct((places, rows // 2, COLUMNS), jnp.float32),
            jax.ShapeDtypeStruct(labels.shape, jnp.int32),
        ],
        scratch_shapes=brick_scratch(rows // 2, bricks, places, bricks),
        compiler_params=pltpu.CompilerParams(vmem_limit_bytes=24 * 1024 * 1024),
        cost_estimate=pl.CostEstimate(
            flops=rows * 15 * 10**6, bytes_accessed=rows * 5 * 10**4, transcendentals=0
        ),
        name="brick_sums",
    )(split, labels)


def core_sum_kernel(passed, kept_ref, received_ref, *refs):
    outs = refs[passed:]
    for last in range(2):
        outs[last][...] = kept_ref[:, last] + received_ref[:, last]
    for i in range(passed):
        outs[2 + i][...] = refs[i][...]


def last_core_sum_kernel(kept_ref, received_ref, own_ref, *outs):
    for last, out_ref in enumerate(outs):
        out_ref[...] = kept_ref[:, last] + received_ref[:, last]
        pairs, rests, rows, columns = out_ref.shape
        out_ref[:, :, rows - 3 : rows, :] = jnp.zeros((pairs, rests, 3, columns), jnp.float32)
    for c in range(3):
        row = rows - 3 + c
        outs[1][0, :, row : row + 1, :] = jnp.broadcast_to(own_ref[c][None], (rests, 1, columns))


def core_sum(kept, received, passed, name):
    pairs, rests = lax.axis_size("ca") // 2, lax.axis_size("fe") // 2
    shape = (pairs, 2, rests) + kept.shape[1:]
    half = jax.ShapeDtypeStruct((pairs, rests) + kept.shape[1:], jnp.float32)
    return pl.pallas_call(
        functools.partial(core_sum_kernel, len(passed)),
        out_shape=[half, half]
        + [jax.ShapeDtypeStruct(array.shape, array.dtype) for array in passed],
        compiler_params=pltpu.CompilerParams(vmem_limit_bytes=16 * 1024 * 1024),
        name=name,
    )(kept.reshape(shape), received.reshape(shape), *passed)


def last_core_sum(kept, received, own):
    pairs, rests = lax.axis_size("ca") // 2, lax.axis_size("fe") // 2
    shape = (pairs, 2, rests) + kept.shape[1:]
    half = jax.ShapeDtypeStruct((pairs, rests) + kept.shape[1:], jnp.float32)
    return pl.pallas_call(
        last_core_sum_kernel,
        out_shape=[half, half],
        compiler_params=pltpu.CompilerParams(vmem_limit_bytes=16 * 1024 * 1024),
        name="core_sum_b",
    )(kept.reshape(shape), received.reshape(shape), own)


def plane_sum_kernel(sources, passed, *refs):
    outs = refs[sources + passed :]
    height = 0
    for out_ref in outs[: len(outs) - passed]:
        total = sum(ref[pl.ds(height, out_ref.shape[0])] for ref in refs[:sources])
        out_ref[...] = total
        height += out_ref.shape[0]
    for i in range(passed):
        outs[len(outs) - passed + i][...] = refs[sources + i][...]


def plane_sum(parts, passed, cuts, name):
    rest = parts[0].shape[1:]
    out = pl.pallas_call(
        functools.partial(plane_sum_kernel, len(parts), len(passed)),
        out_shape=[jax.ShapeDtypeStruct((cut,) + rest, jnp.float32) for cut in cuts]
        + [jax.ShapeDtypeStruct(array.shape, array.dtype) for array in passed],
        compiler_params=pltpu.CompilerParams(vmem_limit_bytes=16 * 1024 * 1024),
        name=name,
    )(*parts, *passed)
    return out[: len(cuts)], *out[len(cuts) :]


def last_sum_kernel(sources, kept_ref, received_ref, *refs):
    parts, outs = refs[:sources], refs[sources:]
    rows = kept_ref.shape[1]
    outs[0][...] = kept_ref[0] + received_ref[0]
    outs[2][0:rows, :] = kept_ref[1] + received_ref[1]
    for height, out_ref in enumerate(outs[1:]):
        first = out_ref.shape[0] - parts[0].shape[2]
        out_ref[first:, :] = sum(ref[0, height] for ref in parts)


def last_sum(kept, received, parts):
    heights, rows, columns = parts[0].shape[1:]
    part = jax.ShapeDtypeStruct((rows, columns), jnp.float32)
    both = jax.ShapeDtypeStruct((kept.shape[1] + rows, columns), jnp.float32)
    return pl.pallas_call(
        functools.partial(last_sum_kernel, len(parts)),
        out_shape=[jax.ShapeDtypeStruct(kept.shape[1:], jnp.float32), part, both]
        + [part] * (heights - 2),
        compiler_params=pltpu.CompilerParams(vmem_limit_bytes=16 * 1024 * 1024),
        name="last_sum",
    )(kept, received, *parts)


def to_relative(block, core, pair, last, rest):
    groups, members = lax.axis_size("ca"), lax.axis_size("fe")
    flip = (2 * pair + core) * members + 2 * rest + last
    return lax.ppermute(block, ("ca", "fe"), [(i, i ^ flip) for i in range(groups * members)])


def across_pairs(parts):
    return [parts[0]] + [to_relative(parts[pair], 0, pair, 0, 0) for pair in range(1, len(parts))]


def across_height(parts):
    return [parts[0]] + [to_relative(parts[rest], 0, 0, 0, rest) for rest in range(1, len(parts))]


def three_parts(value):
    first = value.astype(jnp.bfloat16)
    rest = value - first.astype(jnp.float32)
    second = rest.astype(jnp.bfloat16)
    third = (rest - second.astype(jnp.float32)).astype(jnp.bfloat16)
    return first, second, third


def joined(parts, axis):
    whole = jnp.concatenate([part.astype(jnp.float32) for part in parts], axis=axis)
    return whole.astype(jnp.bfloat16)


def six_terms(value):
    first, second, third = three_parts(value)
    return joined([first, second, third, first, second, first], 0)


def six_terms_of(table):
    first = table.astype(ml_dtypes.bfloat16)
    rest = table - first.astype(np.float32)
    second = rest.astype(ml_dtypes.bfloat16)
    third = (rest - second.astype(np.float32)).astype(ml_dtypes.bfloat16)
    terms = np.concatenate([first, first, first, second, second, third], axis=1)
    return np.pad(terms, ((0, -terms.shape[0] % 16), (0, 0)))


def dot_selected(value, selector, contract):
    rows = value.shape[0]
    product = lax.dot_general(
        joined(three_parts(value), 0),
        selector,
        (((1,), (contract,)), ((), ())),
        preferred_element_type=jnp.float32,
    )
    return product[:rows] + product[rows : 2 * rows] + product[2 * rows :]


def update_kernel(heights, *refs):
    first_ref, second_refs = refs[0], refs[1 : 1 + heights]
    own_ref, stress_ref, resistance_ref, weights_ref, table_ref, turned_ref = refs[1 + heights : -2]
    stress_out_ref, nodal_ref = refs[-2:]
    elements = stress_ref.shape[2]
    rows, second_rows = first_ref.shape[0], second_refs[0].shape[0]
    gathered = [
        first_ref[:, 0:elements] + second_refs[1][0:rows, 0:elements],
        sum(ref[ref.shape[0] - second_rows :, 0:elements] for ref in second_refs),
    ]
    counted = 9 * CHUNKS[1][1]
    counts = gathered[1][counted : counted + 1]
    per_brick = 1.0 / (8.0 * jnp.maximum(counts, 1.0))
    frames = [
        jnp.concatenate(
            [
                sums[count * k : count * (k + 1)]
                for sums, (first, count) in zip(gathered, CHUNKS)
            ],
            axis=0,
        )
        * per_brick
        for k in range(9)
    ]

    node = lax.broadcasted_iota(jnp.int32, (COLUMNS, elements), 0)
    element = lax.broadcasted_iota(jnp.int32, (COLUMNS, elements), 1)
    base = element + element // GX
    selectors = [
        (node == base + (step_y * (GX + 1) + step_x)).astype(jnp.bfloat16)
        for step_x in range(2)
        for step_y in range(2)
    ]
    corner = lax.broadcasted_iota(jnp.int32, (24, 1), 0) & 7
    upper_corner = (corner & 1) == 1
    height = lax.axis_index("fe") // 2
    above = height + (lax.axis_index("fe") & 1)
    upper = jnp.zeros((3, COLUMNS), jnp.float32)
    for flip, ref in enumerate(second_refs):
        wanted = (height ^ flip) == above
        upper = upper + jnp.where(wanted, ref[ref.shape[0] - 3 :, :], 0.0)
    values = jnp.where(
        upper_corner,
        jnp.concatenate(
            [jnp.broadcast_to(upper[c : c + 1], (8, COLUMNS)) for c in range(3)], axis=0
        ),
        jnp.concatenate([jnp.broadcast_to(own_ref[c], (8, COLUMNS)) for c in range(3)], axis=0),
    )
    corners = dot_selected(
        jnp.concatenate(
            [jnp.where(corner >> 1 == step, values, 0.0) for step in range(4)], axis=1
        ),
        jnp.concatenate(selectors, axis=0),
        0,
    )
    gradients = []
    for c in range(3):
        product = jnp.dot(
            table_ref[...],
            six_terms(corners[8 * c : 8 * c + 8]),
            preferred_element_type=jnp.float32,
        )
        gradients.append([product[8 * d : 8 * d + 8] for d in range(3)])
    strain = [
        gradients[0][0],
        gradients[1][1],
        gradients[2][2],
        0.5 * (gradients[1][2] + gradients[2][1]),
        0.5 * (gradients[0][2] + gradients[2][0]),
        0.5 * (gradients[0][1] + gradients[1][0]),
    ]
    volume = strain[0] + strain[1] + strain[2]
    trial = []
    for component in range(6):
        change = 2.0 * SHEAR_MODULUS * strain[component]
        if component < 3:
            change = change + LAMBDA_ELASTIC * volume
        trial.append(stress_ref[component] + change)
    correction = [jnp.zeros_like(trial[0]) for component in range(6)]
    for system in range(12):
        rotated_dir = [
            sum(
                frames[3 * row + axis_id] * SLIP_DIRECTIONS[system][axis_id]
                for axis_id in range(3)
                if SLIP_DIRECTIONS[system][axis_id] != 0.0
            )
            for row in range(3)
        ]
        rotated_normal = [
            sum(frames[3 * row + axis_id] * SLIP_PLANES[system][axis_id] for axis_id in range(3))
            for row in range(3)
        ]
        schmid = [
            rotated_dir[0] * rotated_normal[0],
            rotated_dir[1] * rotated_normal[1],
            rotated_dir[2] * rotated_normal[2],
            0.5 * (rotated_dir[1] * rotated_normal[2] + rotated_dir[2] * rotated_normal[1]),
            0.5 * (rotated_dir[0] * rotated_normal[2] + rotated_dir[2] * rotated_normal[0]),
            0.5 * (rotated_dir[0] * rotated_normal[1] + rotated_dir[1] * rotated_normal[0]),
        ]
        resolved = (
            trial[0] * schmid[0]
            + trial[1] * schmid[1]
            + trial[2] * schmid[2]
            + 2.0 * (trial[3] * schmid[3] + trial[4] * schmid[4] + trial[5] * schmid[5])
        )
        slip_ratio = resolved / resistance_ref[system]
        slip_step = RATE_STEP * slip_ratio * jnp.abs(slip_ratio)
        correction = [
            correction[component] + slip_step * schmid[component] for component in range(6)
        ]
    updated = [
        trial[component] - 2.0 * SHEAR_MODULUS * correction[component] for component in range(6)
    ]
    for component in range(6):
        stress_out_ref[component] = updated[component]
    point_scale = weights_ref[...].astype(jnp.float32) * (1.0 / (FIXED_POINT * 8.0))
    scaled = [value * point_scale for value in updated]
    forces = []
    for rows in [(0, 5, 4), (5, 1, 3), (4, 3, 2)]:
        forces.append(
            jnp.dot(
                turned_ref[...],
                six_terms(jnp.concatenate([scaled[row] for row in rows], axis=0)),
                preferred_element_type=jnp.float32,
            )[:8]
        )
    forces = jnp.concatenate(forces, axis=0)
    nodal = jnp.zeros((24, COLUMNS), jnp.float32)
    for step in range(4):
        part = jnp.where(corner >> 1 == step, forces, 0.0)
        nodal = nodal + dot_selected(part, selectors[step], 1)
    lower = jnp.where(upper_corner, 0.0, nodal)
    above = jnp.where(upper_corner, nodal, 0.0)
    for c in range(3):
        nodal_ref[0, c] = jnp.sum(lower[8 * c : 8 * c + 8], axis=0, keepdims=True)
        nodal_ref[1, c] = jnp.sum(above[8 * c : 8 * c + 8], axis=0, keepdims=True)


def element_update(first, second, own, stress_old, resistance, quad_weights):
    grad_table = shape_gradients()
    table = np.asarray(
        [
            [grad_table[quadrature][corner][direction] for corner in range(8)]
            for direction in range(3)
            for quadrature in range(8)
        ],
        dtype=np.float32,
    )
    tables = [jnp.asarray(six_terms_of(part)) for part in (table, table.T)]
    return pl.pallas_call(
        functools.partial(update_kernel, len(second)),
        out_shape=(
            jax.ShapeDtypeStruct(stress_old.shape, jnp.float32),
            jax.ShapeDtypeStruct((2,) + own.shape, jnp.float32),
        ),
        compiler_params=pltpu.CompilerParams(vmem_limit_bytes=8 * 1024 * 1024),
        name="stress_update",
    )(first, *second, own, stress_old, resistance, quad_weights, *tables)


def body(
    grain_ids,
    euler_angles,
    brick_active,
    brick_owner,
    brick_element,
    displacement,
    stress_old,
    resistance,
    quad_weights,
):
    half = lax.axis_size("ca") * lax.axis_size("fe") // 2
    bricks = grain_ids.shape[1]
    owner = lax.optimization_barrier(brick_owner.reshape(bricks))
    labels = jnp.where(brick_active > 0, owner * COLUMNS + brick_element, -1).reshape(1, bricks)
    per_octant = grain_ids.shape[0] // 8
    table = rotation_table(euler_angles)
    labels, send, split, ids = cell_sums(CHUNKS[0], per_octant, grain_ids, labels, table, half)
    keep, labels = brick_sums(split, labels, half)
    kept, sent, labels, own = core_sum(
        keep, across_cores(send), [labels, displacement], "core_sum_a"
    )
    received = to_relative(sent, 0, 0, 1, 0)
    send, keep = cell_sums(CHUNKS[1], per_octant, ids, labels, table, half)
    pairs, heights = lax.axis_size("ca") // 2, lax.axis_size("fe") // 2
    plane_a, own, send = plane_sum([kept, received], [own, send], [1] * pairs, "x_sum_a")
    plane_a = [part.reshape(part.shape[1:]) for part in across_pairs(plane_a)]
    kept_b, sent_b = last_core_sum(keep, across_cores(send), own)
    received_b = to_relative(sent_b, 0, 0, 1, 0)
    flip = heights // 2
    (kept, sent), kept_b = plane_sum(plane_a, [kept_b], [flip, flip], "y_sum_a")
    received = to_relative(sent, 0, 0, 0, flip)
    while flip > 2:
        flip //= 2
        (kept, sent) = plane_sum([kept, received], [], [flip, flip], "height_sum_a")[0]
        received = to_relative(sent, 0, 0, 0, flip)
    plane_b = across_pairs(plane_sum([kept_b, received_b], [], [1] * pairs, "x_sum_b")[0])
    first, *second = last_sum(kept, received, plane_b)
    stress_new, nodal = element_update(
        first, across_height(second), displacement, stress_old, resistance, quad_weights
    )
    forces = nodal[0] + passed_along(nodal[1], "fe", 1)
    return (stress_new, forces)


def solution(mesh):
    placed = (
        P(None, ("ca", "fe")),
        P(),
        P(("ca", "fe")),
        P(("ca", "fe"), None),
        P(("ca", "fe")),
        P(None, ("ca", "fe"), None),
        P(None, None, ("ca", "fe")),
        P(None, None, ("ca", "fe")),
        P(None, ("ca", "fe")),
    )
    return jax.shard_map(
        body,
        mesh=mesh,
        in_specs=placed,
        out_specs=(P(None, None, ("ca", "fe")), P(None, ("ca", "fe"), None)),
        check_vma=False,
    )
```

```python
import functools
import functools
import math

import jax
import jax.numpy as jnp
import ml_dtypes
import numpy as np
from jax import lax
from jax.experimental import pallas as pl
from jax.experimental.pallas import tpu as pltpu
from jax.sharding import PartitionSpec as P

GX = 15
LANES = 128
COLUMNS = 256
CHUNKS = ((0, 6), (6, 2))
QUANTUM = float((1 << 15) - 1)

SLIP_PLANES = [
    [value / math.sqrt(3.0) for value in row]
    for row in [[1, 1, 1]] * 3 + [[-1, 1, 1]] * 3 + [[1, -1, 1]] * 3 + [[1, 1, -1]] * 3
]
SLIP_DIRECTIONS = [
    [value / math.sqrt(2.0) for value in row]
    for row in [
        [0, 1, -1],
        [1, 0, -1],
        [1, -1, 0],
        [0, 1, -1],
        [1, 0, 1],
        [1, 1, 0],
        [0, 1, 1],
        [1, 0, -1],
        [1, 1, 0],
        [0, 1, 1],
        [1, 0, 1],
        [1, -1, 0],
    ]
]
LAMBDA_ELASTIC = 1.5
SHEAR_MODULUS = 1.0
RATE_STEP = 0.1
FIXED_POINT = 65536.0


def passed_along(block, axis, distance):
    devices = range(lax.axis_size(axis))
    route = [(i - distance, i) for i in devices if i - distance in devices]
    return lax.ppermute(block, axis, route)


def shape_gradients():
    grad_table = [[[0.0, 0.0, 0.0] for corner in range(8)] for quadrature in range(8)]
    point_offset = 1.0 / math.sqrt(3.0)
    for quadrature in range(8):
        natural = [
            (2 * (quadrature >> shift_bits & 1) - 1) * point_offset for shift_bits in (2, 1, 0)
        ]
        for corner in range(8):
            sign_list = [2 * (corner >> shift_bits & 1) - 1 for shift_bits in (2, 1, 0)]
            factors = [1.0 + sign_list[axis_id] * natural[axis_id] for axis_id in range(3)]
            for direction in range(3):
                others = 1.0
                for axis_id in range(3):
                    if axis_id != direction:
                        others = others * factors[axis_id]
                grad_table[quadrature][corner][direction] = (
                    2.0 * sign_list[direction] * others / 8.0
                )
    return grad_table


def cos_sin(angle):
    square = angle * angle
    cosine = 1.0 / math.factorial(12)
    for power in (10, 8, 6, 4, 2, 0):
        cosine = cosine * square + (-1.0) ** (power // 2) / math.factorial(power)
    sine = 1.0 / math.factorial(13)
    for power in (11, 9, 7, 5, 3, 1):
        sine = sine * square + (-1.0) ** (power // 2) / math.factorial(power)
    return cosine, sine * angle


def rotation_coordinates(euler):
    cos_one, sin_one = cos_sin(0.5 * euler[0 : 0 + 1])
    cos_mid, sin_mid = cos_sin(0.5 * euler[1 : 1 + 1])
    cos_two, sin_two = cos_sin(0.5 * euler[2 : 2 + 1])
    w = cos_mid * (cos_one * cos_two - sin_one * sin_two)
    factor = jnp.where(w < 0.0, -QUANTUM, QUANTUM) / (1.0 + jnp.abs(w))
    x = sin_mid * (cos_one * cos_two + sin_one * sin_two) * factor
    y = sin_mid * (sin_one * cos_two - cos_one * sin_two) * factor
    z = cos_mid * (sin_one * cos_two + cos_one * sin_two) * factor
    x, y, z = [
        jnp.clip(jnp.round(value), -QUANTUM, QUANTUM).astype(jnp.int32) for value in (x, y, z)
    ]
    return [x, y, z]


def table_kernel(euler_ref, table_ref):
    at = 0
    for coordinate in rotation_coordinates(euler_ref[...]):
        for row in range(0, coordinate.shape[1] // LANES, 2):
            low = coordinate[:, row * LANES : (row + 1) * LANES]
            high = coordinate[:, (row + 1) * LANES : (row + 2) * LANES]
            table_ref[at] = jnp.broadcast_to(lax.shift_left(high, 16) | (low & 0xFFFF), (8, LANES))
            at += 1


def rotation_table(euler_angles):
    height = euler_angles.shape[1] // LANES * 3 // 2
    return pl.pallas_call(
        table_kernel,
        out_shape=jax.ShapeDtypeStruct((height, 8, LANES), jnp.int32),
        compiler_params=pltpu.CompilerParams(vmem_limit_bytes=8 * 1024 * 1024),
        cost_estimate=pl.CostEstimate(flops=10**6, bytes_accessed=10**7, transcendentals=0),
        name="rotation_table",
    )(euler_angles)


def looked_up(table_ref, first_row, rows, lane, bits):
    if rows == 1:
        return lax.gather(
            table_ref[first_row],
            lane,
            lax.GatherDimensionNumbers(
                offset_dims=(),
                collapsed_slice_dims=(1,),
                start_index_map=(1,),
                operand_batching_dims=(0,),
                start_indices_batching_dims=(0,),
            ),
            slice_sizes=(1, 1),
            mode=lax.GatherScatterMode.PROMISE_IN_BOUNDS,
        )
    half = rows // 2
    level = half.bit_length() - 1
    low = looked_up(table_ref, first_row, half, lane, bits)
    high = looked_up(table_ref, first_row + half, half, lane, bits)
    return jnp.where(bits[level], high, low)


def looked_up_words(table_ref, ids):
    lane = (ids & (LANES - 1))[:, :, None]
    row = lax.shift_right_logical(ids, 7)
    words = table_ref.shape[0] // 3
    bits = [(row & (2 << level)) != 0 for level in range(words.bit_length() - 1)]
    shift = lax.shift_left((row & 1) ^ 1, 4)
    return [
        lax.shift_left(looked_up(table_ref, words * axis, words, lane, bits), shift)
        for axis in range(3)
    ]


def rotation_products(words):
    x, y, z = [lax.shift_right_arithmetic(word, 16).astype(jnp.float32) for word in words]
    length = (x * x + y * y + z * z) * (0.5 / (QUANTUM * QUANTUM)) + 0.5
    scale = pl.reciprocal(length, approx=True)
    scale = scale * (2.0 - length * scale)
    w = scale - 1.0
    x, y, z = x * scale, y * scale, z * scale
    return [x * x, y * y, z * z, x * y, x * z, y * z, w * x, w * y, w * z]


ENTRIES = (
    ((1, -1.0), (2, -1.0)),
    ((3, 1.0), (8, -1.0)),
    ((4, 1.0), (7, 1.0)),
    ((3, 1.0), (8, 1.0)),
    ((0, -1.0), (2, -1.0)),
    ((5, 1.0), (6, -1.0)),
    ((4, 1.0), (7, -1.0)),
    ((5, 1.0), (6, 1.0)),
    ((0, -1.0), (1, -1.0)),
)


def remainder(value, divisor):
    return value - value // divisor * divisor


def cell_sum_kernel(
    octants,
    per_octant,
    ids_ref,
    label_ref,
    table_ref,
    *refs,
):
    first, count = octants
    start = ids_ref.shape[0] - (8 - first) * per_octant
    tile_ref, raw_ref, place_ref, masked_ref = refs[-4:]
    if first + count < 8:
        label_out_ref, send_ref, split_ref, rest_ref = refs[:-4]
        label_out_ref[...] = label_ref[...]
        rest_ref[...] = ids_ref[pl.ds(ids_ref.shape[0] - rest_ref.shape[0], rest_ref.shape[0]), :]
        targets = [(send_ref.shape[0], send_ref)]
    else:
        send_ref, keep_ref, split_ref = refs[:-4]
        targets = [(send_ref.shape[0], send_ref), (0, keep_ref)]
    groups = tile_ref.shape[1] // 8
    rows_left = count * per_octant - 8 * (groups - 1)
    turns = count // math.gcd(count, 8)
    rows = send_ref.shape[1]
    width = masked_ref.shape[1]
    pairs = ids_ref.shape[1] // width

    out_row = lax.broadcasted_iota(jnp.int32, (rows, raw_ref.shape[0]), 0)
    raw_row = lax.broadcasted_iota(jnp.int32, (rows, raw_ref.shape[0]), 1)
    entry, product = out_row // count, raw_row // (8 * turns)
    fold = jnp.zeros(out_row.shape, jnp.float32)
    for index, terms in enumerate(ENTRIES):
        for other, sign in terms:
            fold = jnp.where((entry == index) & (product == other), sign, fold)
    fold = jnp.where(remainder(out_row, count) == remainder(raw_row, count), fold, 0.0)
    fold = fold.astype(jnp.bfloat16)
    row = lax.broadcasted_iota(jnp.int32, (rows, width), 0)
    diagonal = (row // count == 0) | (row // count == 4) | (row // count == 8)
    constant = jnp.where(diagonal, float(per_octant), jnp.where(row < 9 * count, 0.0, 1.0))

    def lanes_of(pair):
        return pl.ds(pl.multiple_of(pair * width, width), width)

    def look_up(pair):
        for tile in range(width // LANES):
            lanes = pl.ds(pl.multiple_of(pair * width + tile * LANES, LANES), LANES)
            for octant in range(count):
                tile_ref[tile, pl.ds(octant, per_octant, stride=count), :] = ids_ref[
                    pl.ds(start + octant * per_octant, per_octant), lanes
                ]
            sums = [[jnp.zeros((8, LANES), jnp.float32)] * 9 for turn in range(turns)]
            found = None
            for group in range(groups + 1):
                last = found
                if group < groups:
                    ids = tile_ref[tile, pl.ds(8 * group, 8), :]
                    found = looked_up_words(table_ref, ids)
                if group == 0:
                    continue
                products = rotation_products(last)
                if group == groups and rows_left < 8:
                    there = lax.broadcasted_iota(jnp.int32, (8, LANES), 0) < rows_left
                    products = [jnp.where(there, value, 0.0) for value in products]
                turn = (group - 1) % turns
                sums[turn] = [total + value for total, value in zip(sums[turn], products)]
            scales = [2.0 / (QUANTUM * QUANTUM)] * 6 + [2.0 / QUANTUM] * 3
            raw_ref[:, lanes] = jnp.concatenate(
                [sums[turn][index] * scales[index] for index in range(9) for turn in range(turns)],
                axis=0,
            )

    def fold_entries(pair):
        lanes = lanes_of(pair)
        total = constant
        for part in three_parts(raw_ref[:, lanes]):
            total = total + jnp.dot(fold, part, preferred_element_type=jnp.float32)
        leading = total.astype(jnp.bfloat16).astype(jnp.float32)
        split_ref[:, lanes] = jnp.concatenate([leading, total - leading], axis=0).astype(
            jnp.bfloat16
        )

    def add_bricks(pair, counted):
        lanes = lanes_of(pair)
        column = lax.broadcasted_iota(jnp.int32, (COLUMNS, width), 0)
        chosen = (column == label_ref[:, lanes] & (COLUMNS - 1)).astype(jnp.bfloat16)
        place = jnp.where(counted, place_ref[:, lanes], -1)
        for base, out_ref in targets:
            add_places(split_ref, lanes, place - base, chosen, out_ref, masked_ref)

    place_ref[...] = relative_places(label_ref[...])
    for base, out_ref in targets:
        out_ref[...] = jnp.zeros(out_ref.shape, jnp.float32)
    raw_ref[:, pl.ds(0, width)] = jnp.zeros((raw_ref.shape[0], width), jnp.float32)
    split_ref[:, pl.ds(0, width)] = jnp.zeros((split_ref.shape[0], width), jnp.bfloat16)

    def step(pair, carry):
        add_bricks(jnp.maximum(pair - 2, 0), pair >= 2)
        fold_entries(jnp.maximum(pair - 1, 0))
        look_up(pair)
        return carry

    lax.fori_loop(0, pairs, step, 0, unroll=4 if first == 0 else 2)
    add_bricks(pairs - 2, True)
    fold_entries(pairs - 1)
    add_bricks(pairs - 1, True)


def relative_places(labels):
    place = place_of(lax.shift_right_arithmetic(labels, COLUMNS.bit_length() - 1))
    return jnp.where(labels < 0, -1, place)


def add_places(split_ref, lanes, place, chosen, out_ref, masked_ref):
    split_rows = split_ref.shape[0]
    half_rows = split_rows // 2
    members = masked_ref.shape[0] // split_rows
    for first in range(0, out_ref.shape[0], members):
        split = split_ref[:, lanes]
        for member in range(members):
            mask = (place == first + member).astype(jnp.bfloat16)
            masked_ref[pl.ds(member * split_rows, split_rows), :] = split * mask
        product = lax.dot_general(
            masked_ref[...],
            chosen,
            (((1,), (1,)), ((), ())),
            preferred_element_type=jnp.float32,
        )
        for member in range(members):
            at = member * split_rows
            out_ref[first + member] += (
                product[at : at + half_rows] + product[at + half_rows : at + split_rows]
            )


def across_cores(block):
    groups = lax.axis_size("ca")
    return lax.ppermute(block, "ca", [(i, i ^ 1) for i in range(groups)])


def brick_sum_kernel(split_ref, label_ref, out_ref, label_out_ref, place_ref, masked_ref):
    labels = label_ref[...]
    label_out_ref[...] = labels
    place_ref[...] = relative_places(labels)
    bricks = split_ref.shape[1]
    column = lax.broadcasted_iota(jnp.int32, (COLUMNS, bricks), 0)
    chosen = (column == labels & (COLUMNS - 1)).astype(jnp.bfloat16)
    split_rows = split_ref.shape[0]
    half_rows = split_rows // 2
    members = masked_ref.shape[0] // split_rows

    def place_group(step, carry):
        for member in range(members):
            mask = (place_ref[...] == step * members + member).astype(jnp.bfloat16)
            masked_ref[pl.ds(member * split_rows, split_rows), :] = split_ref[...] * mask
        product = lax.dot_general(
            masked_ref[...],
            chosen,
            (((1,), (1,)), ((), ())),
            preferred_element_type=jnp.float32,
        )
        for member in range(members):
            at = member * split_rows
            out_ref[step * members + member] = (
                product[at : at + half_rows] + product[at + half_rows : at + split_rows]
            )
        return carry

    lax.fori_loop(0, out_ref.shape[0] // members, place_group, 0)


def place_of(owner):
    groups, members = lax.axis_size("ca"), lax.axis_size("fe")
    owner_ca = lax.shift_right_logical(owner, members.bit_length() - 1) ^ lax.axis_index("ca")
    owner_fe = (owner & (members - 1)) ^ lax.axis_index("fe")
    place = (owner_ca & 1) * (groups // 2) + lax.shift_right_logical(owner_ca, 1)
    place = place * 2 + (owner_fe & 1)
    return place * (members // 2) + lax.shift_right_logical(owner_fe, 1)


def cell_sums(octants, per_octant, ids, labels, table, places):
    first, count = octants
    bricks = ids.shape[1]
    rows = padded_rows(count)
    half = jax.ShapeDtypeStruct((places, rows, COLUMNS), jnp.float32)
    split = jax.ShapeDtypeStruct((2 * rows, bricks), jnp.bfloat16)
    scratch = []
    left = 8 - first - count
    if left:
        out_shape = [
            jax.ShapeDtypeStruct(labels.shape, jnp.int32),
            half,
            split,
            jax.ShapeDtypeStruct((-(-left * per_octant // 8) * 8, bricks), jnp.int32),
        ]
    else:
        out_shape = [half, half]
        scratch.append(pltpu.VMEM(split.shape, split.dtype))
    return pl.pallas_call(
        functools.partial(cell_sum_kernel, octants, per_octant),
        out_shape=out_shape,
        scratch_shapes=scratch
        + [
            pltpu.VMEM((2, -(-count * per_octant // 8) * 8, LANES), jnp.int32),
            pltpu.VMEM((72 * (count // math.gcd(count, 8)), bricks), jnp.float32),
        ]
        + brick_scratch(rows, bricks, places, 2 * LANES),
        compiler_params=pltpu.CompilerParams(vmem_limit_bytes=28 * 1024 * 1024),
        cost_estimate=pl.CostEstimate(
            flops=count * 4 * 10**9, bytes_accessed=count * 10**7, transcendentals=0
        ),
        name="cell_sums",
    )(ids, labels, table)


def padded_rows(count):
    return -(-9 * count // 8) * 8


def brick_scratch(rows, bricks, places, width):
    return [
        pltpu.VMEM((1, bricks), jnp.int32),
        pltpu.VMEM((min(16, places) * 2 * rows, width), jnp.bfloat16),
    ]


def brick_sums(split, labels, places):
    rows, bricks = split.shape
    return pl.pallas_call(
        brick_sum_kernel,
        out_shape=[
            jax.ShapeDtypeStruct((places, rows // 2, COLUMNS), jnp.float32),
            jax.ShapeDtypeStruct(labels.shape, jnp.int32),
        ],
        scratch_shapes=brick_scratch(rows // 2, bricks, places, bricks),
        compiler_params=pltpu.CompilerParams(vmem_limit_bytes=24 * 1024 * 1024),
        cost_estimate=pl.CostEstimate(
            flops=rows * 15 * 10**6, bytes_accessed=rows * 5 * 10**4, transcendentals=0
        ),
        name="brick_sums",
    )(split, labels)


def core_sum_kernel(passed, kept_ref, received_ref, *refs):
    outs = refs[passed:]
    for index, out_ref in enumerate(outs[: len(outs) - passed]):
        out_ref[...] = kept_ref[index] + received_ref[index]
    for i in range(passed):
        outs[len(outs) - passed + i][...] = refs[i][...]


def last_core_sum_kernel(kept_ref, received_ref, own_ref, *outs):
    for index, out_ref in enumerate(outs):
        out_ref[...] = kept_ref[index] + received_ref[index]
        for c in range(3):
            row = out_ref.shape[1] - 3 + c
            out_ref[:, row : row + 1, :] = jnp.broadcast_to(
                own_ref[c][None], (out_ref.shape[0], 1, COLUMNS)
            )


def last_core_sum(kept, received, own):
    pairs, rests = lax.axis_size("ca") // 2, lax.axis_size("fe") // 2
    shape = (2 * pairs, rests) + kept.shape[1:]
    return pl.pallas_call(
        last_core_sum_kernel,
        out_shape=[jax.ShapeDtypeStruct(shape[1:], jnp.float32)] * shape[0],
        compiler_params=pltpu.CompilerParams(vmem_limit_bytes=16 * 1024 * 1024),
        name="core_sum_b",
    )(kept.reshape(shape), received.reshape(shape), own)


def core_sum(kept, received, passed, name):
    pairs, rests = lax.axis_size("ca") // 2, lax.axis_size("fe") // 2
    shape = (2 * pairs, rests) + kept.shape[1:]
    out = pl.pallas_call(
        functools.partial(core_sum_kernel, len(passed)),
        out_shape=[jax.ShapeDtypeStruct(shape[1:], jnp.float32)] * shape[0]
        + [jax.ShapeDtypeStruct(array.shape, array.dtype) for array in passed],
        compiler_params=pltpu.CompilerParams(vmem_limit_bytes=16 * 1024 * 1024),
        name=name,
    )(kept.reshape(shape), received.reshape(shape), *passed)
    return out[: shape[0]], *out[shape[0] :]


def plane_sum_kernel(sources, passed, *refs):
    outs = refs[sources + passed :]
    height = 0
    for out_ref in outs[: len(outs) - passed]:
        out_ref[...] = sum(ref[pl.ds(height, out_ref.shape[0])] for ref in refs[:sources])
        height += out_ref.shape[0]
    for i in range(passed):
        outs[len(outs) - passed + i][...] = refs[sources + i][...]


def plane_sum(parts, passed, cuts, name):
    rest = parts[0].shape[1:]
    out = pl.pallas_call(
        functools.partial(plane_sum_kernel, len(parts), len(passed)),
        out_shape=[jax.ShapeDtypeStruct((cut,) + rest, jnp.float32) for cut in cuts]
        + [jax.ShapeDtypeStruct(array.shape, array.dtype) for array in passed],
        compiler_params=pltpu.CompilerParams(vmem_limit_bytes=16 * 1024 * 1024),
        name=name,
    )(*parts, *passed)
    return out[: len(cuts)], *out[len(cuts) :]


def last_sum_kernel(sources, spare, kept_ref, received_ref, *refs):
    parts, outs = refs[:sources], refs[sources:]
    rows = kept_ref.shape[1]
    outs[0][...] = kept_ref[0] + received_ref[0]
    outs[2][0:rows, :] = kept_ref[1] + received_ref[1]
    for height, out_ref in enumerate(outs[1:]):
        first = out_ref.shape[0] - parts[0].shape[1]
        out_ref[first:, :] = sum(ref[height] for ref in parts)
        out_ref[out_ref.shape[0] - spare :, :] = parts[-1][height, -spare:, :]


def last_sum(kept, received, parts, spare):
    heights, rows, columns = parts[0].shape
    part = jax.ShapeDtypeStruct((rows, columns), jnp.float32)
    both = jax.ShapeDtypeStruct((kept.shape[1] + rows, columns), jnp.float32)
    return pl.pallas_call(
        functools.partial(last_sum_kernel, len(parts), spare),
        out_shape=[jax.ShapeDtypeStruct(kept.shape[1:], jnp.float32), part, both]
        + [part] * (heights - 2),
        compiler_params=pltpu.CompilerParams(vmem_limit_bytes=16 * 1024 * 1024),
        name="last_sum",
    )(kept, received, *parts)


def to_relative(block, core, pair, last, rest):
    groups, members = lax.axis_size("ca"), lax.axis_size("fe")
    flip = (2 * pair + core) * members + 2 * rest + last
    return lax.ppermute(block, ("ca", "fe"), [(i, i ^ flip) for i in range(groups * members)])


def across_plane(parts):
    return [parts[0]] + [
        to_relative(parts[index], 0, index // 2, index % 2, 0)
        for index in range(len(parts) - 1, 0, -1)
    ]


def height_order(heights):
    return [0] + list(range(2, heights)) + [1]


def across_height(parts):
    order = height_order(len(parts))
    return [parts[0]] + [to_relative(parts[rest], 0, 0, 0, rest) for rest in order[1:]]


def three_parts(value):
    first = value.astype(jnp.bfloat16)
    rest = value - first.astype(jnp.float32)
    second = rest.astype(jnp.bfloat16)
    third = (rest - second.astype(jnp.float32)).astype(jnp.bfloat16)
    return first, second, third


def joined(parts, axis):
    whole = jnp.concatenate([part.astype(jnp.float32) for part in parts], axis=axis)
    return whole.astype(jnp.bfloat16)


def six_terms(value):
    first, second, third = three_parts(value)
    return joined([first, second, third, first, second, first], 0)


def six_terms_of(table):
    first = table.astype(ml_dtypes.bfloat16)
    rest = table - first.astype(np.float32)
    second = rest.astype(ml_dtypes.bfloat16)
    third = (rest - second.astype(np.float32)).astype(ml_dtypes.bfloat16)
    terms = np.concatenate([first, first, first, second, second, third], axis=1)
    return np.pad(terms, ((0, -terms.shape[0] % 16), (0, 0)))


def dot_selected(value, selector, contract):
    rows = value.shape[0]
    product = lax.dot_general(
        joined(three_parts(value), 0),
        selector,
        (((1,), (contract,)), ((), ())),
        preferred_element_type=jnp.float32,
    )
    return product[:rows] + product[rows : 2 * rows] + product[2 * rows :]


def update_kernel(heights, *refs):
    first_ref, second_refs = refs[0], refs[1 : 1 + heights]
    own_ref, stress_ref, resistance_ref, weights_ref, table_ref, turned_ref = refs[1 + heights : -2]
    stress_out_ref, nodal_ref = refs[-2:]
    elements = stress_ref.shape[2]
    rows, second_rows = first_ref.shape[0], second_refs[0].shape[0]
    gathered = [
        first_ref[:, 0:elements] + second_refs[-1][0:rows, 0:elements],
        sum(ref[ref.shape[0] - second_rows :, 0:elements] for ref in second_refs),
    ]
    counted = 9 * CHUNKS[1][1]
    counts = gathered[1][counted : counted + 1]
    per_brick = 1.0 / (8.0 * jnp.maximum(counts, 1.0))
    frames = [
        jnp.concatenate(
            [
                sums[count * k : count * (k + 1)]
                for sums, (first, count) in zip(gathered, CHUNKS)
            ],
            axis=0,
        )
        * per_brick
        for k in range(9)
    ]

    node = lax.broadcasted_iota(jnp.int32, (COLUMNS, elements), 0)
    element = lax.broadcasted_iota(jnp.int32, (COLUMNS, elements), 1)
    base = element + element // GX
    selectors = [
        (node == base + (step_y * (GX + 1) + step_x)).astype(jnp.bfloat16)
        for step_x in range(2)
        for step_y in range(2)
    ]
    corner = lax.broadcasted_iota(jnp.int32, (24, 1), 0) & 7
    upper_corner = (corner & 1) == 1
    height = lax.axis_index("fe") // 2
    above = height + (lax.axis_index("fe") & 1)
    upper = jnp.zeros((3, COLUMNS), jnp.float32)
    for flip, ref in zip(height_order(heights), second_refs):
        wanted = (height ^ flip) == above
        upper = upper + jnp.where(wanted, ref[ref.shape[0] - 3 :, :], 0.0)
    values = jnp.where(
        upper_corner,
        jnp.concatenate(
            [jnp.broadcast_to(upper[c : c + 1], (8, COLUMNS)) for c in range(3)], axis=0
        ),
        jnp.concatenate([jnp.broadcast_to(own_ref[c], (8, COLUMNS)) for c in range(3)], axis=0),
    )
    corners = dot_selected(
        jnp.concatenate(
            [jnp.where(corner >> 1 == step, values, 0.0) for step in range(4)], axis=1
        ),
        jnp.concatenate(selectors, axis=0),
        0,
    )
    gradients = []
    for c in range(3):
        product = jnp.dot(
            table_ref[...],
            six_terms(corners[8 * c : 8 * c + 8]),
            preferred_element_type=jnp.float32,
        )
        gradients.append([product[8 * d : 8 * d + 8] for d in range(3)])
    strain = [
        gradients[0][0],
        gradients[1][1],
        gradients[2][2],
        0.5 * (gradients[1][2] + gradients[2][1]),
        0.5 * (gradients[0][2] + gradients[2][0]),
        0.5 * (gradients[0][1] + gradients[1][0]),
    ]
    volume = strain[0] + strain[1] + strain[2]
    trial = []
    for component in range(6):
        change = 2.0 * SHEAR_MODULUS * strain[component]
        if component < 3:
            change = change + LAMBDA_ELASTIC * volume
        trial.append(stress_ref[component] + change)
    correction = [jnp.zeros_like(trial[0]) for component in range(6)]
    for system in range(12):
        rotated_dir = [
            sum(
                frames[3 * row + axis_id] * SLIP_DIRECTIONS[system][axis_id]
                for axis_id in range(3)
                if SLIP_DIRECTIONS[system][axis_id] != 0.0
            )
            for row in range(3)
        ]
        rotated_normal = [
            sum(frames[3 * row + axis_id] * SLIP_PLANES[system][axis_id] for axis_id in range(3))
            for row in range(3)
        ]
        schmid = [
            rotated_dir[0] * rotated_normal[0],
            rotated_dir[1] * rotated_normal[1],
            rotated_dir[2] * rotated_normal[2],
            0.5 * (rotated_dir[1] * rotated_normal[2] + rotated_dir[2] * rotated_normal[1]),
            0.5 * (rotated_dir[0] * rotated_normal[2] + rotated_dir[2] * rotated_normal[0]),
            0.5 * (rotated_dir[0] * rotated_normal[1] + rotated_dir[1] * rotated_normal[0]),
        ]
        resolved = (
            trial[0] * schmid[0]
            + trial[1] * schmid[1]
            + trial[2] * schmid[2]
            + 2.0 * (trial[3] * schmid[3] + trial[4] * schmid[4] + trial[5] * schmid[5])
        )
        slip_ratio = resolved / resistance_ref[system]
        slip_step = RATE_STEP * slip_ratio * jnp.abs(slip_ratio)
        correction = [
            correction[component] + slip_step * schmid[component] for component in range(6)
        ]
    updated = [
        trial[component] - 2.0 * SHEAR_MODULUS * correction[component] for component in range(6)
    ]
    for component in range(6):
        stress_out_ref[component] = updated[component]
    point_scale = weights_ref[...].astype(jnp.float32) * (1.0 / (FIXED_POINT * 8.0))
    scaled = [value * point_scale for value in updated]
    forces = []
    for rows in [(0, 5, 4), (5, 1, 3), (4, 3, 2)]:
        forces.append(
            jnp.dot(
                turned_ref[...],
                six_terms(jnp.concatenate([scaled[row] for row in rows], axis=0)),
                preferred_element_type=jnp.float32,
            )[:8]
        )
    forces = jnp.concatenate(forces, axis=0)
    nodal = jnp.zeros((24, COLUMNS), jnp.float32)
    for step in range(4):
        part = jnp.where(corner >> 1 == step, forces, 0.0)
        nodal = nodal + dot_selected(part, selectors[step], 1)
    lower = jnp.where(upper_corner, 0.0, nodal)
    above = jnp.where(upper_corner, nodal, 0.0)
    for c in range(3):
        nodal_ref[0, c] = jnp.sum(lower[8 * c : 8 * c + 8], axis=0, keepdims=True)
        nodal_ref[1, c] = jnp.sum(above[8 * c : 8 * c + 8], axis=0, keepdims=True)


def element_update(first, second, own, stress_old, resistance, quad_weights):
    grad_table = shape_gradients()
    table = np.asarray(
        [
            [grad_table[quadrature][corner][direction] for corner in range(8)]
            for direction in range(3)
            for quadrature in range(8)
        ],
        dtype=np.float32,
    )
    tables = [jnp.asarray(six_terms_of(part)) for part in (table, table.T)]
    return pl.pallas_call(
        functools.partial(update_kernel, len(second)),
        out_shape=(
            jax.ShapeDtypeStruct(stress_old.shape, jnp.float32),
            jax.ShapeDtypeStruct((2,) + own.shape, jnp.float32),
        ),
        compiler_params=pltpu.CompilerParams(vmem_limit_bytes=8 * 1024 * 1024),
        name="stress_update",
    )(first, *second, own, stress_old, resistance, quad_weights, *tables)


def body(
    grain_ids,
    euler_angles,
    brick_active,
    brick_owner,
    brick_element,
    displacement,
    stress_old,
    resistance,
    quad_weights,
):
    half = lax.axis_size("ca") * lax.axis_size("fe") // 2
    bricks = grain_ids.shape[1]
    owner = lax.optimization_barrier(brick_owner.reshape(bricks))
    labels = jnp.where(brick_active > 0, owner * COLUMNS + brick_element, -1).reshape(1, bricks)
    per_octant = grain_ids.shape[0] // 8
    table = rotation_table(euler_angles)
    labels, send, split, ids = cell_sums(CHUNKS[0], per_octant, grain_ids, labels, table, half)
    keep, labels = brick_sums(split, labels, half)
    core_a, labels, own = core_sum(
        keep, across_cores(send), [labels, displacement], "core_sum_a"
    )
    send, keep = cell_sums(CHUNKS[1], per_octant, ids, labels, table, half)
    flip = lax.axis_size("fe") // 4
    (kept, sent), own, send = plane_sum(
        across_plane(core_a), [own, send], [flip, flip], "plane_sum_a"
    )
    received = to_relative(sent, 0, 0, 0, flip)
    core_b = last_core_sum(keep, across_cores(send), own)
    while flip > 2:
        flip //= 2
        (kept, sent) = plane_sum([kept, received], [], [flip, flip], "height_sum_a")[0]
        received = to_relative(sent, 0, 0, 0, flip)
    first, *second = last_sum(kept, received, across_plane(core_b), 3)
    stress_new, nodal = element_update(
        first, across_height(second), displacement, stress_old, resistance, quad_weights
    )
    forces = nodal[0] + passed_along(nodal[1], "fe", 1)
    return (stress_new, forces)


def solution(mesh):
    placed = (
        P(None, ("ca", "fe")),
        P(),
        P(("ca", "fe")),
        P(("ca", "fe"), None),
        P(("ca", "fe")),
        P(None, ("ca", "fe"), None),
        P(None, None, ("ca", "fe")),
        P(None, None, ("ca", "fe")),
        P(None, ("ca", "fe")),
    )
    return jax.shard_map(
        body,
        mesh=mesh,
        in_specs=placed,
        out_specs=(P(None, None, ("ca", "fe")), P(None, ("ca", "fe"), None)),
        check_vma=False,
    )
```

```python
import functools
import functools
import math

import jax
import jax.numpy as jnp
import ml_dtypes
import numpy as np
from jax import lax
from jax.experimental import pallas as pl
from jax.experimental.pallas import tpu as pltpu
from jax.sharding import PartitionSpec as P

GX = 15
LANES = 128
COLUMNS = 256
CHUNKS = ((0, 6), (6, 2))
QUANTUM = float((1 << 15) - 1)

SLIP_PLANES = [
    [value / math.sqrt(3.0) for value in row]
    for row in [[1, 1, 1]] * 3 + [[-1, 1, 1]] * 3 + [[1, -1, 1]] * 3 + [[1, 1, -1]] * 3
]
SLIP_DIRECTIONS = [
    [value / math.sqrt(2.0) for value in row]
    for row in [
        [0, 1, -1],
        [1, 0, -1],
        [1, -1, 0],
        [0, 1, -1],
        [1, 0, 1],
        [1, 1, 0],
        [0, 1, 1],
        [1, 0, -1],
        [1, 1, 0],
        [0, 1, 1],
        [1, 0, 1],
        [1, -1, 0],
    ]
]
LAMBDA_ELASTIC = 1.5
SHEAR_MODULUS = 1.0
RATE_STEP = 0.1
FIXED_POINT = 65536.0


def passed_along(block, axis, distance):
    devices = range(lax.axis_size(axis))
    route = [(i - distance, i) for i in devices if i - distance in devices]
    return lax.ppermute(block, axis, route)


def shape_gradients():
    grad_table = [[[0.0, 0.0, 0.0] for corner in range(8)] for quadrature in range(8)]
    point_offset = 1.0 / math.sqrt(3.0)
    for quadrature in range(8):
        natural = [
            (2 * (quadrature >> shift_bits & 1) - 1) * point_offset for shift_bits in (2, 1, 0)
        ]
        for corner in range(8):
            sign_list = [2 * (corner >> shift_bits & 1) - 1 for shift_bits in (2, 1, 0)]
            factors = [1.0 + sign_list[axis_id] * natural[axis_id] for axis_id in range(3)]
            for direction in range(3):
                others = 1.0
                for axis_id in range(3):
                    if axis_id != direction:
                        others = others * factors[axis_id]
                grad_table[quadrature][corner][direction] = (
                    2.0 * sign_list[direction] * others / 8.0
                )
    return grad_table


def cos_sin(angle):
    square = angle * angle
    cosine = 1.0 / math.factorial(12)
    for power in (10, 8, 6, 4, 2, 0):
        cosine = cosine * square + (-1.0) ** (power // 2) / math.factorial(power)
    sine = 1.0 / math.factorial(13)
    for power in (11, 9, 7, 5, 3, 1):
        sine = sine * square + (-1.0) ** (power // 2) / math.factorial(power)
    return cosine, sine * angle


def rotation_coordinates(euler):
    cos_one, sin_one = cos_sin(0.5 * euler[0 : 0 + 1])
    cos_mid, sin_mid = cos_sin(0.5 * euler[1 : 1 + 1])
    cos_two, sin_two = cos_sin(0.5 * euler[2 : 2 + 1])
    w = cos_mid * (cos_one * cos_two - sin_one * sin_two)
    factor = jnp.where(w < 0.0, -QUANTUM, QUANTUM) / (1.0 + jnp.abs(w))
    x = sin_mid * (cos_one * cos_two + sin_one * sin_two) * factor
    y = sin_mid * (sin_one * cos_two - cos_one * sin_two) * factor
    z = cos_mid * (sin_one * cos_two + cos_one * sin_two) * factor
    x, y, z = [
        jnp.clip(jnp.round(value), -QUANTUM, QUANTUM).astype(jnp.int32) for value in (x, y, z)
    ]
    return [x, y, z]


def table_kernel(euler_ref, table_ref):
    at = 0
    for coordinate in rotation_coordinates(euler_ref[...]):
        for row in range(0, coordinate.shape[1] // LANES, 2):
            low = coordinate[:, row * LANES : (row + 1) * LANES]
            high = coordinate[:, (row + 1) * LANES : (row + 2) * LANES]
            table_ref[at] = jnp.broadcast_to(lax.shift_left(high, 16) | (low & 0xFFFF), (8, LANES))
            at += 1


def rotation_table(euler_angles):
    height = euler_angles.shape[1] // LANES * 3 // 2
    return pl.pallas_call(
        table_kernel,
        out_shape=jax.ShapeDtypeStruct((height, 8, LANES), jnp.int32),
        compiler_params=pltpu.CompilerParams(vmem_limit_bytes=8 * 1024 * 1024),
        cost_estimate=pl.CostEstimate(flops=10**6, bytes_accessed=10**7, transcendentals=0),
        name="rotation_table",
    )(euler_angles)


def looked_up(table_ref, first_row, rows, lane, bits):
    if rows == 1:
        return lax.gather(
            table_ref[first_row],
            lane,
            lax.GatherDimensionNumbers(
                offset_dims=(),
                collapsed_slice_dims=(1,),
                start_index_map=(1,),
                operand_batching_dims=(0,),
                start_indices_batching_dims=(0,),
            ),
            slice_sizes=(1, 1),
            mode=lax.GatherScatterMode.PROMISE_IN_BOUNDS,
        )
    half = rows // 2
    level = half.bit_length() - 1
    low = looked_up(table_ref, first_row, half, lane, bits)
    high = looked_up(table_ref, first_row + half, half, lane, bits)
    return jnp.where(bits[level], high, low)


def looked_up_words(table_ref, ids):
    lane = (ids & (LANES - 1))[:, :, None]
    row = lax.shift_right_logical(ids, 7)
    words = table_ref.shape[0] // 3
    bits = [(row & (2 << level)) != 0 for level in range(words.bit_length() - 1)]
    shift = lax.shift_left((row & 1) ^ 1, 4)
    return [
        lax.shift_left(looked_up(table_ref, words * axis, words, lane, bits), shift)
        for axis in range(3)
    ]


def rotation_products(words):
    x, y, z = [lax.shift_right_arithmetic(word, 16).astype(jnp.float32) for word in words]
    length = (x * x + y * y + z * z) * (0.5 / (QUANTUM * QUANTUM)) + 0.5
    scale = pl.reciprocal(length, approx=True)
    scale = scale * (2.0 - length * scale)
    w = scale - 1.0
    x, y, z = x * scale, y * scale, z * scale
    return [x * x, y * y, z * z, x * y, x * z, y * z, w * x, w * y, w * z]


ENTRIES = (
    ((1, -1.0), (2, -1.0)),
    ((3, 1.0), (8, -1.0)),
    ((4, 1.0), (7, 1.0)),
    ((3, 1.0), (8, 1.0)),
    ((0, -1.0), (2, -1.0)),
    ((5, 1.0), (6, -1.0)),
    ((4, 1.0), (7, -1.0)),
    ((5, 1.0), (6, 1.0)),
    ((0, -1.0), (1, -1.0)),
)


def remainder(value, divisor):
    return value - value // divisor * divisor


def cell_sum_kernel(
    octants,
    per_octant,
    ids_ref,
    label_ref,
    table_ref,
    *refs,
):
    first, count = octants
    start = ids_ref.shape[0] - (8 - first) * per_octant
    tile_ref, raw_ref, place_ref, masked_ref = refs[-4:]
    if first + count < 8:
        label_out_ref, send_ref, split_ref, rest_ref = refs[:-4]
        label_out_ref[...] = label_ref[...]
        rest_ref[...] = ids_ref[pl.ds(ids_ref.shape[0] - rest_ref.shape[0], rest_ref.shape[0]), :]
        targets = [(send_ref.shape[0], send_ref)]
    else:
        send_ref, keep_ref, split_ref = refs[:-4]
        targets = [(send_ref.shape[0], send_ref), (0, keep_ref)]
    groups = tile_ref.shape[1] // 8
    rows_left = count * per_octant - 8 * (groups - 1)
    turns = count // math.gcd(count, 8)
    rows = send_ref.shape[1]
    width = masked_ref.shape[1]
    pairs = ids_ref.shape[1] // width

    out_row = lax.broadcasted_iota(jnp.int32, (rows, raw_ref.shape[0]), 0)
    raw_row = lax.broadcasted_iota(jnp.int32, (rows, raw_ref.shape[0]), 1)
    entry, product = out_row // count, raw_row // (8 * turns)
    fold = jnp.zeros(out_row.shape, jnp.float32)
    for index, terms in enumerate(ENTRIES):
        for other, sign in terms:
            fold = jnp.where((entry == index) & (product == other), sign, fold)
    fold = jnp.where(remainder(out_row, count) == remainder(raw_row, count), fold, 0.0)
    fold = fold.astype(jnp.bfloat16)
    row = lax.broadcasted_iota(jnp.int32, (rows, width), 0)
    diagonal = (row // count == 0) | (row // count == 4) | (row // count == 8)
    constant = jnp.where(diagonal, float(per_octant), jnp.where(row < 9 * count, 0.0, 1.0))

    def lanes_of(pair):
        return pl.ds(pl.multiple_of(pair * width, width), width)

    def look_up(pair):
        for tile in range(width // LANES):
            lanes = pl.ds(pl.multiple_of(pair * width + tile * LANES, LANES), LANES)
            for octant in range(count):
                tile_ref[tile, pl.ds(octant, per_octant, stride=count), :] = ids_ref[
                    pl.ds(start + octant * per_octant, per_octant), lanes
                ]
            sums = [[jnp.zeros((8, LANES), jnp.float32)] * 9 for turn in range(turns)]
            found = None
            for group in range(groups + 1):
                last = found
                if group < groups:
                    ids = tile_ref[tile, pl.ds(8 * group, 8), :]
                    found = looked_up_words(table_ref, ids)
                if group == 0:
                    continue
                products = rotation_products(last)
                if group == groups and rows_left < 8:
                    there = lax.broadcasted_iota(jnp.int32, (8, LANES), 0) < rows_left
                    products = [jnp.where(there, value, 0.0) for value in products]
                turn = (group - 1) % turns
                sums[turn] = [total + value for total, value in zip(sums[turn], products)]
            scales = [2.0 / (QUANTUM * QUANTUM)] * 6 + [2.0 / QUANTUM] * 3
            raw_ref[:, lanes] = jnp.concatenate(
                [sums[turn][index] * scales[index] for index in range(9) for turn in range(turns)],
                axis=0,
            )

    def fold_entries(pair):
        lanes = lanes_of(pair)
        total = constant
        for part in three_parts(raw_ref[:, lanes]):
            total = total + jnp.dot(fold, part, preferred_element_type=jnp.float32)
        leading = total.astype(jnp.bfloat16).astype(jnp.float32)
        split_ref[:, lanes] = jnp.concatenate([leading, total - leading], axis=0).astype(
            jnp.bfloat16
        )

    def add_bricks(pair, counted):
        lanes = lanes_of(pair)
        column = lax.broadcasted_iota(jnp.int32, (COLUMNS, width), 0)
        chosen = (column == label_ref[:, lanes] & (COLUMNS - 1)).astype(jnp.bfloat16)
        place = jnp.where(counted, place_ref[:, lanes], -1)
        for base, out_ref in targets:
            add_places(split_ref, lanes, place - base, chosen, out_ref, masked_ref)

    place_ref[...] = relative_places(label_ref[...])
    for base, out_ref in targets:
        out_ref[...] = jnp.zeros(out_ref.shape, jnp.float32)
    raw_ref[:, pl.ds(0, width)] = jnp.zeros((raw_ref.shape[0], width), jnp.float32)
    split_ref[:, pl.ds(0, width)] = jnp.zeros((split_ref.shape[0], width), jnp.bfloat16)

    def step(pair, carry):
        add_bricks(jnp.maximum(pair - 2, 0), pair >= 2)
        fold_entries(jnp.maximum(pair - 1, 0))
        look_up(pair)
        return carry

    lax.fori_loop(0, pairs, step, 0, unroll=2)
    add_bricks(pairs - 2, True)
    fold_entries(pairs - 1)
    add_bricks(pairs - 1, True)


def relative_places(labels):
    place = place_of(lax.shift_right_arithmetic(labels, COLUMNS.bit_length() - 1))
    return jnp.where(labels < 0, -1, place)


def add_places(split_ref, lanes, place, chosen, out_ref, masked_ref):
    split_rows = split_ref.shape[0]
    half_rows = split_rows // 2
    members = masked_ref.shape[0] // split_rows
    for first in range(0, out_ref.shape[0], members):
        split = split_ref[:, lanes]
        for member in range(members):
            mask = (place == first + member).astype(jnp.bfloat16)
            masked_ref[pl.ds(member * split_rows, split_rows), :] = split * mask
        product = lax.dot_general(
            masked_ref[...],
            chosen,
            (((1,), (1,)), ((), ())),
            preferred_element_type=jnp.float32,
        )
        for member in range(members):
            at = member * split_rows
            out_ref[first + member] += (
                product[at : at + half_rows] + product[at + half_rows : at + split_rows]
            )


def across_cores(block):
    groups = lax.axis_size("ca")
    return lax.ppermute(block, "ca", [(i, i ^ 1) for i in range(groups)])


def brick_sum_kernel(split_ref, label_ref, out_ref, label_out_ref, place_ref, masked_ref):
    labels = label_ref[...]
    label_out_ref[...] = labels
    place_ref[...] = relative_places(labels)
    bricks = split_ref.shape[1]
    column = lax.broadcasted_iota(jnp.int32, (COLUMNS, bricks), 0)
    chosen = (column == labels & (COLUMNS - 1)).astype(jnp.bfloat16)
    split_rows = split_ref.shape[0]
    half_rows = split_rows // 2
    members = masked_ref.shape[0] // split_rows

    def place_group(step, carry):
        for member in range(members):
            mask = (place_ref[...] == step * members + member).astype(jnp.bfloat16)
            masked_ref[pl.ds(member * split_rows, split_rows), :] = split_ref[...] * mask
        product = lax.dot_general(
            masked_ref[...],
            chosen,
            (((1,), (1,)), ((), ())),
            preferred_element_type=jnp.float32,
        )
        for member in range(members):
            at = member * split_rows
            out_ref[step * members + member] = (
                product[at : at + half_rows] + product[at + half_rows : at + split_rows]
            )
        return carry

    lax.fori_loop(0, out_ref.shape[0] // members, place_group, 0)


def place_of(owner):
    groups, members = lax.axis_size("ca"), lax.axis_size("fe")
    owner_ca = lax.shift_right_logical(owner, members.bit_length() - 1) ^ lax.axis_index("ca")
    owner_fe = (owner & (members - 1)) ^ lax.axis_index("fe")
    place = (owner_ca & 1) * (groups // 2) + lax.shift_right_logical(owner_ca, 1)
    place = place * 2 + (owner_fe & 1)
    return place * (members // 2) + lax.shift_right_logical(owner_fe, 1)


def cell_sums(octants, per_octant, ids, labels, table, places):
    first, count = octants
    bricks = ids.shape[1]
    rows = padded_rows(count)
    half = jax.ShapeDtypeStruct((places, rows, COLUMNS), jnp.float32)
    split = jax.ShapeDtypeStruct((2 * rows, bricks), jnp.bfloat16)
    scratch = []
    left = 8 - first - count
    if left:
        out_shape = [
            jax.ShapeDtypeStruct(labels.shape, jnp.int32),
            half,
            split,
            jax.ShapeDtypeStruct((-(-left * per_octant // 8) * 8, bricks), jnp.int32),
        ]
    else:
        out_shape = [half, half]
        scratch.append(pltpu.VMEM(split.shape, split.dtype))
    return pl.pallas_call(
        functools.partial(cell_sum_kernel, octants, per_octant),
        out_shape=out_shape,
        scratch_shapes=scratch
        + [
            pltpu.VMEM((2, -(-count * per_octant // 8) * 8, LANES), jnp.int32),
            pltpu.VMEM((72 * (count // math.gcd(count, 8)), bricks), jnp.float32),
        ]
        + brick_scratch(rows, bricks, places, 2 * LANES),
        compiler_params=pltpu.CompilerParams(vmem_limit_bytes=28 * 1024 * 1024),
        cost_estimate=pl.CostEstimate(
            flops=count * 4 * 10**9, bytes_accessed=count * 10**7, transcendentals=0
        ),
        name="cell_sums",
    )(ids, labels, table)


def padded_rows(count):
    return -(-9 * count // 8) * 8


def brick_scratch(rows, bricks, places, width):
    return [
        pltpu.VMEM((1, bricks), jnp.int32),
        pltpu.VMEM((min(16, places) * 2 * rows, width), jnp.bfloat16),
    ]


def brick_sums(split, labels, places):
    rows, bricks = split.shape
    return pl.pallas_call(
        brick_sum_kernel,
        out_shape=[
            jax.ShapeDtypeStruct((places, rows // 2, COLUMNS), jnp.float32),
            jax.ShapeDtypeStruct(labels.shape, jnp.int32),
        ],
        scratch_shapes=brick_scratch(rows // 2, bricks, places, bricks),
        compiler_params=pltpu.CompilerParams(vmem_limit_bytes=24 * 1024 * 1024),
        cost_estimate=pl.CostEstimate(
            flops=rows * 15 * 10**6, bytes_accessed=rows * 5 * 10**4, transcendentals=0
        ),
        name="brick_sums",
    )(split, labels)


def core_sum_kernel(passed, kept_ref, received_ref, *refs):
    outs = refs[passed:]
    for index, out_ref in enumerate(outs[: len(outs) - passed]):
        out_ref[...] = kept_ref[index] + received_ref[index]
    for i in range(passed):
        outs[len(outs) - passed + i][...] = refs[i][...]


def last_core_sum_kernel(kept_ref, received_ref, own_ref, *outs):
    for index, out_ref in enumerate(outs):
        out_ref[...] = kept_ref[index] + received_ref[index]
        for c in range(3):
            row = out_ref.shape[1] - 3 + c
            out_ref[:, row : row + 1, :] = jnp.broadcast_to(
                own_ref[c][None], (out_ref.shape[0], 1, COLUMNS)
            )


def last_core_sum(kept, received, own):
    pairs, rests = lax.axis_size("ca") // 2, lax.axis_size("fe") // 2
    shape = (2 * pairs, rests) + kept.shape[1:]
    return pl.pallas_call(
        last_core_sum_kernel,
        out_shape=[jax.ShapeDtypeStruct(shape[1:], jnp.float32)] * shape[0],
        compiler_params=pltpu.CompilerParams(vmem_limit_bytes=16 * 1024 * 1024),
        name="core_sum_b",
    )(kept.reshape(shape), received.reshape(shape), own)


def core_sum(kept, received, passed, name):
    pairs, rests = lax.axis_size("ca") // 2, lax.axis_size("fe") // 2
    shape = (2 * pairs, rests) + kept.shape[1:]
    out = pl.pallas_call(
        functools.partial(core_sum_kernel, len(passed)),
        out_shape=[jax.ShapeDtypeStruct(shape[1:], jnp.float32)] * shape[0]
        + [jax.ShapeDtypeStruct(array.shape, array.dtype) for array in passed],
        compiler_params=pltpu.CompilerParams(vmem_limit_bytes=16 * 1024 * 1024),
        name=name,
    )(kept.reshape(shape), received.reshape(shape), *passed)
    return out[: shape[0]], *out[shape[0] :]


def plane_sum_kernel(sources, passed, *refs):
    outs = refs[sources + passed :]
    height = 0
    for out_ref in outs[: len(outs) - passed]:
        out_ref[...] = sum(ref[pl.ds(height, out_ref.shape[0])] for ref in refs[:sources])
        height += out_ref.shape[0]
    for i in range(passed):
        outs[len(outs) - passed + i][...] = refs[sources + i][...]


def plane_sum(parts, passed, cuts, name):
    rest = parts[0].shape[1:]
    out = pl.pallas_call(
        functools.partial(plane_sum_kernel, len(parts), len(passed)),
        out_shape=[jax.ShapeDtypeStruct((cut,) + rest, jnp.float32) for cut in cuts]
        + [jax.ShapeDtypeStruct(array.shape, array.dtype) for array in passed],
        compiler_params=pltpu.CompilerParams(vmem_limit_bytes=16 * 1024 * 1024),
        name=name,
    )(*parts, *passed)
    return out[: len(cuts)], *out[len(cuts) :]


def last_sum_kernel(sources, spare, kept_ref, received_ref, *refs):
    parts, outs = refs[:sources], refs[sources:]
    rows = kept_ref.shape[1]
    outs[0][...] = kept_ref[0] + received_ref[0]
    outs[2][0:rows, :] = kept_ref[1] + received_ref[1]
    for height, out_ref in enumerate(outs[1:]):
        first = out_ref.shape[0] - parts[0].shape[1]
        out_ref[first:, :] = sum(ref[height] for ref in parts)
        out_ref[out_ref.shape[0] - spare :, :] = parts[-1][height, -spare:, :]


def last_sum(kept, received, parts, spare):
    heights, rows, columns = parts[0].shape
    part = jax.ShapeDtypeStruct((rows, columns), jnp.float32)
    both = jax.ShapeDtypeStruct((kept.shape[1] + rows, columns), jnp.float32)
    return pl.pallas_call(
        functools.partial(last_sum_kernel, len(parts), spare),
        out_shape=[jax.ShapeDtypeStruct(kept.shape[1:], jnp.float32), part, both]
        + [part] * (heights - 2),
        compiler_params=pltpu.CompilerParams(vmem_limit_bytes=16 * 1024 * 1024),
        name="last_sum",
    )(kept, received, *parts)


def to_relative(block, core, pair, last, rest):
    groups, members = lax.axis_size("ca"), lax.axis_size("fe")
    flip = (2 * pair + core) * members + 2 * rest + last
    return lax.ppermute(block, ("ca", "fe"), [(i, i ^ flip) for i in range(groups * members)])


def across_plane(parts):
    return [parts[0]] + [
        to_relative(parts[index], 0, index // 2, index % 2, 0)
        for index in list(range(2, len(parts))) + [1]
    ]


def across_height(parts):
    return [parts[0]] + [to_relative(parts[rest], 0, 0, 0, rest) for rest in range(1, len(parts))]


def three_parts(value):
    first = value.astype(jnp.bfloat16)
    rest = value - first.astype(jnp.float32)
    second = rest.astype(jnp.bfloat16)
    third = (rest - second.astype(jnp.float32)).astype(jnp.bfloat16)
    return first, second, third


def joined(parts, axis):
    whole = jnp.concatenate([part.astype(jnp.float32) for part in parts], axis=axis)
    return whole.astype(jnp.bfloat16)


def six_terms(value):
    first, second, third = three_parts(value)
    return joined([first, second, third, first, second, first], 0)


def six_terms_of(table):
    first = table.astype(ml_dtypes.bfloat16)
    rest = table - first.astype(np.float32)
    second = rest.astype(ml_dtypes.bfloat16)
    third = (rest - second.astype(np.float32)).astype(ml_dtypes.bfloat16)
    terms = np.concatenate([first, first, first, second, second, third], axis=1)
    return np.pad(terms, ((0, -terms.shape[0] % 16), (0, 0)))


def dot_selected(value, selector, contract):
    rows = value.shape[0]
    product = lax.dot_general(
        joined(three_parts(value), 0),
        selector,
        (((1,), (contract,)), ((), ())),
        preferred_element_type=jnp.float32,
    )
    return product[:rows] + product[rows : 2 * rows] + product[2 * rows :]


def update_kernel(heights, *refs):
    first_ref, second_refs = refs[0], refs[1 : 1 + heights]
    own_ref, stress_ref, resistance_ref, weights_ref, table_ref, turned_ref = refs[1 + heights : -2]
    stress_out_ref, nodal_ref = refs[-2:]
    elements = stress_ref.shape[2]
    rows, second_rows = first_ref.shape[0], second_refs[0].shape[0]
    gathered = [
        first_ref[:, 0:elements] + second_refs[1][0:rows, 0:elements],
        sum(ref[ref.shape[0] - second_rows :, 0:elements] for ref in second_refs),
    ]
    counted = 9 * CHUNKS[1][1]
    counts = gathered[1][counted : counted + 1]
    per_brick = 1.0 / (8.0 * jnp.maximum(counts, 1.0))
    frames = [
        jnp.concatenate(
            [
                sums[count * k : count * (k + 1)]
                for sums, (first, count) in zip(gathered, CHUNKS)
            ],
            axis=0,
        )
        * per_brick
        for k in range(9)
    ]

    node = lax.broadcasted_iota(jnp.int32, (COLUMNS, elements), 0)
    element = lax.broadcasted_iota(jnp.int32, (COLUMNS, elements), 1)
    base = element + element // GX
    selectors = [
        (node == base + (step_y * (GX + 1) + step_x)).astype(jnp.bfloat16)
        for step_x in range(2)
        for step_y in range(2)
    ]
    corner = lax.broadcasted_iota(jnp.int32, (24, 1), 0) & 7
    upper_corner = (corner & 1) == 1
    height = lax.axis_index("fe") // 2
    above = height + (lax.axis_index("fe") & 1)
    upper = jnp.zeros((3, COLUMNS), jnp.float32)
    for flip, ref in enumerate(second_refs):
        wanted = (height ^ flip) == above
        upper = upper + jnp.where(wanted, ref[ref.shape[0] - 3 :, :], 0.0)
    values = jnp.where(
        upper_corner,
        jnp.concatenate(
            [jnp.broadcast_to(upper[c : c + 1], (8, COLUMNS)) for c in range(3)], axis=0
        ),
        jnp.concatenate([jnp.broadcast_to(own_ref[c], (8, COLUMNS)) for c in range(3)], axis=0),
    )
    corners = dot_selected(
        jnp.concatenate(
            [jnp.where(corner >> 1 == step, values, 0.0) for step in range(4)], axis=1
        ),
        jnp.concatenate(selectors, axis=0),
        0,
    )
    gradients = []
    for c in range(3):
        product = jnp.dot(
            table_ref[...],
            six_terms(corners[8 * c : 8 * c + 8]),
            preferred_element_type=jnp.float32,
        )
        gradients.append([product[8 * d : 8 * d + 8] for d in range(3)])
    strain = [
        gradients[0][0],
        gradients[1][1],
        gradients[2][2],
        0.5 * (gradients[1][2] + gradients[2][1]),
        0.5 * (gradients[0][2] + gradients[2][0]),
        0.5 * (gradients[0][1] + gradients[1][0]),
    ]
    volume = strain[0] + strain[1] + strain[2]
    trial = []
    for component in range(6):
        change = 2.0 * SHEAR_MODULUS * strain[component]
        if component < 3:
            change = change + LAMBDA_ELASTIC * volume
        trial.append(stress_ref[component] + change)
    correction = [jnp.zeros_like(trial[0]) for component in range(6)]
    for system in range(12):
        rotated_dir = [
            sum(
                frames[3 * row + axis_id] * SLIP_DIRECTIONS[system][axis_id]
                for axis_id in range(3)
                if SLIP_DIRECTIONS[system][axis_id] != 0.0
            )
            for row in range(3)
        ]
        rotated_normal = [
            sum(frames[3 * row + axis_id] * SLIP_PLANES[system][axis_id] for axis_id in range(3))
            for row in range(3)
        ]
        schmid = [
            rotated_dir[0] * rotated_normal[0],
            rotated_dir[1] * rotated_normal[1],
            rotated_dir[2] * rotated_normal[2],
            0.5 * (rotated_dir[1] * rotated_normal[2] + rotated_dir[2] * rotated_normal[1]),
            0.5 * (rotated_dir[0] * rotated_normal[2] + rotated_dir[2] * rotated_normal[0]),
            0.5 * (rotated_dir[0] * rotated_normal[1] + rotated_dir[1] * rotated_normal[0]),
        ]
        resolved = (
            trial[0] * schmid[0]
            + trial[1] * schmid[1]
            + trial[2] * schmid[2]
            + 2.0 * (trial[3] * schmid[3] + trial[4] * schmid[4] + trial[5] * schmid[5])
        )
        slip_ratio = resolved / resistance_ref[system]
        slip_step = RATE_STEP * slip_ratio * jnp.abs(slip_ratio)
        correction = [
            correction[component] + slip_step * schmid[component] for component in range(6)
        ]
    updated = [
        trial[component] - 2.0 * SHEAR_MODULUS * correction[component] for component in range(6)
    ]
    for component in range(6):
        stress_out_ref[component] = updated[component]
    point_scale = weights_ref[...].astype(jnp.float32) * (1.0 / (FIXED_POINT * 8.0))
    scaled = [value * point_scale for value in updated]
    forces = []
    for rows in [(0, 5, 4), (5, 1, 3), (4, 3, 2)]:
        forces.append(
            jnp.dot(
                turned_ref[...],
                six_terms(jnp.concatenate([scaled[row] for row in rows], axis=0)),
                preferred_element_type=jnp.float32,
            )[:8]
        )
    forces = jnp.concatenate(forces, axis=0)
    nodal = jnp.zeros((24, COLUMNS), jnp.float32)
    for step in range(4):
        part = jnp.where(corner >> 1 == step, forces, 0.0)
        nodal = nodal + dot_selected(part, selectors[step], 1)
    lower = jnp.where(upper_corner, 0.0, nodal)
    above = jnp.where(upper_corner, nodal, 0.0)
    for c in range(3):
        nodal_ref[0, c] = jnp.sum(lower[8 * c : 8 * c + 8], axis=0, keepdims=True)
        nodal_ref[1, c] = jnp.sum(above[8 * c : 8 * c + 8], axis=0, keepdims=True)


def element_update(first, second, own, stress_old, resistance, quad_weights):
    grad_table = shape_gradients()
    table = np.asarray(
        [
            [grad_table[quadrature][corner][direction] for corner in range(8)]
            for direction in range(3)
            for quadrature in range(8)
        ],
        dtype=np.float32,
    )
    tables = [jnp.asarray(six_terms_of(part)) for part in (table, table.T)]
    return pl.pallas_call(
        functools.partial(update_kernel, len(second)),
        out_shape=(
            jax.ShapeDtypeStruct(stress_old.shape, jnp.float32),
            jax.ShapeDtypeStruct((2,) + own.shape, jnp.float32),
        ),
        compiler_params=pltpu.CompilerParams(vmem_limit_bytes=8 * 1024 * 1024),
        name="stress_update",
    )(first, *second, own, stress_old, resistance, quad_weights, *tables)


def body(
    grain_ids,
    euler_angles,
    brick_active,
    brick_owner,
    brick_element,
    displacement,
    stress_old,
    resistance,
    quad_weights,
):
    half = lax.axis_size("ca") * lax.axis_size("fe") // 2
    bricks = grain_ids.shape[1]
    owner = lax.optimization_barrier(brick_owner.reshape(bricks))
    labels = jnp.where(brick_active > 0, owner * COLUMNS + brick_element, -1).reshape(1, bricks)
    per_octant = grain_ids.shape[0] // 8
    table = rotation_table(euler_angles)
    labels, send, split, ids = cell_sums(CHUNKS[0], per_octant, grain_ids, labels, table, half)
    keep, labels = brick_sums(split, labels, half)
    core_a, labels, own = core_sum(
        keep, across_cores(send), [labels, displacement], "core_sum_a"
    )
    send, keep = cell_sums(CHUNKS[1], per_octant, ids, labels, table, half)
    flip = lax.axis_size("fe") // 4
    (kept, sent), own, send = plane_sum(
        across_plane(core_a), [own, send], [flip, flip], "plane_sum_a"
    )
    received = to_relative(sent, 0, 0, 0, flip)
    core_b = last_core_sum(keep, across_cores(send), own)
    while flip > 2:
        flip //= 2
        (kept, sent) = plane_sum([kept, received], [], [flip, flip], "height_sum_a")[0]
        received = to_relative(sent, 0, 0, 0, flip)
    first, *second = last_sum(kept, received, across_plane(core_b), 3)
    stress_new, nodal = element_update(
        first, across_height(second), displacement, stress_old, resistance, quad_weights
    )
    forces = nodal[0] + passed_along(nodal[1], "fe", 1)
    return (stress_new, forces)


def solution(mesh):
    placed = (
        P(None, ("ca", "fe")),
        P(),
        P(("ca", "fe")),
        P(("ca", "fe"), None),
        P(("ca", "fe")),
        P(None, ("ca", "fe"), None),
        P(None, None, ("ca", "fe")),
        P(None, None, ("ca", "fe")),
        P(None, ("ca", "fe")),
    )
    return jax.shard_map(
        body,
        mesh=mesh,
        in_specs=placed,
        out_specs=(P(None, None, ("ca", "fe")), P(None, ("ca", "fe"), None)),
        check_vma=False,
    )
```

```python
import functools
import functools
import math

import jax
import jax.numpy as jnp
import ml_dtypes
import numpy as np
from jax import lax
from jax.experimental import pallas as pl
from jax.experimental.pallas import tpu as pltpu
from jax.sharding import PartitionSpec as P

GX = 15
LANES = 128
COLUMNS = 256
CHUNKS = ((0, 6), (6, 2))
QUANTUM = float((1 << 15) - 1)

SLIP_PLANES = [
    [value / math.sqrt(3.0) for value in row]
    for row in [[1, 1, 1]] * 3 + [[-1, 1, 1]] * 3 + [[1, -1, 1]] * 3 + [[1, 1, -1]] * 3
]
SLIP_DIRECTIONS = [
    [value / math.sqrt(2.0) for value in row]
    for row in [
        [0, 1, -1],
        [1, 0, -1],
        [1, -1, 0],
        [0, 1, -1],
        [1, 0, 1],
        [1, 1, 0],
        [0, 1, 1],
        [1, 0, -1],
        [1, 1, 0],
        [0, 1, 1],
        [1, 0, 1],
        [1, -1, 0],
    ]
]
LAMBDA_ELASTIC = 1.5
SHEAR_MODULUS = 1.0
RATE_STEP = 0.1
FIXED_POINT = 65536.0


def passed_along(block, axis, distance):
    devices = range(lax.axis_size(axis))
    route = [(i - distance, i) for i in devices if i - distance in devices]
    return lax.ppermute(block, axis, route)


def shape_gradients():
    grad_table = [[[0.0, 0.0, 0.0] for corner in range(8)] for quadrature in range(8)]
    point_offset = 1.0 / math.sqrt(3.0)
    for quadrature in range(8):
        natural = [
            (2 * (quadrature >> shift_bits & 1) - 1) * point_offset for shift_bits in (2, 1, 0)
        ]
        for corner in range(8):
            sign_list = [2 * (corner >> shift_bits & 1) - 1 for shift_bits in (2, 1, 0)]
            factors = [1.0 + sign_list[axis_id] * natural[axis_id] for axis_id in range(3)]
            for direction in range(3):
                others = 1.0
                for axis_id in range(3):
                    if axis_id != direction:
                        others = others * factors[axis_id]
                grad_table[quadrature][corner][direction] = (
                    2.0 * sign_list[direction] * others / 8.0
                )
    return grad_table


def cos_sin(angle):
    square = angle * angle
    cosine = 1.0 / math.factorial(12)
    for power in (10, 8, 6, 4, 2, 0):
        cosine = cosine * square + (-1.0) ** (power // 2) / math.factorial(power)
    sine = 1.0 / math.factorial(13)
    for power in (11, 9, 7, 5, 3, 1):
        sine = sine * square + (-1.0) ** (power // 2) / math.factorial(power)
    return cosine, sine * angle


def rotation_coordinates(euler):
    cos_one, sin_one = cos_sin(0.5 * euler[0 : 0 + 1])
    cos_mid, sin_mid = cos_sin(0.5 * euler[1 : 1 + 1])
    cos_two, sin_two = cos_sin(0.5 * euler[2 : 2 + 1])
    w = cos_mid * (cos_one * cos_two - sin_one * sin_two)
    factor = jnp.where(w < 0.0, -QUANTUM, QUANTUM) / (1.0 + jnp.abs(w))
    x = sin_mid * (cos_one * cos_two + sin_one * sin_two) * factor
    y = sin_mid * (sin_one * cos_two - cos_one * sin_two) * factor
    z = cos_mid * (sin_one * cos_two + cos_one * sin_two) * factor
    x, y, z = [
        jnp.clip(jnp.round(value), -QUANTUM, QUANTUM).astype(jnp.int32) for value in (x, y, z)
    ]
    return [x, y, z]


def table_kernel(euler_ref, table_ref):
    at = 0
    for coordinate in rotation_coordinates(euler_ref[...]):
        for row in range(0, coordinate.shape[1] // LANES, 2):
            low = coordinate[:, row * LANES : (row + 1) * LANES]
            high = coordinate[:, (row + 1) * LANES : (row + 2) * LANES]
            table_ref[at] = jnp.broadcast_to(lax.shift_left(high, 16) | (low & 0xFFFF), (8, LANES))
            at += 1


def rotation_table(euler_angles):
    height = euler_angles.shape[1] // LANES * 3 // 2
    return pl.pallas_call(
        table_kernel,
        out_shape=jax.ShapeDtypeStruct((height, 8, LANES), jnp.int32),
        compiler_params=pltpu.CompilerParams(vmem_limit_bytes=8 * 1024 * 1024),
        cost_estimate=pl.CostEstimate(flops=10**6, bytes_accessed=10**7, transcendentals=0),
        name="rotation_table",
    )(euler_angles)


def looked_up(table_ref, first_row, rows, lane, bits):
    if rows == 1:
        return lax.gather(
            table_ref[first_row],
            lane,
            lax.GatherDimensionNumbers(
                offset_dims=(),
                collapsed_slice_dims=(1,),
                start_index_map=(1,),
                operand_batching_dims=(0,),
                start_indices_batching_dims=(0,),
            ),
            slice_sizes=(1, 1),
            mode=lax.GatherScatterMode.PROMISE_IN_BOUNDS,
        )
    half = rows // 2
    level = half.bit_length() - 1
    low = looked_up(table_ref, first_row, half, lane, bits)
    high = looked_up(table_ref, first_row + half, half, lane, bits)
    return jnp.where(bits[level], high, low)


def looked_up_words(table_ref, ids):
    lane = (ids & (LANES - 1))[:, :, None]
    row = lax.shift_right_logical(ids, 7)
    words = table_ref.shape[0] // 3
    bits = [(row & (2 << level)) != 0 for level in range(words.bit_length() - 1)]
    shift = lax.shift_left((row & 1) ^ 1, 4)
    return [
        lax.shift_left(looked_up(table_ref, words * axis, words, lane, bits), shift)
        for axis in range(3)
    ]


def rotation_products(words):
    x, y, z = [lax.shift_right_arithmetic(word, 16).astype(jnp.float32) for word in words]
    length = (x * x + y * y + z * z) * (0.5 / (QUANTUM * QUANTUM)) + 0.5
    scale = pl.reciprocal(length, approx=True)
    scale = scale * (2.0 - length * scale)
    w = scale - 1.0
    x, y, z = x * scale, y * scale, z * scale
    return [x * x, y * y, z * z, x * y, x * z, y * z, w * x, w * y, w * z]


ENTRIES = (
    ((1, -1.0), (2, -1.0)),
    ((3, 1.0), (8, -1.0)),
    ((4, 1.0), (7, 1.0)),
    ((3, 1.0), (8, 1.0)),
    ((0, -1.0), (2, -1.0)),
    ((5, 1.0), (6, -1.0)),
    ((4, 1.0), (7, -1.0)),
    ((5, 1.0), (6, 1.0)),
    ((0, -1.0), (1, -1.0)),
)


def remainder(value, divisor):
    return value - value // divisor * divisor


def cell_sum_kernel(
    octants,
    per_octant,
    ids_ref,
    label_ref,
    table_ref,
    *refs,
):
    first, count = octants
    start = first * per_octant % 8
    tile_ref, raw_ref, place_ref, masked_ref = refs[-4:]
    if first + count < 8:
        label_out_ref, send_ref, split_ref = refs[:-4]
        label_out_ref[...] = label_ref[...]
        targets = [(send_ref.shape[0], send_ref)]
    else:
        send_ref, keep_ref, split_ref = refs[:-4]
        targets = [(send_ref.shape[0], send_ref), (0, keep_ref)]
    groups = tile_ref.shape[1] // 8
    rows_left = count * per_octant - 8 * (groups - 1)
    turns = count // math.gcd(count, 8)
    rows = send_ref.shape[1]
    width = masked_ref.shape[1]
    pairs = ids_ref.shape[1] // width

    out_row = lax.broadcasted_iota(jnp.int32, (rows, raw_ref.shape[0]), 0)
    raw_row = lax.broadcasted_iota(jnp.int32, (rows, raw_ref.shape[0]), 1)
    entry, product = out_row // count, raw_row // (8 * turns)
    fold = jnp.zeros(out_row.shape, jnp.float32)
    for index, terms in enumerate(ENTRIES):
        for other, sign in terms:
            fold = jnp.where((entry == index) & (product == other), sign, fold)
    fold = jnp.where(remainder(out_row, count) == remainder(raw_row, count), fold, 0.0)
    fold = fold.astype(jnp.bfloat16)
    row = lax.broadcasted_iota(jnp.int32, (rows, width), 0)
    diagonal = (row // count == 0) | (row // count == 4) | (row // count == 8)
    constant = jnp.where(diagonal, float(per_octant), jnp.where(row < 9 * count, 0.0, 1.0))

    def lanes_of(pair):
        return pl.ds(pl.multiple_of(pair * width, width), width)

    def look_up(pair):
        for tile in range(width // LANES):
            lanes = pl.ds(pl.multiple_of(pair * width + tile * LANES, LANES), LANES)
            for octant in range(count):
                tile_ref[tile, pl.ds(octant, per_octant, stride=count), :] = ids_ref[
                    pl.ds(start + octant * per_octant, per_octant), lanes
                ]
            sums = [[jnp.zeros((8, LANES), jnp.float32)] * 9 for turn in range(turns)]
            found = None
            for group in range(groups + 1):
                last = found
                if group < groups:
                    ids = tile_ref[tile, pl.ds(8 * group, 8), :]
                    found = looked_up_words(table_ref, ids)
                if group == 0:
                    continue
                products = rotation_products(last)
                if group == groups and rows_left < 8:
                    there = lax.broadcasted_iota(jnp.int32, (8, LANES), 0) < rows_left
                    products = [jnp.where(there, value, 0.0) for value in products]
                turn = (group - 1) % turns
                sums[turn] = [total + value for total, value in zip(sums[turn], products)]
            scales = [2.0 / (QUANTUM * QUANTUM)] * 6 + [2.0 / QUANTUM] * 3
            raw_ref[:, lanes] = jnp.concatenate(
                [sums[turn][index] * scales[index] for index in range(9) for turn in range(turns)],
                axis=0,
            )

    def fold_entries(pair):
        lanes = lanes_of(pair)
        total = constant
        for part in three_parts(raw_ref[:, lanes]):
            total = total + jnp.dot(fold, part, preferred_element_type=jnp.float32)
        leading = total.astype(jnp.bfloat16).astype(jnp.float32)
        split_ref[:, lanes] = jnp.concatenate([leading, total - leading], axis=0).astype(
            jnp.bfloat16
        )

    def add_bricks(pair, counted):
        lanes = lanes_of(pair)
        column = lax.broadcasted_iota(jnp.int32, (COLUMNS, width), 0)
        chosen = (column == label_ref[:, lanes] & (COLUMNS - 1)).astype(jnp.bfloat16)
        place = jnp.where(counted, place_ref[:, lanes], -1)
        for base, out_ref in targets:
            add_places(split_ref, lanes, place - base, chosen, out_ref, masked_ref)

    place_ref[...] = relative_places(label_ref[...])
    for base, out_ref in targets:
        out_ref[...] = jnp.zeros(out_ref.shape, jnp.float32)
    raw_ref[:, pl.ds(0, width)] = jnp.zeros((raw_ref.shape[0], width), jnp.float32)
    split_ref[:, pl.ds(0, width)] = jnp.zeros((split_ref.shape[0], width), jnp.bfloat16)

    def step(pair, carry):
        add_bricks(jnp.maximum(pair - 2, 0), pair >= 2)
        fold_entries(jnp.maximum(pair - 1, 0))
        look_up(pair)
        return carry

    lax.fori_loop(0, pairs, step, 0, unroll=2)
    add_bricks(pairs - 2, True)
    fold_entries(pairs - 1)
    add_bricks(pairs - 1, True)


def relative_places(labels):
    place = place_of(lax.shift_right_arithmetic(labels, COLUMNS.bit_length() - 1))
    return jnp.where(labels < 0, -1, place)


def add_places(split_ref, lanes, place, chosen, out_ref, masked_ref):
    split_rows = split_ref.shape[0]
    half_rows = split_rows // 2
    members = masked_ref.shape[0] // split_rows
    for first in range(0, out_ref.shape[0], members):
        split = split_ref[:, lanes]
        for member in range(members):
            mask = (place == first + member).astype(jnp.bfloat16)
            masked_ref[pl.ds(member * split_rows, split_rows), :] = split * mask
        product = lax.dot_general(
            masked_ref[...],
            chosen,
            (((1,), (1,)), ((), ())),
            preferred_element_type=jnp.float32,
        )
        for member in range(members):
            at = member * split_rows
            out_ref[first + member] += (
                product[at : at + half_rows] + product[at + half_rows : at + split_rows]
            )


def across_cores(block):
    groups = lax.axis_size("ca")
    return lax.ppermute(block, "ca", [(i, i ^ 1) for i in range(groups)])


def brick_sum_kernel(split_ref, label_ref, out_ref, label_out_ref, place_ref, masked_ref):
    labels = label_ref[...]
    label_out_ref[...] = labels
    place_ref[...] = relative_places(labels)
    bricks = split_ref.shape[1]
    column = lax.broadcasted_iota(jnp.int32, (COLUMNS, bricks), 0)
    chosen = (column == labels & (COLUMNS - 1)).astype(jnp.bfloat16)
    split_rows = split_ref.shape[0]
    half_rows = split_rows // 2
    members = masked_ref.shape[0] // split_rows

    def place_group(step, carry):
        for member in range(members):
            mask = (place_ref[...] == step * members + member).astype(jnp.bfloat16)
            masked_ref[pl.ds(member * split_rows, split_rows), :] = split_ref[...] * mask
        product = lax.dot_general(
            masked_ref[...],
            chosen,
            (((1,), (1,)), ((), ())),
            preferred_element_type=jnp.float32,
        )
        for member in range(members):
            at = member * split_rows
            out_ref[step * members + member] = (
                product[at : at + half_rows] + product[at + half_rows : at + split_rows]
            )
        return carry

    lax.fori_loop(0, out_ref.shape[0] // members, place_group, 0)


def place_of(owner):
    groups, members = lax.axis_size("ca"), lax.axis_size("fe")
    owner_ca = lax.shift_right_logical(owner, members.bit_length() - 1) ^ lax.axis_index("ca")
    owner_fe = (owner & (members - 1)) ^ lax.axis_index("fe")
    place = (owner_ca & 1) * (groups // 2) + lax.shift_right_logical(owner_ca, 1)
    place = place * 2 + (owner_fe & 1)
    return place * (members // 2) + lax.shift_right_logical(owner_fe, 1)


def cell_sums(octants, per_octant, ids, labels, table, places):
    first, count = octants
    bricks = ids.shape[1]
    begin = first * per_octant // 8 * 8
    ids = ids[begin : -(-(first + count) * per_octant // 8) * 8]
    rows = padded_rows(count)
    half = jax.ShapeDtypeStruct((places, rows, COLUMNS), jnp.float32)
    split = jax.ShapeDtypeStruct((2 * rows, bricks), jnp.bfloat16)
    scratch = []
    left = 8 - first - count
    if left:
        out_shape = [
            jax.ShapeDtypeStruct(labels.shape, jnp.int32),
            half,
            split,
        ]
    else:
        out_shape = [half, half]
        scratch.append(pltpu.VMEM(split.shape, split.dtype))
    return pl.pallas_call(
        functools.partial(cell_sum_kernel, octants, per_octant),
        out_shape=out_shape,
        scratch_shapes=scratch
        + [
            pltpu.VMEM((2, -(-count * per_octant // 8) * 8, LANES), jnp.int32),
            pltpu.VMEM((72 * (count // math.gcd(count, 8)), bricks), jnp.float32),
        ]
        + brick_scratch(rows, bricks, places, 2 * LANES),
        compiler_params=pltpu.CompilerParams(vmem_limit_bytes=28 * 1024 * 1024),
        cost_estimate=pl.CostEstimate(
            flops=count * 4 * 10**9, bytes_accessed=count * 10**7, transcendentals=0
        ),
        name="cell_sums",
    )(ids, labels, table)


def padded_rows(count):
    return -(-9 * count // 8) * 8


def brick_scratch(rows, bricks, places, width):
    return [
        pltpu.VMEM((1, bricks), jnp.int32),
        pltpu.VMEM((min(16, places) * 2 * rows, width), jnp.bfloat16),
    ]


def brick_sums(split, labels, places):
    rows, bricks = split.shape
    return pl.pallas_call(
        brick_sum_kernel,
        out_shape=[
            jax.ShapeDtypeStruct((places, rows // 2, COLUMNS), jnp.float32),
            jax.ShapeDtypeStruct(labels.shape, jnp.int32),
        ],
        scratch_shapes=brick_scratch(rows // 2, bricks, places, bricks),
        compiler_params=pltpu.CompilerParams(vmem_limit_bytes=24 * 1024 * 1024),
        cost_estimate=pl.CostEstimate(
            flops=rows * 15 * 10**6, bytes_accessed=rows * 5 * 10**4, transcendentals=0
        ),
        name="brick_sums",
    )(split, labels)


def core_sum_kernel(passed, kept_ref, received_ref, *refs):
    outs = refs[passed:]
    for index, out_ref in enumerate(outs[: len(outs) - passed]):
        out_ref[...] = kept_ref[index] + received_ref[index]
    for i in range(passed):
        outs[len(outs) - passed + i][...] = refs[i][...]


def last_core_sum_kernel(kept_ref, received_ref, own_ref, *outs):
    for index, out_ref in enumerate(outs):
        out_ref[...] = kept_ref[index] + received_ref[index]
        for c in range(3):
            row = out_ref.shape[1] - 3 + c
            out_ref[:, row : row + 1, :] = jnp.broadcast_to(
                own_ref[c][None], (out_ref.shape[0], 1, COLUMNS)
            )


def last_core_sum(kept, received, own):
    pairs, rests = lax.axis_size("ca") // 2, lax.axis_size("fe") // 2
    shape = (2 * pairs, rests) + kept.shape[1:]
    return pl.pallas_call(
        last_core_sum_kernel,
        out_shape=[jax.ShapeDtypeStruct(shape[1:], jnp.float32)] * shape[0],
        compiler_params=pltpu.CompilerParams(vmem_limit_bytes=16 * 1024 * 1024),
        name="core_sum_b",
    )(kept.reshape(shape), received.reshape(shape), own)


def core_sum(kept, received, passed, name):
    pairs, rests = lax.axis_size("ca") // 2, lax.axis_size("fe") // 2
    shape = (2 * pairs, rests) + kept.shape[1:]
    out = pl.pallas_call(
        functools.partial(core_sum_kernel, len(passed)),
        out_shape=[jax.ShapeDtypeStruct(shape[1:], jnp.float32)] * shape[0]
        + [jax.ShapeDtypeStruct(array.shape, array.dtype) for array in passed],
        compiler_params=pltpu.CompilerParams(vmem_limit_bytes=16 * 1024 * 1024),
        name=name,
    )(kept.reshape(shape), received.reshape(shape), *passed)
    return out[: shape[0]], *out[shape[0] :]


def plane_sum_kernel(sources, passed, *refs):
    outs = refs[sources + passed :]
    height = 0
    for out_ref in outs[: len(outs) - passed]:
        out_ref[...] = sum(ref[pl.ds(height, out_ref.shape[0])] for ref in refs[:sources])
        height += out_ref.shape[0]
    for i in range(passed):
        outs[len(outs) - passed + i][...] = refs[sources + i][...]


def plane_sum(parts, passed, cuts, name):
    rest = parts[0].shape[1:]
    out = pl.pallas_call(
        functools.partial(plane_sum_kernel, len(parts), len(passed)),
        out_shape=[jax.ShapeDtypeStruct((cut,) + rest, jnp.float32) for cut in cuts]
        + [jax.ShapeDtypeStruct(array.shape, array.dtype) for array in passed],
        compiler_params=pltpu.CompilerParams(vmem_limit_bytes=16 * 1024 * 1024),
        name=name,
    )(*parts, *passed)
    return out[: len(cuts)], *out[len(cuts) :]


def last_sum_kernel(sources, spare, kept_ref, received_ref, *refs):
    parts, outs = refs[:sources], refs[sources:]
    rows = kept_ref.shape[1]
    outs[0][...] = kept_ref[0] + received_ref[0]
    outs[2][0:rows, :] = kept_ref[1] + received_ref[1]
    for height, out_ref in enumerate(outs[1:]):
        first = out_ref.shape[0] - parts[0].shape[1]
        out_ref[first:, :] = sum(ref[height] for ref in parts)
        out_ref[out_ref.shape[0] - spare :, :] = parts[-1][height, -spare:, :]


def last_sum(kept, received, parts, spare):
    heights, rows, columns = parts[0].shape
    part = jax.ShapeDtypeStruct((rows, columns), jnp.float32)
    both = jax.ShapeDtypeStruct((kept.shape[1] + rows, columns), jnp.float32)
    return pl.pallas_call(
        functools.partial(last_sum_kernel, len(parts), spare),
        out_shape=[jax.ShapeDtypeStruct(kept.shape[1:], jnp.float32), part, both]
        + [part] * (heights - 2),
        compiler_params=pltpu.CompilerParams(vmem_limit_bytes=16 * 1024 * 1024),
        name="last_sum",
    )(kept, received, *parts)


def to_relative(block, core, pair, last, rest):
    groups, members = lax.axis_size("ca"), lax.axis_size("fe")
    flip = (2 * pair + core) * members + 2 * rest + last
    return lax.ppermute(block, ("ca", "fe"), [(i, i ^ flip) for i in range(groups * members)])


def across_plane(parts):
    return [parts[0]] + [
        to_relative(parts[index], 0, index // 2, index % 2, 0)
        for index in range(len(parts) - 1, 0, -1)
    ]


def across_height(parts):
    return [parts[0]] + [to_relative(parts[rest], 0, 0, 0, rest) for rest in range(1, len(parts))]


def three_parts(value):
    first = value.astype(jnp.bfloat16)
    rest = value - first.astype(jnp.float32)
    second = rest.astype(jnp.bfloat16)
    third = (rest - second.astype(jnp.float32)).astype(jnp.bfloat16)
    return first, second, third


def joined(parts, axis):
    whole = jnp.concatenate([part.astype(jnp.float32) for part in parts], axis=axis)
    return whole.astype(jnp.bfloat16)


def six_terms(value):
    first, second, third = three_parts(value)
    return joined([first, second, third, first, second, first], 0)


def six_terms_of(table):
    first = table.astype(ml_dtypes.bfloat16)
    rest = table - first.astype(np.float32)
    second = rest.astype(ml_dtypes.bfloat16)
    third = (rest - second.astype(np.float32)).astype(ml_dtypes.bfloat16)
    terms = np.concatenate([first, first, first, second, second, third], axis=1)
    return np.pad(terms, ((0, -terms.shape[0] % 16), (0, 0)))


def dot_selected(value, selector, contract):
    rows = value.shape[0]
    product = lax.dot_general(
        joined(three_parts(value), 0),
        selector,
        (((1,), (contract,)), ((), ())),
        preferred_element_type=jnp.float32,
    )
    return product[:rows] + product[rows : 2 * rows] + product[2 * rows :]


def update_kernel(heights, *refs):
    first_ref, second_refs = refs[0], refs[1 : 1 + heights]
    own_ref, stress_ref, resistance_ref, weights_ref, table_ref, turned_ref = refs[1 + heights : -2]
    stress_out_ref, nodal_ref = refs[-2:]
    elements = stress_ref.shape[2]
    rows, second_rows = first_ref.shape[0], second_refs[0].shape[0]
    gathered = [
        first_ref[:, 0:elements] + second_refs[1][0:rows, 0:elements],
        sum(ref[ref.shape[0] - second_rows :, 0:elements] for ref in second_refs),
    ]
    counted = 9 * CHUNKS[1][1]
    counts = gathered[1][counted : counted + 1]
    per_brick = 1.0 / (8.0 * jnp.maximum(counts, 1.0))
    frames = [
        jnp.concatenate(
            [
                sums[count * k : count * (k + 1)]
                for sums, (first, count) in zip(gathered, CHUNKS)
            ],
            axis=0,
        )
        * per_brick
        for k in range(9)
    ]

    node = lax.broadcasted_iota(jnp.int32, (COLUMNS, elements), 0)
    element = lax.broadcasted_iota(jnp.int32, (COLUMNS, elements), 1)
    base = element + element // GX
    selectors = [
        (node == base + (step_y * (GX + 1) + step_x)).astype(jnp.bfloat16)
        for step_x in range(2)
        for step_y in range(2)
    ]
    corner = lax.broadcasted_iota(jnp.int32, (24, 1), 0) & 7
    upper_corner = (corner & 1) == 1
    height = lax.axis_index("fe") // 2
    above = height + (lax.axis_index("fe") & 1)
    upper = jnp.zeros((3, COLUMNS), jnp.float32)
    for flip, ref in enumerate(second_refs):
        wanted = (height ^ flip) == above
        upper = upper + jnp.where(wanted, ref[ref.shape[0] - 3 :, :], 0.0)
    values = jnp.where(
        upper_corner,
        jnp.concatenate(
            [jnp.broadcast_to(upper[c : c + 1], (8, COLUMNS)) for c in range(3)], axis=0
        ),
        jnp.concatenate([jnp.broadcast_to(own_ref[c], (8, COLUMNS)) for c in range(3)], axis=0),
    )
    corners = dot_selected(
        jnp.concatenate(
            [jnp.where(corner >> 1 == step, values, 0.0) for step in range(4)], axis=1
        ),
        jnp.concatenate(selectors, axis=0),
        0,
    )
    gradients = []
    for c in range(3):
        product = jnp.dot(
            table_ref[...],
            six_terms(corners[8 * c : 8 * c + 8]),
            preferred_element_type=jnp.float32,
        )
        gradients.append([product[8 * d : 8 * d + 8] for d in range(3)])
    strain = [
        gradients[0][0],
        gradients[1][1],
        gradients[2][2],
        0.5 * (gradients[1][2] + gradients[2][1]),
        0.5 * (gradients[0][2] + gradients[2][0]),
        0.5 * (gradients[0][1] + gradients[1][0]),
    ]
    volume = strain[0] + strain[1] + strain[2]
    trial = []
    for component in range(6):
        change = 2.0 * SHEAR_MODULUS * strain[component]
        if component < 3:
            change = change + LAMBDA_ELASTIC * volume
        trial.append(stress_ref[component] + change)
    correction = [jnp.zeros_like(trial[0]) for component in range(6)]
    for system in range(12):
        rotated_dir = [
            sum(
                frames[3 * row + axis_id] * SLIP_DIRECTIONS[system][axis_id]
                for axis_id in range(3)
                if SLIP_DIRECTIONS[system][axis_id] != 0.0
            )
            for row in range(3)
        ]
        rotated_normal = [
            sum(frames[3 * row + axis_id] * SLIP_PLANES[system][axis_id] for axis_id in range(3))
            for row in range(3)
        ]
        schmid = [
            rotated_dir[0] * rotated_normal[0],
            rotated_dir[1] * rotated_normal[1],
            rotated_dir[2] * rotated_normal[2],
            0.5 * (rotated_dir[1] * rotated_normal[2] + rotated_dir[2] * rotated_normal[1]),
            0.5 * (rotated_dir[0] * rotated_normal[2] + rotated_dir[2] * rotated_normal[0]),
            0.5 * (rotated_dir[0] * rotated_normal[1] + rotated_dir[1] * rotated_normal[0]),
        ]
        resolved = (
            trial[0] * schmid[0]
            + trial[1] * schmid[1]
            + trial[2] * schmid[2]
            + 2.0 * (trial[3] * schmid[3] + trial[4] * schmid[4] + trial[5] * schmid[5])
        )
        slip_ratio = resolved / resistance_ref[system]
        slip_step = RATE_STEP * slip_ratio * jnp.abs(slip_ratio)
        correction = [
            correction[component] + slip_step * schmid[component] for component in range(6)
        ]
    updated = [
        trial[component] - 2.0 * SHEAR_MODULUS * correction[component] for component in range(6)
    ]
    for component in range(6):
        stress_out_ref[component] = updated[component]
    point_scale = weights_ref[...].astype(jnp.float32) * (1.0 / (FIXED_POINT * 8.0))
    scaled = [value * point_scale for value in updated]
    forces = []
    for rows in [(0, 5, 4), (5, 1, 3), (4, 3, 2)]:
        forces.append(
            jnp.dot(
                turned_ref[...],
                six_terms(jnp.concatenate([scaled[row] for row in rows], axis=0)),
                preferred_element_type=jnp.float32,
            )[:8]
        )
    forces = jnp.concatenate(forces, axis=0)
    nodal = jnp.zeros((24, COLUMNS), jnp.float32)
    for step in range(4):
        part = jnp.where(corner >> 1 == step, forces, 0.0)
        nodal = nodal + dot_selected(part, selectors[step], 1)
    lower = jnp.where(upper_corner, 0.0, nodal)
    above = jnp.where(upper_corner, nodal, 0.0)
    for c in range(3):
        nodal_ref[0, c] = jnp.sum(lower[8 * c : 8 * c + 8], axis=0, keepdims=True)
        nodal_ref[1, c] = jnp.sum(above[8 * c : 8 * c + 8], axis=0, keepdims=True)


def element_update(first, second, own, stress_old, resistance, quad_weights):
    grad_table = shape_gradients()
    table = np.asarray(
        [
            [grad_table[quadrature][corner][direction] for corner in range(8)]
            for direction in range(3)
            for quadrature in range(8)
        ],
        dtype=np.float32,
    )
    tables = [jnp.asarray(six_terms_of(part)) for part in (table, table.T)]
    return pl.pallas_call(
        functools.partial(update_kernel, len(second)),
        out_shape=(
            jax.ShapeDtypeStruct(stress_old.shape, jnp.float32),
            jax.ShapeDtypeStruct((2,) + own.shape, jnp.float32),
        ),
        compiler_params=pltpu.CompilerParams(vmem_limit_bytes=8 * 1024 * 1024),
        name="stress_update",
    )(first, *second, own, stress_old, resistance, quad_weights, *tables)


def body(
    grain_ids,
    euler_angles,
    brick_active,
    brick_owner,
    brick_element,
    displacement,
    stress_old,
    resistance,
    quad_weights,
):
    half = lax.axis_size("ca") * lax.axis_size("fe") // 2
    bricks = grain_ids.shape[1]
    owner = lax.optimization_barrier(brick_owner.reshape(bricks))
    labels = jnp.where(brick_active > 0, owner * COLUMNS + brick_element, -1).reshape(1, bricks)
    per_octant = grain_ids.shape[0] // 8
    table = rotation_table(euler_angles)
    labels, send, split = cell_sums(CHUNKS[0], per_octant, grain_ids, labels, table, half)
    keep, labels = brick_sums(split, labels, half)
    core_a, labels, own = core_sum(
        keep, across_cores(send), [labels, displacement], "core_sum_a"
    )
    send, keep = cell_sums(CHUNKS[1], per_octant, grain_ids, labels, table, half)
    flip = lax.axis_size("fe") // 4
    (kept, sent), own, send = plane_sum(
        across_plane(core_a), [own, send], [flip, flip], "plane_sum_a"
    )
    received = to_relative(sent, 0, 0, 0, flip)
    core_b = last_core_sum(keep, across_cores(send), own)
    while flip > 2:
        flip //= 2
        (kept, sent) = plane_sum([kept, received], [], [flip, flip], "height_sum_a")[0]
        received = to_relative(sent, 0, 0, 0, flip)
    first, *second = last_sum(kept, received, across_plane(core_b), 3)
    stress_new, nodal = element_update(
        first, across_height(second), displacement, stress_old, resistance, quad_weights
    )
    forces = nodal[0] + passed_along(nodal[1], "fe", 1)
    return (stress_new, forces)


def solution(mesh):
    placed = (
        P(None, ("ca", "fe")),
        P(),
        P(("ca", "fe")),
        P(("ca", "fe"), None),
        P(("ca", "fe")),
        P(None, ("ca", "fe"), None),
        P(None, None, ("ca", "fe")),
        P(None, None, ("ca", "fe")),
        P(None, ("ca", "fe")),
    )
    return jax.shard_map(
        body,
        mesh=mesh,
        in_specs=placed,
        out_specs=(P(None, None, ("ca", "fe")), P(None, ("ca", "fe"), None)),
        check_vma=False,
    )
```
